32 devices in a mesh: seq: 4 (over y, core), fsdp: 8 (over z, x).
Axes of the slice: x: 2, y: 2, z: 4, core: 2. Of those that a mesh axis runs over, the one named last changes fastest.
Arguments:
- tokens: bfloat16 [8, 2048, 1024], P('fsdp', 'seq'), may hold values from -6 to 6
- value_routes: int32 [8, 2048, 4, 2], P('fsdp', 'seq'), may hold values from 0 to 4, all different within a row
- output_routes: int32 [8, 2048, 4, 2], P('fsdp', 'seq'), may hold values from 0 to 4, all different within a row
- cont_gap: int32 [2, 4], replicated, may hold values from 0 to 4095
- query_weight: bfloat16 [1024, 448], P('fsdp'), may hold values from -0.1875 to 0.1875
- key_weight: bfloat16 [1024, 448], P('fsdp'), may hold values from -0.1875 to 0.1875
- value_weight: bfloat16 [1024, 2240], P('fsdp'), may hold values from -0.1875 to 0.1875
- value_router: bfloat16 [1024, 20], P('fsdp'), may hold values from -0.125 to 0.125
- output_router: bfloat16 [1024, 20], P('fsdp'), may hold values from -0.125 to 0.125
- output_weight: bfloat16 [2240, 1024], P('fsdp'), may hold values from -2 to 2
- norm_gain: bfloat16 [1024], P('fsdp'), may hold values from 0.5 to 1.5
- norm_bias: bfloat16 [1024], P('fsdp'), may hold values from -2 to 2
- inner_weight: bfloat16 [1024, 4096], P('fsdp'), may hold values from -0.1875 to 0.1875
- outer_weight: bfloat16 [4096, 1024], P('fsdp'), may hold values from -0.09375 to 0.09375
- cotangent: bfloat16 [8, 2048, 1024], P('fsdp', 'seq'), may hold values from -6 to 6
Outputs:
- layer_out: bfloat16 [8, 2048, 1024], P('fsdp', 'seq')
- d_tokens: float32 [8, 2048, 1024], P('fsdp', 'seq')
- grad_query_weight: float32 [1024, 448], P('fsdp')
- grad_key_weight: float32 [1024, 448], P('fsdp')
- grad_value_weight: float32 [1024, 2240], P('fsdp')
- grad_value_router: float32 [1024, 20], P('fsdp')
- grad_output_router: float32 [1024, 20], P('fsdp')
- grad_output_weight: float32 [2240, 1024], P('fsdp')
- grad_norm_gain: float32 [1024], P('fsdp')
- grad_norm_bias: float32 [1024], P('fsdp')
- grad_inner_weight: float32 [1024, 4096], P('fsdp')
- grad_outer_weight: float32 [4096, 1024], P('fsdp')
The draws below stay inside these ranges and needn't reach their ends.
All inputs are finite; a program needn't handle non-finite values.
Results may differ from the reference program's by a relative error of at most 0.017.
Values may be sent and summed in bfloat16 or wider, within the bound.
A program may use at most 192 MiB of HBM per device.

```python
import jax
import jax.numpy as jnp
from jax import lax

D = 1024
FF = 4096
HEADS = 4
DH = 112
EXP = 5
TOP = 2
CONT = 1024
GSLOTS = 4
SLOT_TOK = 2048
SLOTS = 8
GROUPS = 2
PROMPT = 4096
NCONT = 4
BLOCK = 512


def with_ends(drawn, rng, least, top_value):
    spot = [jax.random.randint(jax.random.fold_in(rng, axis), (), 0, length) for axis, length in enumerate(drawn.shape)]
    longest = drawn.shape.index(max(drawn.shape))
    next_to = spot[:longest] + [(spot[longest] + 1) % drawn.shape[longest]] + spot[longest + 1:]
    return drawn.at[tuple(spot)].set(least).at[tuple(next_to)].set(top_value)


def shard_levels(stream_key, shape, pieces, least, top_value):
    loudness = 1.0
    for position, shards_of in pieces:
        draws = jax.random.uniform(jax.random.fold_in(jax.random.fold_in(stream_key, 6), position), (shards_of,), jnp.float32, least / len(pieces), top_value / len(pieces))
        loudness = loudness * jnp.repeat(jnp.exp(draws), shape[position] // shards_of).reshape((-1,) + (1,) * (len(shape) - 1 - position))
    return loudness


def different_ones(stream_key, rows, count, top, lift):
    ranking = jax.random.permutation(jax.random.fold_in(stream_key, 1), count)
    boost = ranking
    for power in range(3):
        boost = boost * boost // count
    boost = boost * lift // count
    lots = jax.random.randint(jax.random.fold_in(stream_key, 2), (rows, count), 0, 4096) + boost
    fixed_rows = jax.random.permutation(jax.random.fold_in(stream_key, 3), rows)[jnp.arange(count) % rows]
    lots = jnp.where(jnp.arange(rows)[:, None] == fixed_rows[None, :], 1 << 14, lots)
    priority = lots * count + jnp.arange(count)
    return lax.top_k(priority.astype(jnp.int32), top)[1].astype(jnp.int32)


def scatter_about(rng, dims, deviation, reach, shards=(), kind=jnp.bfloat16):
    drawn = deviation * jax.random.normal(rng, dims, jnp.float32)
    if shards:
        drawn = drawn * shard_levels(rng, dims, shards, -0.22, 0.18)
    return jnp.clip(drawn, -reach, reach).astype(kind)


def setup_inputs(seed: int = 0) -> dict:
    key_list = jax.random.split(jax.random.key(seed), 16)
    tokens = scatter_about(key_list[0], (SLOTS, SLOT_TOK, D), 1.0, 6.0, ((0, 8), (1, 4)))
    value_routes = different_ones(key_list[1], SLOTS * SLOT_TOK * HEADS, EXP, TOP, 3276).reshape((SLOTS, SLOT_TOK, HEADS, TOP))
    output_routes = different_ones(key_list[2], SLOTS * SLOT_TOK * HEADS, EXP, TOP, 3276).reshape((SLOTS, SLOT_TOK, HEADS, TOP))
    cont_gap = with_ends(jax.random.randint(key_list[3], (GROUPS, NCONT), 0, PROMPT), jax.random.fold_in(key_list[3], 1), 0, PROMPT - 1).astype(jnp.int32)
    query_weight = scatter_about(key_list[4], (D, HEADS * DH), D ** -0.5, 0.1875, ((0, 8),))
    key_weight = scatter_about(key_list[5], (D, HEADS * DH), D ** -0.5, 0.1875, ((0, 8),))
    value_weight = scatter_about(key_list[6], (D, HEADS * EXP * DH), D ** -0.5, 0.1875, ((0, 8),))
    value_router = scatter_about(key_list[7], (D, HEADS * EXP), (2 * D) ** -0.5, 0.125, ((0, 8),))
    output_router = scatter_about(key_list[8], (D, HEADS * EXP), (2 * D) ** -0.5, 0.125, ((0, 8),))
    output_weight = scatter_about(key_list[9], (HEADS * EXP * DH, D), 8 ** -0.5, 2.0, ((0, 8),))
    norm_gain = jnp.clip(1.0 + 0.1 * jax.random.normal(key_list[10], (D,), jnp.float32), 0.5, 1.5).astype(jnp.bfloat16)
    norm_bias = scatter_about(key_list[11], (D,), 0.3, 2.0, ((0, 8),))
    inner_weight = scatter_about(key_list[12], (D, FF), D ** -0.5, 0.1875, ((0, 8),))
    outer_weight = scatter_about(key_list[13], (FF, D), FF ** -0.5, 0.09375, ((0, 8),))
    cotangent = scatter_about(key_list[14], (SLOTS, SLOT_TOK, D), 1.0, 6.0, ((0, 8), (1, 4)))
    return {"tokens": tokens, "value_routes": value_routes, "output_routes": output_routes, "cont_gap": cont_gap, "query_weight": query_weight, "key_weight": key_weight, "value_weight": value_weight, "value_router": value_router, "output_router": output_router, "output_weight": output_weight, "norm_gain": norm_gain, "norm_bias": norm_bias, "inner_weight": inner_weight, "outer_weight": outer_weight, "cotangent": cotangent}


HIGH = lax.Precision.HIGHEST
EPSILON = 1e-05
NEGATIVE = -1e+30

@jax.custom_vjp
def low(v):
    return lax.optimization_barrier(v.astype(jnp.bfloat16)).astype(jnp.float32)

@jax.custom_vjp
def low_back(v):
    return v

def low_keep(v):
    return (low(v), None)

def low_pass(kept, grad):
    return (grad,)

def back_keep(v):
    return (v, None)

def back_low(kept, grad):
    return (low(grad),)
low.defvjp(low_keep, low_pass)
low_back.defvjp(back_keep, back_low)

def both_ways(value):
    return low_back(low(value))

def smooth_gate(value):
    return jax.nn.gelu(value, approximate=True)

def group_positions(gaps):
    token_index = jnp.arange(GSLOTS * SLOT_TOK, dtype=jnp.int32)
    later = jnp.maximum(token_index - PROMPT, 0)
    cont_index = later // CONT
    segment_ids = jnp.where(token_index < PROMPT, 0, cont_index + 1).astype(jnp.int32)
    places = jnp.where(token_index < PROMPT, token_index, PROMPT + gaps[cont_index] + later % CONT).astype(jnp.int32)
    return (places, segment_ids)

def visible(query_place, query_segment, key_place, key_segment):
    before = key_place[None, :] <= query_place[:, None]
    from_prompt = (key_segment[None, :] == 0) & ((query_segment[:, None] > 0) | before)
    same_part = (key_segment[None, :] == query_segment[:, None]) & before
    return from_prompt | same_part

def head_block(inputs, key_rows, values, places, segment_ids, slope):
    query_block, query_place, query_segment = inputs
    raw_scores = low_back(jnp.dot(query_block, key_rows.T, precision=HIGH))
    distance = jnp.maximum(query_place[:, None] - places[None, :], 0).astype(jnp.float32)
    scores = raw_scores * DH ** (-0.5) + slope * jnp.log1p(distance)
    allowed = visible(query_place, query_segment, places, segment_ids)
    weights = jax.nn.softmax(jnp.where(allowed, scores, NEGATIVE), axis=-1)
    return jnp.dot(low(weights), values, precision=HIGH)

def make_block(key_rows, values, places, segment_ids, slope):

    def block_fn(inputs):
        return head_block(inputs, key_rows, values, places, segment_ids, slope)
    return jax.checkpoint(block_fn)

def attention(queries, key_rows, values, places, segment_ids):
    block_count = queries.shape[0] // BLOCK
    outputs = []
    for head_number in range(HEADS):
        first_col = head_number * DH
        query_blocks = queries[:, first_col:first_col + DH].reshape(block_count, BLOCK, DH)
        run_block = make_block(key_rows[:, first_col:first_col + DH], values[:, first_col:first_col + DH], places, segment_ids, -0.5 * 0.5 ** head_number)
        result = lax.map(run_block, (query_blocks, places.reshape(block_count, BLOCK), segment_ids.reshape(block_count, BLOCK)))
        outputs.append(result.reshape(block_count * BLOCK, DH))
    return jnp.concatenate(outputs, axis=1)

def forward(tokens, query_weight, key_weight, value_weight, value_router, output_router, output_weight, norm_gain, norm_bias, inner_weight, outer_weight, masks, places, segment_ids):
    value_mask, output_mask = masks
    token_count = tokens.shape[0]
    queries = both_ways(jnp.dot(tokens, query_weight, precision=HIGH))
    key_rows = both_ways(jnp.dot(tokens, key_weight, precision=HIGH))
    expert_values = low_back(jnp.dot(tokens, value_weight, precision=HIGH))
    value_logit = low_back(jnp.dot(tokens, value_router, precision=HIGH))
    value_gate = jax.nn.sigmoid(value_logit) * value_mask
    values = both_ways(lax.optimization_barrier(jnp.sum(value_gate.reshape(token_count, HEADS, EXP, 1) * expert_values.reshape(token_count, HEADS, EXP, DH), axis=2)).reshape(token_count, HEADS * DH))
    output_logit = low_back(jnp.dot(tokens, output_router, precision=HIGH))
    output_gate = jax.nn.sigmoid(output_logit) * output_mask
    attended = both_ways(attention(queries, key_rows, values, places, segment_ids))
    mixed = low((output_gate.reshape(token_count, HEADS, EXP, 1) * attended.reshape(token_count, HEADS, 1, DH)).reshape(token_count, HEADS * EXP * DH))
    branch = low_back(jnp.dot(mixed, output_weight, precision=HIGH))
    residual = tokens + branch
    average = lax.optimization_barrier(jnp.mean(residual, axis=-1, keepdims=True))
    centred = residual - average
    inverse = lax.rsqrt(lax.optimization_barrier(jnp.mean(centred * centred, axis=-1, keepdims=True)) + EPSILON)
    scaled = low(centred * inverse * norm_gain + norm_bias)
    inner = low_back(jnp.dot(scaled, inner_weight, precision=HIGH))
    active = low(smooth_gate(inner))
    return residual + jnp.dot(active, outer_weight, precision=HIGH)

def reference(tokens, value_routes, output_routes, cont_gap, query_weight, key_weight, value_weight, value_router, output_router, output_weight, norm_gain, norm_bias, inner_weight, outer_weight, cotangent):
    group_len = GSLOTS * SLOT_TOK
    params = tuple((array.astype(jnp.float32) for array in (query_weight, key_weight, value_weight, value_router, output_router, output_weight, norm_gain, norm_bias, inner_weight, outer_weight)))
    expert_ids = jnp.arange(EXP, dtype=jnp.int32)

    def route_mask(routes):
        matched = jnp.any(routes[:, :, :, None] == expert_ids, axis=2)
        return matched.astype(jnp.float32).reshape(routes.shape[0], HEADS * EXP)

    def one_group(running, group_inputs):
        group_tokens, group_value_routes, group_output_routes, group_gaps, group_cotangent = group_inputs
        places, segment_ids = group_positions(group_gaps)
        masks = (route_mask(group_value_routes), route_mask(group_output_routes))

        def closed(*arrays):
            return forward(*arrays, masks, places, segment_ids)
        result, pullback = jax.vjp(closed, group_tokens, *params)
        gradients = pullback(group_cotangent)
        running = tuple((earlier + addend for earlier, addend in zip(running, gradients[1:])))
        return (running, (result.astype(jnp.bfloat16), gradients[0]))
    inputs = (tokens.astype(jnp.float32).reshape(GROUPS, group_len, D), value_routes.reshape(GROUPS, group_len, HEADS, TOP), output_routes.reshape(GROUPS, group_len, HEADS, TOP), cont_gap, cotangent.astype(jnp.float32).reshape(GROUPS, group_len, D))
    zero_sums = tuple((jnp.zeros(array.shape, jnp.float32) for array in params))
    totals, (layer_out, d_tokens) = lax.scan(one_group, zero_sums, inputs)
    grad_query, grad_key, grad_value, grad_value_router, grad_output_router, grad_output, grad_gain, grad_bias, grad_inner, grad_outer = totals
    return (layer_out.reshape(SLOTS, SLOT_TOK, D), d_tokens.reshape(SLOTS, SLOT_TOK, D), grad_query, grad_key, grad_value, grad_value_router, grad_output_router, grad_output, grad_gain, grad_bias, grad_inner, grad_outer)
```

```python
import functools
import jax
import jax.numpy as jnp
from jax import lax
from jax.experimental import pallas as pl
from jax.experimental.pallas import tpu as pltpu
from jax.sharding import PartitionSpec as P

HEADS = 4
DH = 112
EXP = 5
CONT = 1024
GSLOTS = 4
PSLOTS = 2
BLOCK = 512
LANES = 128
EPSILON = 1e-05
NEGATIVE = -1e30
LOG2E = 1.4426950408889634
MESH = pl.DeviceIdType.MESH
ANY = pl.BlockSpec(memory_space=pl.ANY)
VMEM = pl.BlockSpec(memory_space=pltpu.VMEM)
SMEM = pl.BlockSpec(memory_space=pltpu.SMEM)
DMA = pltpu.SemaphoreType.DMA

QCOLS = HEADS * DH
VCOLS = HEADS * EXP * DH
ROUTERS = 2 * QCOLS + VCOLS
NORM = ROUTERS + 2 * HEADS * EXP
JOINT = 3328
SPLITS = {"joint": (640, 512), "output": (0, 256), "inner": (768, 640), "outer": (256, 128)}


def ring_place(index, count):
    return (index // 2) * (1 - index % 2) + (count - 1 - index // 2) * (index % 2)


def ring_index(place, count):
    upper = place // (count // 2)
    return 2 * place * (1 - upper) + (2 * (count - 1 - place) + 1) * upper


def enter(devices):
    barrier = pltpu.get_barrier_semaphore()
    for device in devices:
        pl.semaphore_signal(barrier, inc=1, device_id=device, device_id_type=MESH)
    pl.semaphore_wait(barrier, len(devices))


class Ring:
    def __init__(self, count, splits):
        self.count, self.splits = count, splits
        self.seq, self.fsdp = lax.axis_index("seq"), lax.axis_index("fsdp")
        self.plane, self.core = self.seq // 2, self.seq % 2
        self.place = ring_place(self.fsdp, count)
        self.right = (self.seq, ring_index((self.place + 1) % count, count))
        self.left = (self.seq, ring_index((self.place + count - 1) % count, count))
        self.core_mate = (self.seq + 1 - 2 * self.core, self.fsdp)
        self.plane_mate = ((self.seq + 2) % 4, self.fsdp)
        self.far = count // 2

    def neighbours(self):
        return [self.right, self.left, self.core_mate, self.plane_mate]

    def reach(self, kind, way):
        return self.far if kind == way else self.count - 1 - self.far

    def kinds(self, t):
        return [kind for kind in (1, 0) if self.splits[t][kind] > 0]

    def half(self, t):
        return self.splits[t][0] + 2 * self.splits[t][1]

    def cols(self, t, kind, plane, core):
        both, single = self.splits[t]
        if kind == 0:
            return pl.ds(pl.multiple_of(core * self.half(t), LANES), both)
        return pl.ds(pl.multiple_of(core * self.half(t) + both + plane * single, LANES), single)

    def behind(self, way, k):
        step = self.count - k if way == 0 else k
        return ring_index((self.place + step) % self.count, self.count)

    def next(self, way):
        return self.right if way == 0 else self.left

    def slot(self, kind, way, k):
        return k - 1 if way == 0 else self.reach(kind, 0) + k - 1


class Gather(Ring):
    def __init__(self, count, splits, shards, at, send, recv, local):
        super().__init__(count, splits)
        self.shards, self.at, self.send, self.recv, self.local = shards, at, send, recv, local

    @staticmethod
    def sems(count, tensors):
        return [DMA((6 * tensors * (count - 1),)), DMA((6 * tensors * (count - 1),)), DMA((tensors,))]

    def copy(self, src, dst, group, t, slot, device):
        i = (group * len(self.splits) + t) * (self.count - 1) + slot
        return pltpu.make_async_remote_copy(
            src, dst, self.send.at[i], self.recv.at[i], device_id=device, device_id_type=MESH
        )

    def same(self, group, t, kind, way, k, plane, core, device):
        ref = self.at(t, self.behind(way, k), self.cols(t, kind, plane, core))
        return self.copy(ref, ref, group, t, self.slot(kind, way, k), device)

    def hop(self, t, kind, way, k):
        if k > 1:
            ref = self.at(t, self.behind(way, k - 1), self.cols(t, kind, self.plane, self.core))
            return self.copy(ref, ref, kind, t, self.slot(kind, way, k), self.next(way))
        cols = self.cols(t, kind, self.plane, self.core)
        return self.copy(
            self.shards[t].at[:, cols], self.at(t, self.fsdp, cols), kind, t, self.slot(kind, way, 1), self.next(way)
        )

    def arrived(self, t, kind, way, k):
        return self.same(kind, t, kind, way, k, self.plane, self.core, self.next(way))

    def to_core(self, t, kind, way, k, core):
        return self.same(2 + kind, t, kind, way, k, self.plane, core, self.core_mate)

    def to_plane(self, t, way, k, plane):
        return self.same(4, t, 1, way, k, plane, self.core, self.plane_mate)

    def plane_to_core(self, t, way, k, core):
        return self.same(5, t, 1, way, k, 1 - self.plane, core, self.core_mate)

    def own(self, t):
        return pltpu.make_async_copy(self.shards[t], self.at(t, self.fsdp, slice(None)), self.local.at[t])

    def start(self, t):
        for kind in self.kinds(t):
            for way in (0, 1):
                if self.reach(kind, way):
                    self.hop(t, kind, way, 1).start()
        self.own(t).start()

    def arrive(self, t, k):
        for kind in self.kinds(t):
            for way in (0, 1):
                if k <= self.reach(kind, way):
                    self.arrived(t, kind, way, k).wait_recv()
                    if k < self.reach(kind, way):
                        self.hop(t, kind, way, k + 1).start()
                    if kind:
                        self.to_plane(t, way, k, self.plane).start()
                    self.to_core(t, kind, way, k, self.core).start()

    def plane_arrive(self, t, k):
        if 1 in self.kinds(t):
            for way in (0, 1):
                if k <= self.reach(1, way):
                    self.to_plane(t, way, k, 1 - self.plane).wait_recv()
                    self.plane_to_core(t, way, k, self.core).start()

    def finish(self, t):
        self.own(t).wait()
        for kind in self.kinds(t):
            for way in (0, 1):
                for k in range(1, self.reach(kind, way) + 1):
                    self.hop(t, kind, way, k).wait_send()
                    self.to_core(t, kind, way, k, self.core).wait_send()
                    self.to_core(t, kind, way, k, 1 - self.core).wait_recv()
                    if kind:
                        self.to_plane(t, way, k, self.plane).wait_send()
                        self.plane_to_core(t, way, k, self.core).wait_send()
                        self.plane_to_core(t, way, k, 1 - self.core).wait_recv()

    def events(self):
        tensors = range(len(self.splits))
        out = []
        for k in range(1, self.far + 1):
            for t in tensors:
                out.append(functools.partial(self.arrive, t, k))
                if k > 1:
                    out.append(functools.partial(self.plane_arrive, t, k - 1))
        for t in tensors:
            out.append(functools.partial(self.plane_arrive, t, self.far))
        for t in tensors:
            out.append(functools.partial(self.finish, t))
        return out


TABLE = 5632
TABLE_ZERO = 5120
TURNED_ZERO = 512


def route_lanes(routes, lane):
    hit = None
    for head in range(2 * HEADS):
        for choice in range(2):
            place = head * EXP + routes[:, 2 * head + choice : 2 * head + choice + 1]
            here = lane == place
            hit = here if hit is None else hit | here
    return hit.astype(jnp.float32)


def project_kernel(count, query, key, value, routers, tokens, routes, gaps, joint, qkv, experts, gates, norms, tables, turned_tables,
                   shard, product, send, recv, local):
    rows = shard.shape[0]
    splits = (SPLITS["joint"],)
    at = lambda t, g, cols: joint.at[pl.ds(pl.multiple_of(g * rows, rows), rows), cols]
    ring = Gather(count, splits, [shard], at, send, recv, local)
    wide = jnp.concatenate([ref[...].astype(jnp.float32) for ref in (query, key, value, routers)], axis=1)
    shard[...] = wide.astype(jnp.bfloat16)
    enter(ring.neighbours())
    ring.start(0)
    slope = jnp.float32(0.0)
    for head in range(HEADS):
        slope = jnp.where(ring.seq // 1 == head, -0.5 * 0.5**head * LOG2E, slope)
    group = ring.fsdp // GSLOTS
    pair = jnp.maximum(ring.fsdp % GSLOTS - PSLOTS, 0) * 2
    gap_values = [jnp.int32(0), gaps[group, pair], gaps[group, pair + 1]]

    def table_column(step, carry):
        start = pl.multiple_of(step * 256, 256)
        lanes = lax.broadcasted_iota(jnp.int32, (8, 256 + LANES), 1) + (start - LANES)
        for which in range(3):
            for turned in range(2):
                if turned:
                    distance = lanes - TURNED_ZERO + gap_values[which]
                else:
                    distance = TABLE_ZERO - lanes + gap_values[which]
                bias = slope * jnp.log(1.0 + jnp.maximum(distance, 0).astype(jnp.float32))
                bias = jnp.where(distance >= 0, bias, NEGATIVE)
                wide = jnp.broadcast_to(bias[:1], (LANES, 256 + LANES))
                rolled = pltpu.roll(wide, 0, 1, stride=1, stride_axis=0)
                target = turned_tables if turned else tables
                target[which, :, pl.ds(start, 256)] = rolled[:, LANES:]
        return carry

    events = ring.events()
    cut = max(1, (TABLE // 256) // max(1, ring.far))
    done = 0
    for i, event in enumerate(events):
        upto = min(TABLE // 256, (i + 1) * cut)
        if upto > done:
            lax.fori_loop(done, upto, table_column, 0)
            done = upto
        event()
    if done < TABLE // 256:
        lax.fori_loop(done, TABLE // 256, table_column, 0)

    def column(step, carry):
        cols = pl.ds(pl.multiple_of(step * 256, 256), 256)
        product[:, cols] = jnp.dot(tokens[...], joint[:, cols], preferred_element_type=jnp.float32)
        return carry

    lax.fori_loop(0, JOINT // 256, column, 0)
    norm_tile = NORM // LANES * LANES
    turned_norm = joint[:, norm_tile : norm_tile + LANES].astype(jnp.float32).T
    norms[...] = turned_norm[NORM - norm_tile : NORM - norm_tile + 8]
    logits = product[:, ROUTERS : ROUTERS + 2 * HEADS * EXP]
    local_rows = tokens.shape[0]
    wide = jnp.concatenate([logits, jnp.zeros((local_rows, LANES - 2 * HEADS * EXP), jnp.float32)], axis=1)
    lane = lax.broadcasted_iota(jnp.int32, (local_rows, LANES), 1)
    mask = route_lanes(routes[...], lane)
    gate = 1.0 / (1.0 + jnp.exp(-wide))
    gates[0] = gate * mask
    gates[1] = gate * mask * (1.0 - gate)
    pad = jnp.zeros((local_rows, LANES - DH), jnp.float32)
    ones = jnp.ones((local_rows, LANES - DH), jnp.float32)
    for head in range(HEADS):
        first = head * DH
        qkv[head, 0] = jnp.concatenate([product[:, first : first + DH], pad], axis=1).astype(jnp.bfloat16)
        first = QCOLS + head * DH
        qkv[head, 1] = jnp.concatenate([product[:, first : first + DH], pad], axis=1).astype(jnp.bfloat16)
        total = None
        for expert in range(EXP):
            which = head * EXP + expert
            first = 2 * QCOLS + which * DH
            piece = product[:, first : first + DH]
            experts[which] = jnp.concatenate([piece, pad], axis=1).astype(jnp.bfloat16)
            term = piece * gates[0, :, which : which + 1]
            total = term if total is None else total + term
        qkv[head, 2] = jnp.concatenate([total, ones], axis=1).astype(jnp.bfloat16)


def project(count, query, key, value, routers, tokens, routes, gaps):
    rows, (shard_rows, _) = tokens.shape[0], query.shape
    f32, bf = jnp.float32, jnp.bfloat16
    return pl.pallas_call(
        functools.partial(project_kernel, count),
        out_shape=[
            jax.ShapeDtypeStruct((shard_rows * count, JOINT), bf),
            jax.ShapeDtypeStruct((HEADS, 3, rows, LANES), bf),
            jax.ShapeDtypeStruct((HEADS * EXP, rows, LANES), bf),
            jax.ShapeDtypeStruct((2, rows, LANES), f32),
            jax.ShapeDtypeStruct((8, shard_rows * count), f32),
            jax.ShapeDtypeStruct((3, LANES, TABLE), f32),
            jax.ShapeDtypeStruct((3, LANES, TABLE), f32),
        ],
        in_specs=[VMEM] * 6 + [SMEM],
        out_specs=[VMEM] * 7,
        scratch_shapes=[pltpu.VMEM((shard_rows, JOINT), bf), pltpu.VMEM((rows, JOINT), f32)] + Gather.sems(count, 1),
        compiler_params=pltpu.CompilerParams(collective_id=1, has_side_effects=True, vmem_limit_bytes=56 << 20),
    )(query, key, value, routers, tokens, routes, gaps)


def seq_mates(ring):
    return [ring.core_mate, ring.plane_mate, (3 - ring.seq, ring.fsdp)]


def slot_mates(ring):
    f = ring.fsdp
    return [(ring.seq, f + 1 - 2 * (f % 2)), (ring.seq, f + 2 - 4 * ((f // 2) % 2))]


def tile_place(slot, seq, phase, key_block, query_block):
    cont = slot // PSLOTS
    own = 1 - jnp.minimum(phase, 1)
    piece = jnp.where(slot == 3, 2 - phase, phase - 1)
    source = jnp.where(phase == 0, 0, 1 + piece)
    first = cont * 2 * (query_block // 2)
    active = jnp.where(
        phase == 0,
        (key_block <= query_block) & (key_block >= first),
        jnp.where(phase == 1, slot >= 1, slot >= 2),
    )
    far_column = jnp.where(
        cont == 1,
        2048 * piece + BLOCK * key_block - BLOCK * (query_block % 2) - 4096,
        BLOCK * key_block - 2048 - BLOCK * query_block,
    )
    column = jnp.where(phase == 0, BLOCK * (key_block - query_block), far_column)
    table = jnp.where((phase > 0) & (cont == 1), 1 + query_block // 2, 0)
    return source, active, table, column


def block_rows(block):
    return pl.ds(pl.multiple_of(block * BLOCK, BLOCK), BLOCK)


def attend_kernel(count, splits, steps, qkv, tables, *refs):
    T = len(splits)
    shards, refs = refs[:T], refs[T:]
    att, store, outputs, logs = refs[:4]
    fulls, refs = refs[4 : 4 + T], refs[4 + T :]
    acc, top, att_low, kv_send, kv_recv, q_send, q_recv, sh_send, sh_recv, out_send, out_recv, here = refs[:12]
    at = lambda t, g, cols: fulls[t].at[g, :, cols]
    ring = Gather(count, splits, shards, at, *refs[12:])
    seq, slot = ring.seq, ring.fsdp % GSLOTS
    mates, (x_mate, z_mate) = seq_mates(ring), slot_mates(ring)
    enter(ring.neighbours() + mates[2:] + [x_mate, z_mate])

    def remote(src, dst, send, recv, device):
        return pltpu.make_async_remote_copy(src, dst, send, recv, device_id=device, device_id_type=MESH)

    mine = block_rows(seq)

    def kv_copy(mate):
        return remote(qkv.at[mate[0], pl.ds(1, 2)], store.at[pl.ds(1, 2), mine], kv_send.at[mate[0]], kv_recv.at[seq], mate)

    def q_copy(mate):
        return remote(qkv.at[mate[0], 0], store.at[0, mine], q_send.at[mate[0]], q_recv.at[seq], mate)

    for mate in mates[1:] + mates[:1]:
        kv_copy(mate).start()
    own_copy = pltpu.make_async_copy(qkv.at[seq], store.at[pl.ds(0, 3), mine], here.at[0])
    own_copy.start()
    for mate in mates[1:] + mates[:1]:
        q_copy(mate).start()
    acc[...] = jnp.zeros_like(acc)
    top[...] = jnp.full_like(top, NEGATIVE)

    def far_rows(piece, chunk):
        return store.at[pl.ds(3 + 2 * piece, 2), block_rows(chunk)]

    def first_hop(chunk, way):
        src = store.at[pl.ds(1, 2), block_rows(chunk)]
        piece = slot % 2
        return remote(src, far_rows(piece, chunk), sh_send.at[4 * way + chunk], sh_recv.at[4 * piece + chunk],
                      x_mate if way == 0 else z_mate)

    def second_hop(chunk):
        piece = slot % 2
        return remote(far_rows(piece, chunk), far_rows(piece, chunk), sh_send.at[8 + chunk], sh_recv.at[4 * piece + chunk], x_mate)

    def share(chunk):
        @pl.when(slot < 2)
        def _():
            first_hop(chunk, 1).start()

        @pl.when(slot == 0)
        def _():
            first_hop(chunk, 0).start()

    def pass_on(chunk):
        @pl.when(slot >= 1)
        def _():
            piece = jnp.where(slot == 3, 1, 0)
            remote(far_rows(piece, chunk), far_rows(piece, chunk), sh_send.at[chunk], sh_recv.at[4 * piece + chunk], x_mate).wait_recv()

        @pl.when(slot >= 2)
        def _():
            second_hop(chunk).start()

    def last_piece(chunk):
        @pl.when(slot >= 2)
        def _():
            piece = 3 - slot
            remote(far_rows(piece, chunk), far_rows(piece, chunk), sh_send.at[chunk], sh_recv.at[4 * piece + chunk], x_mate).wait_recv()

    own_copy.wait()
    share(seq)
    for mate in mates:
        other = mate[0]
        src = store.at[pl.ds(1, 2), block_rows(other)]
        remote(src, src, kv_send.at[other], kv_recv.at[other], mate).wait_recv()
        share(other)
    for mate in mates:
        src = store.at[0, block_rows(mate[0])]
        remote(src, src, q_send.at[mate[0]], q_recv.at[mate[0]], mate).wait_recv()

    def tile(step):
        phase, key_block, query_block = step // 16, (step // 4) % 4, step % 4
        source, active, table, column = tile_place(slot, seq, phase, key_block, query_block)

        @pl.when(active)
        def _():
            rows = block_rows(query_block)
            keys = store[1 + 2 * source, block_rows(key_block), :]
            values = store[2 + 2 * source, block_rows(key_block), :]
            scores = lax.dot_general(store[0, rows, :], keys, (((1,), (1,)), ((), ())), preferred_element_type=jnp.float32)
            bias = jnp.concatenate(
                [tables[table, :, pl.ds(pl.multiple_of(column + TABLE_ZERO - LANES * part, LANES), BLOCK)] for part in range(BLOCK // LANES)],
                axis=0,
            )
            scores = scores * (DH**-0.5 * LOG2E) + bias
            before = top[rows, :]
            after = jnp.maximum(before, jnp.max(scores, axis=1, keepdims=True))
            factor = jnp.exp2(before - after)
            terms = jnp.exp2(scores - after[:, :1])
            acc[rows, :] = acc[rows, :] * factor + jnp.dot(terms.astype(jnp.bfloat16), values, preferred_element_type=jnp.float32)
            top[rows, :] = after

    events = {}
    for chunk in range(4):
        events.setdefault(4 * chunk, []).append(functools.partial(pass_on, chunk))
        events.setdefault(32 + 4 * chunk, []).append(functools.partial(last_piece, chunk))
    begin, gap = steps
    events.setdefault(begin, []).extend([functools.partial(ring.start, t) for t in range(T)])
    rest = []
    for i, event in enumerate(ring.events()):
        step = begin + gap * (i + 1)
        if step < 48:
            events.setdefault(step, []).append(event)
        else:
            rest.append(event)

    def step_body(step, carry):
        for when, actions in sorted(events.items()):
            @pl.when(step == when)
            def _():
                for action in actions:
                    action()
        tile(step)
        return carry

    lax.fori_loop(0, 48, step_body, 0)
    total = acc[:, DH : DH + 1]
    result = acc[...] / total
    outputs[...] = result
    log_total = top[...] + jnp.log2(total)
    for block in range(4):
        logs[:, block * BLOCK : (block + 1) * BLOCK] = log_total[block * BLOCK : (block + 1) * BLOCK].T[:8]
    att_low[...] = result.astype(jnp.bfloat16)

    def out_copy(mate):
        return remote(att_low.at[block_rows(mate[0])], att.at[seq], out_send.at[mate[0]], out_recv.at[seq], mate)

    for mate in mates[1:] + mates[:1]:
        out_copy(mate).start()
    own_out = pltpu.make_async_copy(att_low.at[mine], att.at[seq], here.at[1])
    own_out.start()
    for event in rest:
        event()
    own_out.wait()
    for mate in mates:
        kv_copy(mate).wait_send()
        q_copy(mate).wait_send()
        out_copy(mate).wait_send()
        ref = att.at[mate[0]]
        remote(ref, ref, out_send.at[mate[0]], out_recv.at[mate[0]], mate).wait_recv()
    for chunk in range(4):
        @pl.when(slot < 2)
        def _():
            first_hop(chunk, 1).wait_send()

        @pl.when(slot == 0)
        def _():
            first_hop(chunk, 0).wait_send()

        @pl.when(slot >= 2)
        def _():
            second_hop(chunk).wait_send()


def attend(count, qkv, tables, shards, splits, steps=(8, 2)):
    rows = qkv.shape[2]
    own = 4 * rows
    T = len(shards)
    return pl.pallas_call(
        functools.partial(attend_kernel, count, splits, steps),
        out_shape=[
            jax.ShapeDtypeStruct((HEADS, rows, LANES), jnp.bfloat16),
            jax.ShapeDtypeStruct((7, own, LANES), jnp.bfloat16),
            jax.ShapeDtypeStruct((own, LANES), jnp.float32),
            jax.ShapeDtypeStruct((8, own), jnp.float32),
        ]
        + [jax.ShapeDtypeStruct((count,) + w.shape, w.dtype) for w in shards],
        in_specs=[VMEM, VMEM] + [ANY] * T,
        out_specs=[VMEM] * 4 + [ANY] * T,
        scratch_shapes=[
            pltpu.VMEM((own, LANES), jnp.float32),
            pltpu.VMEM((own, LANES), jnp.float32),
            pltpu.VMEM((own, LANES), jnp.bfloat16),
            DMA((4,)), DMA((4,)), DMA((4,)), DMA((4,)), DMA((12,)), DMA((8,)), DMA((4,)), DMA((4,)), DMA((2,)),
        ]
        + Gather.sems(count, T),
        compiler_params=pltpu.CompilerParams(collective_id=2, has_side_effects=True, vmem_limit_bytes=56 << 20),
    )(qkv, tables, *shards)


class Scatter(Ring):
    def __init__(self, count, splits, parts, outs, bufs, sems):
        super().__init__(count, splits)
        self.parts, self.outs = parts, outs
        T = len(splits)
        self.mine, self.plane_in = bufs[:T], bufs[T : 2 * T]
        self.ring0, self.ring1 = bufs[2 * T : 3 * T], bufs[3 * T : 4 * T]
        self.low, self.low_in, self.done = bufs[4 * T : 5 * T], bufs[5 * T : 6 * T], bufs[6 * T : 7 * T]
        (self.load, self.plane_s, self.plane_r, self.ring_s, self.ring_r, self.end_s, self.end_r, self.put) = sems

    @staticmethod
    def scratch(count, splits, rows):
        half = [a + 2 * b for a, b in splits]
        bf = jnp.bfloat16
        out = [pltpu.VMEM((count, r, h), bf) for r, h in zip(rows, half)]
        out += [pltpu.VMEM((count, r, b), bf) for r, (a, b) in zip(rows, splits)]
        out += [pltpu.VMEM((count - 1 if a else 1, r, max(a, LANES)), bf) for r, (a, b) in zip(rows, splits)]
        out += [pltpu.VMEM((count - 1, r, b), bf) for r, (a, b) in zip(rows, splits)]
        out += [pltpu.VMEM((r, a + b), bf) for r, (a, b) in zip(rows, splits)]
        out += [pltpu.VMEM((r, a + b), bf) for r, (a, b) in zip(rows, splits)]
        out += [pltpu.VMEM((r, h), jnp.float32) for r, h in zip(rows, half)]
        T = len(splits)
        return out + [DMA((T * count,))] * 3 + [DMA((2 * T * (count - 1),))] * 2 + [DMA((2 * T,))] * 2 + [DMA((T,))]

    def dest(self, rel):
        return ring_index((self.place + rel) % self.count, self.count)

    def load_copy(self, t, rel):
        return pltpu.make_async_copy(self.parts[t].at[self.dest(rel)], self.mine[t].at[rel], self.load.at[t * self.count + rel])

    def remote(self, src, dst, s, r, i, device):
        return pltpu.make_async_remote_copy(src, dst, s.at[i], r.at[i], device_id=device, device_id_type=MESH)

    def single(self, t, plane):
        both, single = self.splits[t]
        return pl.ds(pl.multiple_of(both + plane * single, LANES), single)

    def plane_copy(self, t, rel):
        src = self.mine[t].at[rel, :, self.single(t, 1 - self.plane)]
        return self.remote(src, self.plane_in[t].at[rel], self.plane_s, self.plane_r, t * self.count + rel, self.plane_mate)

    def rels(self, D):
        return sorted({D % self.count, (-D) % self.count})

    def order(self):
        out = []
        for D in range(self.far, -1, -1):
            out += self.rels(D)
        return out

    def start(self, t):
        for rel in self.order():
            self.load_copy(t, rel).start()

    def prepare(self, t, D):
        for rel in self.rels(D):
            if self.parts:
                self.load_copy(t, rel).wait()
            self.plane_copy(t, rel).start()

    def buffer(self, t, kind, slot):
        if kind:
            return self.ring1[t].at[slot]
        return self.ring0[t].at[slot]

    def own_ref(self, t, kind, rel):
        if kind:
            return self.mine[t].at[rel, :, self.single(t, self.plane)]
        return self.mine[t].at[rel, :, pl.ds(0, self.splits[t][0])]

    def ring_copy(self, t, kind, way, D):
        slot = self.slot(kind, way, D)
        if D == self.reach(kind, way):
            src = self.own_ref(t, kind, D % self.count if way == 0 else (-D) % self.count)
        else:
            src = self.buffer(t, kind, self.slot(kind, way, D + 1))
        i = (2 * t + kind) * (self.count - 1) + slot
        return self.remote(src, self.buffer(t, kind, slot), self.ring_s, self.ring_r, i, self.next(way))

    def ring_wait(self, t, kind, way, D):
        slot = self.slot(kind, way, D)
        ref = self.buffer(t, kind, slot)
        i = (2 * t + kind) * (self.count - 1) + slot
        self.remote(ref, ref, self.ring_s, self.ring_r, i, self.next(way)).wait_recv()

    def combine(self, t, D):
        for rel in self.rels(D):
            self.plane_copy(t, rel).wait_send()
            ref = self.plane_in[t].at[rel]
            self.remote(ref, ref, self.plane_s, self.plane_r, t * self.count + rel, self.plane_mate).wait_recv()
            own = self.own_ref(t, 1, rel)
            own[...] = (own[...].astype(jnp.float32) + self.plane_in[t][rel].astype(jnp.float32)).astype(jnp.bfloat16)

    def chain(self, t, D):
        for kind in self.kinds(t):
            for way in (0, 1):
                if D > self.reach(kind, way):
                    continue
                if D < self.reach(kind, way):
                    self.ring_wait(t, kind, way, D + 1)
                    rel = D % self.count if way == 0 else (-D) % self.count
                    ref = self.buffer(t, kind, self.slot(kind, way, D + 1))
                    ref[...] = (ref[...].astype(jnp.float32) + self.own_ref(t, kind, rel)[...].astype(jnp.float32)).astype(jnp.bfloat16)
                self.ring_copy(t, kind, way, D).start()

    def end_copy(self, t):
        return self.remote(self.low[t], self.low_in[t], self.end_s, self.end_r, 2 * t, self.plane_mate)

    def close(self, t):
        both, single = self.splits[t]
        for kind in self.kinds(t):
            total = self.own_ref(t, kind, 0)[...].astype(jnp.float32)
            for way in (0, 1):
                if self.reach(kind, way):
                    self.ring_wait(t, kind, way, 1)
                    total = total + self.buffer(t, kind, self.slot(kind, way, 1))[...].astype(jnp.float32)
            if kind:
                self.low[t][:, both:] = total.astype(jnp.bfloat16)
            else:
                self.low[t][:, :both] = total.astype(jnp.bfloat16)
        self.end_copy(t).start()

    def out_ref(self, t, core):
        half = self.half(t)
        return self.outs[t].at[:, pl.ds(pl.multiple_of(core * half, LANES), half)]

    def out_copy(self, t):
        return self.remote(self.done[t], self.out_ref(t, self.core), self.end_s, self.end_r, 2 * t + 1, self.core_mate)

    def put_copy(self, t):
        return pltpu.make_async_copy(self.done[t], self.out_ref(t, self.core), self.put.at[t])

    def deliver(self, t):
        both, single = self.splits[t]
        self.end_copy(t).wait_send()
        ref = self.low_in[t]
        self.remote(ref, ref, self.end_s, self.end_r, 2 * t, self.plane_mate).wait_recv()
        if both:
            self.done[t][:, :both] = self.low[t][:, :both].astype(jnp.float32) + self.low_in[t][:, :both].astype(jnp.float32)
        if single:
            self.done[t][:, self.single(t, self.plane)] = self.low[t][:, both:].astype(jnp.float32)
            self.done[t][:, self.single(t, 1 - self.plane)] = self.low_in[t][:, both:].astype(jnp.float32)
        self.out_copy(t).start()
        self.put_copy(t).start()

    def finish(self, t):
        for kind in self.kinds(t):
            for way in (0, 1):
                for D in range(1, self.reach(kind, way) + 1):
                    self.ring_copy(t, kind, way, D).wait_send()
        self.out_copy(t).wait_send()
        self.put_copy(t).wait()
        ref = self.out_ref(t, 1 - self.core)
        self.remote(ref, ref, self.end_s, self.end_r, 2 * t + 1, self.core_mate).wait_recv()

    def events(self):
        tensors = range(len(self.splits))
        part = functools.partial
        out = [part(self.prepare, t, self.far) for t in tensors]
        for D in range(self.far, 0, -1):
            for t in tensors:
                out.append(part(self.prepare, t, D - 1))
            for t in tensors:
                out.append(part(self.combine, t, D))
                out.append(part(self.chain, t, D))
        for t in tensors:
            out.append(part(self.combine, t, 0))
            out.append(part(self.close, t))
        for t in tensors:
            out.append(part(self.deliver, t))
        for t in tensors:
            out.append(part(self.finish, t))
        return out


def retreat_kernel(count, splits, steps, grad_att, turned, store, outputs, logs, *refs):
    T = len(splits)
    parts, refs = refs[:T], refs[T:]
    back, outs, refs = refs[0], refs[1 : 1 + T], refs[1 + T :]
    (grads, delta, grad_q, grad_kv, send_kv, kv_in0, kv_in1, low, in_send, in_recv, up_send, up_recv,
     out_send, out_recv, here) = refs[:15]
    refs = refs[15:]
    ring = Scatter(count, splits, parts, outs, refs[: 7 * T], refs[7 * T :]) if T else Ring(count, splits)
    seq, slot = ring.seq, ring.fsdp % GSLOTS
    mates, (x_mate, z_mate) = seq_mates(ring), slot_mates(ring)
    enter(ring.neighbours() + mates[2:] + [x_mate, z_mate])

    def remote(src, dst, send, recv, device):
        return pltpu.make_async_remote_copy(src, dst, send, recv, device_id=device, device_id_type=MESH)

    mine = block_rows(seq)

    def in_copy(mate):
        return remote(grad_att.at[mate[0]], grads.at[mine], in_send.at[mate[0]], in_recv.at[seq], mate)

    for mate in mates[1:] + mates[:1]:
        in_copy(mate).start()
    own_copy = pltpu.make_async_copy(grad_att.at[seq], grads.at[mine], here.at[0])
    own_copy.start()
    grad_q[...] = jnp.zeros_like(grad_q)
    grad_kv[...] = jnp.zeros_like(grad_kv)
    own_copy.wait()
    for mate in mates:
        ref = grads.at[block_rows(mate[0])]
        remote(ref, ref, in_send.at[mate[0]], in_recv.at[mate[0]], mate).wait_recv()
    for block in range(4):
        rows = pl.ds(block * BLOCK, BLOCK)
        sums = jnp.sum(grads[rows, :].astype(jnp.float32) * outputs[rows, :], axis=1, keepdims=True)
        delta[:, rows] = jnp.broadcast_to(sums, (BLOCK, LANES)).T[:8]

    def tile(step):
        phase, key_block, query_block = step // 16, (step // 4) % 4, step % 4
        piece = jnp.where(slot == 2, 1 - phase, phase)
        forward_phase = jnp.where(phase == 2, 0, jnp.where(slot == 3, 2 - piece, 1 + piece))
        source, active, table, column = tile_place(slot, seq, forward_phase, key_block, query_block)

        @pl.when(active)
        def _():
            rows, key_rows = block_rows(query_block), block_rows(key_block)
            keys, values = store[1 + 2 * source, key_rows, :], store[2 + 2 * source, key_rows, :]
            queries, tops = store[0, rows, :], grads[rows, :]
            scores = lax.dot_general(keys, queries, (((1,), (1,)), ((), ())), preferred_element_type=jnp.float32)
            bias = jnp.concatenate(
                [turned[table, :, pl.ds(pl.multiple_of(TURNED_ZERO - column - LANES * part, LANES), BLOCK)] for part in range(BLOCK // LANES)],
                axis=0,
            )
            weights = jnp.exp2(scores * (DH**-0.5 * LOG2E) + (bias - logs[:1, rows]))
            grad_weights = lax.dot_general(values, tops, (((1,), (1,)), ((), ())), preferred_element_type=jnp.float32)
            grad_scores = (weights * (grad_weights - delta[:1, rows])).astype(jnp.bfloat16)
            grad_kv[source, 1, key_rows, :] += jnp.dot(weights.astype(jnp.bfloat16), tops, preferred_element_type=jnp.float32)
            grad_kv[source, 0, key_rows, :] += jnp.dot(grad_scores, queries, preferred_element_type=jnp.float32)
            grad_q[rows, :] += lax.dot_general(grad_scores, keys, (((0,), (0,)), ((), ())), preferred_element_type=jnp.float32)

    scale = DH**-0.5

    def rounded(source, chunk, extra):
        rows = block_rows(chunk)
        keys = grad_kv[source, 0, rows, :] * scale
        values = grad_kv[source, 1, rows, :]
        for more in extra:
            keys = keys + more[0].astype(jnp.float32)
            values = values + more[1].astype(jnp.float32)
        return keys.astype(jnp.bfloat16), values.astype(jnp.bfloat16)

    def x_send(chunk):
        src = send_kv.at[0, :, block_rows(chunk)]
        return remote(src, kv_in0.at[:, block_rows(chunk)], up_send.at[chunk], up_recv.at[chunk], x_mate)

    def z_send(chunk):
        src = send_kv.at[1, :, block_rows(chunk)]
        return remote(src, kv_in1.at[:, block_rows(chunk)], up_send.at[4 + chunk], up_recv.at[4 + chunk], z_mate)

    def x_wait(chunk):
        ref = kv_in0.at[:, block_rows(chunk)]
        remote(ref, ref, up_send.at[chunk], up_recv.at[chunk], x_mate).wait_recv()

    def z_wait(chunk):
        ref = kv_in1.at[:, block_rows(chunk)]
        remote(ref, ref, up_send.at[4 + chunk], up_recv.at[4 + chunk], z_mate).wait_recv()

    def first_done(chunk):
        @pl.when(slot >= 1)
        def _():
            source = jnp.where(slot == 2, 2, 1)
            keys, values = rounded(source, chunk, [])
            send_kv[0, 0, block_rows(chunk), :] = keys
            send_kv[0, 1, block_rows(chunk), :] = values
            x_send(chunk).start()

    def second_done(chunk):
        @pl.when(slot >= 2)
        def _():
            x_wait(chunk)
            source = slot - 1
            keys, values = rounded(source, chunk, [kv_in0[:, block_rows(chunk), :]])
            send_kv[1, 0, block_rows(chunk), :] = keys
            send_kv[1, 1, block_rows(chunk), :] = values
            z_send(chunk).start()

    def out_copy(mate):
        src = low.at[:, block_rows(mate[0])]
        return remote(src, back.at[seq], out_send.at[mate[0]], out_recv.at[seq], mate)

    def own_done(chunk):
        rows = block_rows(chunk)
        low[0, rows, :] = (grad_q[rows, :] * scale).astype(jnp.bfloat16)

        @pl.when(slot == 0)
        def _():
            x_wait(chunk)
            z_wait(chunk)
            low[1, rows, :], low[2, rows, :] = rounded(0, chunk, [kv_in0[:, rows, :], kv_in1[:, rows, :]])

        @pl.when(slot == 1)
        def _():
            z_wait(chunk)
            low[1, rows, :], low[2, rows, :] = rounded(0, chunk, [kv_in1[:, rows, :]])

        @pl.when(slot >= 2)
        def _():
            low[1, rows, :], low[2, rows, :] = rounded(0, chunk, [])

    events = {}
    for chunk in range(4):
        events.setdefault(4 * chunk + 4, []).append(functools.partial(first_done, chunk))
        events.setdefault(20 + 4 * chunk, []).append(functools.partial(second_done, chunk))
    rest = []
    if T:
        begin, gap = steps
        events.setdefault(begin, []).extend([functools.partial(ring.start, t) for t in range(T)])
        for i, event in enumerate(ring.events()):
            step = begin + int(gap * (i + 1))
            if step < 48:
                events.setdefault(step, []).append(event)
            else:
                rest.append(event)

    def step_body(step, carry):
        for when, actions in sorted(events.items()):
            @pl.when(step == when)
            def _():
                for action in actions:
                    action()
        tile(step)
        return carry

    lax.fori_loop(0, 48, step_body, 0)
    for chunk in range(4):
        own_done(chunk)
    for mate in mates[1:] + mates[:1]:
        out_copy(mate).start()
    own_out = pltpu.make_async_copy(low.at[:, mine], back.at[seq], here.at[1])
    own_out.start()
    for event in rest:
        event()
    own_out.wait()
    for mate in mates:
        in_copy(mate).wait_send()
        out_copy(mate).wait_send()
        ref = back.at[mate[0]]
        remote(ref, ref, out_send.at[mate[0]], out_recv.at[mate[0]], mate).wait_recv()
    for chunk in range(4):
        @pl.when(slot >= 1)
        def _():
            x_send(chunk).wait_send()

        @pl.when(slot >= 2)
        def _():
            z_send(chunk).wait_send()


def retreat(count, grad_att, turned, store, outputs, logs, parts, splits, steps=(0, 1)):
    rows = grad_att.shape[1]
    own = 4 * rows
    T = len(parts)
    shard_rows = [p.shape[1] for p in parts]
    return pl.pallas_call(
        functools.partial(retreat_kernel, count, splits, steps),
        out_shape=[jax.ShapeDtypeStruct((HEADS, 3, rows, LANES), jnp.bfloat16)]
        + [jax.ShapeDtypeStruct((p.shape[1], 2 * p.shape[2]), jnp.float32) for p in parts],
        in_specs=[VMEM] * 5 + [ANY] * T,
        out_specs=[VMEM] + [ANY] * T,
        scratch_shapes=[
            pltpu.VMEM((own, LANES), jnp.bfloat16),
            pltpu.VMEM((8, own), jnp.float32),
            pltpu.VMEM((own, LANES), jnp.float32),
            pltpu.VMEM((3, 2, own, LANES), jnp.float32),
            pltpu.VMEM((2, 2, own, LANES), jnp.bfloat16),
            pltpu.VMEM((2, own, LANES), jnp.bfloat16),
            pltpu.VMEM((2, own, LANES), jnp.bfloat16),
            pltpu.VMEM((3, own, LANES), jnp.bfloat16),
            DMA((4,)), DMA((4,)), DMA((8,)), DMA((8,)), DMA((4,)), DMA((4,)), DMA((2,)),
        ]
        + (Scatter.scratch(count, splits, shard_rows) if T else []),
        compiler_params=pltpu.CompilerParams(collective_id=3, has_side_effects=True, vmem_limit_bytes=63 << 20),
    )(grad_att, turned, store, outputs, logs, *parts)


CHUNK = 512


def gelu_pair(v):
    root = 0.7978845608028654
    square = v * v
    t = jnp.tanh(root * (v + 0.044715 * square * v))
    up = 0.5 * (1.0 + t)
    return v * up, up + 0.5 * v * (1.0 - t * t) * (root * (1.0 + 3.0 * 0.044715 * square))


def contract(left, right, left_axis, right_axis):
    return lax.dot_general(left, right, (((left_axis,), (right_axis,)), ((), ())), preferred_element_type=jnp.float32)


def feed_kernel(att, gates, tokens, cotangent, norms, output_w, inner_w, outer_w,
                layer_out, grad_residual, grad_att, grad_logit, grad_norms, part_output, part_inner, part_outer,
                w_out, w_in, w_up, acts, act_in, slopes, slope_in, scaled, scaled_in, scaled_t, cot_in, cot_t,
                acc, normed, grad_scaled, branch_low, branch_in, branch_t, att_in, gates_in,
                stage_outer, stage_inner, stage_output,
                load_out, load_in, load_up, pair_s, pair_r, act_s, act_r, slope_s, slope_r, put_outer, put_inner, put_output):
    seq, fsdp = lax.axis_index("seq"), lax.axis_index("fsdp")
    core = seq % 2
    mate = (seq + 1 - 2 * core, fsdp)
    experts = HEADS * EXP
    half = cotangent.shape[1] // 2
    quarter = inner_w.shape[1] // CHUNK // 2

    def out_load(e):
        return pltpu.make_async_copy(output_w.at[pl.ds(e * DH, DH)], w_out.at[e, pl.ds(0, DH)], load_out.at[e])

    def ffn_load(chunk, slot):
        cols = pl.ds(pl.multiple_of(chunk * CHUNK, CHUNK), CHUNK)
        return (pltpu.make_async_copy(inner_w.at[:, cols], w_in.at[slot], load_in.at[slot]),
                pltpu.make_async_copy(outer_w.at[cols], w_up.at[slot], load_up.at[slot]))

    def chunk_of(i, sub):
        return (core * quarter if sub else (1 - core) * quarter) + i

    for e in range(experts):
        out_load(e).start()
    for sub in range(2):
        for copy in ffn_load(chunk_of(0, sub), sub):
            copy.start()
    enter([mate])

    def remote(src, dst, send, recv):
        return pltpu.make_async_remote_copy(src, dst, send, recv, device_id=mate, device_id_type=MESH)

    mine = pl.ds(pl.multiple_of(core * half, LANES), half)
    yours = pl.ds(pl.multiple_of((1 - core) * half, LANES), half)
    pair = [
        remote(att, att_in, pair_s.at[0], pair_r.at[0]),
        remote(gates.at[0], gates_in, pair_s.at[1], pair_r.at[1]),
        remote(cotangent.at[:, yours], cot_in, pair_s.at[2], pair_r.at[2]),
        remote(scaled, scaled_in, pair_s.at[3], pair_r.at[3]),
        remote(branch_low.at[:, yours], branch_in, pair_s.at[4], pair_r.at[4]),
    ]
    for copy in pair[:3]:
        copy.start()

    def mixed_pair(att_ref, gate, two):
        tiles = []
        for which in (2 * two, 2 * two + 1):
            column = gate[:, experts + which : experts + which + 1]
            tiles.append((att_ref[which // EXP].astype(jnp.float32) * column).astype(jnp.bfloat16))
        return jnp.concatenate(tiles, axis=1)

    w_out[:, DH:, :] = jnp.zeros((experts, LANES - DH, w_out.shape[2]), jnp.bfloat16)
    acc[...] = tokens[...].astype(jnp.float32)
    for two in range(experts // 2):
        out_load(2 * two).wait()
        out_load(2 * two + 1).wait()
        weights = w_out[2 * two : 2 * two + 2].reshape(2 * LANES, w_out.shape[2])
        acc[...] += jnp.dot(mixed_pair(att, gates.at[0], two), weights, preferred_element_type=jnp.float32)
    residual = acc[...]
    centred = residual - jnp.mean(residual, axis=1, keepdims=True)
    inverse = lax.rsqrt(jnp.mean(centred * centred, axis=1, keepdims=True) + EPSILON)
    normed[...] = centred * inverse
    scaled[...] = (normed[...] * norms[:1] + norms[1:2]).astype(jnp.bfloat16)
    pair[3].start()
    rows = tokens.shape[0]
    scaled_t[:, :rows] = scaled[...].T
    cot_t[:, :rows] = cotangent[:, mine].T
    grad_scaled[...] = jnp.zeros_like(grad_scaled)
    pair[2].wait_recv()
    cot_t[:, rows:] = cot_in[...].T
    pair[3].wait_recv()
    scaled_t[:, rows:] = scaled_in[...].T

    def act_copy(chunk, sub):
        return remote(acts.at[sub], act_in.at[chunk], act_s.at[sub], act_r.at[chunk])

    def slope_copy(i):
        return remote(slopes.at[0], slope_in.at[i], slope_s.at[0], slope_r.at[i])

    def put_outer_copy(chunk, sub):
        cols = pl.ds(pl.multiple_of(chunk * CHUNK, CHUNK), CHUNK)
        return pltpu.make_async_copy(stage_outer.at[sub], part_outer.at[cols], put_outer.at[sub])

    def put_inner_copy(i):
        cols = pl.ds(pl.multiple_of(i * CHUNK, CHUNK), CHUNK)
        return pltpu.make_async_copy(stage_inner, part_inner.at[:, cols], put_inner.at[0])

    def forward_backward(i, sub):
        chunk = chunk_of(i, sub)
        for copy in ffn_load(chunk, sub):
            copy.wait()

        @pl.when(i > 0)
        def _():
            act_copy(chunk, sub).wait_send()
            if sub == 0:
                slope_copy(i).wait_send()

        act, slope = gelu_pair(jnp.dot(scaled[...], w_in[sub], preferred_element_type=jnp.float32))
        acts[sub] = act.astype(jnp.bfloat16)
        act_copy(chunk, sub).start()
        slopes[sub] = (contract(cotangent[...], w_up[sub], 1, 1) * slope).astype(jnp.bfloat16)
        if sub == 0:
            slope_copy(i).start()
        acc[...] += jnp.dot(acts[sub], w_up[sub], preferred_element_type=jnp.float32)
        grad_scaled[...] += contract(slopes[sub], w_in[sub], 1, 1)

        @pl.when(i < quarter - 1)
        def _():
            for copy in ffn_load(chunk_of(i + 1, sub), sub):
                copy.start()

    def outer_part(i, sub):
        chunk = chunk_of(i, sub)
        ref = act_in.at[chunk]
        remote(ref, ref, act_s.at[sub], act_r.at[chunk]).wait_recv()

        @pl.when(i > 0)
        def _():
            put_outer_copy(chunk, sub).wait()

        total = jnp.dot(cot_t[:, :rows], acts[sub], preferred_element_type=jnp.float32)
        total = total + jnp.dot(cot_t[:, rows:], act_in[chunk], preferred_element_type=jnp.float32)
        stage_outer[sub] = total.astype(jnp.bfloat16).T
        put_outer_copy(chunk, sub).start()

    def inner_part(i):
        ref = slope_in.at[i]
        remote(ref, ref, slope_s.at[0], slope_r.at[i]).wait_recv()

        @pl.when(i > 0)
        def _():
            put_inner_copy(i).wait()

        total = jnp.dot(scaled_t[:, :rows], slopes[1], preferred_element_type=jnp.float32)
        total = total + jnp.dot(scaled_t[:, rows:], slope_in[i], preferred_element_type=jnp.float32)
        stage_inner[...] = total.astype(jnp.bfloat16)
        put_inner_copy(i).start()

    def iteration(i, carry):
        forward_backward(i, 0)
        forward_backward(i, 1)
        outer_part(i, 1)
        inner_part(i)
        outer_part(i, 0)
        return carry

    lax.fori_loop(0, quarter, iteration, 0)
    layer_out[...] = acc[...].astype(jnp.bfloat16)
    slope = grad_scaled[...]
    grad_norms[...] = jnp.concatenate(
        [jnp.sum(slope * normed[...], axis=0, keepdims=True), jnp.sum(slope, axis=0, keepdims=True),
         jnp.zeros((6, slope.shape[1]), jnp.float32)], axis=0)
    slope = slope * norms[:1]
    total = cotangent[...].astype(jnp.float32) + inverse * (
        slope - jnp.mean(slope, axis=1, keepdims=True)
        - normed[...] * jnp.mean(slope * normed[...], axis=1, keepdims=True))
    grad_residual[...] = total
    branch_low[...] = total.astype(jnp.bfloat16)
    pair[4].start()
    branch_t[:, :rows] = branch_low[:, mine].T
    lane = lax.broadcasted_iota(jnp.int32, (rows, LANES), 1)
    logit = jnp.zeros((rows, LANES), jnp.float32)
    head_total = None
    for which in range(experts):
        if which % 2 == 0:
            weights = w_out[which : which + 2].reshape(2 * LANES, w_out.shape[2])
            both = contract(branch_low[...], weights, 1, 1)
        grad_mixed = both[:, which % 2 * LANES : (which % 2 + 1) * LANES]
        head, expert = which // EXP, which % EXP
        column = slice(experts + which, experts + which + 1)
        term = grad_mixed * gates[0, :, column]
        head_total = term if expert == 0 else head_total + term
        if expert == EXP - 1:
            grad_att[head] = head_total.astype(jnp.bfloat16)
        sums = jnp.sum(grad_mixed * att[head].astype(jnp.float32), axis=1, keepdims=True)
        logit = jnp.where(lane == experts + which, sums, logit)
    grad_logit[...] = logit * gates[1]
    pair[0].wait_recv()
    pair[1].wait_recv()
    pair[4].wait_recv()
    branch_t[:, rows:] = branch_in[...].T

    def put_output_copy(which):
        return pltpu.make_async_copy(stage_output.at[which % 4, pl.ds(0, DH)], part_output.at[pl.ds(which * DH, DH)], put_output.at[which % 4])

    for two in range(experts // 2):
        total = jnp.dot(branch_t[:, :rows], mixed_pair(att, gates.at[0], two), preferred_element_type=jnp.float32)
        total = total + jnp.dot(branch_t[:, rows:], mixed_pair(att_in, gates_in, two), preferred_element_type=jnp.float32)
        turned = total.astype(jnp.bfloat16).T
        for side in range(2):
            which = 2 * two + side
            if which >= 4:
                put_output_copy(which - 4).wait()
            stage_output[which % 4] = turned[side * LANES : (side + 1) * LANES]
            put_output_copy(which).start()
    for which in range(experts - 4, experts):
        put_output_copy(which).wait()
    for sub in range(2):
        put_outer_copy(0, sub).wait()
        act_copy(0, sub).wait_send()
    put_inner_copy(0).wait()
    slope_copy(0).wait_send()
    for copy in pair:
        copy.wait_send()


def feed(att, gates, tokens, cotangent, norms, output_w, inner_w, outer_w):
    rows, width = tokens.shape
    wide = inner_w.shape[1]
    half = width // 2
    f32, bf = jnp.float32, jnp.bfloat16
    experts, chunks = HEADS * EXP, wide // CHUNK
    V = pltpu.VMEM
    return pl.pallas_call(
        feed_kernel,
        out_shape=[
            jax.ShapeDtypeStruct((rows, width), bf),
            jax.ShapeDtypeStruct((rows, width), f32),
            jax.ShapeDtypeStruct((HEADS, rows, LANES), bf),
            jax.ShapeDtypeStruct((rows, LANES), f32),
            jax.ShapeDtypeStruct((8, width), f32),
            jax.ShapeDtypeStruct((VCOLS, half), bf),
            jax.ShapeDtypeStruct((width, wide // 2), bf),
            jax.ShapeDtypeStruct((wide, half), bf),
        ],
        in_specs=[VMEM] * 5 + [ANY] * 3,
        out_specs=[VMEM] * 5 + [ANY] * 3,
        scratch_shapes=[
            V((experts, LANES, width), bf), V((2, width, CHUNK), bf), V((2, CHUNK, width), bf),
            V((2, rows, CHUNK), bf), V((chunks, rows, CHUNK), bf), V((2, rows, CHUNK), bf), V((chunks // 2, rows, CHUNK), bf),
            V((rows, width), bf), V((rows, width), bf), V((width, 2 * rows), bf), V((rows, half), bf), V((half, 2 * rows), bf),
            V((rows, width), f32), V((rows, width), f32), V((rows, width), f32),
            V((rows, width), bf), V((rows, half), bf), V((half, 2 * rows), bf), V((HEADS, rows, LANES), bf), V((rows, LANES), f32),
            V((2, CHUNK, half), bf), V((width, CHUNK), bf), V((4, LANES, half), bf),
            DMA((experts,)), DMA((2,)), DMA((2,)), DMA((5,)), DMA((5,)), DMA((2,)), DMA((chunks,)), DMA((1,)), DMA((chunks // 2,)),
            DMA((2,)), DMA((1,)), DMA((4,)),
        ],
        compiler_params=pltpu.CompilerParams(collective_id=4, has_side_effects=True, vmem_limit_bytes=62 << 20),
    )(att, gates, tokens, cotangent, norms, output_w, inner_w, outer_w)


def settle_kernel(count, back, experts, gates, grad_logit, tokens, joint, grad_residual, grad_norms,
                  grad_tokens, joint_out, grads, grads_in, tokens_in, tokens_t, norms_in, norm_columns, *refs):
    splits = (SPLITS["joint"],)
    pair_s, pair_r = refs[-2:]
    ring = Scatter(count, splits, [], [joint_out], refs[:7], refs[7:-2])
    enter(ring.neighbours())
    core = ring.core
    half = JOINT // 2

    def remote(src, dst, i):
        return pltpu.make_async_remote_copy(src, dst, pair_s.at[i], pair_r.at[i], device_id=ring.core_mate, device_id_type=MESH)

    mine = pl.ds(pl.multiple_of(core * half, LANES), half)
    yours = pl.ds(pl.multiple_of((1 - core) * half, LANES), half)
    pair = [remote(tokens, tokens_in, 0), remote(grad_norms, norms_in, 1), remote(grads.at[:, yours], grads_in, 2)]
    pair[0].start()
    pair[1].start()
    rows = tokens.shape[0]
    lane = lax.broadcasted_iota(jnp.int32, (LANES, LANES), 1)
    width = HEADS * EXP

    def assemble(block, carry):
        part = pl.ds(pl.multiple_of(block * LANES, LANES), LANES)
        pieces = [back[head, which, part, :][:, :DH].astype(jnp.float32) for which in range(2) for head in range(HEADS)]
        logit = grad_logit[part, :]
        for head in range(HEADS):
            values = back[head, 2, part, :].astype(jnp.float32)
            for expert in range(EXP):
                which = head * EXP + expert
                pieces.append((values * gates[0, part, which : which + 1])[:, :DH])
                sums = jnp.sum(values * experts[which, part, :].astype(jnp.float32), axis=1, keepdims=True)
                logit = jnp.where(lane == which, sums * gates[1, part, which : which + 1], logit)
        pieces.append(jnp.where(lane < 2 * width, logit, 0.0))
        pieces.append(jnp.zeros((LANES, JOINT - ROUTERS - LANES), jnp.float32))
        grads[part, :] = jnp.concatenate(pieces, axis=1).astype(jnp.bfloat16)
        return carry

    lax.fori_loop(0, rows // LANES, assemble, 0)
    pair[2].start()
    tokens_t[:, :rows] = tokens[...].T
    for copy in pair[:2]:
        copy.wait_recv()
    tokens_t[:, rows:] = tokens_in[...].T
    norm_tile = NORM // LANES * LANES - half
    first = NORM - half - norm_tile
    both = grad_norms[...] + norms_in[...]
    for block in range(both.shape[1] // LANES):
        columns = jnp.concatenate([both[:, block * LANES : (block + 1) * LANES], jnp.zeros((LANES - 8, LANES), jnp.float32)], axis=0)
        norm_columns[block * LANES : (block + 1) * LANES, :] = columns.T
    pair[2].wait_recv()
    shard_rows = tokens_t.shape[0] // count
    tile_lane = lax.broadcasted_iota(jnp.int32, (shard_rows, LANES), 1)

    def fill(rel):
        part = pl.ds(pl.multiple_of(ring.dest(rel) * shard_rows, shard_rows), shard_rows)
        total = jnp.dot(tokens_t[part, :rows], grads[:, mine], preferred_element_type=jnp.float32)
        total = total + jnp.dot(tokens_t[part, rows:], grads_in[...], preferred_element_type=jnp.float32)
        ring.mine[0][rel] = total.astype(jnp.bfloat16)
        extra = jnp.where(tile_lane == first, norm_columns[part, 0:1], 0.0) + jnp.where(tile_lane == first + 1, norm_columns[part, 1:2], 0.0)
        tile = total[:, norm_tile : norm_tile + LANES] + extra * core.astype(jnp.float32)
        ring.mine[0][rel, :, norm_tile : norm_tile + LANES] = tile.astype(jnp.bfloat16)

    for rel in ring.order():
        fill(rel)
    events = ring.events()
    for event in events[:2]:
        event()
    grad_tokens[...] = grad_residual[...] + contract(grads[...], joint[...], 1, 1)
    for event in events[2:]:
        event()
    for copy in pair:
        copy.wait_send()


def settle(count, back, experts, gates, grad_logit, tokens, joint, grad_residual, grad_norms):
    rows, width = tokens.shape
    shard_rows = width // count
    f32, bf = jnp.float32, jnp.bfloat16
    V = pltpu.VMEM
    return pl.pallas_call(
        functools.partial(settle_kernel, count),
        out_shape=[jax.ShapeDtypeStruct((rows, width), f32), jax.ShapeDtypeStruct((shard_rows, JOINT), f32)],
        in_specs=[VMEM] * 8,
        out_specs=[VMEM] * 2,
        scratch_shapes=[V((rows, JOINT), bf), V((rows, JOINT // 2), bf), V((rows, width), bf), V((width, 2 * rows), bf), V((8, width), f32), V((width, LANES), f32)]
        + Scatter.scratch(count, (SPLITS["joint"],), [shard_rows])
        + [DMA((3,)), DMA((3,))],
        compiler_params=pltpu.CompilerParams(collective_id=5, has_side_effects=True, vmem_limit_bytes=60 << 20),
    )(back, experts, gates, grad_logit, tokens, joint, grad_residual, grad_norms)


def on_device(
    tokens, value_routes, output_routes, cont_gap, query_weight, key_weight, value_weight, value_router,
    output_router, output_weight, norm_gain, norm_bias, inner_weight, outer_weight, cotangent,
):
    count = lax.axis_size("fsdp")
    inputs = tokens[0]
    rows, width = inputs.shape
    routers = jnp.concatenate(
        [value_router, output_router, norm_gain[:, None], norm_bias[:, None],
         jnp.zeros((query_weight.shape[0], JOINT - NORM - 2), jnp.bfloat16)], axis=1)
    routes = jnp.concatenate([value_routes[0].reshape(rows, -1), output_routes[0].reshape(rows, -1)], axis=1)
    joint, qkv, experts, gates, norms, tables, turned = project(
        count, query_weight, key_weight, value_weight, routers, inputs, routes, cont_gap)
    splits = tuple(SPLITS[name] for name in ("output", "inner", "outer"))
    att, store, outputs, logs, output_full, inner_full, outer_full = attend(
        count, qkv, tables, (output_weight, inner_weight, outer_weight), splits)
    layer_out, grad_residual, grad_att, grad_logit, grad_norms, *parts = feed(
        att, gates, inputs, cotangent[0], norms, output_full.reshape(VCOLS, width), inner_full.reshape(width, -1),
        outer_full.reshape(-1, width))
    parts = tuple(part.reshape(count, -1, part.shape[1]) for part in parts)
    back, out_w, in_w, outer_w = retreat(count, grad_att, turned, store, outputs, logs, parts, splits)
    grad_input, joint_w = settle(count, back, experts, gates, grad_logit, inputs, joint, grad_residual, grad_norms)
    return (
        layer_out[None], grad_input[None], joint_w[:, :QCOLS], joint_w[:, QCOLS : 2 * QCOLS], joint_w[:, 2 * QCOLS : ROUTERS],
        joint_w[:, ROUTERS : ROUTERS + HEADS * EXP], joint_w[:, ROUTERS + HEADS * EXP : NORM], out_w, joint_w[:, NORM],
        joint_w[:, NORM + 1], in_w, outer_w,
    )


def solution(mesh):
    wide = P("fsdp", None)
    part = P("fsdp", "seq", None)
    routes = P("fsdp", "seq", None, None)
    return jax.shard_map(
        on_device,
        mesh=mesh,
        in_specs=(part, routes, routes, P()) + (wide,) * 6 + (P("fsdp"), P("fsdp"), wide, wide, part),
        out_specs=(part, part) + (wide,) * 6 + (P("fsdp"), P("fsdp"), wide, wide),
        check_vma=False,
    )
```

```python
import functools
import jax
import jax.numpy as jnp
from jax import lax
from jax.experimental import pallas as pl
from jax.experimental.pallas import tpu as pltpu
from jax.sharding import PartitionSpec as P

HEADS = 4
DH = 112
EXP = 5
CONT = 1024
GSLOTS = 4
PSLOTS = 2
BLOCK = 512
LANES = 128
EPSILON = 1e-05
NEGATIVE = -1e30
LOG2E = 1.4426950408889634
MESH = pl.DeviceIdType.MESH
ANY = pl.BlockSpec(memory_space=pl.ANY)
VMEM = pl.BlockSpec(memory_space=pltpu.VMEM)
SMEM = pl.BlockSpec(memory_space=pltpu.SMEM)
DMA = pltpu.SemaphoreType.DMA

QCOLS = HEADS * DH
VCOLS = HEADS * EXP * DH
ROUTERS = 2 * QCOLS + VCOLS
NORM = ROUTERS + 2 * HEADS * EXP
JOINT = 3328
SPLITS = {"joint": (640, 512), "output": (256, 128), "inner": (768, 640), "outer": (256, 128)}
INNER_PARTS = ((512, 256), (512, 256))


def ring_place(index, count):
    return (index // 2) * (1 - index % 2) + (count - 1 - index // 2) * (index % 2)


def ring_index(place, count):
    upper = place // (count // 2)
    return 2 * place * (1 - upper) + (2 * (count - 1 - place) + 1) * upper


def enter(devices):
    barrier = pltpu.get_barrier_semaphore()
    for device in devices:
        pl.semaphore_signal(barrier, inc=1, device_id=device, device_id_type=MESH)
    pl.semaphore_wait(barrier, len(devices))


class Ring:
    def __init__(self, count, splits):
        self.count, self.splits = count, splits
        self.seq, self.fsdp = lax.axis_index("seq"), lax.axis_index("fsdp")
        self.plane, self.core = self.seq // 2, self.seq % 2
        self.place = ring_place(self.fsdp, count)
        self.right = (self.seq, ring_index((self.place + 1) % count, count))
        self.left = (self.seq, ring_index((self.place + count - 1) % count, count))
        self.core_mate = (self.seq + 1 - 2 * self.core, self.fsdp)
        self.plane_mate = ((self.seq + 2) % 4, self.fsdp)
        self.far = count // 2

    def neighbours(self):
        return [self.right, self.left, self.core_mate, self.plane_mate]

    def reach(self, kind, way):
        return self.far if kind == way else self.count - 1 - self.far

    def kinds(self, t):
        return [kind for kind in (1, 0) if self.splits[t][kind] > 0]

    def half(self, t):
        return self.splits[t][0] + 2 * self.splits[t][1]

    def cols(self, t, kind, plane, core):
        both, single = self.splits[t]
        if kind == 0:
            return pl.ds(pl.multiple_of(core * self.half(t), LANES), both)
        return pl.ds(pl.multiple_of(core * self.half(t) + both + plane * single, LANES), single)

    def behind(self, way, k):
        step = self.count - k if way == 0 else k
        return ring_index((self.place + step) % self.count, self.count)

    def next(self, way):
        return self.right if way == 0 else self.left

    def slot(self, kind, way, k):
        return k - 1 if way == 0 else self.reach(kind, 0) + k - 1


class Gather(Ring):
    def __init__(self, count, splits, shards, at, send, recv, local):
        super().__init__(count, splits)
        self.shards, self.at, self.send, self.recv, self.local = shards, at, send, recv, local

    @staticmethod
    def sems(count, tensors):
        return [DMA((6 * tensors * (count - 1),)), DMA((6 * tensors * (count - 1),)), DMA((tensors,))]

    def copy(self, src, dst, group, t, slot, device):
        i = (group * len(self.splits) + t) * (self.count - 1) + slot
        return pltpu.make_async_remote_copy(
            src, dst, self.send.at[i], self.recv.at[i], device_id=device, device_id_type=MESH
        )

    def same(self, group, t, kind, way, k, plane, core, device):
        ref = self.at(t, self.behind(way, k), self.cols(t, kind, plane, core))
        return self.copy(ref, ref, group, t, self.slot(kind, way, k), device)

    def hop(self, t, kind, way, k):
        if k > 1:
            ref = self.at(t, self.behind(way, k - 1), self.cols(t, kind, self.plane, self.core))
            return self.copy(ref, ref, kind, t, self.slot(kind, way, k), self.next(way))
        cols = self.cols(t, kind, self.plane, self.core)
        return self.copy(
            self.shards[t].at[:, cols], self.at(t, self.fsdp, cols), kind, t, self.slot(kind, way, 1), self.next(way)
        )

    def arrived(self, t, kind, way, k):
        return self.same(kind, t, kind, way, k, self.plane, self.core, self.next(way))

    def to_core(self, t, kind, way, k, core):
        return self.same(2 + kind, t, kind, way, k, self.plane, core, self.core_mate)

    def to_plane(self, t, way, k, plane):
        return self.same(4, t, 1, way, k, plane, self.core, self.plane_mate)

    def plane_to_core(self, t, way, k, core):
        return self.same(5, t, 1, way, k, 1 - self.plane, core, self.core_mate)

    def own(self, t):
        return pltpu.make_async_copy(self.shards[t], self.at(t, self.fsdp, slice(None)), self.local.at[t])

    def start(self, t):
        for kind in self.kinds(t):
            for way in (0, 1):
                if self.reach(kind, way):
                    self.hop(t, kind, way, 1).start()
        self.own(t).start()

    def arrive(self, t, k):
        for kind in self.kinds(t):
            for way in (0, 1):
                if k <= self.reach(kind, way):
                    self.arrived(t, kind, way, k).wait_recv()
                    if k < self.reach(kind, way):
                        self.hop(t, kind, way, k + 1).start()
                    if kind:
                        self.to_plane(t, way, k, self.plane).start()
                    self.to_core(t, kind, way, k, self.core).start()

    def plane_arrive(self, t, k):
        if 1 in self.kinds(t):
            for way in (0, 1):
                if k <= self.reach(1, way):
                    self.to_plane(t, way, k, 1 - self.plane).wait_recv()
                    self.plane_to_core(t, way, k, self.core).start()

    def finish(self, t):
        self.own(t).wait()
        for kind in self.kinds(t):
            for way in (0, 1):
                for k in range(1, self.reach(kind, way) + 1):
                    self.hop(t, kind, way, k).wait_send()
                    self.to_core(t, kind, way, k, self.core).wait_send()
                    self.to_core(t, kind, way, k, 1 - self.core).wait_recv()
                    if kind:
                        self.to_plane(t, way, k, self.plane).wait_send()
                        self.plane_to_core(t, way, k, self.core).wait_send()
                        self.plane_to_core(t, way, k, 1 - self.core).wait_recv()

    def events(self):
        tensors = range(len(self.splits))
        out = []
        for k in range(1, self.far + 1):
            for t in tensors:
                out.append(functools.partial(self.arrive, t, k))
                if k > 1:
                    out.append(functools.partial(self.plane_arrive, t, k - 1))
        for t in tensors:
            out.append(functools.partial(self.plane_arrive, t, self.far))
        for t in tensors:
            out.append(functools.partial(self.finish, t))
        return out


TABLE = 5632
TABLE_ZERO = 5120
TURNED_ZERO = 512


def route_lanes(routes, lane):
    hit = None
    for head in range(2 * HEADS):
        for choice in range(2):
            place = head * EXP + routes[:, 2 * head + choice : 2 * head + choice + 1]
            here = lane == place
            hit = here if hit is None else hit | here
    return hit.astype(jnp.float32)


def project_kernel(count, query, key, value, routers, tokens, routes, output_shard, gaps, joint, output_w, qkv, experts, gates, norms, tables, turned_tables,
                   shard, product, send, recv, local):
    rows = shard.shape[0]
    splits = (SPLITS["joint"], SPLITS["output"])

    def at(t, g, cols):
        if t:
            return output_w.at[g, :, cols]
        return joint.at[pl.ds(pl.multiple_of(g * rows, rows), rows), cols]

    ring = Gather(count, splits, [shard, output_shard], at, send, recv, local)
    wide = jnp.concatenate([ref[...].astype(jnp.float32) for ref in (query, key, value, routers)], axis=1)
    shard[...] = wide.astype(jnp.bfloat16)
    enter(ring.neighbours())
    ring.start(0)
    slope = jnp.float32(0.0)
    for head in range(HEADS):
        slope = jnp.where(ring.seq // 1 == head, -0.5 * 0.5**head * LOG2E, slope)
    group = ring.fsdp // GSLOTS
    pair = jnp.maximum(ring.fsdp % GSLOTS - PSLOTS, 0) * 2
    gap_values = [jnp.int32(0), gaps[group, pair], gaps[group, pair + 1]]

    def table_column(step, carry):
        start = pl.multiple_of(step * 256, 256)
        lanes = lax.broadcasted_iota(jnp.int32, (8, 256 + LANES), 1) + (start - LANES)
        for which in range(3):
            for turned in range(2):
                if turned:
                    distance = lanes - TURNED_ZERO + gap_values[which]
                else:
                    distance = TABLE_ZERO - lanes + gap_values[which]
                bias = slope * jnp.log(1.0 + jnp.maximum(distance, 0).astype(jnp.float32))
                bias = jnp.where(distance >= 0, bias, NEGATIVE)
                wide = jnp.broadcast_to(bias[:1], (LANES, 256 + LANES))
                rolled = pltpu.roll(wide, 0, 1, stride=1, stride_axis=0)
                target = turned_tables if turned else tables
                target[which, :, pl.ds(start, 256)] = rolled[:, LANES:]
        return carry

    late = max(1, ring.far - 1)
    steps, later = [], []
    for k in range(1, ring.far + 1):
        steps.append(functools.partial(ring.arrive, 0, k))
        if k > 1:
            steps.append(functools.partial(ring.plane_arrive, 0, k - 1))
        if k == late:
            steps.append(functools.partial(ring.start, 1))
        later.append(functools.partial(ring.arrive, 1, k))
        if k > 1:
            later.append(functools.partial(ring.plane_arrive, 1, k - 1))
    steps += [functools.partial(ring.plane_arrive, 0, ring.far), functools.partial(ring.finish, 0)]
    later += [functools.partial(ring.plane_arrive, 1, ring.far)]
    early = later[:1]
    later = later[1:]
    steps = steps[:-1] + early + steps[-1:]
    cut = max(1, TABLE // 256 // len(steps))
    done = 0
    for i, event in enumerate(steps):
        upto = TABLE // 256 if i == len(steps) - 1 else min(TABLE // 256, (i + 1) * cut)
        if upto > done:
            lax.fori_loop(done, upto, table_column, 0)
            done = upto
        event()

    def column(step, carry):
        cols = pl.ds(pl.multiple_of(step * 256, 256), 256)
        product[:, cols] = jnp.dot(tokens[...], joint[:, cols], preferred_element_type=jnp.float32)
        return carry

    columns = JOINT // 256
    for i in range(3):
        lax.fori_loop(i * columns // 3, (i + 1) * columns // 3, column, 0)
        for event in later[i * len(later) // 4 : (i + 1) * len(later) // 4]:
            event()
    norm_tile = NORM // LANES * LANES
    turned_norm = joint[:, norm_tile : norm_tile + LANES].astype(jnp.float32).T
    norms[...] = turned_norm[NORM - norm_tile : NORM - norm_tile + 8]
    logits = product[:, ROUTERS : ROUTERS + 2 * HEADS * EXP]
    local_rows = tokens.shape[0]
    wide = jnp.concatenate([logits, jnp.zeros((local_rows, LANES - 2 * HEADS * EXP), jnp.float32)], axis=1)
    lane = lax.broadcasted_iota(jnp.int32, (local_rows, LANES), 1)
    mask = route_lanes(routes[...], lane)
    gate = 1.0 / (1.0 + jnp.exp(-wide))
    gates[0] = gate * mask
    gates[1] = gate * mask * (1.0 - gate)
    pad = jnp.zeros((local_rows, LANES - DH), jnp.float32)
    ones = jnp.ones((local_rows, LANES - DH), jnp.float32)
    for head in range(HEADS):
        first = head * DH
        qkv[head, 0] = jnp.concatenate([product[:, first : first + DH], pad], axis=1).astype(jnp.bfloat16)
        first = QCOLS + head * DH
        qkv[head, 1] = jnp.concatenate([product[:, first : first + DH], pad], axis=1).astype(jnp.bfloat16)
        total = None
        for expert in range(EXP):
            which = head * EXP + expert
            first = 2 * QCOLS + which * DH
            piece = product[:, first : first + DH]
            experts[which] = jnp.concatenate([piece, pad], axis=1).astype(jnp.bfloat16)
            term = piece * gates[0, :, which : which + 1]
            total = term if total is None else total + term
        qkv[head, 2] = jnp.concatenate([total, ones], axis=1).astype(jnp.bfloat16)
    for event in later[3 * len(later) // 4 :]:
        event()
    ring.finish(1)


def project(count, query, key, value, routers, tokens, routes, output_shard, gaps):
    rows, (shard_rows, _) = tokens.shape[0], query.shape
    f32, bf = jnp.float32, jnp.bfloat16
    return pl.pallas_call(
        functools.partial(project_kernel, count),
        out_shape=[
            jax.ShapeDtypeStruct((shard_rows * count, JOINT), bf),
            jax.ShapeDtypeStruct((count,) + output_shard.shape, bf),
            jax.ShapeDtypeStruct((HEADS, 3, rows, LANES), bf),
            jax.ShapeDtypeStruct((HEADS * EXP, rows, LANES), bf),
            jax.ShapeDtypeStruct((2, rows, LANES), f32),
            jax.ShapeDtypeStruct((8, shard_rows * count), f32),
            jax.ShapeDtypeStruct((3, LANES, TABLE), f32),
            jax.ShapeDtypeStruct((3, LANES, TABLE), f32),
        ],
        in_specs=[VMEM] * 6 + [ANY, SMEM],
        out_specs=[VMEM, ANY] + [VMEM] * 6,
        scratch_shapes=[pltpu.VMEM((shard_rows, JOINT), bf), pltpu.VMEM((rows, JOINT), f32)] + Gather.sems(count, 2),
        compiler_params=pltpu.CompilerParams(collective_id=1, has_side_effects=True, vmem_limit_bytes=56 << 20),
    )(query, key, value, routers, tokens, routes, output_shard, gaps)


def seq_mates(ring):
    return [ring.core_mate, ring.plane_mate, (3 - ring.seq, ring.fsdp)]


def slot_mates(ring):
    f = ring.fsdp
    return [(ring.seq, f + 1 - 2 * (f % 2)), (ring.seq, f + 2 - 4 * ((f // 2) % 2))]


def tile_place(slot, seq, phase, key_block, query_block):
    cont = slot // PSLOTS
    own = 1 - jnp.minimum(phase, 1)
    piece = jnp.where(slot == 3, 2 - phase, phase - 1)
    source = jnp.where(phase == 0, 0, 1 + piece)
    first = cont * 2 * (query_block // 2)
    active = jnp.where(
        phase == 0,
        (key_block <= query_block) & (key_block >= first),
        jnp.where(phase == 1, slot >= 1, slot >= 2),
    )
    far_column = jnp.where(
        cont == 1,
        2048 * piece + BLOCK * key_block - BLOCK * (query_block % 2) - 4096,
        BLOCK * key_block - 2048 - BLOCK * query_block,
    )
    column = jnp.where(phase == 0, BLOCK * (key_block - query_block), far_column)
    table = jnp.where((phase > 0) & (cont == 1), 1 + query_block // 2, 0)
    return source, active, table, column


def block_rows(block):
    return pl.ds(pl.multiple_of(block * BLOCK, BLOCK), BLOCK)


def attend_kernel(count, splits, steps, qkv, tables, *refs):
    T = len(splits)
    shards, refs = refs[:T], refs[T:]
    att, store, outputs, logs = refs[:4]
    fulls, refs = refs[4 : 4 + T], refs[4 + T :]
    acc, top, att_low, kv_send, kv_recv, q_send, q_recv, sh_send, sh_recv, out_send, out_recv, here = refs[:12]
    at = lambda t, g, cols: fulls[t].at[g, :, cols]
    ring = Gather(count, splits, shards, at, *refs[12:])
    seq, slot = ring.seq, ring.fsdp % GSLOTS
    mates, (x_mate, z_mate) = seq_mates(ring), slot_mates(ring)
    enter(ring.neighbours() + mates[2:] + [x_mate, z_mate])

    def remote(src, dst, send, recv, device):
        return pltpu.make_async_remote_copy(src, dst, send, recv, device_id=device, device_id_type=MESH)

    mine = block_rows(seq)

    def kv_copy(mate):
        return remote(qkv.at[mate[0], pl.ds(1, 2)], store.at[pl.ds(1, 2), mine], kv_send.at[mate[0]], kv_recv.at[seq], mate)

    def q_copy(mate):
        return remote(qkv.at[mate[0], 0], store.at[0, mine], q_send.at[mate[0]], q_recv.at[seq], mate)

    for mate in mates[1:] + mates[:1]:
        kv_copy(mate).start()
    own_copy = pltpu.make_async_copy(qkv.at[seq], store.at[pl.ds(0, 3), mine], here.at[0])
    own_copy.start()
    for mate in mates[1:] + mates[:1]:
        q_copy(mate).start()
    acc[...] = jnp.zeros_like(acc)
    top[...] = jnp.full_like(top, NEGATIVE)

    def far_rows(piece, chunk):
        return store.at[pl.ds(3 + 2 * piece, 2), block_rows(chunk)]

    def first_hop(chunk, way):
        src = store.at[pl.ds(1, 2), block_rows(chunk)]
        piece = slot % 2
        return remote(src, far_rows(piece, chunk), sh_send.at[4 * way + chunk], sh_recv.at[4 * piece + chunk],
                      x_mate if way == 0 else z_mate)

    def second_hop(chunk):
        piece = slot % 2
        return remote(far_rows(piece, chunk), far_rows(piece, chunk), sh_send.at[8 + chunk], sh_recv.at[4 * piece + chunk], x_mate)

    def share(chunk):
        @pl.when(slot < 2)
        def _():
            first_hop(chunk, 1).start()

        @pl.when(slot == 0)
        def _():
            first_hop(chunk, 0).start()

    def pass_on(chunk):
        @pl.when(slot >= 1)
        def _():
            piece = jnp.where(slot == 3, 1, 0)
            remote(far_rows(piece, chunk), far_rows(piece, chunk), sh_send.at[chunk], sh_recv.at[4 * piece + chunk], x_mate).wait_recv()

        @pl.when(slot >= 2)
        def _():
            second_hop(chunk).start()

    def last_piece(chunk):
        @pl.when(slot >= 2)
        def _():
            piece = 3 - slot
            remote(far_rows(piece, chunk), far_rows(piece, chunk), sh_send.at[chunk], sh_recv.at[4 * piece + chunk], x_mate).wait_recv()

    own_copy.wait()
    share(seq)
    for mate in mates:
        other = mate[0]
        src = store.at[pl.ds(1, 2), block_rows(other)]
        remote(src, src, kv_send.at[other], kv_recv.at[other], mate).wait_recv()
        share(other)
    for mate in mates:
        src = store.at[0, block_rows(mate[0])]
        remote(src, src, q_send.at[mate[0]], q_recv.at[mate[0]], mate).wait_recv()

    def tile(step):
        phase, key_block, query_block = step // 16, (step // 4) % 4, step % 4
        source, active, table, column = tile_place(slot, seq, phase, key_block, query_block)

        @pl.when(active)
        def _():
            rows = block_rows(query_block)
            keys = store[1 + 2 * source, block_rows(key_block), :]
            values = store[2 + 2 * source, block_rows(key_block), :]
            scores = lax.dot_general(store[0, rows, :], keys, (((1,), (1,)), ((), ())), preferred_element_type=jnp.float32)
            bias = jnp.concatenate(
                [tables[table, :, pl.ds(pl.multiple_of(column + TABLE_ZERO - LANES * part, LANES), BLOCK)] for part in range(BLOCK // LANES)],
                axis=0,
            )
            scores = scores * (DH**-0.5 * LOG2E) + bias
            before = top[rows, :]
            after = jnp.maximum(before, jnp.max(scores, axis=1, keepdims=True))
            factor = jnp.exp2(before - after)
            terms = jnp.exp2(scores - after[:, :1])
            acc[rows, :] = acc[rows, :] * factor + jnp.dot(terms.astype(jnp.bfloat16), values, preferred_element_type=jnp.float32)
            top[rows, :] = after

    events = {}
    for chunk in range(4):
        events.setdefault(4 * chunk, []).append(functools.partial(pass_on, chunk))
        events.setdefault(32 + 4 * chunk, []).append(functools.partial(last_piece, chunk))
    begin, gap = steps
    events.setdefault(begin, []).extend([functools.partial(ring.start, t) for t in range(T)])
    rest = []
    for i, event in enumerate(ring.events()):
        step = begin + gap * (i + 1)
        if step < 48:
            events.setdefault(step, []).append(event)
        else:
            rest.append(event)

    def step_body(step, carry):
        for when, actions in sorted(events.items()):
            @pl.when(step == when)
            def _():
                for action in actions:
                    action()
        tile(step)
        return carry

    lax.fori_loop(0, 48, step_body, 0)
    total = acc[:, DH : DH + 1]
    result = acc[...] / total
    outputs[...] = result
    log_total = top[...] + jnp.log2(total)
    for block in range(4):
        logs[:, block * BLOCK : (block + 1) * BLOCK] = log_total[block * BLOCK : (block + 1) * BLOCK].T[:8]
    att_low[...] = result.astype(jnp.bfloat16)

    def out_copy(mate):
        return remote(att_low.at[block_rows(mate[0])], att.at[seq], out_send.at[mate[0]], out_recv.at[seq], mate)

    for mate in mates[1:] + mates[:1]:
        out_copy(mate).start()
    own_out = pltpu.make_async_copy(att_low.at[mine], att.at[seq], here.at[1])
    own_out.start()
    for event in rest:
        event()
    own_out.wait()
    for mate in mates:
        kv_copy(mate).wait_send()
        q_copy(mate).wait_send()
        out_copy(mate).wait_send()
        ref = att.at[mate[0]]
        remote(ref, ref, out_send.at[mate[0]], out_recv.at[mate[0]], mate).wait_recv()
    for chunk in range(4):
        @pl.when(slot < 2)
        def _():
            first_hop(chunk, 1).wait_send()

        @pl.when(slot == 0)
        def _():
            first_hop(chunk, 0).wait_send()

        @pl.when(slot >= 2)
        def _():
            second_hop(chunk).wait_send()


def attend(count, qkv, tables, shards, splits, steps=(8, 2)):
    rows = qkv.shape[2]
    own = 4 * rows
    T = len(shards)
    return pl.pallas_call(
        functools.partial(attend_kernel, count, splits, steps),
        out_shape=[
            jax.ShapeDtypeStruct((HEADS, rows, LANES), jnp.bfloat16),
            jax.ShapeDtypeStruct((7, own, LANES), jnp.bfloat16),
            jax.ShapeDtypeStruct((own, LANES), jnp.float32),
            jax.ShapeDtypeStruct((8, own), jnp.float32),
        ]
        + [jax.ShapeDtypeStruct((count,) + w.shape, w.dtype) for w in shards],
        in_specs=[VMEM, VMEM] + [ANY] * T,
        out_specs=[VMEM] * 4 + [ANY] * T,
        scratch_shapes=[
            pltpu.VMEM((own, LANES), jnp.float32),
            pltpu.VMEM((own, LANES), jnp.float32),
            pltpu.VMEM((own, LANES), jnp.bfloat16),
            DMA((4,)), DMA((4,)), DMA((4,)), DMA((4,)), DMA((12,)), DMA((8,)), DMA((4,)), DMA((4,)), DMA((2,)),
        ]
        + Gather.sems(count, T),
        compiler_params=pltpu.CompilerParams(collective_id=2, has_side_effects=True, vmem_limit_bytes=56 << 20),
    )(qkv, tables, *shards)


class Scatter(Ring):
    def __init__(self, count, splits, parts, outs, bufs, sems):
        super().__init__(count, splits)
        self.parts, self.outs = parts, outs
        T = len(splits)
        self.mine, self.plane_in = bufs[:T], bufs[T : 2 * T]
        self.ring0, self.ring1 = bufs[2 * T : 3 * T], bufs[3 * T : 4 * T]
        self.low, self.low_in, self.done = bufs[4 * T : 5 * T], bufs[5 * T : 6 * T], bufs[6 * T : 7 * T]
        (self.load, self.plane_s, self.plane_r, self.ring_s, self.ring_r, self.end_s, self.end_r, self.put) = sems

    @staticmethod
    def scratch(count, splits, rows):
        half = [a + 2 * b for a, b in splits]
        bf = jnp.bfloat16
        out = [pltpu.VMEM((count, r, h), bf) for r, h in zip(rows, half)]
        out += [pltpu.VMEM((count, r, b), bf) for r, (a, b) in zip(rows, splits)]
        out += [pltpu.VMEM((count - 1 if a else 1, r, max(a, LANES)), bf) for r, (a, b) in zip(rows, splits)]
        out += [pltpu.VMEM((count - 1, r, b), bf) for r, (a, b) in zip(rows, splits)]
        out += [pltpu.VMEM((r, a + b), bf) for r, (a, b) in zip(rows, splits)]
        out += [pltpu.VMEM((r, a + b), bf) for r, (a, b) in zip(rows, splits)]
        out += [pltpu.VMEM((r, h), jnp.float32) for r, h in zip(rows, half)]
        T = len(splits)
        return out + [DMA((T * count,))] * 3 + [DMA((2 * T * (count - 1),))] * 2 + [DMA((2 * T,))] * 2 + [DMA((T,))]

    def dest(self, rel):
        return ring_index((self.place + rel) % self.count, self.count)

    def load_copy(self, t, rel):
        part, first = self.parts[t]
        src = part.at[self.dest(rel), :, pl.ds(first, self.half(t))]
        return pltpu.make_async_copy(src, self.mine[t].at[rel], self.load.at[t * self.count + rel])

    def remote(self, src, dst, s, r, i, device):
        return pltpu.make_async_remote_copy(src, dst, s.at[i], r.at[i], device_id=device, device_id_type=MESH)

    def single(self, t, plane):
        both, single = self.splits[t]
        return pl.ds(pl.multiple_of(both + plane * single, LANES), single)

    def plane_copy(self, t, rel):
        src = self.mine[t].at[rel, :, self.single(t, 1 - self.plane)]
        return self.remote(src, self.plane_in[t].at[rel], self.plane_s, self.plane_r, t * self.count + rel, self.plane_mate)

    def rels(self, D):
        return sorted({D % self.count, (-D) % self.count})

    def order(self):
        out = []
        for D in range(self.far, -1, -1):
            out += self.rels(D)
        return out

    def start(self, t):
        for rel in self.order():
            self.load_copy(t, rel).start()

    def ready(self, t, rel):
        if self.parts[t]:
            self.load_copy(t, rel).wait()
        self.plane_copy(t, rel).start()

    def all_ready(self, t):
        for rel in self.order():
            self.ready(t, rel)

    def step(self, t, D):
        self.combine(t, D)
        if D:
            self.chain(t, D)
        else:
            self.close(t)

    def buffer(self, t, kind, slot):
        if kind:
            return self.ring1[t].at[slot]
        return self.ring0[t].at[slot]

    def own_ref(self, t, kind, rel):
        if kind:
            return self.mine[t].at[rel, :, self.single(t, self.plane)]
        return self.mine[t].at[rel, :, pl.ds(0, self.splits[t][0])]

    def ring_copy(self, t, kind, way, D):
        slot = self.slot(kind, way, D)
        if D == self.reach(kind, way):
            src = self.own_ref(t, kind, D % self.count if way == 0 else (-D) % self.count)
        else:
            src = self.buffer(t, kind, self.slot(kind, way, D + 1))
        i = (2 * t + kind) * (self.count - 1) + slot
        return self.remote(src, self.buffer(t, kind, slot), self.ring_s, self.ring_r, i, self.next(way))

    def ring_wait(self, t, kind, way, D):
        slot = self.slot(kind, way, D)
        ref = self.buffer(t, kind, slot)
        i = (2 * t + kind) * (self.count - 1) + slot
        self.remote(ref, ref, self.ring_s, self.ring_r, i, self.next(way)).wait_recv()

    def combine(self, t, D):
        for rel in self.rels(D):
            self.plane_copy(t, rel).wait_send()
            ref = self.plane_in[t].at[rel]
            self.remote(ref, ref, self.plane_s, self.plane_r, t * self.count + rel, self.plane_mate).wait_recv()
            own = self.own_ref(t, 1, rel)
            own[...] = (own[...].astype(jnp.float32) + self.plane_in[t][rel].astype(jnp.float32)).astype(jnp.bfloat16)

    def chain(self, t, D):
        for kind in self.kinds(t):
            for way in (0, 1):
                if D > self.reach(kind, way):
                    continue
                if D < self.reach(kind, way):
                    self.ring_wait(t, kind, way, D + 1)
                    rel = D % self.count if way == 0 else (-D) % self.count
                    ref = self.buffer(t, kind, self.slot(kind, way, D + 1))
                    ref[...] = (ref[...].astype(jnp.float32) + self.own_ref(t, kind, rel)[...].astype(jnp.float32)).astype(jnp.bfloat16)
                self.ring_copy(t, kind, way, D).start()

    def end_copy(self, t):
        return self.remote(self.low[t], self.low_in[t], self.end_s, self.end_r, 2 * t, self.plane_mate)

    def close(self, t):
        both, single = self.splits[t]
        for kind in self.kinds(t):
            total = self.own_ref(t, kind, 0)[...].astype(jnp.float32)
            for way in (0, 1):
                if self.reach(kind, way):
                    self.ring_wait(t, kind, way, 1)
                    total = total + self.buffer(t, kind, self.slot(kind, way, 1))[...].astype(jnp.float32)
            if kind:
                self.low[t][:, both:] = total.astype(jnp.bfloat16)
            else:
                self.low[t][:, :both] = total.astype(jnp.bfloat16)
        self.end_copy(t).start()

    def out_ref(self, t, core):
        out, whole, first = self.outs[t]
        return out.at[:, pl.ds(pl.multiple_of(core * whole + first, LANES), self.half(t))]

    def out_copy(self, t):
        return self.remote(self.done[t], self.out_ref(t, self.core), self.end_s, self.end_r, 2 * t + 1, self.core_mate)

    def put_copy(self, t):
        return pltpu.make_async_copy(self.done[t], self.out_ref(t, self.core), self.put.at[t])

    def deliver(self, t):
        both, single = self.splits[t]
        self.end_copy(t).wait_send()
        ref = self.low_in[t]
        self.remote(ref, ref, self.end_s, self.end_r, 2 * t, self.plane_mate).wait_recv()
        if both:
            self.done[t][:, :both] = self.low[t][:, :both].astype(jnp.float32) + self.low_in[t][:, :both].astype(jnp.float32)
        if single:
            self.done[t][:, self.single(t, self.plane)] = self.low[t][:, both:].astype(jnp.float32)
            self.done[t][:, self.single(t, 1 - self.plane)] = self.low_in[t][:, both:].astype(jnp.float32)
        self.out_copy(t).start()
        self.put_copy(t).start()

    def finish(self, t):
        for kind in self.kinds(t):
            for way in (0, 1):
                for D in range(1, self.reach(kind, way) + 1):
                    self.ring_copy(t, kind, way, D).wait_send()
        self.out_copy(t).wait_send()
        self.put_copy(t).wait()
        ref = self.out_ref(t, 1 - self.core)
        self.remote(ref, ref, self.end_s, self.end_r, 2 * t + 1, self.core_mate).wait_recv()


def retreat_kernel(count, splits, steps, grad_att, turned, store, outputs, logs, part, back, out, *refs):
    T = len(splits)
    (grads, delta, grad_q, grad_kv, send_kv, kv_in0, kv_in1, low, in_send, in_recv, up_send, up_recv,
     out_send, out_recv, here) = refs[:15]
    refs = refs[15:]
    halves = [a + 2 * b for a, b in splits]
    firsts = [sum(halves[:t]) for t in range(T)]
    ring = Scatter(
        count, splits, [(part, first) for first in firsts], [(out, sum(halves), first) for first in firsts],
        refs[: 7 * T], refs[7 * T :])
    seq, slot = ring.seq, ring.fsdp % GSLOTS
    mates, (x_mate, z_mate) = seq_mates(ring), slot_mates(ring)
    enter(ring.neighbours() + mates[2:] + [x_mate, z_mate])

    def remote(src, dst, send, recv, device):
        return pltpu.make_async_remote_copy(src, dst, send, recv, device_id=device, device_id_type=MESH)

    mine = block_rows(seq)

    def in_copy(mate):
        return remote(grad_att.at[mate[0]], grads.at[mine], in_send.at[mate[0]], in_recv.at[seq], mate)

    for mate in mates[1:] + mates[:1]:
        in_copy(mate).start()
    own_copy = pltpu.make_async_copy(grad_att.at[seq], grads.at[mine], here.at[0])
    own_copy.start()
    grad_q[...] = jnp.zeros_like(grad_q)
    grad_kv[...] = jnp.zeros_like(grad_kv)
    own_copy.wait()
    for mate in mates:
        ref = grads.at[block_rows(mate[0])]
        remote(ref, ref, in_send.at[mate[0]], in_recv.at[mate[0]], mate).wait_recv()
    for block in range(4):
        rows = pl.ds(block * BLOCK, BLOCK)
        sums = jnp.sum(grads[rows, :].astype(jnp.float32) * outputs[rows, :], axis=1, keepdims=True)
        delta[:, rows] = jnp.broadcast_to(sums, (BLOCK, LANES)).T[:8]

    def tile(step):
        phase, key_block, query_block = step // 16, (step // 4) % 4, step % 4
        piece = jnp.where(slot == 2, 1 - phase, phase)
        forward_phase = jnp.where(phase == 2, 0, jnp.where(slot == 3, 2 - piece, 1 + piece))
        source, active, table, column = tile_place(slot, seq, forward_phase, key_block, query_block)

        @pl.when(active)
        def _():
            rows, key_rows = block_rows(query_block), block_rows(key_block)
            keys, values = store[1 + 2 * source, key_rows, :], store[2 + 2 * source, key_rows, :]
            queries, tops = store[0, rows, :], grads[rows, :]
            scores = lax.dot_general(keys, queries, (((1,), (1,)), ((), ())), preferred_element_type=jnp.float32)
            bias = jnp.concatenate(
                [turned[table, :, pl.ds(pl.multiple_of(TURNED_ZERO - column - LANES * part, LANES), BLOCK)] for part in range(BLOCK // LANES)],
                axis=0,
            )
            weights = jnp.exp2(scores * (DH**-0.5 * LOG2E) + (bias - logs[:1, rows]))
            grad_weights = lax.dot_general(values, tops, (((1,), (1,)), ((), ())), preferred_element_type=jnp.float32)
            grad_scores = (weights * (grad_weights - delta[:1, rows])).astype(jnp.bfloat16)
            grad_kv[source, 1, key_rows, :] += jnp.dot(weights.astype(jnp.bfloat16), tops, preferred_element_type=jnp.float32)
            grad_kv[source, 0, key_rows, :] += jnp.dot(grad_scores, queries, preferred_element_type=jnp.float32)
            grad_q[rows, :] += lax.dot_general(grad_scores, keys, (((0,), (0,)), ((), ())), preferred_element_type=jnp.float32)

    scale = DH**-0.5

    def rounded(source, chunk, extra):
        rows = block_rows(chunk)
        keys = grad_kv[source, 0, rows, :] * scale
        values = grad_kv[source, 1, rows, :]
        for more in extra:
            keys = keys + more[0].astype(jnp.float32)
            values = values + more[1].astype(jnp.float32)
        return keys.astype(jnp.bfloat16), values.astype(jnp.bfloat16)

    def x_send(chunk):
        src = send_kv.at[0, :, block_rows(chunk)]
        return remote(src, kv_in0.at[:, block_rows(chunk)], up_send.at[chunk], up_recv.at[chunk], x_mate)

    def z_send(chunk):
        src = send_kv.at[1, :, block_rows(chunk)]
        return remote(src, kv_in1.at[:, block_rows(chunk)], up_send.at[4 + chunk], up_recv.at[4 + chunk], z_mate)

    def x_wait(chunk):
        ref = kv_in0.at[:, block_rows(chunk)]
        remote(ref, ref, up_send.at[chunk], up_recv.at[chunk], x_mate).wait_recv()

    def z_wait(chunk):
        ref = kv_in1.at[:, block_rows(chunk)]
        remote(ref, ref, up_send.at[4 + chunk], up_recv.at[4 + chunk], z_mate).wait_recv()

    def first_done(chunk):
        @pl.when(slot >= 1)
        def _():
            source = jnp.where(slot == 2, 2, 1)
            keys, values = rounded(source, chunk, [])
            send_kv[0, 0, block_rows(chunk), :] = keys
            send_kv[0, 1, block_rows(chunk), :] = values
            x_send(chunk).start()

    def second_done(chunk):
        @pl.when(slot >= 2)
        def _():
            x_wait(chunk)
            source = slot - 1
            keys, values = rounded(source, chunk, [kv_in0[:, block_rows(chunk), :]])
            send_kv[1, 0, block_rows(chunk), :] = keys
            send_kv[1, 1, block_rows(chunk), :] = values
            z_send(chunk).start()

    def out_copy(mate):
        src = low.at[:, block_rows(mate[0])]
        return remote(src, back.at[seq], out_send.at[mate[0]], out_recv.at[seq], mate)

    def own_done(chunk):
        rows = block_rows(chunk)
        low[0, rows, :] = (grad_q[rows, :] * scale).astype(jnp.bfloat16)

        @pl.when(slot == 0)
        def _():
            x_wait(chunk)
            z_wait(chunk)
            low[1, rows, :], low[2, rows, :] = rounded(0, chunk, [kv_in0[:, rows, :], kv_in1[:, rows, :]])

        @pl.when(slot == 1)
        def _():
            z_wait(chunk)
            low[1, rows, :], low[2, rows, :] = rounded(0, chunk, [kv_in1[:, rows, :]])

        @pl.when(slot >= 2)
        def _():
            low[1, rows, :], low[2, rows, :] = rounded(0, chunk, [])

    events = {}
    for chunk in range(4):
        events.setdefault(4 * chunk + 4, []).append(functools.partial(first_done, chunk))
        events.setdefault(20 + 4 * chunk, []).append(functools.partial(second_done, chunk))
    begin, ready, first, hop, lag = steps
    rest = []
    for t in range(T):
        plan = [(begin, functools.partial(ring.start, t)), (ready, functools.partial(ring.all_ready, t))]
        when = first + lag * t
        for D in range(ring.far, -1, -1):
            plan.append((when, functools.partial(ring.step, t, D)))
            when += hop
        plan.append((when, functools.partial(ring.deliver, t)))
        plan.append((when + hop, functools.partial(ring.finish, t)))
        for when, event in plan:
            if when < 48:
                events.setdefault(int(when), []).append(event)
            else:
                rest.append((when, event))
    rest = [event for when, event in sorted(rest, key=lambda pair: pair[0])]

    def step_body(step, carry):
        for when, actions in sorted(events.items()):
            @pl.when(step == when)
            def _():
                for action in actions:
                    action()
        tile(step)
        return carry

    lax.fori_loop(0, 48, step_body, 0)
    for chunk in range(4):
        own_done(chunk)
    for mate in mates[1:] + mates[:1]:
        out_copy(mate).start()
    own_out = pltpu.make_async_copy(low.at[:, mine], back.at[seq], here.at[1])
    own_out.start()
    for event in rest:
        event()
    own_out.wait()
    for mate in mates:
        in_copy(mate).wait_send()
        out_copy(mate).wait_send()
        ref = back.at[mate[0]]
        remote(ref, ref, out_send.at[mate[0]], out_recv.at[mate[0]], mate).wait_recv()
    for chunk in range(4):
        @pl.when(slot >= 1)
        def _():
            x_send(chunk).wait_send()

        @pl.when(slot >= 2)
        def _():
            z_send(chunk).wait_send()


def retreat(count, grad_att, turned, store, outputs, logs, part, splits, steps=(0, 1, 6, 6, 2)):
    rows = grad_att.shape[1]
    own = 4 * rows
    _, shard_rows, half = part.shape
    return pl.pallas_call(
        functools.partial(retreat_kernel, count, splits, steps),
        out_shape=[jax.ShapeDtypeStruct((HEADS, 3, rows, LANES), jnp.bfloat16), jax.ShapeDtypeStruct((shard_rows, 2 * half), jnp.float32)],
        in_specs=[VMEM] * 5 + [ANY],
        out_specs=[VMEM, ANY],
        scratch_shapes=[
            pltpu.VMEM((own, LANES), jnp.bfloat16),
            pltpu.VMEM((8, own), jnp.float32),
            pltpu.VMEM((own, LANES), jnp.float32),
            pltpu.VMEM((3, 2, own, LANES), jnp.float32),
            pltpu.VMEM((2, 2, own, LANES), jnp.bfloat16),
            pltpu.VMEM((2, own, LANES), jnp.bfloat16),
            pltpu.VMEM((2, own, LANES), jnp.bfloat16),
            pltpu.VMEM((3, own, LANES), jnp.bfloat16),
            DMA((4,)), DMA((4,)), DMA((8,)), DMA((8,)), DMA((4,)), DMA((4,)), DMA((2,)),
        ]
        + Scatter.scratch(count, splits, [shard_rows] * len(splits)),
        compiler_params=pltpu.CompilerParams(collective_id=3, has_side_effects=True, vmem_limit_bytes=60 << 20),
    )(grad_att, turned, store, outputs, logs, part)


CHUNK = 512


def gelu_pair(v):
    root = 0.7978845608028654
    square = v * v
    t = jnp.tanh(root * (v + 0.044715 * square * v))
    up = 0.5 * (1.0 + t)
    return v * up, up + 0.5 * v * (1.0 - t * t) * (root * (1.0 + 3.0 * 0.044715 * square))


def contract(left, right, left_axis, right_axis):
    return lax.dot_general(left, right, (((left_axis,), (right_axis,)), ((), ())), preferred_element_type=jnp.float32)


def feed_kernel(count, att, gates, tokens, cotangent, norms, output_w, inner_w, outer_w,
                layer_out, grad_residual, grad_att, grad_logit, grad_norms, part_output, part_inner, outer_out,
                w_out, w_in, w_up, acts, act_in, slopes, slope_in, scaled, scaled_in, scaled_t, cot_in, cot_t,
                acc, normed, grad_scaled, branch_low, branch_in, branch_t, att_in, gates_in,
                stage_inner, stage_output,
                load_out, load_in, load_up, pair_s, pair_r, act_s, act_r, slope_s, slope_r, put_inner, put_output, *refs):
    half = cotangent.shape[1] // 2
    ring = Scatter(count, (SPLITS["outer"],), [None], [(outer_out, half, 0)], refs[:7], refs[7:])
    core, mate = ring.core, ring.core_mate
    experts = HEADS * EXP
    chunks = inner_w.shape[1] // CHUNK
    small = CHUNK // 2
    shards = max(1, count // chunks)

    def out_load(e):
        return pltpu.make_async_copy(output_w.at[pl.ds(e * DH, DH)], w_out.at[e, pl.ds(0, DH)], load_out.at[e])

    def ffn_load(chunk, slot):
        cols = pl.ds(pl.multiple_of(chunk * CHUNK, CHUNK), CHUNK)
        return (pltpu.make_async_copy(inner_w.at[:, cols], w_in.at[slot], load_in.at[slot]),
                pltpu.make_async_copy(outer_w.at[cols], w_up.at[slot], load_up.at[slot]))

    def chunk_of(step):
        if count != chunks:
            return step
        D = ring.far - (step + 1) // 2
        odd = step % 2
        return ring.dest((odd * D + (1 - odd) * (count - D)) % count)

    for e in range(experts):
        out_load(e).start()
    for sub in range(2):
        for copy in ffn_load(chunk_of(sub), sub):
            copy.start()
    enter(ring.neighbours())

    def remote(src, dst, send, recv):
        return pltpu.make_async_remote_copy(src, dst, send, recv, device_id=mate, device_id_type=MESH)

    mine = pl.ds(pl.multiple_of(core * half, LANES), half)
    yours = pl.ds(pl.multiple_of((1 - core) * half, LANES), half)
    pair = [
        remote(att, att_in, pair_s.at[0], pair_r.at[0]),
        remote(gates.at[0], gates_in, pair_s.at[1], pair_r.at[1]),
        remote(cotangent.at[:, yours], cot_in, pair_s.at[2], pair_r.at[2]),
        remote(scaled, scaled_in, pair_s.at[3], pair_r.at[3]),
        remote(branch_low.at[:, yours], branch_in, pair_s.at[4], pair_r.at[4]),
    ]
    for copy in pair[:3]:
        copy.start()

    def mixed_pair(att_ref, gate, two):
        tiles = []
        for which in (2 * two, 2 * two + 1):
            column = gate[:, experts + which : experts + which + 1]
            tiles.append((att_ref[which // EXP].astype(jnp.float32) * column).astype(jnp.bfloat16))
        return jnp.concatenate(tiles, axis=1)

    w_out[:, DH:, :] = jnp.zeros((experts, LANES - DH, w_out.shape[2]), jnp.bfloat16)
    acc[...] = tokens[...].astype(jnp.float32)
    for two in range(experts // 2):
        out_load(2 * two).wait()
        out_load(2 * two + 1).wait()
        weights = w_out[2 * two : 2 * two + 2].reshape(2 * LANES, w_out.shape[2])
        acc[...] += jnp.dot(mixed_pair(att, gates.at[0], two), weights, preferred_element_type=jnp.float32)
    residual = acc[...]
    centred = residual - jnp.mean(residual, axis=1, keepdims=True)
    inverse = lax.rsqrt(jnp.mean(centred * centred, axis=1, keepdims=True) + EPSILON)
    normed[...] = centred * inverse
    scaled[...] = (normed[...] * norms[:1] + norms[1:2]).astype(jnp.bfloat16)
    pair[3].start()
    rows = tokens.shape[0]
    scaled_t[:, :rows] = scaled[...].T
    cot_t[:, :rows] = cotangent[:, mine].T
    grad_scaled[...] = jnp.zeros_like(grad_scaled)
    pair[2].wait_recv()
    cot_t[:, rows:] = cot_in[...].T
    pair[3].wait_recv()
    scaled_t[:, rows:] = scaled_in[...].T

    small_mine = pl.ds(pl.multiple_of(core * small, LANES), small)
    small_yours = pl.ds(pl.multiple_of((1 - core) * small, LANES), small)

    def act_copy(step, sub):
        return remote(acts.at[sub], act_in.at[step], act_s.at[sub], act_r.at[step])

    def slope_copy(step, sub):
        return remote(slopes.at[sub, :, small_yours], slope_in.at[step], slope_s.at[sub], slope_r.at[step])

    def put_inner_copy(step, sub):
        cols = pl.ds(pl.multiple_of(chunk_of(step) * small, small), small)
        return pltpu.make_async_copy(stage_inner.at[sub], part_inner.at[:, cols], put_inner.at[sub])

    def forward_backward(step, sub):
        for copy in ffn_load(chunk_of(step), sub):
            copy.wait()

        @pl.when(step > 1)
        def _():
            act_copy(step, sub).wait_send()
            slope_copy(step, sub).wait_send()

        act, slope = gelu_pair(jnp.dot(scaled[...], w_in[sub], preferred_element_type=jnp.float32))
        acts[sub] = act.astype(jnp.bfloat16)
        act_copy(step, sub).start()
        slopes[sub] = (contract(cotangent[...], w_up[sub], 1, 1) * slope).astype(jnp.bfloat16)
        slope_copy(step, sub).start()
        acc[...] += jnp.dot(acts[sub], w_up[sub], preferred_element_type=jnp.float32)
        grad_scaled[...] += contract(slopes[sub], w_in[sub], 1, 1)

        @pl.when(step + 2 < chunks)
        def _():
            for copy in ffn_load(chunk_of(step + 2), sub):
                copy.start()

    def weight_parts(step, sub):
        remote(act_in.at[step], act_in.at[step], act_s.at[sub], act_r.at[step]).wait_recv()
        total = jnp.dot(cot_t[:, :rows], acts[sub], preferred_element_type=jnp.float32)
        total = total + jnp.dot(cot_t[:, rows:], act_in[step], preferred_element_type=jnp.float32)
        turned = total.astype(jnp.bfloat16).T
        shard_rows = CHUNK // shards
        for q in range(shards):
            rel = (ring_place(chunk_of(step) * shards + q, count) - ring.place + count) % count
            ring.mine[0][rel] = turned[q * shard_rows : (q + 1) * shard_rows]
        remote(slope_in.at[step], slope_in.at[step], slope_s.at[sub], slope_r.at[step]).wait_recv()

        @pl.when(step > 1)
        def _():
            put_inner_copy(step, sub).wait()

        total = jnp.dot(scaled_t[:, :rows], slopes[sub, :, small_mine], preferred_element_type=jnp.float32)
        total = total + jnp.dot(scaled_t[:, rows:], slope_in[step], preferred_element_type=jnp.float32)
        stage_inner[sub] = total.astype(jnp.bfloat16)
        put_inner_copy(step, sub).start()

    events = {}
    if count == chunks:
        for step, rel in enumerate(ring.order()):
            events.setdefault(step, []).append(functools.partial(ring.ready, 0, rel))
        for D in range(ring.far, 0, -1):
            events.setdefault(2 * (ring.far - D) + 1, []).append(functools.partial(ring.step, 0, D))

    def after_parts(step):
        for when, actions in sorted(events.items()):
            @pl.when(step == when)
            def _():
                for action in actions:
                    action()

    def iteration(i, carry):
        forward_backward(2 * i, 0)

        @pl.when(i > 0)
        def _():
            weight_parts(2 * i - 1, 1)
            after_parts(2 * i - 1)

        forward_backward(2 * i + 1, 1)
        weight_parts(2 * i, 0)
        after_parts(2 * i)
        return carry

    lax.fori_loop(0, chunks // 2, iteration, 0)
    weight_parts(chunks - 1, 1)
    if count == chunks:
        for action in events[chunks - 1]:
            action()
    else:
        ring.all_ready(0)
        for D in range(ring.far, 0, -1):
            ring.step(0, D)
    layer_out[...] = acc[...].astype(jnp.bfloat16)
    slope = grad_scaled[...]
    grad_norms[...] = jnp.concatenate(
        [jnp.sum(slope * normed[...], axis=0, keepdims=True), jnp.sum(slope, axis=0, keepdims=True),
         jnp.zeros((6, slope.shape[1]), jnp.float32)], axis=0)
    slope = slope * norms[:1]
    total = cotangent[...].astype(jnp.float32) + inverse * (
        slope - jnp.mean(slope, axis=1, keepdims=True)
        - normed[...] * jnp.mean(slope * normed[...], axis=1, keepdims=True))
    grad_residual[...] = total
    branch_low[...] = total.astype(jnp.bfloat16)
    pair[4].start()
    branch_t[:, :rows] = branch_low[:, mine].T
    ring.step(0, 0)
    lane = lax.broadcasted_iota(jnp.int32, (rows, LANES), 1)
    logit = jnp.zeros((rows, LANES), jnp.float32)
    head_total = None
    for which in range(experts):
        if which % 2 == 0:
            weights = w_out[which : which + 2].reshape(2 * LANES, w_out.shape[2])
            both = contract(branch_low[...], weights, 1, 1)
        grad_mixed = both[:, which % 2 * LANES : (which % 2 + 1) * LANES]
        head, expert = which // EXP, which % EXP
        column = slice(experts + which, experts + which + 1)
        term = grad_mixed * gates[0, :, column]
        head_total = term if expert == 0 else head_total + term
        if expert == EXP - 1:
            grad_att[head] = head_total.astype(jnp.bfloat16)
        sums = jnp.sum(grad_mixed * att[head].astype(jnp.float32), axis=1, keepdims=True)
        logit = jnp.where(lane == experts + which, sums, logit)
    grad_logit[...] = logit * gates[1]
    ring.deliver(0)
    pair[0].wait_recv()
    pair[1].wait_recv()
    pair[4].wait_recv()
    branch_t[:, rows:] = branch_in[...].T

    def put_output_copy(which):
        return pltpu.make_async_copy(stage_output.at[which % 4, pl.ds(0, DH)], part_output.at[pl.ds(which * DH, DH)], put_output.at[which % 4])

    for two in range(experts // 2):
        total = jnp.dot(branch_t[:, :rows], mixed_pair(att, gates.at[0], two), preferred_element_type=jnp.float32)
        total = total + jnp.dot(branch_t[:, rows:], mixed_pair(att_in, gates_in, two), preferred_element_type=jnp.float32)
        turned = total.astype(jnp.bfloat16).T
        for side in range(2):
            which = 2 * two + side
            if which >= 4:
                put_output_copy(which - 4).wait()
            stage_output[which % 4] = turned[side * LANES : (side + 1) * LANES]
            put_output_copy(which).start()
    for which in range(experts - 4, experts):
        put_output_copy(which).wait()
    for sub in range(2):
        put_inner_copy(sub, sub).wait()
        act_copy(sub, sub).wait_send()
        slope_copy(sub, sub).wait_send()
    ring.finish(0)
    for copy in pair:
        copy.wait_send()


def feed(count, att, gates, tokens, cotangent, norms, output_w, inner_w, outer_w):
    rows, width = tokens.shape
    wide = inner_w.shape[1]
    half = width // 2
    f32, bf = jnp.float32, jnp.bfloat16
    experts, chunks = HEADS * EXP, wide // CHUNK
    V = pltpu.VMEM
    return pl.pallas_call(
        functools.partial(feed_kernel, count),
        out_shape=[
            jax.ShapeDtypeStruct((rows, width), bf),
            jax.ShapeDtypeStruct((rows, width), f32),
            jax.ShapeDtypeStruct((HEADS, rows, LANES), bf),
            jax.ShapeDtypeStruct((rows, LANES), f32),
            jax.ShapeDtypeStruct((8, width), f32),
            jax.ShapeDtypeStruct((VCOLS, half), bf),
            jax.ShapeDtypeStruct((width, wide // 2), bf),
            jax.ShapeDtypeStruct((wide // count, width), f32),
        ],
        in_specs=[VMEM] * 5 + [ANY] * 3,
        out_specs=[VMEM] * 5 + [ANY] * 3,
        scratch_shapes=[
            V((experts, LANES, width), bf), V((2, width, CHUNK), bf), V((2, CHUNK, width), bf),
            V((2, rows, CHUNK), bf), V((chunks, rows, CHUNK), bf), V((2, rows, CHUNK), bf), V((chunks, rows, CHUNK // 2), bf),
            V((rows, width), bf), V((rows, width), bf), V((width, 2 * rows), bf), V((rows, half), bf), V((half, 2 * rows), bf),
            V((rows, width), f32), V((rows, width), f32), V((rows, width), f32),
            V((rows, width), bf), V((rows, half), bf), V((half, 2 * rows), bf), V((HEADS, rows, LANES), bf), V((rows, LANES), f32),
            V((2, width, CHUNK // 2), bf), V((4, LANES, half), bf),
            DMA((experts,)), DMA((2,)), DMA((2,)), DMA((5,)), DMA((5,)), DMA((2,)), DMA((chunks,)), DMA((2,)), DMA((chunks,)),
            DMA((2,)), DMA((4,)),
        ]
        + Scatter.scratch(count, (SPLITS["outer"],), [wide // count]),
        compiler_params=pltpu.CompilerParams(collective_id=4, has_side_effects=True, vmem_limit_bytes=63 << 20),
    )(att, gates, tokens, cotangent, norms, output_w, inner_w, outer_w)


def settle_kernel(count, back, experts, gates, grad_logit, tokens, joint, grad_residual, grad_norms, part_output,
                  grad_tokens, joint_out, output_out, grads, grads_in, tokens_in, tokens_t, norms_in, norm_columns, *refs):
    splits = (SPLITS["joint"], SPLITS["output"])
    pair_s, pair_r = refs[-2:]
    half, output_half = JOINT // 2, part_output.shape[2]
    outs = [(joint_out, half, 0), (output_out, output_half, 0)]
    ring = Scatter(count, splits, [None, (part_output, 0)], outs, refs[:14], refs[14:-2])
    ring.start(1)
    enter(ring.neighbours())
    core = ring.core

    def remote(src, dst, i):
        return pltpu.make_async_remote_copy(src, dst, pair_s.at[i], pair_r.at[i], device_id=ring.core_mate, device_id_type=MESH)

    mine = pl.ds(pl.multiple_of(core * half, LANES), half)
    yours = pl.ds(pl.multiple_of((1 - core) * half, LANES), half)
    pair = [remote(tokens, tokens_in, 0), remote(grad_norms, norms_in, 1), remote(grads.at[:, yours], grads_in, 2)]
    pair[0].start()
    pair[1].start()
    ring.all_ready(1)
    rows = tokens.shape[0]
    lane = lax.broadcasted_iota(jnp.int32, (LANES, LANES), 1)
    width = HEADS * EXP

    def assemble(block, carry):
        part = pl.ds(pl.multiple_of(block * LANES, LANES), LANES)
        pieces = [back[head, which, part, :][:, :DH].astype(jnp.float32) for which in range(2) for head in range(HEADS)]
        logit = grad_logit[part, :]
        for head in range(HEADS):
            values = back[head, 2, part, :].astype(jnp.float32)
            for expert in range(EXP):
                which = head * EXP + expert
                pieces.append((values * gates[0, part, which : which + 1])[:, :DH])
                sums = jnp.sum(values * experts[which, part, :].astype(jnp.float32), axis=1, keepdims=True)
                logit = jnp.where(lane == which, sums * gates[1, part, which : which + 1], logit)
        pieces.append(jnp.where(lane < 2 * width, logit, 0.0))
        pieces.append(jnp.zeros((LANES, JOINT - ROUTERS - LANES), jnp.float32))
        grads[part, :] = jnp.concatenate(pieces, axis=1).astype(jnp.bfloat16)
        return carry

    lax.fori_loop(0, rows // LANES, assemble, 0)
    pair[2].start()
    ring.step(1, ring.far)
    tokens_t[:, :rows] = tokens[...].T
    for copy in pair[:2]:
        copy.wait_recv()
    tokens_t[:, rows:] = tokens_in[...].T
    norm_tile = NORM // LANES * LANES - half
    first = NORM - half - norm_tile
    both = grad_norms[...] + norms_in[...]
    for block in range(both.shape[1] // LANES):
        columns = jnp.concatenate([both[:, block * LANES : (block + 1) * LANES], jnp.zeros((LANES - 8, LANES), jnp.float32)], axis=0)
        norm_columns[block * LANES : (block + 1) * LANES, :] = columns.T
    pair[2].wait_recv()
    shard_rows = tokens_t.shape[0] // count
    tile_lane = lax.broadcasted_iota(jnp.int32, (shard_rows, LANES), 1)

    def fill(rel):
        part = pl.ds(pl.multiple_of(ring.dest(rel) * shard_rows, shard_rows), shard_rows)
        total = jnp.dot(tokens_t[part, :rows], grads[:, mine], preferred_element_type=jnp.float32)
        total = total + jnp.dot(tokens_t[part, rows:], grads_in[...], preferred_element_type=jnp.float32)
        ring.mine[0][rel] = total.astype(jnp.bfloat16)
        extra = jnp.where(tile_lane == first, norm_columns[part, 0:1], 0.0) + jnp.where(tile_lane == first + 1, norm_columns[part, 1:2], 0.0)
        tile = total[:, norm_tile : norm_tile + LANES] + extra * core.astype(jnp.float32)
        ring.mine[0][rel, :, norm_tile : norm_tile + LANES] = tile.astype(jnp.bfloat16)

    for rel in ring.order():
        fill(rel)
        ring.ready(0, rel)
    ring.step(0, ring.far)
    for D in range(ring.far - 1, 0, -1):
        ring.step(1, D)
        ring.step(0, D)
        if D == ring.far - 1:
            grad_tokens[...] = grad_residual[...] + contract(grads[...], joint[...], 1, 1)
    ring.step(1, 0)
    ring.step(0, 0)
    ring.deliver(1)
    ring.deliver(0)
    ring.finish(1)
    ring.finish(0)
    for copy in pair:
        copy.wait_send()


def settle(count, back, experts, gates, grad_logit, tokens, joint, grad_residual, grad_norms, part_output):
    rows, width = tokens.shape
    shard_rows = width // count
    f32, bf = jnp.float32, jnp.bfloat16
    V = pltpu.VMEM
    return pl.pallas_call(
        functools.partial(settle_kernel, count),
        out_shape=[jax.ShapeDtypeStruct((rows, width), f32), jax.ShapeDtypeStruct((shard_rows, JOINT), f32),
                   jax.ShapeDtypeStruct((part_output.shape[1], width), f32)],
        in_specs=[VMEM] * 8 + [ANY],
        out_specs=[VMEM, VMEM, ANY],
        scratch_shapes=[V((rows, JOINT), bf), V((rows, JOINT // 2), bf), V((rows, width), bf), V((width, 2 * rows), bf), V((8, width), f32), V((width, LANES), f32)]
        + Scatter.scratch(count, (SPLITS["joint"], SPLITS["output"]), [shard_rows, part_output.shape[1]])
        + [DMA((3,)), DMA((3,))],
        compiler_params=pltpu.CompilerParams(collective_id=5, has_side_effects=True, vmem_limit_bytes=60 << 20),
    )(back, experts, gates, grad_logit, tokens, joint, grad_residual, grad_norms, part_output)


def publish_kernel(joint_w, output_w, inner_w, outer_w, layer, tokens_in,
                   query, key, value, value_router, output_router, norms, output_out, inner_out, outer_out, layer_out, tokens_out, sems):
    half, small = inner_w.shape[1] // 2, CHUNK // 2
    copies = [(output_w, output_out), (outer_w, outer_out), (layer, layer_out), (tokens_in, tokens_out)]
    for core in range(2):
        for chunk in range(half // small):
            copies.append((inner_w.at[:, pl.ds(core * half + chunk * small, small)],
                           inner_out.at[:, pl.ds(chunk * CHUNK + core * small, small)]))
    copies = [pltpu.make_async_copy(src, dst, sems.at[i]) for i, (src, dst) in enumerate(copies)]
    for copy in copies:
        copy.start()
    query[...] = joint_w[:, :QCOLS]
    key[...] = joint_w[:, QCOLS : 2 * QCOLS]
    value[...] = joint_w[:, 2 * QCOLS : ROUTERS]
    value_router[...] = joint_w[:, ROUTERS : ROUTERS + HEADS * EXP]
    output_router[...] = joint_w[:, ROUTERS + HEADS * EXP : NORM]
    norms[...] = joint_w[:, NORM : NORM + 2]
    for copy in copies:
        copy.wait()


def publish(joint_w, output_w, inner_w, outer_w, layer, tokens):
    rows = joint_w.shape[0]
    f32 = jnp.float32
    columns = [QCOLS, QCOLS, VCOLS, HEADS * EXP, HEADS * EXP, 2]
    rest = (output_w, inner_w, outer_w, layer, tokens)
    return pl.pallas_call(
        publish_kernel,
        out_shape=[jax.ShapeDtypeStruct((rows, c), f32) for c in columns] + [jax.ShapeDtypeStruct(x.shape, x.dtype) for x in rest],
        in_specs=[VMEM] + [ANY] * 5,
        out_specs=[VMEM] * 6 + [ANY] * 5,
        scratch_shapes=[DMA((4 + inner_w.shape[1] // (CHUNK // 2),))],
    )(joint_w, *rest)


def on_device(
    tokens, value_routes, output_routes, cont_gap, query_weight, key_weight, value_weight, value_router,
    output_router, output_weight, norm_gain, norm_bias, inner_weight, outer_weight, cotangent,
):
    count = lax.axis_size("fsdp")
    inputs = tokens[0]
    rows, width = inputs.shape
    routers = jnp.concatenate(
        [value_router, output_router, norm_gain[:, None], norm_bias[:, None],
         jnp.zeros((query_weight.shape[0], JOINT - NORM - 2), jnp.bfloat16)], axis=1)
    routes = jnp.concatenate([value_routes[0].reshape(rows, -1), output_routes[0].reshape(rows, -1)], axis=1)
    joint, output_full, qkv, experts, gates, norms, tables, turned = project(
        count, query_weight, key_weight, value_weight, routers, inputs, routes, output_weight, cont_gap)
    att, store, outputs, logs, inner_full, outer_full = attend(
        count, qkv, tables, (inner_weight, outer_weight), (SPLITS["inner"], SPLITS["outer"]))
    layer, grad_residual, grad_att, grad_logit, grad_norms, part_output, part_inner, outer_w = feed(
        count, att, gates, inputs, cotangent[0], norms, output_full.reshape(VCOLS, width), inner_full.reshape(width, -1),
        outer_full.reshape(-1, width))
    back, inner_w = retreat(
        count, grad_att, turned, store, outputs, logs, part_inner.reshape(count, -1, part_inner.shape[1]), INNER_PARTS)
    grad_input, joint_w, output_w = settle(
        count, back, experts, gates, grad_logit, inputs, joint, grad_residual, grad_norms,
        part_output.reshape(count, -1, part_output.shape[1]))
    query, key, value, value_r, output_r, norm_w, output_w, inner_w, outer_w, layer, grad_input = publish(
        joint_w, output_w, inner_w, outer_w, layer, grad_input)
    return (layer[None], grad_input[None], query, key, value, value_r, output_r, output_w, norm_w[:, 0], norm_w[:, 1], inner_w, outer_w)


def solution(mesh):
    wide = P("fsdp", None)
    part = P("fsdp", "seq", None)
    routes = P("fsdp", "seq", None, None)
    return jax.shard_map(
        on_device,
        mesh=mesh,
        in_specs=(part, routes, routes, P()) + (wide,) * 6 + (P("fsdp"), P("fsdp"), wide, wide, part),
        out_specs=(part, part) + (wide,) * 6 + (P("fsdp"), P("fsdp"), wide, wide),
        check_vma=False,
    )
```

```python
import functools
import jax
import jax.numpy as jnp
from jax import lax
from jax.experimental import pallas as pl
from jax.experimental.pallas import tpu as pltpu
from jax.sharding import PartitionSpec as P

HEADS = 4
DH = 112
EXP = 5
CONT = 1024
GSLOTS = 4
PSLOTS = 2
BLOCK = 512
LANES = 128
EPSILON = 1e-05
NEGATIVE = -1e30
LOG2E = 1.4426950408889634
MESH = pl.DeviceIdType.MESH
ANY = pl.BlockSpec(memory_space=pl.ANY)
VMEM = pl.BlockSpec(memory_space=pltpu.VMEM)
SMEM = pl.BlockSpec(memory_space=pltpu.SMEM)
DMA = pltpu.SemaphoreType.DMA

QCOLS = HEADS * DH
VCOLS = HEADS * EXP * DH
ROUTERS = 2 * QCOLS + VCOLS
NORM = ROUTERS + 2 * HEADS * EXP
JOINT = 3328
SPLITS = {"joint": (640, 512), "output": (256, 128), "inner": (768, 640), "outer": (256, 128)}
INNER_PARTS = ((512, 256), (512, 256))


def ring_place(index, count):
    return (index // 2) * (1 - index % 2) + (count - 1 - index // 2) * (index % 2)


def ring_index(place, count):
    upper = place // (count // 2)
    return 2 * place * (1 - upper) + (2 * (count - 1 - place) + 1) * upper


def enter(devices):
    barrier = pltpu.get_barrier_semaphore()
    for device in devices:
        pl.semaphore_signal(barrier, inc=1, device_id=device, device_id_type=MESH)
    pl.semaphore_wait(barrier, len(devices))


class Ring:
    def __init__(self, count, splits):
        self.count, self.splits = count, splits
        self.seq, self.fsdp = lax.axis_index("seq"), lax.axis_index("fsdp")
        self.plane, self.core = self.seq // 2, self.seq % 2
        self.place = ring_place(self.fsdp, count)
        self.right = (self.seq, ring_index((self.place + 1) % count, count))
        self.left = (self.seq, ring_index((self.place + count - 1) % count, count))
        self.core_mate = (self.seq + 1 - 2 * self.core, self.fsdp)
        self.plane_mate = ((self.seq + 2) % 4, self.fsdp)
        self.far = count // 2

    def neighbours(self):
        return [self.right, self.left, self.core_mate, self.plane_mate]

    def reach(self, kind, way):
        return self.far if kind == way else self.count - 1 - self.far

    def kinds(self, t):
        return [kind for kind in (1, 0) if self.splits[t][kind] > 0]

    def half(self, t):
        return self.splits[t][0] + 2 * self.splits[t][1]

    def cols(self, t, kind, plane, core):
        both, single = self.splits[t]
        if kind == 0:
            return pl.ds(pl.multiple_of(core * self.half(t), LANES), both)
        return pl.ds(pl.multiple_of(core * self.half(t) + both + plane * single, LANES), single)

    def behind(self, way, k):
        step = self.count - k if way == 0 else k
        return ring_index((self.place + step) % self.count, self.count)

    def next(self, way):
        return self.right if way == 0 else self.left

    def slot(self, kind, way, k):
        return k - 1 if way == 0 else self.reach(kind, 0) + k - 1


class Gather(Ring):
    def __init__(self, count, splits, shards, at, send, recv, local):
        super().__init__(count, splits)
        self.shards, self.at, self.send, self.recv, self.local = shards, at, send, recv, local

    @staticmethod
    def sems(count, tensors):
        return [DMA((6 * tensors * (count - 1),)), DMA((6 * tensors * (count - 1),)), DMA((tensors,))]

    def copy(self, src, dst, group, t, slot, device):
        i = (group * len(self.splits) + t) * (self.count - 1) + slot
        return pltpu.make_async_remote_copy(
            src, dst, self.send.at[i], self.recv.at[i], device_id=device, device_id_type=MESH
        )

    def same(self, group, t, kind, way, k, plane, core, device):
        ref = self.at(t, self.behind(way, k), self.cols(t, kind, plane, core))
        return self.copy(ref, ref, group, t, self.slot(kind, way, k), device)

    def hop(self, t, kind, way, k):
        if k > 1:
            ref = self.at(t, self.behind(way, k - 1), self.cols(t, kind, self.plane, self.core))
            return self.copy(ref, ref, kind, t, self.slot(kind, way, k), self.next(way))
        cols = self.cols(t, kind, self.plane, self.core)
        return self.copy(
            self.shards[t].at[:, cols], self.at(t, self.fsdp, cols), kind, t, self.slot(kind, way, 1), self.next(way)
        )

    def arrived(self, t, kind, way, k):
        return self.same(kind, t, kind, way, k, self.plane, self.core, self.next(way))

    def to_core(self, t, kind, way, k, core):
        return self.same(2 + kind, t, kind, way, k, self.plane, core, self.core_mate)

    def to_plane(self, t, way, k, plane):
        return self.same(4, t, 1, way, k, plane, self.core, self.plane_mate)

    def plane_to_core(self, t, way, k, core):
        return self.same(5, t, 1, way, k, 1 - self.plane, core, self.core_mate)

    def own(self, t):
        return pltpu.make_async_copy(self.shards[t], self.at(t, self.fsdp, slice(None)), self.local.at[t])

    def start(self, t):
        for kind in self.kinds(t):
            for way in (0, 1):
                if self.reach(kind, way):
                    self.hop(t, kind, way, 1).start()
        self.own(t).start()

    def arrive(self, t, k):
        for kind in self.kinds(t):
            for way in (0, 1):
                if k <= self.reach(kind, way):
                    self.arrived(t, kind, way, k).wait_recv()
                    if k < self.reach(kind, way):
                        self.hop(t, kind, way, k + 1).start()
                    if kind:
                        self.to_plane(t, way, k, self.plane).start()
                    self.to_core(t, kind, way, k, self.core).start()

    def plane_arrive(self, t, k):
        if 1 in self.kinds(t):
            for way in (0, 1):
                if k <= self.reach(1, way):
                    self.to_plane(t, way, k, 1 - self.plane).wait_recv()
                    self.plane_to_core(t, way, k, self.core).start()

    def finish(self, t):
        self.own(t).wait()
        for kind in self.kinds(t):
            for way in (0, 1):
                for k in range(1, self.reach(kind, way) + 1):
                    self.hop(t, kind, way, k).wait_send()
                    self.to_core(t, kind, way, k, self.core).wait_send()
                    self.to_core(t, kind, way, k, 1 - self.core).wait_recv()
                    if kind:
                        self.to_plane(t, way, k, self.plane).wait_send()
                        self.plane_to_core(t, way, k, self.core).wait_send()
                        self.plane_to_core(t, way, k, 1 - self.core).wait_recv()

    def events(self):
        tensors = range(len(self.splits))
        out = []
        for k in range(1, self.far + 1):
            for t in tensors:
                out.append(functools.partial(self.arrive, t, k))
                if k > 1:
                    out.append(functools.partial(self.plane_arrive, t, k - 1))
        for t in tensors:
            out.append(functools.partial(self.plane_arrive, t, self.far))
        for t in tensors:
            out.append(functools.partial(self.finish, t))
        return out


TABLE = 5632
TABLE_ZERO = 5120
TURNED_ZERO = 512


def route_lanes(routes, lane):
    hit = None
    for head in range(2 * HEADS):
        for choice in range(2):
            place = head * EXP + routes[:, 2 * head + choice : 2 * head + choice + 1]
            here = lane == place
            hit = here if hit is None else hit | here
    return hit.astype(jnp.float32)


def project_kernel(count, query, key, value, routers, tokens, routes, output_shard, gaps, joint, output_w, qkv, experts, gates, norms, tables, turned_tables,
                   shard, product, send, recv, local):
    rows = shard.shape[0]
    splits = (SPLITS["joint"], SPLITS["output"])

    def at(t, g, cols):
        if t:
            return output_w.at[g, :, cols]
        return joint.at[pl.ds(pl.multiple_of(g * rows, rows), rows), cols]

    ring = Gather(count, splits, [shard, output_shard], at, send, recv, local)
    wide = jnp.concatenate([ref[...].astype(jnp.float32) for ref in (query, key, value, routers)], axis=1)
    shard[...] = wide.astype(jnp.bfloat16)
    enter(ring.neighbours())
    ring.start(0)
    slope = jnp.float32(0.0)
    for head in range(HEADS):
        slope = jnp.where(ring.seq // 1 == head, -0.5 * 0.5**head * LOG2E, slope)
    group = ring.fsdp // GSLOTS
    pair = jnp.maximum(ring.fsdp % GSLOTS - PSLOTS, 0) * 2
    gap_values = [jnp.int32(0), gaps[group, pair], gaps[group, pair + 1]]

    def table_column(step, carry):
        start = pl.multiple_of(step * 256, 256)
        lanes = lax.broadcasted_iota(jnp.int32, (8, 256 + LANES), 1) + (start - LANES)
        for which in range(3):
            for turned in range(2):
                if turned:
                    distance = lanes - TURNED_ZERO + gap_values[which]
                else:
                    distance = TABLE_ZERO - lanes + gap_values[which]
                bias = slope * jnp.log(1.0 + jnp.maximum(distance, 0).astype(jnp.float32))
                bias = jnp.where(distance >= 0, bias, NEGATIVE)
                wide = jnp.broadcast_to(bias[:1], (LANES, 256 + LANES))
                rolled = pltpu.roll(wide, 0, 1, stride=1, stride_axis=0)
                target = turned_tables if turned else tables
                target[which, :, pl.ds(start, 256)] = rolled[:, LANES:]
        return carry

    late = max(1, ring.far - 1)
    steps, later = [], []
    for k in range(1, ring.far + 1):
        steps.append(functools.partial(ring.arrive, 0, k))
        if k > 1:
            steps.append(functools.partial(ring.plane_arrive, 0, k - 1))
        if k == late:
            steps.append(functools.partial(ring.start, 1))
        later.append(functools.partial(ring.arrive, 1, k))
        if k > 1:
            later.append(functools.partial(ring.plane_arrive, 1, k - 1))
    steps += [functools.partial(ring.plane_arrive, 0, ring.far), functools.partial(ring.finish, 0)]
    later += [functools.partial(ring.plane_arrive, 1, ring.far)]
    early = later[:1]
    later = later[1:]
    steps = steps[:-1] + early + steps[-1:]
    cut = max(1, TABLE // 256 // len(steps))
    done = 0
    for i, event in enumerate(steps):
        upto = TABLE // 256 if i == len(steps) - 1 else min(TABLE // 256, (i + 1) * cut)
        if upto > done:
            lax.fori_loop(done, upto, table_column, 0)
            done = upto
        event()

    def column(step, carry):
        cols = pl.ds(pl.multiple_of(step * 256, 256), 256)
        product[:, cols] = jnp.dot(tokens[...], joint[:, cols], preferred_element_type=jnp.float32)
        return carry

    columns = JOINT // 256
    for i in range(3):
        lax.fori_loop(i * columns // 3, (i + 1) * columns // 3, column, 0)
        for event in later[i * len(later) // 4 : (i + 1) * len(later) // 4]:
            event()
    norm_tile = NORM // LANES * LANES
    turned_norm = joint[:, norm_tile : norm_tile + LANES].astype(jnp.float32).T
    norms[...] = turned_norm[NORM - norm_tile : NORM - norm_tile + 8]
    logits = product[:, ROUTERS : ROUTERS + 2 * HEADS * EXP]
    local_rows = tokens.shape[0]
    wide = jnp.concatenate([logits, jnp.zeros((local_rows, LANES - 2 * HEADS * EXP), jnp.float32)], axis=1)
    lane = lax.broadcasted_iota(jnp.int32, (local_rows, LANES), 1)
    mask = route_lanes(routes[...], lane)
    gate = 1.0 / (1.0 + jnp.exp(-wide))
    gates[0] = gate * mask
    gates[1] = gate * mask * (1.0 - gate)
    pad = jnp.zeros((local_rows, LANES - DH), jnp.float32)
    ones = jnp.ones((local_rows, LANES - DH), jnp.float32)
    for head in range(HEADS):
        first = head * DH
        qkv[head, 0] = jnp.concatenate([product[:, first : first + DH], pad], axis=1).astype(jnp.bfloat16)
        first = QCOLS + head * DH
        qkv[head, 1] = jnp.concatenate([product[:, first : first + DH], pad], axis=1).astype(jnp.bfloat16)
        total = None
        for expert in range(EXP):
            which = head * EXP + expert
            first = 2 * QCOLS + which * DH
            piece = product[:, first : first + DH]
            experts[which] = jnp.concatenate([piece, pad], axis=1).astype(jnp.bfloat16)
            term = piece * gates[0, :, which : which + 1]
            total = term if total is None else total + term
        qkv[head, 2] = jnp.concatenate([total, ones], axis=1).astype(jnp.bfloat16)
    for event in later[3 * len(later) // 4 :]:
        event()
    ring.finish(1)


def project(count, query, key, value, routers, tokens, routes, output_shard, gaps):
    rows, (shard_rows, _) = tokens.shape[0], query.shape
    f32, bf = jnp.float32, jnp.bfloat16
    return pl.pallas_call(
        functools.partial(project_kernel, count),
        out_shape=[
            jax.ShapeDtypeStruct((shard_rows * count, JOINT), bf),
            jax.ShapeDtypeStruct((count,) + output_shard.shape, bf),
            jax.ShapeDtypeStruct((HEADS, 3, rows, LANES), bf),
            jax.ShapeDtypeStruct((HEADS * EXP, rows, LANES), bf),
            jax.ShapeDtypeStruct((2, rows, LANES), f32),
            jax.ShapeDtypeStruct((8, shard_rows * count), f32),
            jax.ShapeDtypeStruct((3, LANES, TABLE), f32),
            jax.ShapeDtypeStruct((3, LANES, TABLE), f32),
        ],
        in_specs=[VMEM] * 7 + [SMEM],
        out_specs=[VMEM, ANY] + [VMEM] * 6,
        scratch_shapes=[pltpu.VMEM((shard_rows, JOINT), bf), pltpu.VMEM((rows, JOINT), f32)] + Gather.sems(count, 2),
        compiler_params=pltpu.CompilerParams(collective_id=1, has_side_effects=True, vmem_limit_bytes=56 << 20),
    )(query, key, value, routers, tokens, routes, output_shard, gaps)


def seq_mates(ring):
    return [ring.core_mate, ring.plane_mate, (3 - ring.seq, ring.fsdp)]


def slot_mates(ring):
    f = ring.fsdp
    return [(ring.seq, f + 1 - 2 * (f % 2)), (ring.seq, f + 2 - 4 * ((f // 2) % 2))]


def tile_place(slot, seq, phase, key_block, query_block):
    cont = slot // PSLOTS
    own = 1 - jnp.minimum(phase, 1)
    piece = jnp.where(slot == 3, 2 - phase, phase - 1)
    source = jnp.where(phase == 0, 0, 1 + piece)
    first = cont * 2 * (query_block // 2)
    active = jnp.where(
        phase == 0,
        (key_block <= query_block) & (key_block >= first),
        jnp.where(phase == 1, slot >= 1, slot >= 2),
    )
    far_column = jnp.where(
        cont == 1,
        2048 * piece + BLOCK * key_block - BLOCK * (query_block % 2) - 4096,
        BLOCK * key_block - 2048 - BLOCK * query_block,
    )
    column = jnp.where(phase == 0, BLOCK * (key_block - query_block), far_column)
    table = jnp.where((phase > 0) & (cont == 1), 1 + query_block // 2, 0)
    return source, active, table, column


def block_rows(block):
    return pl.ds(pl.multiple_of(block * BLOCK, BLOCK), BLOCK)


def attend_kernel(count, splits, steps, qkv, tables, *refs):
    T = len(splits)
    shards, refs = refs[:T], refs[T:]
    att, store, outputs, logs = refs[:4]
    fulls, refs = refs[4 : 4 + T], refs[4 + T :]
    acc, top, att_low, kv_send, kv_recv, q_send, q_recv, sh_send, sh_recv, out_send, out_recv, here = refs[:12]
    at = lambda t, g, cols: fulls[t].at[g, :, cols]
    ring = Gather(count, splits, shards, at, *refs[12:])
    seq, slot = ring.seq, ring.fsdp % GSLOTS
    mates, (x_mate, z_mate) = seq_mates(ring), slot_mates(ring)
    enter(ring.neighbours() + mates[2:] + [x_mate, z_mate])

    def remote(src, dst, send, recv, device):
        return pltpu.make_async_remote_copy(src, dst, send, recv, device_id=device, device_id_type=MESH)

    mine = block_rows(seq)

    def kv_copy(mate):
        return remote(qkv.at[mate[0], pl.ds(1, 2)], store.at[pl.ds(1, 2), mine], kv_send.at[mate[0]], kv_recv.at[seq], mate)

    def q_copy(mate):
        return remote(qkv.at[mate[0], 0], store.at[0, mine], q_send.at[mate[0]], q_recv.at[seq], mate)

    for mate in mates[1:] + mates[:1]:
        kv_copy(mate).start()
    own_copy = pltpu.make_async_copy(qkv.at[seq], store.at[pl.ds(0, 3), mine], here.at[0])
    own_copy.start()
    for mate in mates[1:] + mates[:1]:
        q_copy(mate).start()
    acc[...] = jnp.zeros_like(acc)
    top[...] = jnp.full_like(top, NEGATIVE)

    def far_rows(piece, chunk):
        return store.at[pl.ds(3 + 2 * piece, 2), block_rows(chunk)]

    def first_hop(chunk, way):
        src = store.at[pl.ds(1, 2), block_rows(chunk)]
        piece = slot % 2
        return remote(src, far_rows(piece, chunk), sh_send.at[4 * way + chunk], sh_recv.at[4 * piece + chunk],
                      x_mate if way == 0 else z_mate)

    def second_hop(chunk):
        piece = slot % 2
        return remote(far_rows(piece, chunk), far_rows(piece, chunk), sh_send.at[8 + chunk], sh_recv.at[4 * piece + chunk], x_mate)

    def share(chunk):
        @pl.when(slot < 2)
        def _():
            first_hop(chunk, 1).start()

        @pl.when(slot == 0)
        def _():
            first_hop(chunk, 0).start()

    def pass_on(chunk):
        @pl.when(slot >= 1)
        def _():
            piece = jnp.where(slot == 3, 1, 0)
            remote(far_rows(piece, chunk), far_rows(piece, chunk), sh_send.at[chunk], sh_recv.at[4 * piece + chunk], x_mate).wait_recv()

        @pl.when(slot >= 2)
        def _():
            second_hop(chunk).start()

    def last_piece(chunk):
        @pl.when(slot >= 2)
        def _():
            piece = 3 - slot
            remote(far_rows(piece, chunk), far_rows(piece, chunk), sh_send.at[chunk], sh_recv.at[4 * piece + chunk], x_mate).wait_recv()

    own_copy.wait()
    share(seq)
    for mate in mates:
        other = mate[0]
        src = store.at[pl.ds(1, 2), block_rows(other)]
        remote(src, src, kv_send.at[other], kv_recv.at[other], mate).wait_recv()
        share(other)
    for mate in mates:
        src = store.at[0, block_rows(mate[0])]
        remote(src, src, q_send.at[mate[0]], q_recv.at[mate[0]], mate).wait_recv()

    def tile(step):
        phase, key_block, query_block = step // 16, (step // 4) % 4, step % 4
        source, active, table, column = tile_place(slot, seq, phase, key_block, query_block)

        @pl.when(active)
        def _():
            rows = block_rows(query_block)
            keys = store[1 + 2 * source, block_rows(key_block), :]
            values = store[2 + 2 * source, block_rows(key_block), :]
            scores = lax.dot_general(store[0, rows, :], keys, (((1,), (1,)), ((), ())), preferred_element_type=jnp.float32)
            bias = jnp.concatenate(
                [tables[table, :, pl.ds(pl.multiple_of(column + TABLE_ZERO - LANES * part, LANES), BLOCK)] for part in range(BLOCK // LANES)],
                axis=0,
            )
            scores = scores * (DH**-0.5 * LOG2E) + bias
            before = top[rows, :]
            after = jnp.maximum(before, jnp.max(scores, axis=1, keepdims=True))
            factor = jnp.exp2(before - after)
            terms = jnp.exp2(scores - after[:, :1])
            acc[rows, :] = acc[rows, :] * factor + jnp.dot(terms.astype(jnp.bfloat16), values, preferred_element_type=jnp.float32)
            top[rows, :] = after

    events = {}
    for chunk in range(4):
        events.setdefault(4 * chunk, []).append(functools.partial(pass_on, chunk))
        events.setdefault(32 + 4 * chunk, []).append(functools.partial(last_piece, chunk))
    begin, gap = steps
    events.setdefault(begin, []).extend([functools.partial(ring.start, t) for t in range(T)])
    rest = []
    for i, event in enumerate(ring.events()):
        step = begin + gap * (i + 1)
        if step < 48:
            events.setdefault(step, []).append(event)
        else:
            rest.append(event)

    def step_body(step, carry):
        for when, actions in sorted(events.items()):
            @pl.when(step == when)
            def _():
                for action in actions:
                    action()
        tile(step)
        return carry

    lax.fori_loop(0, 48, step_body, 0)
    total = acc[:, DH : DH + 1]
    result = acc[...] / total
    outputs[...] = result
    log_total = top[...] + jnp.log2(total)
    for block in range(4):
        logs[:, block * BLOCK : (block + 1) * BLOCK] = log_total[block * BLOCK : (block + 1) * BLOCK].T[:8]
    att_low[...] = result.astype(jnp.bfloat16)

    def out_copy(mate):
        return remote(att_low.at[block_rows(mate[0])], att.at[seq], out_send.at[mate[0]], out_recv.at[seq], mate)

    for mate in mates[1:] + mates[:1]:
        out_copy(mate).start()
    own_out = pltpu.make_async_copy(att_low.at[mine], att.at[seq], here.at[1])
    own_out.start()
    for event in rest:
        event()
    own_out.wait()
    for mate in mates:
        kv_copy(mate).wait_send()
        q_copy(mate).wait_send()
        out_copy(mate).wait_send()
        ref = att.at[mate[0]]
        remote(ref, ref, out_send.at[mate[0]], out_recv.at[mate[0]], mate).wait_recv()
    for chunk in range(4):
        @pl.when(slot < 2)
        def _():
            first_hop(chunk, 1).wait_send()

        @pl.when(slot == 0)
        def _():
            first_hop(chunk, 0).wait_send()

        @pl.when(slot >= 2)
        def _():
            second_hop(chunk).wait_send()


def attend(count, qkv, tables, shards, splits, steps=(8, 2)):
    rows = qkv.shape[2]
    own = 4 * rows
    T = len(shards)
    return pl.pallas_call(
        functools.partial(attend_kernel, count, splits, steps),
        out_shape=[
            jax.ShapeDtypeStruct((HEADS, rows, LANES), jnp.bfloat16),
            jax.ShapeDtypeStruct((7, own, LANES), jnp.bfloat16),
            jax.ShapeDtypeStruct((own, LANES), jnp.float32),
            jax.ShapeDtypeStruct((8, own), jnp.float32),
        ]
        + [jax.ShapeDtypeStruct((count,) + w.shape, w.dtype) for w in shards],
        in_specs=[VMEM] * (2 + T),
        out_specs=[VMEM] * 4 + [ANY] * T,
        scratch_shapes=[
            pltpu.VMEM((own, LANES), jnp.float32),
            pltpu.VMEM((own, LANES), jnp.float32),
            pltpu.VMEM((own, LANES), jnp.bfloat16),
            DMA((4,)), DMA((4,)), DMA((4,)), DMA((4,)), DMA((12,)), DMA((8,)), DMA((4,)), DMA((4,)), DMA((2,)),
        ]
        + Gather.sems(count, T),
        compiler_params=pltpu.CompilerParams(collective_id=2, has_side_effects=True, vmem_limit_bytes=56 << 20),
    )(qkv, tables, *shards)


class Scatter(Ring):
    def __init__(self, count, splits, parts, outs, bufs, sems):
        super().__init__(count, splits)
        self.parts, self.outs = parts, outs
        T = len(splits)
        self.mine, self.plane_in = bufs[:T], bufs[T : 2 * T]
        self.ring0, self.ring1 = bufs[2 * T : 3 * T], bufs[3 * T : 4 * T]
        self.low, self.low_in, self.done = bufs[4 * T : 5 * T], bufs[5 * T : 6 * T], bufs[6 * T : 7 * T]
        (self.load, self.plane_s, self.plane_r, self.ring_s, self.ring_r, self.end_s, self.end_r, self.put) = sems

    @staticmethod
    def scratch(count, splits, rows):
        half = [a + 2 * b for a, b in splits]
        bf = jnp.bfloat16
        out = [pltpu.VMEM((count, r, h), bf) for r, h in zip(rows, half)]
        out += [pltpu.VMEM((count, r, b), bf) for r, (a, b) in zip(rows, splits)]
        out += [pltpu.VMEM((count - 1 if a else 1, r, max(a, LANES)), bf) for r, (a, b) in zip(rows, splits)]
        out += [pltpu.VMEM((count - 1, r, b), bf) for r, (a, b) in zip(rows, splits)]
        out += [pltpu.VMEM((r, a + b), bf) for r, (a, b) in zip(rows, splits)]
        out += [pltpu.VMEM((r, a + b), bf) for r, (a, b) in zip(rows, splits)]
        out += [pltpu.VMEM((r, h), jnp.float32) for r, h in zip(rows, half)]
        T = len(splits)
        return out + [DMA((T * count,))] * 3 + [DMA((2 * T * (count - 1),))] * 2 + [DMA((2 * T,))] * 2 + [DMA((T,))]

    def dest(self, rel):
        return ring_index((self.place + rel) % self.count, self.count)

    def load_copy(self, t, rel):
        part, first = self.parts[t]
        src = part.at[self.dest(rel), :, pl.ds(first, self.half(t))]
        return pltpu.make_async_copy(src, self.mine[t].at[rel], self.load.at[t * self.count + rel])

    def remote(self, src, dst, s, r, i, device):
        return pltpu.make_async_remote_copy(src, dst, s.at[i], r.at[i], device_id=device, device_id_type=MESH)

    def single(self, t, plane):
        both, single = self.splits[t]
        return pl.ds(pl.multiple_of(both + plane * single, LANES), single)

    def plane_copy(self, t, rel):
        src = self.mine[t].at[rel, :, self.single(t, 1 - self.plane)]
        return self.remote(src, self.plane_in[t].at[rel], self.plane_s, self.plane_r, t * self.count + rel, self.plane_mate)

    def rels(self, D):
        return sorted({D % self.count, (-D) % self.count})

    def order(self):
        out = []
        for D in range(self.far, -1, -1):
            out += self.rels(D)
        return out

    def start(self, t):
        for rel in self.order():
            self.load_copy(t, rel).start()

    def ready(self, t, rel):
        if self.parts[t]:
            self.load_copy(t, rel).wait()
        self.plane_copy(t, rel).start()

    def all_ready(self, t):
        for rel in self.order():
            self.ready(t, rel)

    def step(self, t, D):
        self.combine(t, D)
        if D:
            self.chain(t, D)
        else:
            self.close(t)

    def buffer(self, t, kind, slot):
        if kind:
            return self.ring1[t].at[slot]
        return self.ring0[t].at[slot]

    def own_ref(self, t, kind, rel):
        if kind:
            return self.mine[t].at[rel, :, self.single(t, self.plane)]
        return self.mine[t].at[rel, :, pl.ds(0, self.splits[t][0])]

    def ring_copy(self, t, kind, way, D):
        slot = self.slot(kind, way, D)
        if D == self.reach(kind, way):
            src = self.own_ref(t, kind, D % self.count if way == 0 else (-D) % self.count)
        else:
            src = self.buffer(t, kind, self.slot(kind, way, D + 1))
        i = (2 * t + kind) * (self.count - 1) + slot
        return self.remote(src, self.buffer(t, kind, slot), self.ring_s, self.ring_r, i, self.next(way))

    def ring_wait(self, t, kind, way, D):
        slot = self.slot(kind, way, D)
        ref = self.buffer(t, kind, slot)
        i = (2 * t + kind) * (self.count - 1) + slot
        self.remote(ref, ref, self.ring_s, self.ring_r, i, self.next(way)).wait_recv()

    def combine(self, t, D):
        for rel in self.rels(D):
            self.plane_copy(t, rel).wait_send()
            ref = self.plane_in[t].at[rel]
            self.remote(ref, ref, self.plane_s, self.plane_r, t * self.count + rel, self.plane_mate).wait_recv()
            own = self.own_ref(t, 1, rel)
            own[...] = (own[...].astype(jnp.float32) + self.plane_in[t][rel].astype(jnp.float32)).astype(jnp.bfloat16)

    def chain(self, t, D):
        for kind in self.kinds(t):
            for way in (0, 1):
                if D > self.reach(kind, way):
                    continue
                if D < self.reach(kind, way):
                    self.ring_wait(t, kind, way, D + 1)
                    rel = D % self.count if way == 0 else (-D) % self.count
                    ref = self.buffer(t, kind, self.slot(kind, way, D + 1))
                    ref[...] = (ref[...].astype(jnp.float32) + self.own_ref(t, kind, rel)[...].astype(jnp.float32)).astype(jnp.bfloat16)
                self.ring_copy(t, kind, way, D).start()

    def end_copy(self, t):
        return self.remote(self.low[t], self.low_in[t], self.end_s, self.end_r, 2 * t, self.plane_mate)

    def close(self, t):
        both, single = self.splits[t]
        for kind in self.kinds(t):
            total = self.own_ref(t, kind, 0)[...].astype(jnp.float32)
            for way in (0, 1):
                if self.reach(kind, way):
                    self.ring_wait(t, kind, way, 1)
                    total = total + self.buffer(t, kind, self.slot(kind, way, 1))[...].astype(jnp.float32)
            if kind:
                self.low[t][:, both:] = total.astype(jnp.bfloat16)
            else:
                self.low[t][:, :both] = total.astype(jnp.bfloat16)
        self.end_copy(t).start()

    def out_ref(self, t, core):
        out, whole, first = self.outs[t]
        return out.at[:, pl.ds(pl.multiple_of(core * whole + first, LANES), self.half(t))]

    def out_copy(self, t):
        return self.remote(self.done[t], self.out_ref(t, self.core), self.end_s, self.end_r, 2 * t + 1, self.core_mate)

    def put_copy(self, t):
        return pltpu.make_async_copy(self.done[t], self.out_ref(t, self.core), self.put.at[t])

    def deliver(self, t):
        both, single = self.splits[t]
        self.end_copy(t).wait_send()
        ref = self.low_in[t]
        self.remote(ref, ref, self.end_s, self.end_r, 2 * t, self.plane_mate).wait_recv()
        if both:
            self.done[t][:, :both] = self.low[t][:, :both].astype(jnp.float32) + self.low_in[t][:, :both].astype(jnp.float32)
        if single:
            self.done[t][:, self.single(t, self.plane)] = self.low[t][:, both:].astype(jnp.float32)
            self.done[t][:, self.single(t, 1 - self.plane)] = self.low_in[t][:, both:].astype(jnp.float32)
        self.out_copy(t).start()
        self.put_copy(t).start()

    def finish(self, t):
        for kind in self.kinds(t):
            for way in (0, 1):
                for D in range(1, self.reach(kind, way) + 1):
                    self.ring_copy(t, kind, way, D).wait_send()
        self.out_copy(t).wait_send()
        self.put_copy(t).wait()
        ref = self.out_ref(t, 1 - self.core)
        self.remote(ref, ref, self.end_s, self.end_r, 2 * t + 1, self.core_mate).wait_recv()


def retreat_kernel(count, splits, steps, grad_att, turned, store, outputs, logs, part, back, out, *refs):
    T = len(splits)
    (grads, delta, grad_q, grad_kv, send_kv, kv_in0, kv_in1, low, in_send, in_recv, up_send, up_recv,
     out_send, out_recv, here) = refs[:15]
    refs = refs[15:]
    halves = [a + 2 * b for a, b in splits]
    firsts = [sum(halves[:t]) for t in range(T)]
    ring = Scatter(
        count, splits, [(part, first) for first in firsts], [(out, sum(halves), first) for first in firsts],
        refs[: 7 * T], refs[7 * T :])
    seq, slot = ring.seq, ring.fsdp % GSLOTS
    mates, (x_mate, z_mate) = seq_mates(ring), slot_mates(ring)
    enter(ring.neighbours() + mates[2:] + [x_mate, z_mate])

    def remote(src, dst, send, recv, device):
        return pltpu.make_async_remote_copy(src, dst, send, recv, device_id=device, device_id_type=MESH)

    mine = block_rows(seq)

    def in_copy(mate):
        return remote(grad_att.at[mate[0]], grads.at[mine], in_send.at[mate[0]], in_recv.at[seq], mate)

    for mate in mates[1:] + mates[:1]:
        in_copy(mate).start()
    own_copy = pltpu.make_async_copy(grad_att.at[seq], grads.at[mine], here.at[0])
    own_copy.start()
    grad_q[...] = jnp.zeros_like(grad_q)
    grad_kv[...] = jnp.zeros_like(grad_kv)
    own_copy.wait()
    for mate in mates:
        ref = grads.at[block_rows(mate[0])]
        remote(ref, ref, in_send.at[mate[0]], in_recv.at[mate[0]], mate).wait_recv()
    for block in range(4):
        rows = pl.ds(block * BLOCK, BLOCK)
        sums = jnp.sum(grads[rows, :].astype(jnp.float32) * outputs[rows, :], axis=1, keepdims=True)
        delta[:, rows] = jnp.broadcast_to(sums, (BLOCK, LANES)).T[:8]

    def tile(step):
        phase, key_block, query_block = step // 16, (step // 4) % 4, step % 4
        piece = jnp.where(slot == 2, 1 - phase, phase)
        forward_phase = jnp.where(phase == 2, 0, jnp.where(slot == 3, 2 - piece, 1 + piece))
        source, active, table, column = tile_place(slot, seq, forward_phase, key_block, query_block)

        @pl.when(active)
        def _():
            rows, key_rows = block_rows(query_block), block_rows(key_block)
            keys, values = store[1 + 2 * source, key_rows, :], store[2 + 2 * source, key_rows, :]
            queries, tops = store[0, rows, :], grads[rows, :]
            scores = lax.dot_general(keys, queries, (((1,), (1,)), ((), ())), preferred_element_type=jnp.float32)
            bias = jnp.concatenate(
                [turned[table, :, pl.ds(pl.multiple_of(TURNED_ZERO - column - LANES * part, LANES), BLOCK)] for part in range(BLOCK // LANES)],
                axis=0,
            )
            weights = jnp.exp2(scores * (DH**-0.5 * LOG2E) + (bias - logs[:1, rows]))
            grad_weights = lax.dot_general(values, tops, (((1,), (1,)), ((), ())), preferred_element_type=jnp.float32)
            grad_scores = (weights * (grad_weights - delta[:1, rows])).astype(jnp.bfloat16)
            grad_kv[source, 1, key_rows, :] += jnp.dot(weights.astype(jnp.bfloat16), tops, preferred_element_type=jnp.float32)
            grad_kv[source, 0, key_rows, :] += jnp.dot(grad_scores, queries, preferred_element_type=jnp.float32)
            grad_q[rows, :] += lax.dot_general(grad_scores, keys, (((0,), (0,)), ((), ())), preferred_element_type=jnp.float32)

    scale = DH**-0.5

    def rounded(source, chunk, extra):
        rows = block_rows(chunk)
        keys = grad_kv[source, 0, rows, :] * scale
        values = grad_kv[source, 1, rows, :]
        for more in extra:
            keys = keys + more[0].astype(jnp.float32)
            values = values + more[1].astype(jnp.float32)
        return keys.astype(jnp.bfloat16), values.astype(jnp.bfloat16)

    def x_send(chunk):
        src = send_kv.at[0, :, block_rows(chunk)]
        return remote(src, kv_in0.at[:, block_rows(chunk)], up_send.at[chunk], up_recv.at[chunk], x_mate)

    def z_send(chunk):
        src = send_kv.at[1, :, block_rows(chunk)]
        return remote(src, kv_in1.at[:, block_rows(chunk)], up_send.at[4 + chunk], up_recv.at[4 + chunk], z_mate)

    def x_wait(chunk):
        ref = kv_in0.at[:, block_rows(chunk)]
        remote(ref, ref, up_send.at[chunk], up_recv.at[chunk], x_mate).wait_recv()

    def z_wait(chunk):
        ref = kv_in1.at[:, block_rows(chunk)]
        remote(ref, ref, up_send.at[4 + chunk], up_recv.at[4 + chunk], z_mate).wait_recv()

    def first_done(chunk):
        @pl.when(slot >= 1)
        def _():
            source = jnp.where(slot == 2, 2, 1)
            keys, values = rounded(source, chunk, [])
            send_kv[0, 0, block_rows(chunk), :] = keys
            send_kv[0, 1, block_rows(chunk), :] = values
            x_send(chunk).start()

    def second_done(chunk):
        @pl.when(slot >= 2)
        def _():
            x_wait(chunk)
            source = slot - 1
            keys, values = rounded(source, chunk, [kv_in0[:, block_rows(chunk), :]])
            send_kv[1, 0, block_rows(chunk), :] = keys
            send_kv[1, 1, block_rows(chunk), :] = values
            z_send(chunk).start()

    def out_copy(mate):
        src = low.at[:, block_rows(mate[0])]
        return remote(src, back.at[seq], out_send.at[mate[0]], out_recv.at[seq], mate)

    def own_done(chunk):
        rows = block_rows(chunk)
        low[0, rows, :] = (grad_q[rows, :] * scale).astype(jnp.bfloat16)

        @pl.when(slot == 0)
        def _():
            x_wait(chunk)
            z_wait(chunk)
            low[1, rows, :], low[2, rows, :] = rounded(0, chunk, [kv_in0[:, rows, :], kv_in1[:, rows, :]])

        @pl.when(slot == 1)
        def _():
            z_wait(chunk)
            low[1, rows, :], low[2, rows, :] = rounded(0, chunk, [kv_in1[:, rows, :]])

        @pl.when(slot >= 2)
        def _():
            low[1, rows, :], low[2, rows, :] = rounded(0, chunk, [])

    events = {}
    for chunk in range(4):
        events.setdefault(4 * chunk + 4, []).append(functools.partial(first_done, chunk))
        events.setdefault(20 + 4 * chunk, []).append(functools.partial(second_done, chunk))
    begin, ready, first, hop, lag = steps
    rest = []
    for t in range(T):
        plan = [(begin, functools.partial(ring.start, t)), (ready, functools.partial(ring.all_ready, t))]
        when = first + lag * t
        for D in range(ring.far, -1, -1):
            plan.append((when, functools.partial(ring.step, t, D)))
            when += hop
        plan.append((when, functools.partial(ring.deliver, t)))
        plan.append((when + hop, functools.partial(ring.finish, t)))
        for when, event in plan:
            if when < 48:
                events.setdefault(int(when), []).append(event)
            else:
                rest.append((when, event))
    rest = [event for when, event in sorted(rest, key=lambda pair: pair[0])]

    def step_body(step, carry):
        for when, actions in sorted(events.items()):
            @pl.when(step == when)
            def _():
                for action in actions:
                    action()
        tile(step)
        return carry

    lax.fori_loop(0, 48, step_body, 0)
    for chunk in range(4):
        own_done(chunk)
    for mate in mates[1:] + mates[:1]:
        out_copy(mate).start()
    own_out = pltpu.make_async_copy(low.at[:, mine], back.at[seq], here.at[1])
    own_out.start()
    for event in rest:
        event()
    own_out.wait()
    for mate in mates:
        in_copy(mate).wait_send()
        out_copy(mate).wait_send()
        ref = back.at[mate[0]]
        remote(ref, ref, out_send.at[mate[0]], out_recv.at[mate[0]], mate).wait_recv()
    for chunk in range(4):
        @pl.when(slot >= 1)
        def _():
            x_send(chunk).wait_send()

        @pl.when(slot >= 2)
        def _():
            z_send(chunk).wait_send()


def retreat(count, grad_att, turned, store, outputs, logs, part, splits, steps=(0, 1, 6, 6, 2)):
    rows = grad_att.shape[1]
    own = 4 * rows
    _, shard_rows, half = part.shape
    return pl.pallas_call(
        functools.partial(retreat_kernel, count, splits, steps),
        out_shape=[jax.ShapeDtypeStruct((HEADS, 3, rows, LANES), jnp.bfloat16), jax.ShapeDtypeStruct((shard_rows, 2 * half), jnp.float32)],
        in_specs=[VMEM] * 5 + [ANY],
        out_specs=[VMEM, ANY],
        scratch_shapes=[
            pltpu.VMEM((own, LANES), jnp.bfloat16),
            pltpu.VMEM((8, own), jnp.float32),
            pltpu.VMEM((own, LANES), jnp.float32),
            pltpu.VMEM((3, 2, own, LANES), jnp.float32),
            pltpu.VMEM((2, 2, own, LANES), jnp.bfloat16),
            pltpu.VMEM((2, own, LANES), jnp.bfloat16),
            pltpu.VMEM((2, own, LANES), jnp.bfloat16),
            pltpu.VMEM((3, own, LANES), jnp.bfloat16),
            DMA((4,)), DMA((4,)), DMA((8,)), DMA((8,)), DMA((4,)), DMA((4,)), DMA((2,)),
        ]
        + Scatter.scratch(count, splits, [shard_rows] * len(splits)),
        compiler_params=pltpu.CompilerParams(collective_id=3, has_side_effects=True, vmem_limit_bytes=60 << 20),
    )(grad_att, turned, store, outputs, logs, part)


CHUNK = 512


def gelu_pair(v):
    root = 0.7978845608028654
    square = v * v
    t = jnp.tanh(root * (v + 0.044715 * square * v))
    up = 0.5 * (1.0 + t)
    return v * up, up + 0.5 * v * (1.0 - t * t) * (root * (1.0 + 3.0 * 0.044715 * square))


def contract(left, right, left_axis, right_axis):
    return lax.dot_general(left, right, (((left_axis,), (right_axis,)), ((), ())), preferred_element_type=jnp.float32)


def feed_kernel(count, att, gates, tokens, cotangent, norms, output_w, inner_w, outer_w,
                layer_out, grad_residual, grad_att, grad_logit, grad_norms, part_output, part_inner, outer_out,
                w_out, w_in, w_up, acts, act_in, slopes, slope_in, scaled, scaled_in, scaled_t, cot_in, cot_t,
                acc, normed, grad_scaled, branch_low, branch_in, branch_t, att_in, gates_in,
                stage_inner, stage_output,
                load_out, load_in, load_up, pair_s, pair_r, act_s, act_r, slope_s, slope_r, put_inner, put_output, *refs):
    half = cotangent.shape[1] // 2
    ring = Scatter(count, (SPLITS["outer"],), [None], [(outer_out, half, 0)], refs[:7], refs[7:])
    core, mate = ring.core, ring.core_mate
    experts = HEADS * EXP
    chunks = inner_w.shape[1] // CHUNK
    small = CHUNK // 2
    shards = max(1, count // chunks)

    def out_load(e):
        return pltpu.make_async_copy(output_w.at[pl.ds(e * DH, DH)], w_out.at[e, pl.ds(0, DH)], load_out.at[e])

    def ffn_load(chunk, slot):
        cols = pl.ds(pl.multiple_of(chunk * CHUNK, CHUNK), CHUNK)
        return (pltpu.make_async_copy(inner_w.at[:, cols], w_in.at[slot], load_in.at[slot]),
                pltpu.make_async_copy(outer_w.at[cols], w_up.at[slot], load_up.at[slot]))

    def chunk_of(step):
        if count != chunks:
            return step
        D = ring.far - (step + 1) // 2
        odd = step % 2
        return ring.dest((odd * D + (1 - odd) * (count - D)) % count)

    for e in range(experts):
        out_load(e).start()
    for sub in range(2):
        for copy in ffn_load(chunk_of(sub), sub):
            copy.start()
    enter(ring.neighbours())

    def remote(src, dst, send, recv):
        return pltpu.make_async_remote_copy(src, dst, send, recv, device_id=mate, device_id_type=MESH)

    mine = pl.ds(pl.multiple_of(core * half, LANES), half)
    yours = pl.ds(pl.multiple_of((1 - core) * half, LANES), half)
    pair = [
        remote(att, att_in, pair_s.at[0], pair_r.at[0]),
        remote(gates.at[0], gates_in, pair_s.at[1], pair_r.at[1]),
        remote(cotangent.at[:, yours], cot_in, pair_s.at[2], pair_r.at[2]),
        remote(scaled, scaled_in, pair_s.at[3], pair_r.at[3]),
        remote(branch_low.at[:, yours], branch_in, pair_s.at[4], pair_r.at[4]),
    ]
    for copy in pair[:3]:
        copy.start()

    def mixed_pair(att_ref, gate, two):
        tiles = []
        for which in (2 * two, 2 * two + 1):
            column = gate[:, experts + which : experts + which + 1]
            tiles.append((att_ref[which // EXP].astype(jnp.float32) * column).astype(jnp.bfloat16))
        return jnp.concatenate(tiles, axis=1)

    w_out[:, DH:, :] = jnp.zeros((experts, LANES - DH, w_out.shape[2]), jnp.bfloat16)
    acc[...] = tokens[...].astype(jnp.float32)
    for two in range(experts // 2):
        out_load(2 * two).wait()
        out_load(2 * two + 1).wait()
        weights = w_out[2 * two : 2 * two + 2].reshape(2 * LANES, w_out.shape[2])
        acc[...] += jnp.dot(mixed_pair(att, gates.at[0], two), weights, preferred_element_type=jnp.float32)
    residual = acc[...]
    centred = residual - jnp.mean(residual, axis=1, keepdims=True)
    inverse = lax.rsqrt(jnp.mean(centred * centred, axis=1, keepdims=True) + EPSILON)
    normed[...] = centred * inverse
    scaled[...] = (normed[...] * norms[:1] + norms[1:2]).astype(jnp.bfloat16)
    pair[3].start()
    rows = tokens.shape[0]
    scaled_t[:, :rows] = scaled[...].T
    cot_t[:, :rows] = cotangent[:, mine].T
    grad_scaled[...] = jnp.zeros_like(grad_scaled)
    pair[2].wait_recv()
    cot_t[:, rows:] = cot_in[...].T
    pair[3].wait_recv()
    scaled_t[:, rows:] = scaled_in[...].T

    small_mine = pl.ds(pl.multiple_of(core * small, LANES), small)
    small_yours = pl.ds(pl.multiple_of((1 - core) * small, LANES), small)

    def act_copy(step, sub):
        return remote(acts.at[sub], act_in.at[step], act_s.at[sub], act_r.at[step])

    def slope_copy(step, sub):
        return remote(slopes.at[sub, :, small_yours], slope_in.at[step], slope_s.at[sub], slope_r.at[step])

    def put_inner_copy(step, sub):
        cols = pl.ds(pl.multiple_of(chunk_of(step) * small, small), small)
        return pltpu.make_async_copy(stage_inner.at[sub], part_inner.at[:, cols], put_inner.at[sub])

    def forward_backward(step, sub):
        for copy in ffn_load(chunk_of(step), sub):
            copy.wait()

        @pl.when(step > 1)
        def _():
            act_copy(step, sub).wait_send()
            slope_copy(step, sub).wait_send()

        act, slope = gelu_pair(jnp.dot(scaled[...], w_in[sub], preferred_element_type=jnp.float32))
        acts[sub] = act.astype(jnp.bfloat16)
        act_copy(step, sub).start()
        slopes[sub] = (contract(cotangent[...], w_up[sub], 1, 1) * slope).astype(jnp.bfloat16)
        slope_copy(step, sub).start()
        acc[...] += jnp.dot(acts[sub], w_up[sub], preferred_element_type=jnp.float32)
        grad_scaled[...] += contract(slopes[sub], w_in[sub], 1, 1)

        @pl.when(step + 2 < chunks)
        def _():
            for copy in ffn_load(chunk_of(step + 2), sub):
                copy.start()

    def weight_parts(step, sub):
        remote(act_in.at[step], act_in.at[step], act_s.at[sub], act_r.at[step]).wait_recv()
        total = jnp.dot(cot_t[:, :rows], acts[sub], preferred_element_type=jnp.float32)
        total = total + jnp.dot(cot_t[:, rows:], act_in[step], preferred_element_type=jnp.float32)
        turned = total.astype(jnp.bfloat16).T
        shard_rows = CHUNK // shards
        for q in range(shards):
            rel = (ring_place(chunk_of(step) * shards + q, count) - ring.place + count) % count
            ring.mine[0][rel] = turned[q * shard_rows : (q + 1) * shard_rows]
        remote(slope_in.at[step], slope_in.at[step], slope_s.at[sub], slope_r.at[step]).wait_recv()

        @pl.when(step > 1)
        def _():
            put_inner_copy(step, sub).wait()

        total = jnp.dot(scaled_t[:, :rows], slopes[sub, :, small_mine], preferred_element_type=jnp.float32)
        total = total + jnp.dot(scaled_t[:, rows:], slope_in[step], preferred_element_type=jnp.float32)
        stage_inner[sub] = total.astype(jnp.bfloat16)
        put_inner_copy(step, sub).start()

    events = {}
    if count == chunks:
        for step, rel in enumerate(ring.order()):
            events.setdefault(step, []).append(functools.partial(ring.ready, 0, rel))
        for D in range(ring.far, 0, -1):
            events.setdefault(2 * (ring.far - D) + 1, []).append(functools.partial(ring.step, 0, D))

    def after_parts(step):
        for when, actions in sorted(events.items()):
            @pl.when(step == when)
            def _():
                for action in actions:
                    action()

    def iteration(i, carry):
        forward_backward(2 * i, 0)

        @pl.when(i > 0)
        def _():
            weight_parts(2 * i - 1, 1)
            after_parts(2 * i - 1)

        forward_backward(2 * i + 1, 1)
        weight_parts(2 * i, 0)
        after_parts(2 * i)
        return carry

    lax.fori_loop(0, chunks // 2, iteration, 0)
    weight_parts(chunks - 1, 1)
    if count == chunks:
        for action in events[chunks - 1]:
            action()
    else:
        ring.all_ready(0)
        for D in range(ring.far, 0, -1):
            ring.step(0, D)
    layer_out[...] = acc[...].astype(jnp.bfloat16)
    slope = grad_scaled[...]
    grad_norms[...] = jnp.concatenate(
        [jnp.sum(slope * normed[...], axis=0, keepdims=True), jnp.sum(slope, axis=0, keepdims=True),
         jnp.zeros((6, slope.shape[1]), jnp.float32)], axis=0)
    slope = slope * norms[:1]
    total = cotangent[...].astype(jnp.float32) + inverse * (
        slope - jnp.mean(slope, axis=1, keepdims=True)
        - normed[...] * jnp.mean(slope * normed[...], axis=1, keepdims=True))
    grad_residual[...] = total
    branch_low[...] = total.astype(jnp.bfloat16)
    pair[4].start()
    branch_t[:, :rows] = branch_low[:, mine].T
    ring.step(0, 0)
    lane = lax.broadcasted_iota(jnp.int32, (rows, LANES), 1)
    logit = jnp.zeros((rows, LANES), jnp.float32)
    head_total = None
    for which in range(experts):
        if which % 2 == 0:
            weights = w_out[which : which + 2].reshape(2 * LANES, w_out.shape[2])
            both = contract(branch_low[...], weights, 1, 1)
        grad_mixed = both[:, which % 2 * LANES : (which % 2 + 1) * LANES]
        head, expert = which // EXP, which % EXP
        column = slice(experts + which, experts + which + 1)
        term = grad_mixed * gates[0, :, column]
        head_total = term if expert == 0 else head_total + term
        if expert == EXP - 1:
            grad_att[head] = head_total.astype(jnp.bfloat16)
        sums = jnp.sum(grad_mixed * att[head].astype(jnp.float32), axis=1, keepdims=True)
        logit = jnp.where(lane == experts + which, sums, logit)
    grad_logit[...] = logit * gates[1]
    ring.deliver(0)
    pair[0].wait_recv()
    pair[1].wait_recv()
    pair[4].wait_recv()
    branch_t[:, rows:] = branch_in[...].T

    def put_output_copy(which):
        return pltpu.make_async_copy(stage_output.at[which % 4, pl.ds(0, DH)], part_output.at[pl.ds(which * DH, DH)], put_output.at[which % 4])

    for two in range(experts // 2):
        total = jnp.dot(branch_t[:, :rows], mixed_pair(att, gates.at[0], two), preferred_element_type=jnp.float32)
        total = total + jnp.dot(branch_t[:, rows:], mixed_pair(att_in, gates_in, two), preferred_element_type=jnp.float32)
        turned = total.astype(jnp.bfloat16).T
        for side in range(2):
            which = 2 * two + side
            if which >= 4:
                put_output_copy(which - 4).wait()
            stage_output[which % 4] = turned[side * LANES : (side + 1) * LANES]
            put_output_copy(which).start()
    for which in range(experts - 4, experts):
        put_output_copy(which).wait()
    for sub in range(2):
        put_inner_copy(sub, sub).wait()
        act_copy(sub, sub).wait_send()
        slope_copy(sub, sub).wait_send()
    ring.finish(0)
    for copy in pair:
        copy.wait_send()


def feed(count, att, gates, tokens, cotangent, norms, output_w, inner_w, outer_w):
    rows, width = tokens.shape
    wide = inner_w.shape[1]
    half = width // 2
    f32, bf = jnp.float32, jnp.bfloat16
    experts, chunks = HEADS * EXP, wide // CHUNK
    V = pltpu.VMEM
    return pl.pallas_call(
        functools.partial(feed_kernel, count),
        out_shape=[
            jax.ShapeDtypeStruct((rows, width), bf),
            jax.ShapeDtypeStruct((rows, width), f32),
            jax.ShapeDtypeStruct((HEADS, rows, LANES), bf),
            jax.ShapeDtypeStruct((rows, LANES), f32),
            jax.ShapeDtypeStruct((8, width), f32),
            jax.ShapeDtypeStruct((VCOLS, half), bf),
            jax.ShapeDtypeStruct((width, wide // 2), bf),
            jax.ShapeDtypeStruct((wide // count, width), f32),
        ],
        in_specs=[VMEM] * 5 + [ANY] * 3,
        out_specs=[VMEM] * 5 + [ANY] * 3,
        scratch_shapes=[
            V((experts, LANES, width), bf), V((2, width, CHUNK), bf), V((2, CHUNK, width), bf),
            V((2, rows, CHUNK), bf), V((chunks, rows, CHUNK), bf), V((2, rows, CHUNK), bf), V((chunks, rows, CHUNK // 2), bf),
            V((rows, width), bf), V((rows, width), bf), V((width, 2 * rows), bf), V((rows, half), bf), V((half, 2 * rows), bf),
            V((rows, width), f32), V((rows, width), f32), V((rows, width), f32),
            V((rows, width), bf), V((rows, half), bf), V((half, 2 * rows), bf), V((HEADS, rows, LANES), bf), V((rows, LANES), f32),
            V((2, width, CHUNK // 2), bf), V((4, LANES, half), bf),
            DMA((experts,)), DMA((2,)), DMA((2,)), DMA((5,)), DMA((5,)), DMA((2,)), DMA((chunks,)), DMA((2,)), DMA((chunks,)),
            DMA((2,)), DMA((4,)),
        ]
        + Scatter.scratch(count, (SPLITS["outer"],), [wide // count]),
        compiler_params=pltpu.CompilerParams(collective_id=4, has_side_effects=True, vmem_limit_bytes=63 << 20),
    )(att, gates, tokens, cotangent, norms, output_w, inner_w, outer_w)


def settle_kernel(count, back, experts, gates, grad_logit, tokens, joint, grad_residual, grad_norms, part_output,
                  grad_tokens, joint_out, output_out, grads, grads_in, tokens_in, tokens_t, norms_in, norm_columns, *refs):
    splits = (SPLITS["joint"], SPLITS["output"])
    pair_s, pair_r = refs[-2:]
    half, output_half = JOINT // 2, part_output.shape[2]
    outs = [(joint_out, half, 0), (output_out, output_half, 0)]
    ring = Scatter(count, splits, [None, (part_output, 0)], outs, refs[:14], refs[14:-2])
    ring.start(1)
    enter(ring.neighbours())
    core = ring.core

    def remote(src, dst, i):
        return pltpu.make_async_remote_copy(src, dst, pair_s.at[i], pair_r.at[i], device_id=ring.core_mate, device_id_type=MESH)

    mine = pl.ds(pl.multiple_of(core * half, LANES), half)
    yours = pl.ds(pl.multiple_of((1 - core) * half, LANES), half)
    pair = [remote(tokens, tokens_in, 0), remote(grad_norms, norms_in, 1), remote(grads.at[:, yours], grads_in, 2)]
    pair[0].start()
    pair[1].start()
    ring.all_ready(1)
    rows = tokens.shape[0]
    lane = lax.broadcasted_iota(jnp.int32, (LANES, LANES), 1)
    width = HEADS * EXP

    def assemble(block, carry):
        part = pl.ds(pl.multiple_of(block * LANES, LANES), LANES)
        pieces = [back[head, which, part, :][:, :DH].astype(jnp.float32) for which in range(2) for head in range(HEADS)]
        logit = grad_logit[part, :]
        for head in range(HEADS):
            values = back[head, 2, part, :].astype(jnp.float32)
            for expert in range(EXP):
                which = head * EXP + expert
                pieces.append((values * gates[0, part, which : which + 1])[:, :DH])
                sums = jnp.sum(values * experts[which, part, :].astype(jnp.float32), axis=1, keepdims=True)
                logit = jnp.where(lane == which, sums * gates[1, part, which : which + 1], logit)
        pieces.append(jnp.where(lane < 2 * width, logit, 0.0))
        pieces.append(jnp.zeros((LANES, JOINT - ROUTERS - LANES), jnp.float32))
        grads[part, :] = jnp.concatenate(pieces, axis=1).astype(jnp.bfloat16)
        return carry

    lax.fori_loop(0, rows // LANES, assemble, 0)
    pair[2].start()
    ring.step(1, ring.far)
    tokens_t[:, :rows] = tokens[...].T
    for copy in pair[:2]:
        copy.wait_recv()
    tokens_t[:, rows:] = tokens_in[...].T
    norm_tile = NORM // LANES * LANES - half
    first = NORM - half - norm_tile
    both = grad_norms[...] + norms_in[...]
    for block in range(both.shape[1] // LANES):
        columns = jnp.concatenate([both[:, block * LANES : (block + 1) * LANES], jnp.zeros((LANES - 8, LANES), jnp.float32)], axis=0)
        norm_columns[block * LANES : (block + 1) * LANES, :] = columns.T
    pair[2].wait_recv()
    shard_rows = tokens_t.shape[0] // count
    tile_lane = lax.broadcasted_iota(jnp.int32, (shard_rows, LANES), 1)

    def fill(rel):
        part = pl.ds(pl.multiple_of(ring.dest(rel) * shard_rows, shard_rows), shard_rows)
        total = jnp.dot(tokens_t[part, :rows], grads[:, mine], preferred_element_type=jnp.float32)
        total = total + jnp.dot(tokens_t[part, rows:], grads_in[...], preferred_element_type=jnp.float32)
        ring.mine[0][rel] = total.astype(jnp.bfloat16)
        extra = jnp.where(tile_lane == first, norm_columns[part, 0:1], 0.0) + jnp.where(tile_lane == first + 1, norm_columns[part, 1:2], 0.0)
        tile = total[:, norm_tile : norm_tile + LANES] + extra * core.astype(jnp.float32)
        ring.mine[0][rel, :, norm_tile : norm_tile + LANES] = tile.astype(jnp.bfloat16)

    for rel in ring.order():
        fill(rel)
        ring.ready(0, rel)
    ring.step(0, ring.far)
    for D in range(ring.far - 1, 0, -1):
        ring.step(1, D)
        ring.step(0, D)
        if D == ring.far - 1:
            grad_tokens[...] = grad_residual[...] + contract(grads[...], joint[...], 1, 1)
    ring.step(1, 0)
    ring.step(0, 0)
    ring.deliver(1)
    ring.deliver(0)
    ring.finish(1)
    ring.finish(0)
    for copy in pair:
        copy.wait_send()


def settle(count, back, experts, gates, grad_logit, tokens, joint, grad_residual, grad_norms, part_output):
    rows, width = tokens.shape
    shard_rows = width // count
    f32, bf = jnp.float32, jnp.bfloat16
    V = pltpu.VMEM
    return pl.pallas_call(
        functools.partial(settle_kernel, count),
        out_shape=[jax.ShapeDtypeStruct((rows, width), f32), jax.ShapeDtypeStruct((shard_rows, JOINT), f32),
                   jax.ShapeDtypeStruct((part_output.shape[1], width), f32)],
        in_specs=[VMEM] * 8 + [ANY],
        out_specs=[VMEM, VMEM, ANY],
        scratch_shapes=[V((rows, JOINT), bf), V((rows, JOINT // 2), bf), V((rows, width), bf), V((width, 2 * rows), bf), V((8, width), f32), V((width, LANES), f32)]
        + Scatter.scratch(count, (SPLITS["joint"], SPLITS["output"]), [shard_rows, part_output.shape[1]])
        + [DMA((3,)), DMA((3,))],
        compiler_params=pltpu.CompilerParams(collective_id=5, has_side_effects=True, vmem_limit_bytes=60 << 20),
    )(back, experts, gates, grad_logit, tokens, joint, grad_residual, grad_norms, part_output)


def publish_kernel(joint_w, output_w, inner_w, outer_w, layer, tokens_in,
                   query, key, value, value_router, output_router, norms, output_out, inner_out, outer_out, layer_out, tokens_out,
                   *refs):
    held, load, store = refs[:-2], refs[-2], refs[-1]
    sources = (tokens_in, inner_w, outer_w, layer, output_w)
    loads = [pltpu.make_async_copy(src, buf, load.at[i]) for i, (src, buf) in enumerate(zip(sources, held))]
    for copy in loads:
        copy.start()
    query[...] = joint_w[:, :QCOLS]
    key[...] = joint_w[:, QCOLS : 2 * QCOLS]
    value[...] = joint_w[:, 2 * QCOLS : ROUTERS]
    value_router[...] = joint_w[:, ROUTERS : ROUTERS + HEADS * EXP]
    output_router[...] = joint_w[:, ROUTERS + HEADS * EXP : NORM]
    norms[...] = joint_w[:, NORM : NORM + 2]
    half, small = inner_w.shape[1] // 2, CHUNK // 2
    stores = []
    for i, target in enumerate((tokens_out, inner_out, outer_out, layer_out, output_out)):
        loads[i].wait()
        pairs = [(held[i], target)]
        if i == 1:
            pairs = [(held[i].at[:, pl.ds(core * half + chunk * small, small)], target.at[:, pl.ds(chunk * CHUNK + core * small, small)])
                     for core in range(2) for chunk in range(half // small)]
        for src, dst in pairs:
            copy = pltpu.make_async_copy(src, dst, store.at[len(stores)])
            copy.start()
            stores.append(copy)
    for copy in stores:
        copy.wait()


def publish(joint_w, output_w, inner_w, outer_w, layer, tokens):
    rows = joint_w.shape[0]
    f32 = jnp.float32
    columns = [QCOLS, QCOLS, VCOLS, HEADS * EXP, HEADS * EXP, 2]
    rest = (output_w, inner_w, outer_w, layer, tokens)
    return pl.pallas_call(
        publish_kernel,
        out_shape=[jax.ShapeDtypeStruct((rows, c), f32) for c in columns] + [jax.ShapeDtypeStruct(x.shape, x.dtype) for x in rest],
        in_specs=[VMEM] + [ANY] * 5,
        out_specs=[VMEM] * 6 + [ANY] * 5,
        scratch_shapes=[pltpu.VMEM(x.shape, x.dtype) for x in (tokens, inner_w, outer_w, layer, output_w)]
        + [DMA((5,)), DMA((4 + inner_w.shape[1] // (CHUNK // 2),))],
        compiler_params=pltpu.CompilerParams(vmem_limit_bytes=32 << 20),
    )(joint_w, *rest)


def on_device(
    tokens, value_routes, output_routes, cont_gap, query_weight, key_weight, value_weight, value_router,
    output_router, output_weight, norm_gain, norm_bias, inner_weight, outer_weight, cotangent,
):
    count = lax.axis_size("fsdp")
    inputs = tokens[0]
    rows, width = inputs.shape
    routers = jnp.concatenate(
        [value_router, output_router, norm_gain[:, None], norm_bias[:, None],
         jnp.zeros((query_weight.shape[0], JOINT - NORM - 2), jnp.bfloat16)], axis=1)
    routes = jnp.concatenate([value_routes[0].reshape(rows, -1), output_routes[0].reshape(rows, -1)], axis=1)
    joint, output_full, qkv, experts, gates, norms, tables, turned = project(
        count, query_weight, key_weight, value_weight, routers, inputs, routes, output_weight, cont_gap)
    att, store, outputs, logs, inner_full, outer_full = attend(
        count, qkv, tables, (inner_weight, outer_weight), (SPLITS["inner"], SPLITS["outer"]))
    layer, grad_residual, grad_att, grad_logit, grad_norms, part_output, part_inner, outer_w = feed(
        count, att, gates, inputs, cotangent[0], norms, output_full.reshape(VCOLS, width), inner_full.reshape(width, -1),
        outer_full.reshape(-1, width))
    back, inner_w = retreat(
        count, grad_att, turned, store, outputs, logs, part_inner.reshape(count, -1, part_inner.shape[1]), INNER_PARTS)
    grad_input, joint_w, output_w = settle(
        count, back, experts, gates, grad_logit, inputs, joint, grad_residual, grad_norms,
        part_output.reshape(count, -1, part_output.shape[1]))
    query, key, value, value_r, output_r, norm_w, output_w, inner_w, outer_w, layer, grad_input = publish(
        joint_w, output_w, inner_w, outer_w, layer, grad_input)
    return (layer[None], grad_input[None], query, key, value, value_r, output_r, output_w, norm_w[:, 0], norm_w[:, 1], inner_w, outer_w)


def solution(mesh):
    wide = P("fsdp", None)
    part = P("fsdp", "seq", None)
    routes = P("fsdp", "seq", None, None)
    return jax.shard_map(
        on_device,
        mesh=mesh,
        in_specs=(part, routes, routes, P()) + (wide,) * 6 + (P("fsdp"), P("fsdp"), wide, wide, part),
        out_specs=(part, part) + (wide,) * 6 + (P("fsdp"), P("fsdp"), wide, wide),
        check_vma=False,
    )
```

```python
import functools
import jax
import jax.numpy as jnp
from jax import lax
from jax.experimental import pallas as pl
from jax.experimental.pallas import tpu as pltpu
from jax.sharding import PartitionSpec as P

HEADS = 4
DH = 112
EXP = 5
CONT = 1024
GSLOTS = 4
PSLOTS = 2
BLOCK = 512
LANES = 128
EPSILON = 1e-05
NEGATIVE = -1e30
LOG2E = 1.4426950408889634
MESH = pl.DeviceIdType.MESH
ANY = pl.BlockSpec(memory_space=pl.ANY)
VMEM = pl.BlockSpec(memory_space=pltpu.VMEM)
SMEM = pl.BlockSpec(memory_space=pltpu.SMEM)
DMA = pltpu.SemaphoreType.DMA

QCOLS = HEADS * DH
VCOLS = HEADS * EXP * DH
ROUTERS = 2 * QCOLS + VCOLS
NORM = ROUTERS + 2 * HEADS * EXP
JOINT = 3328
SPLITS = {"joint": (640, 512), "output": (256, 128), "inner": (768, 640), "outer": (256, 128)}
INNER_PARTS = ((512, 768),)


def ring_place(index, count):
    return (index // 2) * (1 - index % 2) + (count - 1 - index // 2) * (index % 2)


def ring_index(place, count):
    upper = place // (count // 2)
    return 2 * place * (1 - upper) + (2 * (count - 1 - place) + 1) * upper


def enter(devices):
    barrier = pltpu.get_barrier_semaphore()
    for device in devices:
        pl.semaphore_signal(barrier, inc=1, device_id=device, device_id_type=MESH)
    pl.semaphore_wait(barrier, len(devices))


class Ring:
    def __init__(self, count, splits):
        self.count, self.splits = count, splits
        self.seq, self.fsdp = lax.axis_index("seq"), lax.axis_index("fsdp")
        self.plane, self.core = self.seq // 2, self.seq % 2
        self.place = ring_place(self.fsdp, count)
        self.right = (self.seq, ring_index((self.place + 1) % count, count))
        self.left = (self.seq, ring_index((self.place + count - 1) % count, count))
        self.core_mate = (self.seq + 1 - 2 * self.core, self.fsdp)
        self.plane_mate = ((self.seq + 2) % 4, self.fsdp)
        self.far = count // 2

    def neighbours(self):
        return [self.right, self.left, self.core_mate, self.plane_mate]

    def reach(self, kind, way):
        return self.far if kind == way else self.count - 1 - self.far

    def kinds(self, t):
        return [kind for kind in (1, 0) if self.splits[t][kind] > 0]

    def half(self, t):
        return self.splits[t][0] + 2 * self.splits[t][1]

    def cols(self, t, kind, plane, core):
        both, single = self.splits[t]
        if kind == 0:
            return pl.ds(pl.multiple_of(core * self.half(t), LANES), both)
        return pl.ds(pl.multiple_of(core * self.half(t) + both + plane * single, LANES), single)

    def behind(self, way, k):
        step = self.count - k if way == 0 else k
        return ring_index((self.place + step) % self.count, self.count)

    def next(self, way):
        return self.right if way == 0 else self.left

    def slot(self, kind, way, k):
        return k - 1 if way == 0 else self.reach(kind, 0) + k - 1


class Gather(Ring):
    def __init__(self, count, splits, shards, at, send, recv, local):
        super().__init__(count, splits)
        self.shards, self.at, self.send, self.recv, self.local = shards, at, send, recv, local

    @staticmethod
    def sems(count, tensors):
        return [DMA((6 * tensors * (count - 1),)), DMA((6 * tensors * (count - 1),)), DMA((tensors,))]

    def copy(self, src, dst, group, t, slot, device):
        i = (group * len(self.splits) + t) * (self.count - 1) + slot
        return pltpu.make_async_remote_copy(
            src, dst, self.send.at[i], self.recv.at[i], device_id=device, device_id_type=MESH
        )

    def same(self, group, t, kind, way, k, plane, core, device):
        ref = self.at(t, self.behind(way, k), self.cols(t, kind, plane, core))
        return self.copy(ref, ref, group, t, self.slot(kind, way, k), device)

    def hop(self, t, kind, way, k):
        if k > 1:
            ref = self.at(t, self.behind(way, k - 1), self.cols(t, kind, self.plane, self.core))
            return self.copy(ref, ref, kind, t, self.slot(kind, way, k), self.next(way))
        cols = self.cols(t, kind, self.plane, self.core)
        return self.copy(
            self.shards[t].at[:, cols], self.at(t, self.fsdp, cols), kind, t, self.slot(kind, way, 1), self.next(way)
        )

    def arrived(self, t, kind, way, k):
        return self.same(kind, t, kind, way, k, self.plane, self.core, self.next(way))

    def to_core(self, t, kind, way, k, core):
        return self.same(2 + kind, t, kind, way, k, self.plane, core, self.core_mate)

    def to_plane(self, t, way, k, plane):
        return self.same(4, t, 1, way, k, plane, self.core, self.plane_mate)

    def plane_to_core(self, t, way, k, core):
        return self.same(5, t, 1, way, k, 1 - self.plane, core, self.core_mate)

    def own(self, t):
        return pltpu.make_async_copy(self.shards[t], self.at(t, self.fsdp, slice(None)), self.local.at[t])

    def start(self, t):
        for kind in self.kinds(t):
            for way in (0, 1):
                if self.reach(kind, way):
                    self.hop(t, kind, way, 1).start()
        self.own(t).start()

    def arrive(self, t, k):
        for kind in self.kinds(t):
            for way in (0, 1):
                if k <= self.reach(kind, way):
                    self.arrived(t, kind, way, k).wait_recv()
                    if k < self.reach(kind, way):
                        self.hop(t, kind, way, k + 1).start()
                    if kind:
                        self.to_plane(t, way, k, self.plane).start()
                    self.to_core(t, kind, way, k, self.core).start()

    def plane_arrive(self, t, k):
        if 1 in self.kinds(t):
            for way in (0, 1):
                if k <= self.reach(1, way):
                    self.to_plane(t, way, k, 1 - self.plane).wait_recv()
                    self.plane_to_core(t, way, k, self.core).start()

    def finish(self, t):
        self.own(t).wait()
        for kind in self.kinds(t):
            for way in (0, 1):
                for k in range(1, self.reach(kind, way) + 1):
                    self.hop(t, kind, way, k).wait_send()
                    self.to_core(t, kind, way, k, self.core).wait_send()
                    self.to_core(t, kind, way, k, 1 - self.core).wait_recv()
                    if kind:
                        self.to_plane(t, way, k, self.plane).wait_send()
                        self.plane_to_core(t, way, k, self.core).wait_send()
                        self.plane_to_core(t, way, k, 1 - self.core).wait_recv()

    def events(self):
        tensors = range(len(self.splits))
        out = []
        for k in range(1, self.far + 1):
            for t in tensors:
                out.append(functools.partial(self.arrive, t, k))
                if k > 1:
                    out.append(functools.partial(self.plane_arrive, t, k - 1))
        for t in tensors:
            out.append(functools.partial(self.plane_arrive, t, self.far))
        for t in tensors:
            out.append(functools.partial(self.finish, t))
        return out


TABLE = 5632
TABLE_ZERO = 5120
TURNED_ZERO = 512


def route_lanes(routes, lane):
    hit = None
    for head in range(2 * HEADS):
        for choice in range(2):
            place = head * EXP + routes[:, 2 * head + choice : 2 * head + choice + 1]
            here = lane == place
            hit = here if hit is None else hit | here
    return hit.astype(jnp.float32)


def project_kernel(count, query, key, value, value_router, output_router, norm, tokens, routes, output_shard, gaps,
                   joint, output_w, qkv, experts, gates, norms, tables, turned_tables,
                   shard, query_v, key_v, value_v, routers_v, product, load, send, recv, local):
    rows = shard.shape[0]
    splits = (SPLITS["joint"], SPLITS["output"])

    def at(t, g, cols):
        if t:
            return output_w.at[g, :, cols]
        return joint.at[pl.ds(pl.multiple_of(g * rows, rows), rows), cols]

    ring = Gather(count, splits, [shard, output_shard], at, send, recv, local)
    loads = [(query, query_v), (key, key_v), (value, value_v), (value_router, routers_v.at[0]), (output_router, routers_v.at[1])]
    loads = [pltpu.make_async_copy(src, dst, load.at[i]) for i, (src, dst) in enumerate(loads)]
    for copy in loads:
        copy.start()
    for copy in loads:
        copy.wait()
    turned_norm = jnp.concatenate([norm[...].astype(jnp.float32), jnp.zeros((LANES - 2, rows), jnp.float32)], axis=0).T
    wide = [ref[...].astype(jnp.float32) for ref in (query_v, key_v, value_v)]
    wide += [routers_v[0].astype(jnp.float32), routers_v[1].astype(jnp.float32), turned_norm[:, : JOINT - NORM]]
    if JOINT - NORM > LANES:
        wide.append(jnp.zeros((rows, JOINT - NORM - LANES), jnp.float32))
    shard[...] = jnp.concatenate(wide, axis=1).astype(jnp.bfloat16)
    enter(ring.neighbours())
    ring.start(0)
    slope = jnp.float32(0.0)
    for head in range(HEADS):
        slope = jnp.where(ring.seq // 1 == head, -0.5 * 0.5**head * LOG2E, slope)
    group = ring.fsdp // GSLOTS
    pair = jnp.maximum(ring.fsdp % GSLOTS - PSLOTS, 0) * 2
    gap_values = [jnp.int32(0), gaps[group, pair], gaps[group, pair + 1]]

    def table_column(step, carry):
        start = pl.multiple_of(step * 256, 256)
        lanes = lax.broadcasted_iota(jnp.int32, (8, 256 + LANES), 1) + (start - LANES)
        for which in range(3):
            for turned in range(2):
                if turned:
                    distance = lanes - TURNED_ZERO + gap_values[which]
                else:
                    distance = TABLE_ZERO - lanes + gap_values[which]
                bias = slope * jnp.log(1.0 + jnp.maximum(distance, 0).astype(jnp.float32))
                bias = jnp.where(distance >= 0, bias, NEGATIVE)
                wide = jnp.broadcast_to(bias[:1], (LANES, 256 + LANES))
                rolled = pltpu.roll(wide, 0, 1, stride=1, stride_axis=0)
                target = turned_tables if turned else tables
                target[which, :, pl.ds(start, 256)] = rolled[:, LANES:]
        return carry

    late = 1
    steps, later = [], []
    for k in range(1, ring.far + 1):
        steps.append(functools.partial(ring.arrive, 0, k))
        if k > 1:
            steps.append(functools.partial(ring.plane_arrive, 0, k - 1))
        if k == late:
            steps.append(functools.partial(ring.start, 1))
        later.append(functools.partial(ring.arrive, 1, k))
        if k > 1:
            later.append(functools.partial(ring.plane_arrive, 1, k - 1))
    steps += [functools.partial(ring.plane_arrive, 0, ring.far), functools.partial(ring.finish, 0)]
    later += [functools.partial(ring.plane_arrive, 1, ring.far)]
    early, later = later[:3], later[3:]
    steps = steps[:-1] + early + steps[-1:]
    cut = max(1, TABLE // 256 // len(steps))
    done = 0
    for i, event in enumerate(steps):
        upto = TABLE // 256 if i == len(steps) - 1 else min(TABLE // 256, (i + 1) * cut)
        if upto > done:
            lax.fori_loop(done, upto, table_column, 0)
            done = upto
        event()

    def column(step, carry):
        cols = pl.ds(pl.multiple_of(step * 256, 256), 256)
        product[:, cols] = jnp.dot(tokens[...], joint[:, cols], preferred_element_type=jnp.float32)
        return carry

    columns = JOINT // 256
    for i in range(3):
        lax.fori_loop(i * columns // 3, (i + 1) * columns // 3, column, 0)
        for event in later[i * len(later) // 4 : (i + 1) * len(later) // 4]:
            event()
    norm_tile = NORM // LANES * LANES
    turned_norm = joint[:, norm_tile : norm_tile + LANES].astype(jnp.float32).T
    norms[...] = turned_norm[NORM - norm_tile : NORM - norm_tile + 8]
    logits = product[:, ROUTERS : ROUTERS + 2 * HEADS * EXP]
    local_rows = tokens.shape[0]
    wide = jnp.concatenate([logits, jnp.zeros((local_rows, LANES - 2 * HEADS * EXP), jnp.float32)], axis=1)
    lane = lax.broadcasted_iota(jnp.int32, (local_rows, LANES), 1)
    mask = route_lanes(routes[...], lane)
    gate = 1.0 / (1.0 + jnp.exp(-wide))
    gates[0] = gate * mask
    gates[1] = gate * mask * (1.0 - gate)
    pad = jnp.zeros((local_rows, LANES - DH), jnp.float32)
    ones = jnp.ones((local_rows, LANES - DH), jnp.float32)
    for head in range(HEADS):
        first = head * DH
        qkv[head, 0] = jnp.concatenate([product[:, first : first + DH], pad], axis=1).astype(jnp.bfloat16)
        first = QCOLS + head * DH
        qkv[head, 1] = jnp.concatenate([product[:, first : first + DH], pad], axis=1).astype(jnp.bfloat16)
        total = None
        for expert in range(EXP):
            which = head * EXP + expert
            first = 2 * QCOLS + which * DH
            piece = product[:, first : first + DH]
            experts[which] = jnp.concatenate([piece, pad], axis=1).astype(jnp.bfloat16)
            term = piece * gates[0, :, which : which + 1]
            total = term if total is None else total + term
        qkv[head, 2] = jnp.concatenate([total, ones], axis=1).astype(jnp.bfloat16)
    for event in later[3 * len(later) // 4 :]:
        event()
    ring.finish(1)


def project(count, query, key, value, value_router, output_router, norm, tokens, routes, output_shard, gaps):
    rows, (shard_rows, _) = tokens.shape[0], query.shape
    f32, bf = jnp.float32, jnp.bfloat16
    V = pltpu.VMEM
    return pl.pallas_call(
        functools.partial(project_kernel, count),
        out_shape=[
            jax.ShapeDtypeStruct((shard_rows * count, JOINT), bf),
            jax.ShapeDtypeStruct((count,) + output_shard.shape, bf),
            jax.ShapeDtypeStruct((HEADS, 3, rows, LANES), bf),
            jax.ShapeDtypeStruct((HEADS * EXP, rows, LANES), bf),
            jax.ShapeDtypeStruct((2, rows, LANES), f32),
            jax.ShapeDtypeStruct((8, shard_rows * count), f32),
            jax.ShapeDtypeStruct((3, LANES, TABLE), f32),
            jax.ShapeDtypeStruct((3, LANES, TABLE), f32),
        ],
        in_specs=[ANY] * 5 + [VMEM] * 4 + [SMEM],
        out_specs=[VMEM, ANY] + [VMEM] * 6,
        scratch_shapes=[
            V((shard_rows, JOINT), bf), V(query.shape, bf), V(key.shape, bf), V(value.shape, bf), V((2,) + value_router.shape, bf),
            V((rows, JOINT), f32), DMA((5,)),
        ]
        + Gather.sems(count, 2),
        compiler_params=pltpu.CompilerParams(collective_id=1, has_side_effects=True, vmem_limit_bytes=62 << 20),
    )(query, key, value, value_router, output_router, norm, tokens, routes, output_shard, gaps)


def seq_mates(ring):
    return [ring.core_mate, ring.plane_mate, (3 - ring.seq, ring.fsdp)]


def slot_mates(ring):
    f = ring.fsdp
    return [(ring.seq, f + 1 - 2 * (f % 2)), (ring.seq, f + 2 - 4 * ((f // 2) % 2))]


def tile_place(slot, seq, phase, key_block, query_block):
    cont = slot // PSLOTS
    own = 1 - jnp.minimum(phase, 1)
    piece = jnp.where(slot == 3, 2 - phase, phase - 1)
    source = jnp.where(phase == 0, 0, 1 + piece)
    first = cont * 2 * (query_block // 2)
    active = jnp.where(
        phase == 0,
        (key_block <= query_block) & (key_block >= first),
        jnp.where(phase == 1, slot >= 1, slot >= 2),
    )
    far_column = jnp.where(
        cont == 1,
        2048 * piece + BLOCK * key_block - BLOCK * (query_block % 2) - 4096,
        BLOCK * key_block - 2048 - BLOCK * query_block,
    )
    column = jnp.where(phase == 0, BLOCK * (key_block - query_block), far_column)
    table = jnp.where((phase > 0) & (cont == 1), 1 + query_block // 2, 0)
    return source, active, table, column


STRIP = 512


def near_first(ring, j):
    odd, high = j % 2, j // 2
    core = ring.core + odd - 2 * ring.core * odd
    plane = ring.plane + high - 2 * ring.plane * high
    return 2 * plane + core


def block_rows(block):
    return pl.ds(pl.multiple_of(block * BLOCK, BLOCK), BLOCK)


def attend_kernel(count, splits, steps, qkv, tables, *refs):
    T = len(splits)
    shards, refs = refs[:T], refs[T:]
    att, store, outputs, logs = refs[:4]
    fulls, refs = refs[4 : 4 + T], refs[4 + T :]
    acc, top, att_low, kv_send, kv_recv, q_send, q_recv, sh_send, sh_recv, out_send, out_recv, here = refs[:12]
    at = lambda t, g, cols: fulls[t].at[g, :, cols]
    ring = Gather(count, splits, shards, at, *refs[12:])
    seq, slot = ring.seq, ring.fsdp % GSLOTS
    mates, (x_mate, z_mate) = seq_mates(ring), slot_mates(ring)
    enter(ring.neighbours() + mates[2:] + [x_mate, z_mate])

    def remote(src, dst, send, recv, device):
        return pltpu.make_async_remote_copy(src, dst, send, recv, device_id=device, device_id_type=MESH)

    mine = block_rows(seq)

    def kv_copy(mate):
        return remote(qkv.at[mate[0], pl.ds(1, 2)], store.at[pl.ds(1, 2), mine], kv_send.at[mate[0]], kv_recv.at[seq], mate)

    def q_copy(mate):
        return remote(qkv.at[mate[0], 0], store.at[0, mine], q_send.at[mate[0]], q_recv.at[seq], mate)

    for mate in mates[1:] + mates[:1]:
        kv_copy(mate).start()
    own_copy = pltpu.make_async_copy(qkv.at[seq], store.at[pl.ds(0, 3), mine], here.at[0])
    own_copy.start()
    for mate in mates[1:] + mates[:1]:
        q_copy(mate).start()
    acc[...] = jnp.zeros_like(acc)
    top[...] = jnp.full_like(top, NEGATIVE)

    def far_rows(piece, chunk):
        return store.at[pl.ds(3 + 2 * piece, 2), block_rows(near_first(ring, chunk))]

    def first_hop(chunk, way):
        src = store.at[pl.ds(1, 2), block_rows(near_first(ring, chunk))]
        piece = slot % 2
        return remote(src, far_rows(piece, chunk), sh_send.at[4 * way + chunk], sh_recv.at[4 * piece + chunk],
                      x_mate if way == 0 else z_mate)

    def second_hop(chunk):
        piece = slot % 2
        return remote(far_rows(piece, chunk), far_rows(piece, chunk), sh_send.at[8 + chunk], sh_recv.at[4 * piece + chunk], x_mate)

    def share(chunk):
        @pl.when(slot < 2)
        def _():
            first_hop(chunk, 1).start()

        @pl.when(slot == 0)
        def _():
            first_hop(chunk, 0).start()

    def pass_on(chunk):
        @pl.when(slot >= 1)
        def _():
            piece = jnp.where(slot == 3, 1, 0)
            remote(far_rows(piece, chunk), far_rows(piece, chunk), sh_send.at[chunk], sh_recv.at[4 * piece + chunk], x_mate).wait_recv()

        @pl.when(slot >= 2)
        def _():
            second_hop(chunk).start()

    def last_piece(chunk):
        @pl.when(slot >= 2)
        def _():
            piece = 3 - slot
            remote(far_rows(piece, chunk), far_rows(piece, chunk), sh_send.at[chunk], sh_recv.at[4 * piece + chunk], x_mate).wait_recv()

    own_copy.wait()
    share(0)
    for chunk, mate in enumerate(mates):
        other = mate[0]
        src = store.at[pl.ds(1, 2), block_rows(other)]
        remote(src, src, kv_send.at[other], kv_recv.at[other], mate).wait_recv()
        share(1 + chunk)
    for mate in mates:
        src = store.at[0, block_rows(mate[0])]
        remote(src, src, q_send.at[mate[0]], q_recv.at[mate[0]], mate).wait_recv()

    def tile(source, table, column, key_block, first, rows):
        keys = store[1 + 2 * source, block_rows(key_block), :]
        values = store[2 + 2 * source, block_rows(key_block), :]
        for strip in range(rows // STRIP):
            part = pl.ds(pl.multiple_of(first + strip * STRIP, STRIP), STRIP)
            scores = lax.dot_general(store[0, part, :], keys, (((1,), (1,)), ((), ())), preferred_element_type=jnp.float32)
            start = column + TABLE_ZERO - strip * STRIP
            bias = [tables[table, :, pl.ds(pl.multiple_of(start - LANES * i, LANES), BLOCK)] for i in range(STRIP // LANES)]
            scores = scores * (DH**-0.5 * LOG2E) + jnp.concatenate(bias, axis=0)
            before = top[part, :]
            after = jnp.maximum(before, jnp.max(scores, axis=1, keepdims=True))
            terms = jnp.exp2(scores - after[:, :1])
            acc[part, :] = acc[part, :] * jnp.exp2(before - after) + jnp.dot(
                terms.astype(jnp.bfloat16), values, preferred_element_type=jnp.float32)
            top[part, :] = after

    def near_tile(step):
        key_block, query_block = near_first(ring, step // 4), step % 4
        source, active, table, column = tile_place(slot, seq, 0, key_block, query_block)

        @pl.when(active)
        def _():
            tile(source, table, column, key_block, query_block * BLOCK, BLOCK)

    def far_tile(step):
        phase, key_block, query_block = step // 8, near_first(ring, (step // 2) % 4), 2 * (step % 2)
        source, active, table, column = tile_place(slot, seq, phase, key_block, query_block)

        @pl.when(active)
        def _():
            tile(source, table, column, key_block, query_block * BLOCK, 2 * BLOCK)

    events = {}
    for chunk in range(4):
        events.setdefault(4 * chunk + 3, []).append(functools.partial(pass_on, chunk))
        events.setdefault(24 + 2 * chunk, []).append(functools.partial(last_piece, chunk))
    begin, first, gap = steps
    for t in range(T):
        if begin + t < 0:
            ring.start(t)
        else:
            events.setdefault(begin + t, []).append(functools.partial(ring.start, t))
    rest = []
    for i, event in enumerate(ring.events()):
        step = int(first + gap * i)
        if step < 32:
            events.setdefault(step, []).append(event)
        else:
            rest.append(event)

    def step_body(step, carry):
        for when, actions in sorted(events.items()):
            @pl.when(step == when)
            def _():
                for action in actions:
                    action()
        pl.when(step < 16)(lambda: near_tile(step))
        pl.when(step >= 16)(lambda: far_tile(step - 8))
        return carry

    lax.fori_loop(0, 32, step_body, 0)
    total = acc[:, DH : DH + 1]
    result = acc[...] / total
    outputs[...] = result
    log_total = top[...] + jnp.log2(total)
    for block in range(4):
        logs[:, block * BLOCK : (block + 1) * BLOCK] = log_total[block * BLOCK : (block + 1) * BLOCK].T[:8]
    att_low[...] = result.astype(jnp.bfloat16)

    def out_copy(mate):
        return remote(att_low.at[block_rows(mate[0])], att.at[seq], out_send.at[mate[0]], out_recv.at[seq], mate)

    for mate in mates[1:] + mates[:1]:
        out_copy(mate).start()
    own_out = pltpu.make_async_copy(att_low.at[mine], att.at[seq], here.at[1])
    own_out.start()
    for event in rest:
        event()
    own_out.wait()
    for mate in mates:
        kv_copy(mate).wait_send()
        q_copy(mate).wait_send()
        out_copy(mate).wait_send()
        ref = att.at[mate[0]]
        remote(ref, ref, out_send.at[mate[0]], out_recv.at[mate[0]], mate).wait_recv()
    for chunk in range(4):
        @pl.when(slot < 2)
        def _():
            first_hop(chunk, 1).wait_send()

        @pl.when(slot == 0)
        def _():
            first_hop(chunk, 0).wait_send()

        @pl.when(slot >= 2)
        def _():
            second_hop(chunk).wait_send()


def attend(count, qkv, tables, shards, splits, steps=(0, 18, 2)):
    rows = qkv.shape[2]
    own = 4 * rows
    T = len(shards)
    return pl.pallas_call(
        functools.partial(attend_kernel, count, splits, steps),
        out_shape=[
            jax.ShapeDtypeStruct((HEADS, rows, LANES), jnp.bfloat16),
            jax.ShapeDtypeStruct((7, own, LANES), jnp.bfloat16),
            jax.ShapeDtypeStruct((own, LANES), jnp.float32),
            jax.ShapeDtypeStruct((8, own), jnp.float32),
        ]
        + [jax.ShapeDtypeStruct((count,) + w.shape, w.dtype) for w in shards],
        in_specs=[VMEM] * (2 + T),
        out_specs=[VMEM] * 4 + [ANY] * T,
        scratch_shapes=[
            pltpu.VMEM((own, LANES), jnp.float32),
            pltpu.VMEM((own, LANES), jnp.float32),
            pltpu.VMEM((own, LANES), jnp.bfloat16),
            DMA((4,)), DMA((4,)), DMA((4,)), DMA((4,)), DMA((12,)), DMA((8,)), DMA((4,)), DMA((4,)), DMA((2,)),
        ]
        + Gather.sems(count, T),
        compiler_params=pltpu.CompilerParams(collective_id=2, has_side_effects=True, vmem_limit_bytes=56 << 20),
    )(qkv, tables, *shards)


class Scatter(Ring):
    def __init__(self, count, splits, parts, outs, bufs, sems):
        super().__init__(count, splits)
        self.parts, self.outs = parts, outs
        T = len(splits)
        self.mine, self.plane_in = bufs[:T], bufs[T : 2 * T]
        self.ring0, self.ring1 = bufs[2 * T : 3 * T], bufs[3 * T : 4 * T]
        self.low, self.low_in, self.done = bufs[4 * T : 5 * T], bufs[5 * T : 6 * T], bufs[6 * T : 7 * T]
        (self.load, self.plane_s, self.plane_r, self.ring_s, self.ring_r, self.end_s, self.end_r, self.put) = sems

    @staticmethod
    def scratch(count, splits, rows):
        half = [a + 2 * b for a, b in splits]
        bf = jnp.bfloat16
        out = [pltpu.VMEM((count, r, h), bf) for r, h in zip(rows, half)]
        out += [pltpu.VMEM((count, r, b), bf) for r, (a, b) in zip(rows, splits)]
        out += [pltpu.VMEM((count - 1 if a else 1, r, max(a, LANES)), bf) for r, (a, b) in zip(rows, splits)]
        out += [pltpu.VMEM((count - 1, r, b), bf) for r, (a, b) in zip(rows, splits)]
        out += [pltpu.VMEM((r, a + b), bf) for r, (a, b) in zip(rows, splits)]
        out += [pltpu.VMEM((r, a + b), bf) for r, (a, b) in zip(rows, splits)]
        out += [pltpu.VMEM((r, h), jnp.float32) for r, h in zip(rows, half)]
        T = len(splits)
        return out + [DMA((T * count,))] * 3 + [DMA((2 * T * (count - 1),))] * 2 + [DMA((2 * T,))] * 2 + [DMA((T,))]

    def dest(self, rel):
        return ring_index((self.place + rel) % self.count, self.count)

    def load_copy(self, t, rel):
        part, first = self.parts[t]
        src = part.at[self.dest(rel), :, pl.ds(first, self.half(t))]
        return pltpu.make_async_copy(src, self.mine[t].at[rel], self.load.at[t * self.count + rel])

    def remote(self, src, dst, s, r, i, device):
        return pltpu.make_async_remote_copy(src, dst, s.at[i], r.at[i], device_id=device, device_id_type=MESH)

    def single(self, t, plane):
        both, single = self.splits[t]
        return pl.ds(pl.multiple_of(both + plane * single, LANES), single)

    def plane_copy(self, t, rel):
        src = self.mine[t].at[rel, :, self.single(t, 1 - self.plane)]
        return self.remote(src, self.plane_in[t].at[rel], self.plane_s, self.plane_r, t * self.count + rel, self.plane_mate)

    def rels(self, D):
        return sorted({D % self.count, (-D) % self.count})

    def order(self):
        out = []
        for D in range(self.far, -1, -1):
            out += self.rels(D)
        return out

    def start(self, t):
        for rel in self.order():
            self.load_copy(t, rel).start()

    def ready(self, t, rel):
        if self.parts[t]:
            self.load_copy(t, rel).wait()
        self.plane_copy(t, rel).start()

    def all_ready(self, t):
        for rel in self.order():
            self.ready(t, rel)

    def step(self, t, D):
        self.combine(t, D)
        if D:
            self.chain(t, D)
        else:
            self.close(t)

    def buffer(self, t, kind, slot):
        if kind:
            return self.ring1[t].at[slot]
        return self.ring0[t].at[slot]

    def own_ref(self, t, kind, rel):
        if kind:
            return self.mine[t].at[rel, :, self.single(t, self.plane)]
        return self.mine[t].at[rel, :, pl.ds(0, self.splits[t][0])]

    def ring_copy(self, t, kind, way, D):
        slot = self.slot(kind, way, D)
        if D == self.reach(kind, way):
            src = self.own_ref(t, kind, D % self.count if way == 0 else (-D) % self.count)
        else:
            src = self.buffer(t, kind, self.slot(kind, way, D + 1))
        i = (2 * t + kind) * (self.count - 1) + slot
        return self.remote(src, self.buffer(t, kind, slot), self.ring_s, self.ring_r, i, self.next(way))

    def ring_wait(self, t, kind, way, D):
        slot = self.slot(kind, way, D)
        ref = self.buffer(t, kind, slot)
        i = (2 * t + kind) * (self.count - 1) + slot
        self.remote(ref, ref, self.ring_s, self.ring_r, i, self.next(way)).wait_recv()

    def combine(self, t, D):
        for rel in self.rels(D):
            self.plane_copy(t, rel).wait_send()
            ref = self.plane_in[t].at[rel]
            self.remote(ref, ref, self.plane_s, self.plane_r, t * self.count + rel, self.plane_mate).wait_recv()
            own = self.own_ref(t, 1, rel)
            own[...] = (own[...].astype(jnp.float32) + self.plane_in[t][rel].astype(jnp.float32)).astype(jnp.bfloat16)

    def chain(self, t, D):
        for kind in self.kinds(t):
            for way in (0, 1):
                if D > self.reach(kind, way):
                    continue
                if D < self.reach(kind, way):
                    self.ring_wait(t, kind, way, D + 1)
                    rel = D % self.count if way == 0 else (-D) % self.count
                    ref = self.buffer(t, kind, self.slot(kind, way, D + 1))
                    ref[...] = (ref[...].astype(jnp.float32) + self.own_ref(t, kind, rel)[...].astype(jnp.float32)).astype(jnp.bfloat16)
                self.ring_copy(t, kind, way, D).start()

    def end_copy(self, t):
        return self.remote(self.low[t], self.low_in[t], self.end_s, self.end_r, 2 * t, self.plane_mate)

    def close(self, t):
        both, single = self.splits[t]
        for kind in self.kinds(t):
            total = self.own_ref(t, kind, 0)[...].astype(jnp.float32)
            for way in (0, 1):
                if self.reach(kind, way):
                    self.ring_wait(t, kind, way, 1)
                    total = total + self.buffer(t, kind, self.slot(kind, way, 1))[...].astype(jnp.float32)
            if kind:
                self.low[t][:, both:] = total.astype(jnp.bfloat16)
            else:
                self.low[t][:, :both] = total.astype(jnp.bfloat16)
        self.end_copy(t).start()

    def out_ref(self, t, core):
        out, whole, first = self.outs[t]
        return out.at[:, pl.ds(pl.multiple_of(core * whole + first, LANES), self.half(t))]

    def out_copy(self, t):
        return self.remote(self.done[t], self.out_ref(t, self.core), self.end_s, self.end_r, 2 * t + 1, self.core_mate)

    def put_copy(self, t):
        return pltpu.make_async_copy(self.done[t], self.out_ref(t, self.core), self.put.at[t])

    def deliver(self, t):
        both, single = self.splits[t]
        self.end_copy(t).wait_send()
        ref = self.low_in[t]
        self.remote(ref, ref, self.end_s, self.end_r, 2 * t, self.plane_mate).wait_recv()
        if both:
            self.done[t][:, :both] = self.low[t][:, :both].astype(jnp.float32) + self.low_in[t][:, :both].astype(jnp.float32)
        if single:
            self.done[t][:, self.single(t, self.plane)] = self.low[t][:, both:].astype(jnp.float32)
            self.done[t][:, self.single(t, 1 - self.plane)] = self.low_in[t][:, both:].astype(jnp.float32)
        self.out_copy(t).start()
        self.put_copy(t).start()

    def finish(self, t):
        for kind in self.kinds(t):
            for way in (0, 1):
                for D in range(1, self.reach(kind, way) + 1):
                    self.ring_copy(t, kind, way, D).wait_send()
        self.out_copy(t).wait_send()
        self.put_copy(t).wait()
        ref = self.out_ref(t, 1 - self.core)
        self.remote(ref, ref, self.end_s, self.end_r, 2 * t + 1, self.core_mate).wait_recv()


def retreat_kernel(count, splits, steps, grad_att, turned, store, outputs, logs, part, back, out, *refs):
    T = len(splits)
    (grads, delta, grad_q, grad_kv, send_kv, kv_in0, kv_in1, low, in_send, in_recv, up_send, up_recv,
     out_send, out_recv, here) = refs[:15]
    refs = refs[15:]
    halves = [a + 2 * b for a, b in splits]
    firsts = [sum(halves[:t]) for t in range(T)]
    ring = Scatter(
        count, splits, [(part, first) for first in firsts], [(out, sum(halves), first) for first in firsts],
        refs[: 7 * T], refs[7 * T :])
    seq, slot = ring.seq, ring.fsdp % GSLOTS
    mates, (x_mate, z_mate) = seq_mates(ring), slot_mates(ring)
    enter(ring.neighbours() + mates[2:] + [x_mate, z_mate])

    def remote(src, dst, send, recv, device):
        return pltpu.make_async_remote_copy(src, dst, send, recv, device_id=device, device_id_type=MESH)

    mine = block_rows(seq)

    def in_copy(mate):
        return remote(grad_att.at[mate[0]], grads.at[mine], in_send.at[mate[0]], in_recv.at[seq], mate)

    for mate in mates[1:] + mates[:1]:
        in_copy(mate).start()
    own_copy = pltpu.make_async_copy(grad_att.at[seq], grads.at[mine], here.at[0])
    own_copy.start()
    grad_q[...] = jnp.zeros_like(grad_q)
    grad_kv[...] = jnp.zeros_like(grad_kv)
    own_copy.wait()
    for mate in mates:
        ref = grads.at[block_rows(mate[0])]
        remote(ref, ref, in_send.at[mate[0]], in_recv.at[mate[0]], mate).wait_recv()
    for block in range(4):
        rows = pl.ds(block * BLOCK, BLOCK)
        sums = jnp.sum(grads[rows, :].astype(jnp.float32) * outputs[rows, :], axis=1, keepdims=True)
        delta[:, rows] = jnp.broadcast_to(sums, (BLOCK, LANES)).T[:8]

    def tile(forward_phase, key_block, query_block, blocks):
        source, active, table, column = tile_place(slot, seq, forward_phase, key_block, query_block)

        @pl.when(active)
        def _():
            size = blocks * BLOCK
            key_rows, rows = block_rows(key_block), pl.ds(pl.multiple_of(query_block * BLOCK, BLOCK), size)
            keys, values = store[1 + 2 * source, key_rows, :], store[2 + 2 * source, key_rows, :]
            queries, tops = store[0, rows, :], grads[rows, :]
            scores = lax.dot_general(keys, queries, (((1,), (1,)), ((), ())), preferred_element_type=jnp.float32)
            bias = jnp.concatenate(
                [turned[table, :, pl.ds(pl.multiple_of(TURNED_ZERO - column - LANES * part, LANES), size)] for part in range(BLOCK // LANES)],
                axis=0,
            )
            weights = jnp.exp2(scores * (DH**-0.5 * LOG2E) + (bias - logs[:1, rows]))
            grad_weights = lax.dot_general(values, tops, (((1,), (1,)), ((), ())), preferred_element_type=jnp.float32)
            grad_scores = (weights * (grad_weights - delta[:1, rows])).astype(jnp.bfloat16)
            grad_kv[source, 1, key_rows, :] += jnp.dot(weights.astype(jnp.bfloat16), tops, preferred_element_type=jnp.float32)
            grad_kv[source, 0, key_rows, :] += jnp.dot(grad_scores, queries, preferred_element_type=jnp.float32)
            grad_q[rows, :] += lax.dot_general(grad_scores, keys, (((0,), (0,)), ((), ())), preferred_element_type=jnp.float32)

    def far_tile(step):
        phase = step // 8
        piece = jnp.where(slot == 2, 1 - phase, phase)
        tile(jnp.where(slot == 3, 2 - piece, 1 + piece), (step // 2) % 4, 2 * (step % 2), 2)

    def near_tile(step):
        tile(0, step // 4, step % 4, 1)

    scale = DH**-0.5

    def rounded(source, chunk, extra):
        rows = block_rows(chunk)
        keys = grad_kv[source, 0, rows, :] * scale
        values = grad_kv[source, 1, rows, :]
        for more in extra:
            keys = keys + more[0].astype(jnp.float32)
            values = values + more[1].astype(jnp.float32)
        return keys.astype(jnp.bfloat16), values.astype(jnp.bfloat16)

    def x_send(chunk):
        src = send_kv.at[0, :, block_rows(chunk)]
        return remote(src, kv_in0.at[:, block_rows(chunk)], up_send.at[chunk], up_recv.at[chunk], x_mate)

    def z_send(chunk):
        src = send_kv.at[1, :, block_rows(chunk)]
        return remote(src, kv_in1.at[:, block_rows(chunk)], up_send.at[4 + chunk], up_recv.at[4 + chunk], z_mate)

    def x_wait(chunk):
        ref = kv_in0.at[:, block_rows(chunk)]
        remote(ref, ref, up_send.at[chunk], up_recv.at[chunk], x_mate).wait_recv()

    def z_wait(chunk):
        ref = kv_in1.at[:, block_rows(chunk)]
        remote(ref, ref, up_send.at[4 + chunk], up_recv.at[4 + chunk], z_mate).wait_recv()

    def first_done(chunk):
        @pl.when(slot >= 1)
        def _():
            source = jnp.where(slot == 2, 2, 1)
            keys, values = rounded(source, chunk, [])
            send_kv[0, 0, block_rows(chunk), :] = keys
            send_kv[0, 1, block_rows(chunk), :] = values
            x_send(chunk).start()

    def second_done(chunk):
        @pl.when(slot >= 2)
        def _():
            x_wait(chunk)
            source = slot - 1
            keys, values = rounded(source, chunk, [kv_in0[:, block_rows(chunk), :]])
            send_kv[1, 0, block_rows(chunk), :] = keys
            send_kv[1, 1, block_rows(chunk), :] = values
            z_send(chunk).start()

    def out_copy(mate):
        src = low.at[:, block_rows(mate[0])]
        return remote(src, back.at[seq], out_send.at[mate[0]], out_recv.at[seq], mate)

    def own_done(chunk):
        rows = block_rows(chunk)
        low[0, rows, :] = (grad_q[rows, :] * scale).astype(jnp.bfloat16)

        @pl.when(slot == 0)
        def _():
            x_wait(chunk)
            z_wait(chunk)
            low[1, rows, :], low[2, rows, :] = rounded(0, chunk, [kv_in0[:, rows, :], kv_in1[:, rows, :]])

        @pl.when(slot == 1)
        def _():
            z_wait(chunk)
            low[1, rows, :], low[2, rows, :] = rounded(0, chunk, [kv_in1[:, rows, :]])

        @pl.when(slot >= 2)
        def _():
            low[1, rows, :], low[2, rows, :] = rounded(0, chunk, [])

    events = {}
    for chunk in range(4):
        events.setdefault(2 * chunk + 2, []).append(functools.partial(first_done, chunk))
        events.setdefault(10 + 2 * chunk, []).append(functools.partial(second_done, chunk))
    begin, ready, first, hop, lag = steps
    rest = []
    for t in range(T):
        plan = [(begin, functools.partial(ring.start, t)), (ready, functools.partial(ring.all_ready, t))]
        when = first + lag * t
        for D in range(ring.far, -1, -1):
            plan.append((when, functools.partial(ring.step, t, D)))
            when += hop
        plan.append((when, functools.partial(ring.deliver, t)))
        plan.append((when + hop, functools.partial(ring.finish, t)))
        for when, event in plan:
            if when < 32:
                events.setdefault(int(when), []).append(event)
            else:
                rest.append((when, event))
    rest = [event for when, event in sorted(rest, key=lambda pair: pair[0])]

    def step_body(step, carry):
        for when, actions in sorted(events.items()):
            @pl.when(step == when)
            def _():
                for action in actions:
                    action()
        pl.when(step < 16)(lambda: far_tile(step))
        pl.when(step >= 16)(lambda: near_tile(step - 16))
        return carry

    lax.fori_loop(0, 32, step_body, 0)
    for chunk in range(4):
        own_done(chunk)
    for mate in mates[1:] + mates[:1]:
        out_copy(mate).start()
    own_out = pltpu.make_async_copy(low.at[:, mine], back.at[seq], here.at[1])
    own_out.start()
    for event in rest:
        event()
    own_out.wait()
    for mate in mates:
        in_copy(mate).wait_send()
        out_copy(mate).wait_send()
        ref = back.at[mate[0]]
        remote(ref, ref, out_send.at[mate[0]], out_recv.at[mate[0]], mate).wait_recv()
    for chunk in range(4):
        @pl.when(slot >= 1)
        def _():
            x_send(chunk).wait_send()

        @pl.when(slot >= 2)
        def _():
            z_send(chunk).wait_send()


def retreat(count, grad_att, turned, store, outputs, logs, part, splits, steps=(0, 1, 2, 3, 1)):
    rows = grad_att.shape[1]
    own = 4 * rows
    _, shard_rows, half = part.shape
    return pl.pallas_call(
        functools.partial(retreat_kernel, count, splits, steps),
        out_shape=[jax.ShapeDtypeStruct((HEADS, 3, rows, LANES), jnp.bfloat16), jax.ShapeDtypeStruct((shard_rows, 2 * half), jnp.float32)],
        in_specs=[VMEM] * 5 + [ANY],
        out_specs=[VMEM, ANY],
        scratch_shapes=[
            pltpu.VMEM((own, LANES), jnp.bfloat16),
            pltpu.VMEM((8, own), jnp.float32),
            pltpu.VMEM((own, LANES), jnp.float32),
            pltpu.VMEM((3, 2, own, LANES), jnp.float32),
            pltpu.VMEM((2, 2, own, LANES), jnp.bfloat16),
            pltpu.VMEM((2, own, LANES), jnp.bfloat16),
            pltpu.VMEM((2, own, LANES), jnp.bfloat16),
            pltpu.VMEM((3, own, LANES), jnp.bfloat16),
            DMA((4,)), DMA((4,)), DMA((8,)), DMA((8,)), DMA((4,)), DMA((4,)), DMA((2,)),
        ]
        + Scatter.scratch(count, splits, [shard_rows] * len(splits)),
        compiler_params=pltpu.CompilerParams(collective_id=3, has_side_effects=True, vmem_limit_bytes=60 << 20),
    )(grad_att, turned, store, outputs, logs, part)


CHUNK = 512


def gelu_pair(v):
    root = 0.7978845608028654
    square = v * v
    t = jnp.tanh(root * (v + 0.044715 * square * v))
    up = 0.5 * (1.0 + t)
    return v * up, up + 0.5 * v * (1.0 - t * t) * (root * (1.0 + 3.0 * 0.044715 * square))


def contract(left, right, left_axis, right_axis):
    return lax.dot_general(left, right, (((left_axis,), (right_axis,)), ((), ())), preferred_element_type=jnp.float32)


def feed_kernel(count, att, gates, tokens, cotangent, norms, output_w, inner_w, outer_w,
                layer_out, grad_residual, grad_att, grad_logit, grad_norms, part_output, part_inner, outer_out,
                w_out, w_in, w_up, acts, act_in, slopes, slope_in, scaled, scaled_in, scaled_t, cot_in, cot_t,
                acc, normed, grad_scaled, branch_low, branch_in, branch_t, att_in, gates_in,
                stage_inner, stage_output,
                load_out, load_in, load_up, pair_s, pair_r, act_s, act_r, slope_s, slope_r, put_inner, put_output, *refs):
    half = cotangent.shape[1] // 2
    ring = Scatter(count, (SPLITS["outer"],), [None], [(outer_out, half, 0)], refs[:7], refs[7:])
    core, mate = ring.core, ring.core_mate
    experts = HEADS * EXP
    chunks = inner_w.shape[1] // CHUNK
    small = CHUNK // 2
    shards = max(1, count // chunks)

    def out_load(e):
        return pltpu.make_async_copy(output_w.at[pl.ds(e * DH, DH)], w_out.at[e, pl.ds(0, DH)], load_out.at[e])

    def ffn_load(chunk, slot):
        cols = pl.ds(pl.multiple_of(chunk * CHUNK, CHUNK), CHUNK)
        return (pltpu.make_async_copy(inner_w.at[:, cols], w_in.at[slot], load_in.at[slot]),
                pltpu.make_async_copy(outer_w.at[cols], w_up.at[slot], load_up.at[slot]))

    def chunk_of(step):
        if count != chunks:
            return step
        D = ring.far - (step + 1) // 2
        odd = step % 2
        return ring.dest((odd * D + (1 - odd) * (count - D)) % count)

    for e in range(experts):
        out_load(e).start()
    for sub in range(2):
        for copy in ffn_load(chunk_of(sub), sub):
            copy.start()
    enter(ring.neighbours())

    def remote(src, dst, send, recv):
        return pltpu.make_async_remote_copy(src, dst, send, recv, device_id=mate, device_id_type=MESH)

    mine = pl.ds(pl.multiple_of(core * half, LANES), half)
    yours = pl.ds(pl.multiple_of((1 - core) * half, LANES), half)
    pair = [
        remote(att, att_in, pair_s.at[0], pair_r.at[0]),
        remote(gates.at[0], gates_in, pair_s.at[1], pair_r.at[1]),
        remote(cotangent.at[:, yours], cot_in, pair_s.at[2], pair_r.at[2]),
        remote(scaled, scaled_in, pair_s.at[3], pair_r.at[3]),
        remote(branch_low.at[:, yours], branch_in, pair_s.at[4], pair_r.at[4]),
    ]
    for copy in pair[:3]:
        copy.start()

    def mixed_pair(att_ref, gate, two):
        tiles = []
        for which in (2 * two, 2 * two + 1):
            column = gate[:, experts + which : experts + which + 1]
            tiles.append((att_ref[which // EXP].astype(jnp.float32) * column).astype(jnp.bfloat16))
        return jnp.concatenate(tiles, axis=1)

    w_out[:, DH:, :] = jnp.zeros((experts, LANES - DH, w_out.shape[2]), jnp.bfloat16)
    acc[...] = tokens[...].astype(jnp.float32)
    for two in range(experts // 2):
        out_load(2 * two).wait()
        out_load(2 * two + 1).wait()
        weights = w_out[2 * two : 2 * two + 2].reshape(2 * LANES, w_out.shape[2])
        acc[...] += jnp.dot(mixed_pair(att, gates.at[0], two), weights, preferred_element_type=jnp.float32)
    residual = acc[...]
    centred = residual - jnp.mean(residual, axis=1, keepdims=True)
    inverse = lax.rsqrt(jnp.mean(centred * centred, axis=1, keepdims=True) + EPSILON)
    normed[...] = centred * inverse
    scaled[...] = (normed[...] * norms[:1] + norms[1:2]).astype(jnp.bfloat16)
    pair[3].start()
    rows = tokens.shape[0]
    scaled_t[:, :rows] = scaled[...].T
    cot_t[:, :rows] = cotangent[:, mine].T
    grad_scaled[...] = jnp.zeros_like(grad_scaled)
    pair[2].wait_recv()
    cot_t[:, rows:] = cot_in[...].T
    pair[3].wait_recv()
    scaled_t[:, rows:] = scaled_in[...].T

    small_mine = pl.ds(pl.multiple_of(core * small, LANES), small)
    small_yours = pl.ds(pl.multiple_of((1 - core) * small, LANES), small)

    def act_copy(step, sub):
        return remote(acts.at[sub], act_in.at[step], act_s.at[sub], act_r.at[step])

    def slope_copy(step, sub):
        return remote(slopes.at[sub, :, small_yours], slope_in.at[step], slope_s.at[sub], slope_r.at[step])

    def put_inner_copy(step, sub):
        cols = pl.ds(pl.multiple_of(chunk_of(step) * small, small), small)
        return pltpu.make_async_copy(stage_inner.at[sub], part_inner.at[:, cols], put_inner.at[sub])

    def forward_backward(step, sub):
        for copy in ffn_load(chunk_of(step), sub):
            copy.wait()

        @pl.when(step > 1)
        def _():
            act_copy(step, sub).wait_send()
            slope_copy(step, sub).wait_send()

        act, slope = gelu_pair(jnp.dot(scaled[...], w_in[sub], preferred_element_type=jnp.float32))
        acts[sub] = act.astype(jnp.bfloat16)
        act_copy(step, sub).start()
        slopes[sub] = (contract(cotangent[...], w_up[sub], 1, 1) * slope).astype(jnp.bfloat16)
        slope_copy(step, sub).start()
        acc[...] += jnp.dot(acts[sub], w_up[sub], preferred_element_type=jnp.float32)
        grad_scaled[...] += contract(slopes[sub], w_in[sub], 1, 1)

        @pl.when(step + 2 < chunks)
        def _():
            for copy in ffn_load(chunk_of(step + 2), sub):
                copy.start()

    def weight_parts(step, sub):
        remote(act_in.at[step], act_in.at[step], act_s.at[sub], act_r.at[step]).wait_recv()
        total = jnp.dot(cot_t[:, :rows], acts[sub], preferred_element_type=jnp.float32)
        total = total + jnp.dot(cot_t[:, rows:], act_in[step], preferred_element_type=jnp.float32)
        turned = total.astype(jnp.bfloat16).T
        shard_rows = CHUNK // shards
        for q in range(shards):
            rel = (ring_place(chunk_of(step) * shards + q, count) - ring.place + count) % count
            ring.mine[0][rel] = turned[q * shard_rows : (q + 1) * shard_rows]
        remote(slope_in.at[step], slope_in.at[step], slope_s.at[sub], slope_r.at[step]).wait_recv()

        @pl.when(step > 1)
        def _():
            put_inner_copy(step, sub).wait()

        total = jnp.dot(scaled_t[:, :rows], slopes[sub, :, small_mine], preferred_element_type=jnp.float32)
        total = total + jnp.dot(scaled_t[:, rows:], slope_in[step], preferred_element_type=jnp.float32)
        stage_inner[sub] = total.astype(jnp.bfloat16)
        put_inner_copy(step, sub).start()

    events = {}
    if count == chunks:
        for step, rel in enumerate(ring.order()):
            events.setdefault(step, []).append(functools.partial(ring.ready, 0, rel))
        for D in range(ring.far, 0, -1):
            events.setdefault(2 * (ring.far - D) + 1, []).append(functools.partial(ring.step, 0, D))

    def after_parts(step):
        for when, actions in sorted(events.items()):
            @pl.when(step == when)
            def _():
                for action in actions:
                    action()

    def iteration(i, carry):
        forward_backward(2 * i, 0)

        @pl.when(i > 0)
        def _():
            weight_parts(2 * i - 1, 1)
            after_parts(2 * i - 1)

        forward_backward(2 * i + 1, 1)
        weight_parts(2 * i, 0)
        after_parts(2 * i)
        return carry

    lax.fori_loop(0, chunks // 2, iteration, 0)
    weight_parts(chunks - 1, 1)
    if count == chunks:
        for action in events[chunks - 1]:
            action()
    else:
        ring.all_ready(0)
        for D in range(ring.far, 0, -1):
            ring.step(0, D)
    layer_out[...] = acc[...].astype(jnp.bfloat16)
    slope = grad_scaled[...]
    grad_norms[...] = jnp.concatenate(
        [jnp.sum(slope * normed[...], axis=0, keepdims=True), jnp.sum(slope, axis=0, keepdims=True),
         jnp.zeros((6, slope.shape[1]), jnp.float32)], axis=0)
    slope = slope * norms[:1]
    total = cotangent[...].astype(jnp.float32) + inverse * (
        slope - jnp.mean(slope, axis=1, keepdims=True)
        - normed[...] * jnp.mean(slope * normed[...], axis=1, keepdims=True))
    grad_residual[...] = total
    branch_low[...] = total.astype(jnp.bfloat16)
    pair[4].start()
    branch_t[:, :rows] = branch_low[:, mine].T
    ring.step(0, 0)
    lane = lax.broadcasted_iota(jnp.int32, (rows, LANES), 1)
    logit = jnp.zeros((rows, LANES), jnp.float32)
    head_total = None
    for which in range(experts):
        if which % 2 == 0:
            weights = w_out[which : which + 2].reshape(2 * LANES, w_out.shape[2])
            both = contract(branch_low[...], weights, 1, 1)
        grad_mixed = both[:, which % 2 * LANES : (which % 2 + 1) * LANES]
        head, expert = which // EXP, which % EXP
        column = slice(experts + which, experts + which + 1)
        term = grad_mixed * gates[0, :, column]
        head_total = term if expert == 0 else head_total + term
        if expert == EXP - 1:
            grad_att[head] = head_total.astype(jnp.bfloat16)
        sums = jnp.sum(grad_mixed * att[head].astype(jnp.float32), axis=1, keepdims=True)
        logit = jnp.where(lane == experts + which, sums, logit)
    grad_logit[...] = logit * gates[1]
    ring.deliver(0)
    pair[0].wait_recv()
    pair[1].wait_recv()
    pair[4].wait_recv()
    branch_t[:, rows:] = branch_in[...].T

    def put_output_copy(which):
        return pltpu.make_async_copy(stage_output.at[which % 4, pl.ds(0, DH)], part_output.at[pl.ds(which * DH, DH)], put_output.at[which % 4])

    for two in range(experts // 2):
        total = jnp.dot(branch_t[:, :rows], mixed_pair(att, gates.at[0], two), preferred_element_type=jnp.float32)
        total = total + jnp.dot(branch_t[:, rows:], mixed_pair(att_in, gates_in, two), preferred_element_type=jnp.float32)
        turned = total.astype(jnp.bfloat16).T
        for side in range(2):
            which = 2 * two + side
            if which >= 4:
                put_output_copy(which - 4).wait()
            stage_output[which % 4] = turned[side * LANES : (side + 1) * LANES]
            put_output_copy(which).start()
    for which in range(experts - 4, experts):
        put_output_copy(which).wait()
    for sub in range(2):
        put_inner_copy(sub, sub).wait()
        act_copy(sub, sub).wait_send()
        slope_copy(sub, sub).wait_send()
    ring.finish(0)
    for copy in pair:
        copy.wait_send()


def feed(count, att, gates, tokens, cotangent, norms, output_w, inner_w, outer_w):
    rows, width = tokens.shape
    wide = inner_w.shape[1]
    half = width // 2
    f32, bf = jnp.float32, jnp.bfloat16
    experts, chunks = HEADS * EXP, wide // CHUNK
    V = pltpu.VMEM
    return pl.pallas_call(
        functools.partial(feed_kernel, count),
        out_shape=[
            jax.ShapeDtypeStruct((rows, width), bf),
            jax.ShapeDtypeStruct((rows, width), f32),
            jax.ShapeDtypeStruct((HEADS, rows, LANES), bf),
            jax.ShapeDtypeStruct((rows, LANES), f32),
            jax.ShapeDtypeStruct((8, width), f32),
            jax.ShapeDtypeStruct((VCOLS, half), bf),
            jax.ShapeDtypeStruct((width, wide // 2), bf),
            jax.ShapeDtypeStruct((wide // count, width), f32),
        ],
        in_specs=[VMEM] * 5 + [ANY] * 3,
        out_specs=[VMEM] * 5 + [ANY] * 3,
        scratch_shapes=[
            V((experts, LANES, width), bf), V((2, width, CHUNK), bf), V((2, CHUNK, width), bf),
            V((2, rows, CHUNK), bf), V((chunks, rows, CHUNK), bf), V((2, rows, CHUNK), bf), V((chunks, rows, CHUNK // 2), bf),
            V((rows, width), bf), V((rows, width), bf), V((width, 2 * rows), bf), V((rows, half), bf), V((half, 2 * rows), bf),
            V((rows, width), f32), V((rows, width), f32), V((rows, width), f32),
            V((rows, width), bf), V((rows, half), bf), V((half, 2 * rows), bf), V((HEADS, rows, LANES), bf), V((rows, LANES), f32),
            V((2, width, CHUNK // 2), bf), V((4, LANES, half), bf),
            DMA((experts,)), DMA((2,)), DMA((2,)), DMA((5,)), DMA((5,)), DMA((2,)), DMA((chunks,)), DMA((2,)), DMA((chunks,)),
            DMA((2,)), DMA((4,)),
        ]
        + Scatter.scratch(count, (SPLITS["outer"],), [wide // count]),
        compiler_params=pltpu.CompilerParams(collective_id=4, has_side_effects=True, vmem_limit_bytes=63 << 20),
    )(att, gates, tokens, cotangent, norms, output_w, inner_w, outer_w)


def settle_kernel(count, back, experts, gates, grad_logit, tokens, joint, grad_residual, grad_norms, part_output,
                  grad_tokens, joint_out, output_out, grads, grads_in, tokens_in, tokens_t, norms_in, norm_columns, *refs):
    splits = (SPLITS["joint"], SPLITS["output"])
    pair_s, pair_r = refs[-2:]
    half, output_half = JOINT // 2, part_output.shape[2]
    outs = [(joint_out, half, 0), (output_out, output_half, 0)]
    ring = Scatter(count, splits, [None, (part_output, 0)], outs, refs[:14], refs[14:-2])
    ring.start(1)
    enter(ring.neighbours())
    core = ring.core

    def remote(src, dst, i):
        return pltpu.make_async_remote_copy(src, dst, pair_s.at[i], pair_r.at[i], device_id=ring.core_mate, device_id_type=MESH)

    mine = pl.ds(pl.multiple_of(core * half, LANES), half)
    yours = pl.ds(pl.multiple_of((1 - core) * half, LANES), half)
    pair = [remote(tokens, tokens_in, 0), remote(grad_norms, norms_in, 1), remote(grads.at[:, yours], grads_in, 2)]
    pair[0].start()
    pair[1].start()
    ring.all_ready(1)
    rows = tokens.shape[0]
    lane = lax.broadcasted_iota(jnp.int32, (LANES, LANES), 1)
    width = HEADS * EXP

    def assemble(block, carry):
        part = pl.ds(pl.multiple_of(block * LANES, LANES), LANES)
        pieces = [back[head, which, part, :][:, :DH].astype(jnp.float32) for which in range(2) for head in range(HEADS)]
        logit = grad_logit[part, :]
        for head in range(HEADS):
            values = back[head, 2, part, :].astype(jnp.float32)
            for expert in range(EXP):
                which = head * EXP + expert
                pieces.append((values * gates[0, part, which : which + 1])[:, :DH])
                sums = jnp.sum(values * experts[which, part, :].astype(jnp.float32), axis=1, keepdims=True)
                logit = jnp.where(lane == which, sums * gates[1, part, which : which + 1], logit)
        pieces.append(jnp.where(lane < 2 * width, logit, 0.0))
        pieces.append(jnp.zeros((LANES, JOINT - ROUTERS - LANES), jnp.float32))
        grads[part, :] = jnp.concatenate(pieces, axis=1).astype(jnp.bfloat16)
        return carry

    lax.fori_loop(0, rows // LANES, assemble, 0)
    pair[2].start()
    ring.step(1, ring.far)
    tokens_t[:, :rows] = tokens[...].T
    for copy in pair[:2]:
        copy.wait_recv()
    tokens_t[:, rows:] = tokens_in[...].T
    norm_tile = NORM // LANES * LANES - half
    first = NORM - half - norm_tile
    both = grad_norms[...] + norms_in[...]
    for block in range(both.shape[1] // LANES):
        columns = jnp.concatenate([both[:, block * LANES : (block + 1) * LANES], jnp.zeros((LANES - 8, LANES), jnp.float32)], axis=0)
        norm_columns[block * LANES : (block + 1) * LANES, :] = columns.T
    pair[2].wait_recv()
    shard_rows = tokens_t.shape[0] // count
    tile_lane = lax.broadcasted_iota(jnp.int32, (shard_rows, LANES), 1)

    def fill(rel):
        part = pl.ds(pl.multiple_of(ring.dest(rel) * shard_rows, shard_rows), shard_rows)
        total = jnp.dot(tokens_t[part, :rows], grads[:, mine], preferred_element_type=jnp.float32)
        total = total + jnp.dot(tokens_t[part, rows:], grads_in[...], preferred_element_type=jnp.float32)
        ring.mine[0][rel] = total.astype(jnp.bfloat16)
        extra = jnp.where(tile_lane == first, norm_columns[part, 0:1], 0.0) + jnp.where(tile_lane == first + 1, norm_columns[part, 1:2], 0.0)
        tile = total[:, norm_tile : norm_tile + LANES] + extra * core.astype(jnp.float32)
        ring.mine[0][rel, :, norm_tile : norm_tile + LANES] = tile.astype(jnp.bfloat16)

    for rel in ring.order():
        fill(rel)
        ring.ready(0, rel)
    ring.step(0, ring.far)
    for D in range(ring.far - 1, 0, -1):
        ring.step(1, D)
        ring.step(0, D)
        if D == ring.far - 1:
            grad_tokens[...] = grad_residual[...] + contract(grads[...], joint[...], 1, 1)
    ring.step(1, 0)
    ring.step(0, 0)
    ring.deliver(1)
    ring.deliver(0)
    ring.finish(1)
    ring.finish(0)
    for copy in pair:
        copy.wait_send()


def settle(count, back, experts, gates, grad_logit, tokens, joint, grad_residual, grad_norms, part_output):
    rows, width = tokens.shape
    shard_rows = width // count
    f32, bf = jnp.float32, jnp.bfloat16
    V = pltpu.VMEM
    return pl.pallas_call(
        functools.partial(settle_kernel, count),
        out_shape=[jax.ShapeDtypeStruct((rows, width), f32), jax.ShapeDtypeStruct((shard_rows, JOINT), f32),
                   jax.ShapeDtypeStruct((part_output.shape[1], width), f32)],
        in_specs=[VMEM] * 8 + [ANY],
        out_specs=[VMEM, VMEM, ANY],
        scratch_shapes=[V((rows, JOINT), bf), V((rows, JOINT // 2), bf), V((rows, width), bf), V((width, 2 * rows), bf), V((8, width), f32), V((width, LANES), f32)]
        + Scatter.scratch(count, (SPLITS["joint"], SPLITS["output"]), [shard_rows, part_output.shape[1]])
        + [DMA((3,)), DMA((3,))],
        compiler_params=pltpu.CompilerParams(collective_id=5, has_side_effects=True, vmem_limit_bytes=60 << 20),
    )(back, experts, gates, grad_logit, tokens, joint, grad_residual, grad_norms, part_output)


def publish_kernel(joint_w, output_w, inner_w, outer_w, layer, tokens_in,
                   query, key, value, value_router, output_router, norms, output_out, inner_out, outer_out, layer_out, tokens_out,
                   *refs):
    held, parts, load, store = refs[:6], refs[6:-2], refs[-2], refs[-1]
    sources = (joint_w, tokens_in, inner_w, outer_w, layer, output_w)
    loads = [pltpu.make_async_copy(src, buf, load.at[i]) for i, (src, buf) in enumerate(zip(sources, held))]
    for copy in loads:
        copy.start()
    half, small = inner_w.shape[1] // 2, CHUNK // 2
    stores = []

    def put(src, dst):
        copy = pltpu.make_async_copy(src, dst, store.at[len(stores)])
        copy.start()
        stores.append(copy)

    loads[0].wait()
    spots = [(0, QCOLS), (QCOLS, QCOLS), (2 * QCOLS, VCOLS), (ROUTERS, HEADS * EXP), (ROUTERS + HEADS * EXP, HEADS * EXP)]
    for (first, size), part, target in zip(spots, parts, (query, key, value, value_router, output_router)):
        part[...] = held[0][:, first : first + size]
        put(part, target)
    norm_tile = NORM // LANES * LANES
    norms[...] = held[0][:, norm_tile : norm_tile + LANES].T[NORM - norm_tile : NORM - norm_tile + 8]
    for i, target in enumerate((tokens_out, inner_out, outer_out, layer_out, output_out)):
        loads[1 + i].wait()
        if i != 1:
            put(held[1 + i], target)
            continue
        for core in range(2):
            for chunk in range(half // small):
                put(held[1 + i].at[:, pl.ds(core * half + chunk * small, small)], target.at[:, pl.ds(chunk * CHUNK + core * small, small)])
    for copy in stores:
        copy.wait()


def publish(joint_w, output_w, inner_w, outer_w, layer, tokens):
    rows = joint_w.shape[0]
    f32 = jnp.float32
    columns = [QCOLS, QCOLS, VCOLS, HEADS * EXP, HEADS * EXP]
    rest = (output_w, inner_w, outer_w, layer, tokens)
    return pl.pallas_call(
        publish_kernel,
        out_shape=[jax.ShapeDtypeStruct((rows, c), f32) for c in columns] + [jax.ShapeDtypeStruct((8, rows), f32)]
        + [jax.ShapeDtypeStruct(x.shape, x.dtype) for x in rest],
        in_specs=[ANY] * 6,
        out_specs=[ANY] * 5 + [VMEM] + [ANY] * 5,
        scratch_shapes=[pltpu.VMEM(x.shape, x.dtype) for x in (joint_w, tokens, inner_w, outer_w, layer, output_w)]
        + [pltpu.VMEM((rows, c), f32) for c in columns]
        + [DMA((6,)), DMA((9 + inner_w.shape[1] // (CHUNK // 2),))],
        compiler_params=pltpu.CompilerParams(vmem_limit_bytes=63 << 20),
    )(joint_w, *rest)


def on_device(
    tokens, value_routes, output_routes, cont_gap, query_weight, key_weight, value_weight, value_router,
    output_router, output_weight, norm_gain, norm_bias, inner_weight, outer_weight, cotangent,
):
    count = lax.axis_size("fsdp")
    inputs = tokens[0]
    rows, width = inputs.shape
    norm = jnp.stack([norm_gain, norm_bias])
    routes = jnp.concatenate([value_routes[0].reshape(rows, -1), output_routes[0].reshape(rows, -1)], axis=1)
    joint, output_full, qkv, experts, gates, norms, tables, turned = project(
        count, query_weight, key_weight, value_weight, value_router, output_router, norm, inputs, routes, output_weight, cont_gap)
    att, store, outputs, logs, inner_full, outer_full = attend(
        count, qkv, tables, (inner_weight, outer_weight), (SPLITS["inner"], SPLITS["outer"]))
    layer, grad_residual, grad_att, grad_logit, grad_norms, part_output, part_inner, outer_w = feed(
        count, att, gates, inputs, cotangent[0], norms, output_full.reshape(VCOLS, width), inner_full.reshape(width, -1),
        outer_full.reshape(-1, width))
    back, inner_w = retreat(
        count, grad_att, turned, store, outputs, logs, part_inner.reshape(count, -1, part_inner.shape[1]), INNER_PARTS)
    grad_input, joint_w, output_w = settle(
        count, back, experts, gates, grad_logit, inputs, joint, grad_residual, grad_norms,
        part_output.reshape(count, -1, part_output.shape[1]))
    query, key, value, value_r, output_r, norm_w, output_w, inner_w, outer_w, layer, grad_input = publish(
        joint_w, output_w, inner_w, outer_w, layer, grad_input)
    return (layer[None], grad_input[None], query, key, value, value_r, output_r, output_w, norm_w[0], norm_w[1], inner_w, outer_w)


def solution(mesh):
    wide = P("fsdp", None)
    part = P("fsdp", "seq", None)
    routes = P("fsdp", "seq", None, None)
    return jax.shard_map(
        on_device,
        mesh=mesh,
        in_specs=(part, routes, routes, P()) + (wide,) * 6 + (P("fsdp"), P("fsdp"), wide, wide, part),
        out_specs=(part, part) + (wide,) * 6 + (P("fsdp"), P("fsdp"), wide, wide),
        check_vma=False,
    )
```

```python
import functools
import jax
import jax.numpy as jnp
from jax import lax
from jax.experimental import pallas as pl
from jax.experimental.pallas import tpu as pltpu
from jax.sharding import PartitionSpec as P

HEADS = 4
DH = 112
EXP = 5
CONT = 1024
GSLOTS = 4
PSLOTS = 2
BLOCK = 512
LANES = 128
EPSILON = 1e-05
NEGATIVE = -1e30
LOG2E = 1.4426950408889634
MESH = pl.DeviceIdType.MESH
ANY = pl.BlockSpec(memory_space=pl.ANY)
VMEM = pl.BlockSpec(memory_space=pltpu.VMEM)
SMEM = pl.BlockSpec(memory_space=pltpu.SMEM)
DMA = pltpu.SemaphoreType.DMA

QCOLS = HEADS * DH
VCOLS = HEADS * EXP * DH
ROUTERS = 2 * QCOLS + VCOLS
NORM = ROUTERS + 2 * HEADS * EXP
JOINT = 3328
SPLITS = {"joint": (640, 512), "output": (256, 128), "inner": (768, 640), "outer": (256, 128)}
INNER_PARTS = ((512, 768),)


def ring_place(index, count):
    return (index // 2) * (1 - index % 2) + (count - 1 - index // 2) * (index % 2)


def ring_index(place, count):
    upper = place // (count // 2)
    return 2 * place * (1 - upper) + (2 * (count - 1 - place) + 1) * upper


def enter(devices):
    barrier = pltpu.get_barrier_semaphore()
    for device in devices:
        pl.semaphore_signal(barrier, inc=1, device_id=device, device_id_type=MESH)
    pl.semaphore_wait(barrier, len(devices))


class Ring:
    def __init__(self, count, splits):
        self.count, self.splits = count, splits
        self.seq, self.fsdp = lax.axis_index("seq"), lax.axis_index("fsdp")
        self.plane, self.core = self.seq // 2, self.seq % 2
        self.place = ring_place(self.fsdp, count)
        self.right = (self.seq, ring_index((self.place + 1) % count, count))
        self.left = (self.seq, ring_index((self.place + count - 1) % count, count))
        self.core_mate = (self.seq + 1 - 2 * self.core, self.fsdp)
        self.plane_mate = ((self.seq + 2) % 4, self.fsdp)
        self.far = count // 2

    def neighbours(self):
        return [self.right, self.left, self.core_mate, self.plane_mate]

    def reach(self, kind, way):
        return self.far if kind == way else self.count - 1 - self.far

    def kinds(self, t):
        return [kind for kind in (1, 0) if self.splits[t][kind] > 0]

    def half(self, t):
        return self.splits[t][0] + 2 * self.splits[t][1]

    def cols(self, t, kind, plane, core):
        both, single = self.splits[t]
        if kind == 0:
            return pl.ds(pl.multiple_of(core * self.half(t), LANES), both)
        return pl.ds(pl.multiple_of(core * self.half(t) + both + plane * single, LANES), single)

    def behind(self, way, k):
        step = self.count - k if way == 0 else k
        return ring_index((self.place + step) % self.count, self.count)

    def next(self, way):
        return self.right if way == 0 else self.left

    def slot(self, kind, way, k):
        return k - 1 if way == 0 else self.reach(kind, 0) + k - 1


class Gather(Ring):
    def __init__(self, count, splits, shards, at, send, recv, local):
        super().__init__(count, splits)
        self.shards, self.at, self.send, self.recv, self.local = shards, at, send, recv, local

    @staticmethod
    def sems(count, tensors):
        return [DMA((6 * tensors * (count - 1),)), DMA((6 * tensors * (count - 1),)), DMA((tensors,))]

    def copy(self, src, dst, group, t, slot, device):
        i = (group * len(self.splits) + t) * (self.count - 1) + slot
        return pltpu.make_async_remote_copy(
            src, dst, self.send.at[i], self.recv.at[i], device_id=device, device_id_type=MESH
        )

    def same(self, group, t, kind, way, k, plane, core, device):
        ref = self.at(t, self.behind(way, k), self.cols(t, kind, plane, core))
        return self.copy(ref, ref, group, t, self.slot(kind, way, k), device)

    def hop(self, t, kind, way, k):
        if k > 1:
            ref = self.at(t, self.behind(way, k - 1), self.cols(t, kind, self.plane, self.core))
            return self.copy(ref, ref, kind, t, self.slot(kind, way, k), self.next(way))
        cols = self.cols(t, kind, self.plane, self.core)
        return self.copy(
            self.shards[t].at[:, cols], self.at(t, self.fsdp, cols), kind, t, self.slot(kind, way, 1), self.next(way)
        )

    def arrived(self, t, kind, way, k):
        return self.same(kind, t, kind, way, k, self.plane, self.core, self.next(way))

    def to_core(self, t, kind, way, k, core):
        return self.same(2 + kind, t, kind, way, k, self.plane, core, self.core_mate)

    def to_plane(self, t, way, k, plane):
        return self.same(4, t, 1, way, k, plane, self.core, self.plane_mate)

    def plane_to_core(self, t, way, k, core):
        return self.same(5, t, 1, way, k, 1 - self.plane, core, self.core_mate)

    def own(self, t):
        return pltpu.make_async_copy(self.shards[t], self.at(t, self.fsdp, slice(None)), self.local.at[t])

    def start(self, t):
        for kind in self.kinds(t):
            for way in (0, 1):
                if self.reach(kind, way):
                    self.hop(t, kind, way, 1).start()
        self.own(t).start()

    def arrive(self, t, k):
        for kind in self.kinds(t):
            for way in (0, 1):
                if k <= self.reach(kind, way):
                    self.arrived(t, kind, way, k).wait_recv()
                    if k < self.reach(kind, way):
                        self.hop(t, kind, way, k + 1).start()
                    if kind:
                        self.to_plane(t, way, k, self.plane).start()
                    self.to_core(t, kind, way, k, self.core).start()

    def plane_arrive(self, t, k):
        if 1 in self.kinds(t):
            for way in (0, 1):
                if k <= self.reach(1, way):
                    self.to_plane(t, way, k, 1 - self.plane).wait_recv()
                    self.plane_to_core(t, way, k, self.core).start()

    def finish(self, t):
        self.own(t).wait()
        for kind in self.kinds(t):
            for way in (0, 1):
                for k in range(1, self.reach(kind, way) + 1):
                    self.hop(t, kind, way, k).wait_send()
                    self.to_core(t, kind, way, k, self.core).wait_send()
                    self.to_core(t, kind, way, k, 1 - self.core).wait_recv()
                    if kind:
                        self.to_plane(t, way, k, self.plane).wait_send()
                        self.plane_to_core(t, way, k, self.core).wait_send()
                        self.plane_to_core(t, way, k, 1 - self.core).wait_recv()

    def events(self):
        tensors = range(len(self.splits))
        out = []
        for k in range(1, self.far + 1):
            for t in tensors:
                out.append(functools.partial(self.arrive, t, k))
                if k > 1:
                    out.append(functools.partial(self.plane_arrive, t, k - 1))
        for t in tensors:
            out.append(functools.partial(self.plane_arrive, t, self.far))
        for t in tensors:
            out.append(functools.partial(self.finish, t))
        return out


TABLE = 5632
TABLE_ZERO = 5120
TURNED_ZERO = 512


def route_lanes(routes, lane):
    hit = None
    for head in range(2 * HEADS):
        for choice in range(2):
            place = head * EXP + routes[:, 2 * head + choice : 2 * head + choice + 1]
            here = lane == place
            hit = here if hit is None else hit | here
    return hit.astype(jnp.float32)


def project_kernel(count, query, key, value, value_router, output_router, norm, tokens, routes, gaps,
                   joint_out, tables_out, turned_out, qkv, experts, gates, norms,
                   shard, shard_t, joint, tables, turned_tables, product, load, store, send, recv, local):
    rows = shard.shape[0]
    splits = (SPLITS["joint"],)
    at = lambda t, g, cols: joint.at[pl.ds(pl.multiple_of(g * rows, rows), rows), cols]
    ring = Gather(count, splits, [shard], at, send, recv, local)
    loads = []
    for i, (src, first) in enumerate(((query, 0), (key, QCOLS), (value, 2 * QCOLS))):
        loads.append(pltpu.make_async_copy(src, shard_t.at[pl.ds(first, src.shape[0])], load.at[i]))
        loads[-1].start()
    small = [ref[...].astype(jnp.float32) for ref in (value_router, output_router, norm)]
    small.append(jnp.zeros((JOINT - NORM - 2, rows), jnp.float32))
    shard_t[ROUTERS:, :] = jnp.concatenate(small, axis=0).astype(jnp.bfloat16)
    for copy in loads:
        copy.wait()
    shard[...] = shard_t[...].T
    enter(ring.neighbours())
    ring.start(0)
    slope = jnp.float32(0.0)
    for head in range(HEADS):
        slope = jnp.where(ring.seq // 1 == head, -0.5 * 0.5**head * LOG2E, slope)
    group = ring.fsdp // GSLOTS
    pair = jnp.maximum(ring.fsdp % GSLOTS - PSLOTS, 0) * 2
    gap_values = [jnp.int32(0), gaps[group, pair], gaps[group, pair + 1]]

    def table_column(step, carry):
        start = pl.multiple_of(step * 256, 256)
        lanes = lax.broadcasted_iota(jnp.int32, (8, 256 + LANES), 1) + (start - LANES)
        for which in range(3):
            for turned in range(2):
                if turned:
                    distance = lanes - TURNED_ZERO + gap_values[which]
                else:
                    distance = TABLE_ZERO - lanes + gap_values[which]
                bias = slope * jnp.log(1.0 + jnp.maximum(distance, 0).astype(jnp.float32))
                bias = jnp.where(distance >= 0, bias, NEGATIVE)
                wide = jnp.broadcast_to(bias[:1], (LANES, 256 + LANES))
                rolled = pltpu.roll(wide, 0, 1, stride=1, stride_axis=0)
                target = turned_tables if turned else tables
                target[which, :, pl.ds(start, 256)] = rolled[:, LANES:]
        return carry

    events = []
    for k in range(1, ring.far + 1):
        events.append(functools.partial(ring.arrive, 0, k))
        if k > 1:
            events.append(functools.partial(ring.plane_arrive, 0, k - 1))
    events += [functools.partial(ring.plane_arrive, 0, ring.far), functools.partial(ring.finish, 0)]
    cut = max(1, TABLE // 256 // (len(events) - 2))
    done = 0
    saves = [(tables, tables_out), (turned_tables, turned_out), (joint, joint_out)]
    saves = [pltpu.make_async_copy(src, dst, store.at[i]) for i, (src, dst) in enumerate(saves)]
    for i, event in enumerate(events):
        upto = min(TABLE // 256, (i + 1) * cut)
        if i == len(events) - 2:
            upto = TABLE // 256
        if upto > done:
            lax.fori_loop(done, upto, table_column, 0)
            done = upto
            if done == TABLE // 256:
                saves[0].start()
                saves[1].start()
        event()
    saves[2].start()

    def column(step, carry):
        cols = pl.ds(pl.multiple_of(step * 256, 256), 256)
        product[:, cols] = jnp.dot(tokens[...], joint[:, cols], preferred_element_type=jnp.float32)
        return carry

    lax.fori_loop(0, JOINT // 256, column, 0)
    norm_tile = NORM // LANES * LANES
    turned_norm = joint[:, norm_tile : norm_tile + LANES].astype(jnp.float32).T
    norms[...] = turned_norm[NORM - norm_tile : NORM - norm_tile + 8]
    logits = product[:, ROUTERS : ROUTERS + 2 * HEADS * EXP]
    local_rows = tokens.shape[0]
    wide = jnp.concatenate([logits, jnp.zeros((local_rows, LANES - 2 * HEADS * EXP), jnp.float32)], axis=1)
    lane = lax.broadcasted_iota(jnp.int32, (local_rows, LANES), 1)
    mask = route_lanes(routes[...], lane)
    gate = 1.0 / (1.0 + jnp.exp(-wide))
    gates[0] = gate * mask
    gates[1] = gate * mask * (1.0 - gate)
    pad = jnp.zeros((local_rows, LANES - DH), jnp.float32)
    ones = jnp.ones((local_rows, LANES - DH), jnp.float32)
    for head in range(HEADS):
        first = head * DH
        qkv[head, 0] = jnp.concatenate([product[:, first : first + DH], pad], axis=1).astype(jnp.bfloat16)
        first = QCOLS + head * DH
        qkv[head, 1] = jnp.concatenate([product[:, first : first + DH], pad], axis=1).astype(jnp.bfloat16)
        total = None
        for expert in range(EXP):
            which = head * EXP + expert
            first = 2 * QCOLS + which * DH
            piece = product[:, first : first + DH]
            experts[which] = jnp.concatenate([piece, pad], axis=1).astype(jnp.bfloat16)
            term = piece * gates[0, :, which : which + 1]
            total = term if total is None else total + term
        qkv[head, 2] = jnp.concatenate([total, ones], axis=1).astype(jnp.bfloat16)
    for copy in saves:
        copy.wait()


def project(count, query, key, value, value_router, output_router, norm, tokens, routes, gaps):
    rows, shard_rows = tokens.shape[0], query.shape[1]
    f32, bf = jnp.float32, jnp.bfloat16
    V = pltpu.VMEM
    return pl.pallas_call(
        functools.partial(project_kernel, count),
        out_shape=[
            jax.ShapeDtypeStruct((shard_rows * count, JOINT), bf),
            jax.ShapeDtypeStruct((3, LANES, TABLE), f32),
            jax.ShapeDtypeStruct((3, LANES, TABLE), f32),
            jax.ShapeDtypeStruct((HEADS, 3, rows, LANES), bf),
            jax.ShapeDtypeStruct((HEADS * EXP, rows, LANES), bf),
            jax.ShapeDtypeStruct((2, rows, LANES), f32),
            jax.ShapeDtypeStruct((8, shard_rows * count), f32),
        ],
        in_specs=[ANY] * 3 + [VMEM] * 5 + [SMEM],
        out_specs=[ANY] * 3 + [VMEM] * 4,
        scratch_shapes=[
            V((shard_rows, JOINT), bf), V((JOINT, shard_rows), bf), V((shard_rows * count, JOINT), bf),
            V((3, LANES, TABLE), f32), V((3, LANES, TABLE), f32), V((rows, JOINT), f32), DMA((3,)), DMA((3,)),
        ]
        + Gather.sems(count, 1),
        compiler_params=pltpu.CompilerParams(collective_id=1, has_side_effects=True, vmem_limit_bytes=62 << 20),
    )(query, key, value, value_router, output_router, norm, tokens, routes, gaps)


def seq_mates(ring):
    return [ring.core_mate, ring.plane_mate, (3 - ring.seq, ring.fsdp)]


def slot_mates(ring):
    f = ring.fsdp
    return [(ring.seq, f + 1 - 2 * (f % 2)), (ring.seq, f + 2 - 4 * ((f // 2) % 2))]


def tile_place(slot, seq, phase, key_block, query_block):
    cont = slot // PSLOTS
    own = 1 - jnp.minimum(phase, 1)
    piece = jnp.where(slot == 3, 2 - phase, phase - 1)
    source = jnp.where(phase == 0, 0, 1 + piece)
    first = cont * 2 * (query_block // 2)
    active = jnp.where(
        phase == 0,
        (key_block <= query_block) & (key_block >= first),
        jnp.where(phase == 1, slot >= 1, slot >= 2),
    )
    far_column = jnp.where(
        cont == 1,
        2048 * piece + BLOCK * key_block - BLOCK * (query_block % 2) - 4096,
        BLOCK * key_block - 2048 - BLOCK * query_block,
    )
    column = jnp.where(phase == 0, BLOCK * (key_block - query_block), far_column)
    table = jnp.where((phase > 0) & (cont == 1), 1 + query_block // 2, 0)
    return source, active, table, column


STRIP = 512


def near_first(ring, j):
    odd, high = j % 2, j // 2
    core = ring.core + odd - 2 * ring.core * odd
    plane = ring.plane + high - 2 * ring.plane * high
    return 2 * plane + core


def block_rows(block):
    return pl.ds(pl.multiple_of(block * BLOCK, BLOCK), BLOCK)


def attend_kernel(count, splits, steps, qkv, tables_in, *refs):
    T = len(splits)
    shards, refs = refs[:T], refs[T:]
    att, store, outputs, logs = refs[:4]
    fulls, refs = refs[4 : 4 + T], refs[4 + T :]
    acc, top, att_low, tables, kv_send, kv_recv, q_send, q_recv, sh_send, sh_recv, out_send, out_recv, here = refs[:13]
    at = lambda t, g, cols: fulls[t].at[g, :, cols]
    ring = Gather(count, splits, shards, at, *refs[13:])
    table_load = pltpu.make_async_copy(tables_in, tables, here.at[2])
    table_load.start()
    seq, slot = ring.seq, ring.fsdp % GSLOTS
    mates, (x_mate, z_mate) = seq_mates(ring), slot_mates(ring)
    enter(ring.neighbours() + mates[2:] + [x_mate, z_mate])

    def remote(src, dst, send, recv, device):
        return pltpu.make_async_remote_copy(src, dst, send, recv, device_id=device, device_id_type=MESH)

    mine = block_rows(seq)

    def kv_copy(mate):
        return remote(qkv.at[mate[0], pl.ds(1, 2)], store.at[pl.ds(1, 2), mine], kv_send.at[mate[0]], kv_recv.at[seq], mate)

    def q_copy(mate):
        return remote(qkv.at[mate[0], 0], store.at[0, mine], q_send.at[mate[0]], q_recv.at[seq], mate)

    for mate in mates[1:] + mates[:1]:
        kv_copy(mate).start()
    own_copy = pltpu.make_async_copy(qkv.at[seq], store.at[pl.ds(0, 3), mine], here.at[0])
    own_copy.start()
    for mate in mates[1:] + mates[:1]:
        q_copy(mate).start()
    acc[...] = jnp.zeros_like(acc)
    top[...] = jnp.full_like(top, NEGATIVE)

    def far_rows(piece, chunk):
        return store.at[pl.ds(3 + 2 * piece, 2), block_rows(near_first(ring, chunk))]

    def first_hop(chunk, way):
        src = store.at[pl.ds(1, 2), block_rows(near_first(ring, chunk))]
        piece = slot % 2
        return remote(src, far_rows(piece, chunk), sh_send.at[4 * way + chunk], sh_recv.at[4 * piece + chunk],
                      x_mate if way == 0 else z_mate)

    def second_hop(chunk):
        piece = slot % 2
        return remote(far_rows(piece, chunk), far_rows(piece, chunk), sh_send.at[8 + chunk], sh_recv.at[4 * piece + chunk], x_mate)

    def share(chunk):
        @pl.when(slot < 2)
        def _():
            first_hop(chunk, 1).start()

        @pl.when(slot == 0)
        def _():
            first_hop(chunk, 0).start()

    def pass_on(chunk):
        @pl.when(slot >= 1)
        def _():
            piece = jnp.where(slot == 3, 1, 0)
            remote(far_rows(piece, chunk), far_rows(piece, chunk), sh_send.at[chunk], sh_recv.at[4 * piece + chunk], x_mate).wait_recv()

        @pl.when(slot >= 2)
        def _():
            second_hop(chunk).start()

    def last_piece(chunk):
        @pl.when(slot >= 2)
        def _():
            piece = 3 - slot
            remote(far_rows(piece, chunk), far_rows(piece, chunk), sh_send.at[chunk], sh_recv.at[4 * piece + chunk], x_mate).wait_recv()

    own_copy.wait()
    share(0)
    for chunk, mate in enumerate(mates):
        other = mate[0]
        src = store.at[pl.ds(1, 2), block_rows(other)]
        remote(src, src, kv_send.at[other], kv_recv.at[other], mate).wait_recv()
        share(1 + chunk)
    for mate in mates:
        src = store.at[0, block_rows(mate[0])]
        remote(src, src, q_send.at[mate[0]], q_recv.at[mate[0]], mate).wait_recv()

    def tile(source, table, column, key_block, first, rows):
        keys = store[1 + 2 * source, block_rows(key_block), :]
        values = store[2 + 2 * source, block_rows(key_block), :]
        for strip in range(rows // STRIP):
            part = pl.ds(pl.multiple_of(first + strip * STRIP, STRIP), STRIP)
            scores = lax.dot_general(store[0, part, :], keys, (((1,), (1,)), ((), ())), preferred_element_type=jnp.float32)
            start = column + TABLE_ZERO - strip * STRIP
            bias = [tables[table, :, pl.ds(pl.multiple_of(start - LANES * i, LANES), BLOCK)] for i in range(STRIP // LANES)]
            scores = scores * (DH**-0.5 * LOG2E) + jnp.concatenate(bias, axis=0)
            before = top[part, :]
            after = jnp.maximum(before, jnp.max(scores, axis=1, keepdims=True))
            terms = jnp.exp2(scores - after[:, :1])
            acc[part, :] = acc[part, :] * jnp.exp2(before - after) + jnp.dot(
                terms.astype(jnp.bfloat16), values, preferred_element_type=jnp.float32)
            top[part, :] = after

    def near_tile(step):
        key_block, query_block = near_first(ring, step // 4), step % 4
        source, active, table, column = tile_place(slot, seq, 0, key_block, query_block)

        @pl.when(active)
        def _():
            tile(source, table, column, key_block, query_block * BLOCK, BLOCK)

    def far_tile(step):
        phase, key_block, query_block = step // 8, near_first(ring, (step // 2) % 4), 2 * (step % 2)
        source, active, table, column = tile_place(slot, seq, phase, key_block, query_block)

        @pl.when(active)
        def _():
            tile(source, table, column, key_block, query_block * BLOCK, 2 * BLOCK)

    table_load.wait()
    events = {}
    for chunk in range(4):
        events.setdefault(4 * chunk + 3, []).append(functools.partial(pass_on, chunk))
        events.setdefault(24 + 2 * chunk, []).append(functools.partial(last_piece, chunk))
    begin, first, gap = steps
    for t in range(T):
        if begin + t < 0:
            ring.start(t)
        else:
            events.setdefault(begin + t, []).append(functools.partial(ring.start, t))
    rest = []
    for i, event in enumerate(ring.events()):
        step = int(first + gap * i)
        if step < 32:
            events.setdefault(step, []).append(event)
        else:
            rest.append(event)

    def step_body(step, carry):
        for when, actions in sorted(events.items()):
            @pl.when(step == when)
            def _():
                for action in actions:
                    action()
        pl.when(step < 16)(lambda: near_tile(step))
        pl.when(step >= 16)(lambda: far_tile(step - 8))
        return carry

    lax.fori_loop(0, 32, step_body, 0)
    total = acc[:, DH : DH + 1]
    result = acc[...] / total
    outputs[...] = result
    log_total = top[...] + jnp.log2(total)
    for block in range(4):
        logs[:, block * BLOCK : (block + 1) * BLOCK] = log_total[block * BLOCK : (block + 1) * BLOCK].T[:8]
    att_low[...] = result.astype(jnp.bfloat16)

    def out_copy(mate):
        return remote(att_low.at[block_rows(mate[0])], att.at[seq], out_send.at[mate[0]], out_recv.at[seq], mate)

    for mate in mates[1:] + mates[:1]:
        out_copy(mate).start()
    own_out = pltpu.make_async_copy(att_low.at[mine], att.at[seq], here.at[1])
    own_out.start()
    for event in rest:
        event()
    own_out.wait()
    for mate in mates:
        kv_copy(mate).wait_send()
        q_copy(mate).wait_send()
        out_copy(mate).wait_send()
        ref = att.at[mate[0]]
        remote(ref, ref, out_send.at[mate[0]], out_recv.at[mate[0]], mate).wait_recv()
    for chunk in range(4):
        @pl.when(slot < 2)
        def _():
            first_hop(chunk, 1).wait_send()

        @pl.when(slot == 0)
        def _():
            first_hop(chunk, 0).wait_send()

        @pl.when(slot >= 2)
        def _():
            second_hop(chunk).wait_send()


def attend(count, qkv, tables, shards, splits, steps=(0, 18, 2)):
    rows = qkv.shape[2]
    own = 4 * rows
    T = len(shards)
    return pl.pallas_call(
        functools.partial(attend_kernel, count, splits, steps),
        out_shape=[
            jax.ShapeDtypeStruct((HEADS, rows, LANES), jnp.bfloat16),
            jax.ShapeDtypeStruct((7, own, LANES), jnp.bfloat16),
            jax.ShapeDtypeStruct((own, LANES), jnp.float32),
            jax.ShapeDtypeStruct((8, own), jnp.float32),
        ]
        + [jax.ShapeDtypeStruct((count,) + w.shape, w.dtype) for w in shards],
        in_specs=[VMEM, ANY] + [VMEM] * T,
        out_specs=[VMEM] * 4 + [ANY] * T,
        scratch_shapes=[
            pltpu.VMEM((own, LANES), jnp.float32),
            pltpu.VMEM((own, LANES), jnp.float32),
            pltpu.VMEM((own, LANES), jnp.bfloat16),
            pltpu.VMEM((3, LANES, TABLE), jnp.float32),
            DMA((4,)), DMA((4,)), DMA((4,)), DMA((4,)), DMA((12,)), DMA((8,)), DMA((4,)), DMA((4,)), DMA((3,)),
        ]
        + Gather.sems(count, T),
        compiler_params=pltpu.CompilerParams(collective_id=2, has_side_effects=True, vmem_limit_bytes=56 << 20),
    )(qkv, tables, *shards)


class Scatter(Ring):
    def __init__(self, count, splits, parts, outs, bufs, sems):
        super().__init__(count, splits)
        self.parts, self.outs = parts, outs
        T = len(splits)
        self.mine, self.plane_in = bufs[:T], bufs[T : 2 * T]
        self.ring0, self.ring1 = bufs[2 * T : 3 * T], bufs[3 * T : 4 * T]
        self.low, self.low_in, self.done = bufs[4 * T : 5 * T], bufs[5 * T : 6 * T], bufs[6 * T : 7 * T]
        (self.load, self.plane_s, self.plane_r, self.ring_s, self.ring_r, self.end_s, self.end_r, self.put) = sems

    @staticmethod
    def scratch(count, splits, rows):
        half = [a + 2 * b for a, b in splits]
        bf = jnp.bfloat16
        out = [pltpu.VMEM((count, r, h), bf) for r, h in zip(rows, half)]
        out += [pltpu.VMEM((count, r, b), bf) for r, (a, b) in zip(rows, splits)]
        out += [pltpu.VMEM((count - 1 if a else 1, r, max(a, LANES)), bf) for r, (a, b) in zip(rows, splits)]
        out += [pltpu.VMEM((count - 1, r, b), bf) for r, (a, b) in zip(rows, splits)]
        out += [pltpu.VMEM((r, a + b), bf) for r, (a, b) in zip(rows, splits)]
        out += [pltpu.VMEM((r, a + b), bf) for r, (a, b) in zip(rows, splits)]
        out += [pltpu.VMEM((r, h), jnp.float32) for r, h in zip(rows, half)]
        T = len(splits)
        return out + [DMA((T * count,))] * 3 + [DMA((2 * T * (count - 1),))] * 2 + [DMA((2 * T,))] * 2 + [DMA((T,))]

    def dest(self, rel):
        return ring_index((self.place + rel) % self.count, self.count)

    def load_copy(self, t, rel):
        part, first = self.parts[t]
        src = part.at[self.dest(rel), :, pl.ds(first, self.half(t))]
        return pltpu.make_async_copy(src, self.mine[t].at[rel], self.load.at[t * self.count + rel])

    def remote(self, src, dst, s, r, i, device):
        return pltpu.make_async_remote_copy(src, dst, s.at[i], r.at[i], device_id=device, device_id_type=MESH)

    def single(self, t, plane):
        both, single = self.splits[t]
        return pl.ds(pl.multiple_of(both + plane * single, LANES), single)

    def plane_copy(self, t, rel):
        src = self.mine[t].at[rel, :, self.single(t, 1 - self.plane)]
        return self.remote(src, self.plane_in[t].at[rel], self.plane_s, self.plane_r, t * self.count + rel, self.plane_mate)

    def rels(self, D):
        return sorted({D % self.count, (-D) % self.count})

    def order(self):
        out = []
        for D in range(self.far, -1, -1):
            out += self.rels(D)
        return out

    def start(self, t):
        for rel in self.order():
            self.load_copy(t, rel).start()

    def ready(self, t, rel):
        if self.parts[t]:
            self.load_copy(t, rel).wait()
        self.plane_copy(t, rel).start()

    def all_ready(self, t):
        for rel in self.order():
            self.ready(t, rel)

    def step(self, t, D):
        self.combine(t, D)
        if D:
            self.chain(t, D)
        else:
            self.close(t)

    def buffer(self, t, kind, slot):
        if kind:
            return self.ring1[t].at[slot]
        return self.ring0[t].at[slot]

    def own_ref(self, t, kind, rel):
        if kind:
            return self.mine[t].at[rel, :, self.single(t, self.plane)]
        return self.mine[t].at[rel, :, pl.ds(0, self.splits[t][0])]

    def ring_copy(self, t, kind, way, D):
        slot = self.slot(kind, way, D)
        if D == self.reach(kind, way):
            src = self.own_ref(t, kind, D % self.count if way == 0 else (-D) % self.count)
        else:
            src = self.buffer(t, kind, self.slot(kind, way, D + 1))
        i = (2 * t + kind) * (self.count - 1) + slot
        return self.remote(src, self.buffer(t, kind, slot), self.ring_s, self.ring_r, i, self.next(way))

    def ring_wait(self, t, kind, way, D):
        slot = self.slot(kind, way, D)
        ref = self.buffer(t, kind, slot)
        i = (2 * t + kind) * (self.count - 1) + slot
        self.remote(ref, ref, self.ring_s, self.ring_r, i, self.next(way)).wait_recv()

    def combine(self, t, D):
        for rel in self.rels(D):
            self.plane_copy(t, rel).wait_send()
            ref = self.plane_in[t].at[rel]
            self.remote(ref, ref, self.plane_s, self.plane_r, t * self.count + rel, self.plane_mate).wait_recv()
            own = self.own_ref(t, 1, rel)
            own[...] = (own[...].astype(jnp.float32) + self.plane_in[t][rel].astype(jnp.float32)).astype(jnp.bfloat16)

    def chain(self, t, D):
        for kind in self.kinds(t):
            for way in (0, 1):
                if D > self.reach(kind, way):
                    continue
                if D < self.reach(kind, way):
                    self.ring_wait(t, kind, way, D + 1)
                    rel = D % self.count if way == 0 else (-D) % self.count
                    ref = self.buffer(t, kind, self.slot(kind, way, D + 1))
                    ref[...] = (ref[...].astype(jnp.float32) + self.own_ref(t, kind, rel)[...].astype(jnp.float32)).astype(jnp.bfloat16)
                self.ring_copy(t, kind, way, D).start()

    def end_copy(self, t):
        return self.remote(self.low[t], self.low_in[t], self.end_s, self.end_r, 2 * t, self.plane_mate)

    def close(self, t):
        both, single = self.splits[t]
        for kind in self.kinds(t):
            total = self.own_ref(t, kind, 0)[...].astype(jnp.float32)
            for way in (0, 1):
                if self.reach(kind, way):
                    self.ring_wait(t, kind, way, 1)
                    total = total + self.buffer(t, kind, self.slot(kind, way, 1))[...].astype(jnp.float32)
            if kind:
                self.low[t][:, both:] = total.astype(jnp.bfloat16)
            else:
                self.low[t][:, :both] = total.astype(jnp.bfloat16)
        self.end_copy(t).start()

    def out_ref(self, t, core):
        out, whole, first = self.outs[t]
        return out.at[:, pl.ds(pl.multiple_of(core * whole + first, LANES), self.half(t))]

    def out_copy(self, t):
        return self.remote(self.done[t], self.out_ref(t, self.core), self.end_s, self.end_r, 2 * t + 1, self.core_mate)

    def put_copy(self, t):
        return pltpu.make_async_copy(self.done[t], self.out_ref(t, self.core), self.put.at[t])

    def deliver(self, t):
        both, single = self.splits[t]
        self.end_copy(t).wait_send()
        ref = self.low_in[t]
        self.remote(ref, ref, self.end_s, self.end_r, 2 * t, self.plane_mate).wait_recv()
        if both:
            self.done[t][:, :both] = self.low[t][:, :both].astype(jnp.float32) + self.low_in[t][:, :both].astype(jnp.float32)
        if single:
            self.done[t][:, self.single(t, self.plane)] = self.low[t][:, both:].astype(jnp.float32)
            self.done[t][:, self.single(t, 1 - self.plane)] = self.low_in[t][:, both:].astype(jnp.float32)
        self.out_copy(t).start()
        self.put_copy(t).start()

    def finish(self, t):
        for kind in self.kinds(t):
            for way in (0, 1):
                for D in range(1, self.reach(kind, way) + 1):
                    self.ring_copy(t, kind, way, D).wait_send()
        self.out_copy(t).wait_send()
        self.put_copy(t).wait()
        ref = self.out_ref(t, 1 - self.core)
        self.remote(ref, ref, self.end_s, self.end_r, 2 * t + 1, self.core_mate).wait_recv()


def retreat_kernel(count, splits, steps, grad_att, turned_in, store_in, outputs, logs, part, back, out, *refs):
    T = len(splits)
    (grads, delta, grad_q, grad_kv, send_kv, kv_in0, kv_in1, low, in_send, in_recv, up_send, up_recv,
     turned, store, out_send, out_recv, here) = refs[:17]
    refs = refs[17:]
    loads = [pltpu.make_async_copy(turned_in, turned, here.at[2]), pltpu.make_async_copy(store_in, store, here.at[3])]
    for copy in loads:
        copy.start()
    halves = [a + 2 * b for a, b in splits]
    firsts = [sum(halves[:t]) for t in range(T)]
    ring = Scatter(
        count, splits, [(part, first) for first in firsts], [(out, sum(halves), first) for first in firsts],
        refs[: 7 * T], refs[7 * T :])
    seq, slot = ring.seq, ring.fsdp % GSLOTS
    mates, (x_mate, z_mate) = seq_mates(ring), slot_mates(ring)
    enter(ring.neighbours() + mates[2:] + [x_mate, z_mate])

    def remote(src, dst, send, recv, device):
        return pltpu.make_async_remote_copy(src, dst, send, recv, device_id=device, device_id_type=MESH)

    mine = block_rows(seq)

    def in_copy(mate):
        return remote(grad_att.at[mate[0]], grads.at[mine], in_send.at[mate[0]], in_recv.at[seq], mate)

    for mate in mates[1:] + mates[:1]:
        in_copy(mate).start()
    own_copy = pltpu.make_async_copy(grad_att.at[seq], grads.at[mine], here.at[0])
    own_copy.start()
    grad_q[...] = jnp.zeros_like(grad_q)
    grad_kv[...] = jnp.zeros_like(grad_kv)
    own_copy.wait()
    for mate in mates:
        ref = grads.at[block_rows(mate[0])]
        remote(ref, ref, in_send.at[mate[0]], in_recv.at[mate[0]], mate).wait_recv()
    for block in range(4):
        rows = pl.ds(block * BLOCK, BLOCK)
        sums = jnp.sum(grads[rows, :].astype(jnp.float32) * outputs[rows, :], axis=1, keepdims=True)
        delta[:, rows] = jnp.broadcast_to(sums, (BLOCK, LANES)).T[:8]

    for copy in loads:
        copy.wait()

    def tile(forward_phase, key_block, query_block, blocks):
        source, active, table, column = tile_place(slot, seq, forward_phase, key_block, query_block)

        @pl.when(active)
        def _():
            size = blocks * BLOCK
            key_rows, rows = block_rows(key_block), pl.ds(pl.multiple_of(query_block * BLOCK, BLOCK), size)
            keys, values = store[1 + 2 * source, key_rows, :], store[2 + 2 * source, key_rows, :]
            queries, tops = store[0, rows, :], grads[rows, :]
            scores = lax.dot_general(keys, queries, (((1,), (1,)), ((), ())), preferred_element_type=jnp.float32)
            bias = jnp.concatenate(
                [turned[table, :, pl.ds(pl.multiple_of(TURNED_ZERO - column - LANES * part, LANES), size)] for part in range(BLOCK // LANES)],
                axis=0,
            )
            weights = jnp.exp2(scores * (DH**-0.5 * LOG2E) + (bias - logs[:1, rows]))
            grad_weights = lax.dot_general(values, tops, (((1,), (1,)), ((), ())), preferred_element_type=jnp.float32)
            grad_scores = (weights * (grad_weights - delta[:1, rows])).astype(jnp.bfloat16)
            grad_kv[source, 1, key_rows, :] += jnp.dot(weights.astype(jnp.bfloat16), tops, preferred_element_type=jnp.float32)
            grad_kv[source, 0, key_rows, :] += jnp.dot(grad_scores, queries, preferred_element_type=jnp.float32)
            grad_q[rows, :] += lax.dot_general(grad_scores, keys, (((0,), (0,)), ((), ())), preferred_element_type=jnp.float32)

    def far_tile(step):
        phase = step // 8
        piece = jnp.where(slot == 2, 1 - phase, phase)
        tile(jnp.where(slot == 3, 2 - piece, 1 + piece), (step // 2) % 4, 2 * (step % 2), 2)

    def near_tile(step):
        tile(0, step // 4, step % 4, 1)

    scale = DH**-0.5

    def rounded(source, chunk, extra):
        rows = block_rows(chunk)
        keys = grad_kv[source, 0, rows, :] * scale
        values = grad_kv[source, 1, rows, :]
        for more in extra:
            keys = keys + more[0].astype(jnp.float32)
            values = values + more[1].astype(jnp.float32)
        return keys.astype(jnp.bfloat16), values.astype(jnp.bfloat16)

    def x_send(chunk):
        src = send_kv.at[0, :, block_rows(chunk)]
        return remote(src, kv_in0.at[:, block_rows(chunk)], up_send.at[chunk], up_recv.at[chunk], x_mate)

    def z_send(chunk):
        src = send_kv.at[1, :, block_rows(chunk)]
        return remote(src, kv_in1.at[:, block_rows(chunk)], up_send.at[4 + chunk], up_recv.at[4 + chunk], z_mate)

    def x_wait(chunk):
        ref = kv_in0.at[:, block_rows(chunk)]
        remote(ref, ref, up_send.at[chunk], up_recv.at[chunk], x_mate).wait_recv()

    def z_wait(chunk):
        ref = kv_in1.at[:, block_rows(chunk)]
        remote(ref, ref, up_send.at[4 + chunk], up_recv.at[4 + chunk], z_mate).wait_recv()

    def first_done(chunk):
        @pl.when(slot >= 1)
        def _():
            source = jnp.where(slot == 2, 2, 1)
            keys, values = rounded(source, chunk, [])
            send_kv[0, 0, block_rows(chunk), :] = keys
            send_kv[0, 1, block_rows(chunk), :] = values
            x_send(chunk).start()

    def second_done(chunk):
        @pl.when(slot >= 2)
        def _():
            x_wait(chunk)
            source = slot - 1
            keys, values = rounded(source, chunk, [kv_in0[:, block_rows(chunk), :]])
            send_kv[1, 0, block_rows(chunk), :] = keys
            send_kv[1, 1, block_rows(chunk), :] = values
            z_send(chunk).start()

    def out_copy(mate):
        src = low.at[:, block_rows(mate[0])]
        return remote(src, back.at[seq], out_send.at[mate[0]], out_recv.at[seq], mate)

    def own_done(chunk):
        rows = block_rows(chunk)
        low[0, rows, :] = (grad_q[rows, :] * scale).astype(jnp.bfloat16)

        @pl.when(slot == 0)
        def _():
            x_wait(chunk)
            z_wait(chunk)
            low[1, rows, :], low[2, rows, :] = rounded(0, chunk, [kv_in0[:, rows, :], kv_in1[:, rows, :]])

        @pl.when(slot == 1)
        def _():
            z_wait(chunk)
            low[1, rows, :], low[2, rows, :] = rounded(0, chunk, [kv_in1[:, rows, :]])

        @pl.when(slot >= 2)
        def _():
            low[1, rows, :], low[2, rows, :] = rounded(0, chunk, [])

    events = {}
    for chunk in range(4):
        events.setdefault(2 * chunk + 2, []).append(functools.partial(first_done, chunk))
        events.setdefault(10 + 2 * chunk, []).append(functools.partial(second_done, chunk))
    begin, ready, first, hop, lag = steps
    rest = []
    for t in range(T):
        plan = [(begin, functools.partial(ring.start, t)), (ready, functools.partial(ring.all_ready, t))]
        when = first + lag * t
        for D in range(ring.far, -1, -1):
            plan.append((when, functools.partial(ring.step, t, D)))
            when += hop
        plan.append((when, functools.partial(ring.deliver, t)))
        plan.append((when + hop, functools.partial(ring.finish, t)))
        for when, event in plan:
            if when < 32:
                events.setdefault(int(when), []).append(event)
            else:
                rest.append((when, event))
    rest = [event for when, event in sorted(rest, key=lambda pair: pair[0])]

    def step_body(step, carry):
        for when, actions in sorted(events.items()):
            @pl.when(step == when)
            def _():
                for action in actions:
                    action()
        pl.when(step < 16)(lambda: far_tile(step))
        pl.when(step >= 16)(lambda: near_tile(step - 16))
        return carry

    lax.fori_loop(0, 32, step_body, 0)
    for chunk in range(4):
        own_done(chunk)
    for mate in mates[1:] + mates[:1]:
        out_copy(mate).start()
    own_out = pltpu.make_async_copy(low.at[:, mine], back.at[seq], here.at[1])
    own_out.start()
    for event in rest:
        event()
    own_out.wait()
    for mate in mates:
        in_copy(mate).wait_send()
        out_copy(mate).wait_send()
        ref = back.at[mate[0]]
        remote(ref, ref, out_send.at[mate[0]], out_recv.at[mate[0]], mate).wait_recv()
    for chunk in range(4):
        @pl.when(slot >= 1)
        def _():
            x_send(chunk).wait_send()

        @pl.when(slot >= 2)
        def _():
            z_send(chunk).wait_send()


def retreat(count, grad_att, turned, store, outputs, logs, part, splits, steps=(0, 1, 2, 3, 1)):
    rows = grad_att.shape[1]
    own = 4 * rows
    _, shard_rows, half = part.shape
    return pl.pallas_call(
        functools.partial(retreat_kernel, count, splits, steps),
        out_shape=[jax.ShapeDtypeStruct((HEADS, 3, rows, LANES), jnp.bfloat16), jax.ShapeDtypeStruct((shard_rows, 2 * half), jnp.float32)],
        in_specs=[VMEM, ANY, ANY, VMEM, VMEM, ANY],
        out_specs=[VMEM, ANY],
        scratch_shapes=[
            pltpu.VMEM((own, LANES), jnp.bfloat16),
            pltpu.VMEM((8, own), jnp.float32),
            pltpu.VMEM((own, LANES), jnp.float32),
            pltpu.VMEM((3, 2, own, LANES), jnp.float32),
            pltpu.VMEM((2, 2, own, LANES), jnp.bfloat16),
            pltpu.VMEM((2, own, LANES), jnp.bfloat16),
            pltpu.VMEM((2, own, LANES), jnp.bfloat16),
            pltpu.VMEM((3, own, LANES), jnp.bfloat16),
            DMA((4,)), DMA((4,)), DMA((8,)), DMA((8,)),
            pltpu.VMEM((3, LANES, TABLE), jnp.float32), pltpu.VMEM((7, own, LANES), jnp.bfloat16),
            DMA((4,)), DMA((4,)), DMA((4,)),
        ]
        + Scatter.scratch(count, splits, [shard_rows] * len(splits)),
        compiler_params=pltpu.CompilerParams(collective_id=3, has_side_effects=True, vmem_limit_bytes=60 << 20),
    )(grad_att, turned, store, outputs, logs, part)


CHUNK = 512


def gelu_pair(v):
    root = 0.7978845608028654
    square = v * v
    t = jnp.tanh(root * (v + 0.044715 * square * v))
    up = 0.5 * (1.0 + t)
    return v * up, up + 0.5 * v * (1.0 - t * t) * (root * (1.0 + 3.0 * 0.044715 * square))


def contract(left, right, left_axis, right_axis):
    return lax.dot_general(left, right, (((left_axis,), (right_axis,)), ((), ())), preferred_element_type=jnp.float32)


def feed_kernel(count, att, gates, tokens, cotangent, norms, output_w, inner_w, outer_w,
                layer_out, grad_residual, grad_att, grad_logit, grad_norms, part_output, part_inner, outer_out,
                w_out, w_in, w_up, acts, act_in, slopes, slope_in, scaled, scaled_in, scaled_t, cot_in, cot_t,
                acc, normed, grad_scaled, branch_low, branch_in, branch_t, att_in, gates_in,
                stage_inner, stage_output,
                load_out, load_in, load_up, pair_s, pair_r, act_s, act_r, slope_s, slope_r, put_inner, put_output, *refs):
    half = cotangent.shape[1] // 2
    ring = Scatter(count, (SPLITS["outer"],), [None], [(outer_out, half, 0)], refs[:7], refs[7:])
    core, mate = ring.core, ring.core_mate
    experts = HEADS * EXP
    chunks = inner_w.shape[1] // CHUNK
    small = CHUNK // 2
    shards = max(1, count // chunks)

    def out_load(e):
        return pltpu.make_async_copy(output_w.at[pl.ds(e * DH, DH)], w_out.at[e, pl.ds(0, DH)], load_out.at[e])

    def ffn_load(chunk, slot):
        cols = pl.ds(pl.multiple_of(chunk * CHUNK, CHUNK), CHUNK)
        return (pltpu.make_async_copy(inner_w.at[:, cols], w_in.at[slot], load_in.at[slot]),
                pltpu.make_async_copy(outer_w.at[cols], w_up.at[slot], load_up.at[slot]))

    def chunk_of(step):
        if count != chunks:
            return step
        D = ring.far - (step + 1) // 2
        odd = step % 2
        return ring.dest((odd * D + (1 - odd) * (count - D)) % count)

    for e in range(experts):
        out_load(e).start()
    for sub in range(2):
        for copy in ffn_load(chunk_of(sub), sub):
            copy.start()
    enter(ring.neighbours())

    def remote(src, dst, send, recv):
        return pltpu.make_async_remote_copy(src, dst, send, recv, device_id=mate, device_id_type=MESH)

    mine = pl.ds(pl.multiple_of(core * half, LANES), half)
    yours = pl.ds(pl.multiple_of((1 - core) * half, LANES), half)
    pair = [
        remote(att, att_in, pair_s.at[0], pair_r.at[0]),
        remote(gates.at[0], gates_in, pair_s.at[1], pair_r.at[1]),
        remote(cotangent.at[:, yours], cot_in, pair_s.at[2], pair_r.at[2]),
        remote(scaled, scaled_in, pair_s.at[3], pair_r.at[3]),
        remote(branch_low.at[:, yours], branch_in, pair_s.at[4], pair_r.at[4]),
    ]
    for copy in pair[:3]:
        copy.start()

    def mixed_pair(att_ref, gate, two):
        tiles = []
        for which in (2 * two, 2 * two + 1):
            column = gate[:, experts + which : experts + which + 1]
            tiles.append((att_ref[which // EXP].astype(jnp.float32) * column).astype(jnp.bfloat16))
        return jnp.concatenate(tiles, axis=1)

    w_out[:, DH:, :] = jnp.zeros((experts, LANES - DH, w_out.shape[2]), jnp.bfloat16)
    acc[...] = tokens[...].astype(jnp.float32)
    for two in range(experts // 2):
        out_load(2 * two).wait()
        out_load(2 * two + 1).wait()
        weights = w_out[2 * two : 2 * two + 2].reshape(2 * LANES, w_out.shape[2])
        acc[...] += jnp.dot(mixed_pair(att, gates.at[0], two), weights, preferred_element_type=jnp.float32)
    residual = acc[...]
    centred = residual - jnp.mean(residual, axis=1, keepdims=True)
    inverse = lax.rsqrt(jnp.mean(centred * centred, axis=1, keepdims=True) + EPSILON)
    normed[...] = centred * inverse
    scaled[...] = (normed[...] * norms[:1] + norms[1:2]).astype(jnp.bfloat16)
    pair[3].start()
    rows = tokens.shape[0]
    scaled_t[:, :rows] = scaled[...].T
    cot_t[:, :rows] = cotangent[:, mine].T
    grad_scaled[...] = jnp.zeros_like(grad_scaled)
    pair[2].wait_recv()
    cot_t[:, rows:] = cot_in[...].T
    pair[3].wait_recv()
    scaled_t[:, rows:] = scaled_in[...].T

    small_mine = pl.ds(pl.multiple_of(core * small, LANES), small)
    small_yours = pl.ds(pl.multiple_of((1 - core) * small, LANES), small)

    def act_copy(step, sub):
        return remote(acts.at[sub], act_in.at[step], act_s.at[sub], act_r.at[step])

    def slope_copy(step, sub):
        return remote(slopes.at[sub, :, small_yours], slope_in.at[step], slope_s.at[sub], slope_r.at[step])

    def put_inner_copy(step, sub):
        cols = pl.ds(pl.multiple_of(chunk_of(step) * small, small), small)
        return pltpu.make_async_copy(stage_inner.at[sub], part_inner.at[:, cols], put_inner.at[sub])

    def forward_backward(step, sub):
        for copy in ffn_load(chunk_of(step), sub):
            copy.wait()

        @pl.when(step > 1)
        def _():
            act_copy(step, sub).wait_send()
            slope_copy(step, sub).wait_send()

        act, slope = gelu_pair(jnp.dot(scaled[...], w_in[sub], preferred_element_type=jnp.float32))
        acts[sub] = act.astype(jnp.bfloat16)
        act_copy(step, sub).start()
        slopes[sub] = (contract(cotangent[...], w_up[sub], 1, 1) * slope).astype(jnp.bfloat16)
        slope_copy(step, sub).start()
        acc[...] += jnp.dot(acts[sub], w_up[sub], preferred_element_type=jnp.float32)
        grad_scaled[...] += contract(slopes[sub], w_in[sub], 1, 1)

        @pl.when(step + 2 < chunks)
        def _():
            for copy in ffn_load(chunk_of(step + 2), sub):
                copy.start()

    def weight_parts(step, sub):
        remote(act_in.at[step], act_in.at[step], act_s.at[sub], act_r.at[step]).wait_recv()
        total = jnp.dot(cot_t[:, :rows], acts[sub], preferred_element_type=jnp.float32)
        total = total + jnp.dot(cot_t[:, rows:], act_in[step], preferred_element_type=jnp.float32)
        turned = total.astype(jnp.bfloat16).T
        shard_rows = CHUNK // shards
        for q in range(shards):
            rel = (ring_place(chunk_of(step) * shards + q, count) - ring.place + count) % count
            ring.mine[0][rel] = turned[q * shard_rows : (q + 1) * shard_rows]
        remote(slope_in.at[step], slope_in.at[step], slope_s.at[sub], slope_r.at[step]).wait_recv()

        @pl.when(step > 1)
        def _():
            put_inner_copy(step, sub).wait()

        total = jnp.dot(scaled_t[:, :rows], slopes[sub, :, small_mine], preferred_element_type=jnp.float32)
        total = total + jnp.dot(scaled_t[:, rows:], slope_in[step], preferred_element_type=jnp.float32)
        stage_inner[sub] = total.astype(jnp.bfloat16)
        put_inner_copy(step, sub).start()

    events = {}
    if count == chunks:
        for step, rel in enumerate(ring.order()):
            events.setdefault(step, []).append(functools.partial(ring.ready, 0, rel))
        for D in range(ring.far, 0, -1):
            events.setdefault(2 * (ring.far - D) + 1, []).append(functools.partial(ring.step, 0, D))

    def after_parts(step):
        for when, actions in sorted(events.items()):
            @pl.when(step == when)
            def _():
                for action in actions:
                    action()

    def iteration(i, carry):
        forward_backward(2 * i, 0)

        @pl.when(i > 0)
        def _():
            weight_parts(2 * i - 1, 1)
            after_parts(2 * i - 1)

        forward_backward(2 * i + 1, 1)
        weight_parts(2 * i, 0)
        after_parts(2 * i)
        return carry

    lax.fori_loop(0, chunks // 2, iteration, 0)
    weight_parts(chunks - 1, 1)
    if count == chunks:
        for action in events[chunks - 1]:
            action()
    else:
        ring.all_ready(0)
        for D in range(ring.far, 0, -1):
            ring.step(0, D)
    layer_out[...] = acc[...].astype(jnp.bfloat16)
    slope = grad_scaled[...]
    grad_norms[...] = jnp.concatenate(
        [jnp.sum(slope * normed[...], axis=0, keepdims=True), jnp.sum(slope, axis=0, keepdims=True),
         jnp.zeros((6, slope.shape[1]), jnp.float32)], axis=0)
    slope = slope * norms[:1]
    total = cotangent[...].astype(jnp.float32) + inverse * (
        slope - jnp.mean(slope, axis=1, keepdims=True)
        - normed[...] * jnp.mean(slope * normed[...], axis=1, keepdims=True))
    grad_residual[...] = total
    branch_low[...] = total.astype(jnp.bfloat16)
    pair[4].start()
    branch_t[:, :rows] = branch_low[:, mine].T
    ring.step(0, 0)
    lane = lax.broadcasted_iota(jnp.int32, (rows, LANES), 1)
    logit = jnp.zeros((rows, LANES), jnp.float32)
    head_total = None
    for which in range(experts):
        if which % 2 == 0:
            weights = w_out[which : which + 2].reshape(2 * LANES, w_out.shape[2])
            both = contract(branch_low[...], weights, 1, 1)
        grad_mixed = both[:, which % 2 * LANES : (which % 2 + 1) * LANES]
        head, expert = which // EXP, which % EXP
        column = slice(experts + which, experts + which + 1)
        term = grad_mixed * gates[0, :, column]
        head_total = term if expert == 0 else head_total + term
        if expert == EXP - 1:
            grad_att[head] = head_total.astype(jnp.bfloat16)
        sums = jnp.sum(grad_mixed * att[head].astype(jnp.float32), axis=1, keepdims=True)
        logit = jnp.where(lane == experts + which, sums, logit)
    grad_logit[...] = logit * gates[1]
    ring.deliver(0)
    pair[0].wait_recv()
    pair[1].wait_recv()
    pair[4].wait_recv()
    branch_t[:, rows:] = branch_in[...].T

    def put_output_copy(which):
        return pltpu.make_async_copy(stage_output.at[which % 4, pl.ds(0, DH)], part_output.at[pl.ds(which * DH, DH)], put_output.at[which % 4])

    for two in range(experts // 2):
        total = jnp.dot(branch_t[:, :rows], mixed_pair(att, gates.at[0], two), preferred_element_type=jnp.float32)
        total = total + jnp.dot(branch_t[:, rows:], mixed_pair(att_in, gates_in, two), preferred_element_type=jnp.float32)
        turned = total.astype(jnp.bfloat16).T
        for side in range(2):
            which = 2 * two + side
            if which >= 4:
                put_output_copy(which - 4).wait()
            stage_output[which % 4] = turned[side * LANES : (side + 1) * LANES]
            put_output_copy(which).start()
    for which in range(experts - 4, experts):
        put_output_copy(which).wait()
    for sub in range(2):
        put_inner_copy(sub, sub).wait()
        act_copy(sub, sub).wait_send()
        slope_copy(sub, sub).wait_send()
    ring.finish(0)
    for copy in pair:
        copy.wait_send()


def feed(count, att, gates, tokens, cotangent, norms, output_w, inner_w, outer_w):
    rows, width = tokens.shape
    wide = inner_w.shape[1]
    half = width // 2
    f32, bf = jnp.float32, jnp.bfloat16
    experts, chunks = HEADS * EXP, wide // CHUNK
    V = pltpu.VMEM
    return pl.pallas_call(
        functools.partial(feed_kernel, count),
        out_shape=[
            jax.ShapeDtypeStruct((rows, width), bf),
            jax.ShapeDtypeStruct((rows, width), f32),
            jax.ShapeDtypeStruct((HEADS, rows, LANES), bf),
            jax.ShapeDtypeStruct((rows, LANES), f32),
            jax.ShapeDtypeStruct((8, width), f32),
            jax.ShapeDtypeStruct((VCOLS, half), bf),
            jax.ShapeDtypeStruct((width, wide // 2), bf),
            jax.ShapeDtypeStruct((wide // count, width), f32),
        ],
        in_specs=[VMEM] * 5 + [ANY] * 3,
        out_specs=[VMEM] * 5 + [ANY] * 3,
        scratch_shapes=[
            V((experts, LANES, width), bf), V((2, width, CHUNK), bf), V((2, CHUNK, width), bf),
            V((2, rows, CHUNK), bf), V((chunks, rows, CHUNK), bf), V((2, rows, CHUNK), bf), V((chunks, rows, CHUNK // 2), bf),
            V((rows, width), bf), V((rows, width), bf), V((width, 2 * rows), bf), V((rows, half), bf), V((half, 2 * rows), bf),
            V((rows, width), f32), V((rows, width), f32), V((rows, width), f32),
            V((rows, width), bf), V((rows, half), bf), V((half, 2 * rows), bf), V((HEADS, rows, LANES), bf), V((rows, LANES), f32),
            V((2, width, CHUNK // 2), bf), V((4, LANES, half), bf),
            DMA((experts,)), DMA((2,)), DMA((2,)), DMA((5,)), DMA((5,)), DMA((2,)), DMA((chunks,)), DMA((2,)), DMA((chunks,)),
            DMA((2,)), DMA((4,)),
        ]
        + Scatter.scratch(count, (SPLITS["outer"],), [wide // count]),
        compiler_params=pltpu.CompilerParams(collective_id=4, has_side_effects=True, vmem_limit_bytes=63 << 20),
    )(att, gates, tokens, cotangent, norms, output_w, inner_w, outer_w)


def settle_kernel(count, back, experts, gates, grad_logit, tokens, joint_in, residual_in, grad_norms, part_output,
                  grad_tokens, joint_out, output_out, grads, grads_in, tokens_in, tokens_t, norms_in, norm_columns, joint, grad_residual, *refs):
    splits = (SPLITS["joint"], SPLITS["output"])
    pair_s, pair_r, load = refs[-3:]
    loads = [pltpu.make_async_copy(joint_in, joint, load.at[0]), pltpu.make_async_copy(residual_in, grad_residual, load.at[1])]
    for copy in loads:
        copy.start()
    half, output_half = JOINT // 2, part_output.shape[2]
    outs = [(joint_out, half, 0), (output_out, output_half, 0)]
    ring = Scatter(count, splits, [None, (part_output, 0)], outs, refs[:14], refs[14:-3])
    ring.start(1)
    enter(ring.neighbours())
    core = ring.core

    def remote(src, dst, i):
        return pltpu.make_async_remote_copy(src, dst, pair_s.at[i], pair_r.at[i], device_id=ring.core_mate, device_id_type=MESH)

    mine = pl.ds(pl.multiple_of(core * half, LANES), half)
    yours = pl.ds(pl.multiple_of((1 - core) * half, LANES), half)
    pair = [remote(tokens, tokens_in, 0), remote(grad_norms, norms_in, 1)]
    pair[0].start()
    pair[1].start()
    ring.all_ready(1)
    rows = tokens.shape[0]
    lane = lax.broadcasted_iota(jnp.int32, (LANES, LANES), 1)
    width = HEADS * EXP

    def hand_over(block):
        part = pl.ds(pl.multiple_of(block * LANES, LANES), LANES)
        return remote(grads.at[part, yours], grads_in.at[part], 2 + block)


    def assemble(block, carry):
        part = pl.ds(pl.multiple_of(block * LANES, LANES), LANES)
        pieces = [back[head, which, part, :][:, :DH].astype(jnp.float32) for which in range(2) for head in range(HEADS)]
        logit = grad_logit[part, :]
        for head in range(HEADS):
            values = back[head, 2, part, :].astype(jnp.float32)
            for expert in range(EXP):
                which = head * EXP + expert
                pieces.append((values * gates[0, part, which : which + 1])[:, :DH])
                sums = jnp.sum(values * experts[which, part, :].astype(jnp.float32), axis=1, keepdims=True)
                logit = jnp.where(lane == which, sums * gates[1, part, which : which + 1], logit)
        pieces.append(jnp.where(lane < 2 * width, logit, 0.0))
        pieces.append(jnp.zeros((LANES, JOINT - ROUTERS - LANES), jnp.float32))
        grads[part, :] = jnp.concatenate(pieces, axis=1).astype(jnp.bfloat16)
        hand_over(block).start()
        return carry

    lax.fori_loop(0, rows // LANES, assemble, 0)
    ring.step(1, ring.far)
    tokens_t[:, :rows] = tokens[...].T
    for copy in pair:
        copy.wait_recv()
    tokens_t[:, rows:] = tokens_in[...].T
    norm_tile = NORM // LANES * LANES - half
    first = NORM - half - norm_tile
    both = grad_norms[...] + norms_in[...]
    for block in range(both.shape[1] // LANES):
        columns = jnp.concatenate([both[:, block * LANES : (block + 1) * LANES], jnp.zeros((LANES - 8, LANES), jnp.float32)], axis=0)
        norm_columns[block * LANES : (block + 1) * LANES, :] = columns.T
    for block in range(rows // LANES):
        hand_over(block).wait_recv()
    shard_rows = tokens_t.shape[0] // count
    tile_lane = lax.broadcasted_iota(jnp.int32, (shard_rows, LANES), 1)

    def fill(rel):
        part = pl.ds(pl.multiple_of(ring.dest(rel) * shard_rows, shard_rows), shard_rows)
        total = jnp.dot(tokens_t[part, :rows], grads[:, mine], preferred_element_type=jnp.float32)
        total = total + jnp.dot(tokens_t[part, rows:], grads_in[...], preferred_element_type=jnp.float32)
        ring.mine[0][rel] = total.astype(jnp.bfloat16)
        extra = jnp.where(tile_lane == first, norm_columns[part, 0:1], 0.0) + jnp.where(tile_lane == first + 1, norm_columns[part, 1:2], 0.0)
        tile = total[:, norm_tile : norm_tile + LANES] + extra * core.astype(jnp.float32)
        ring.mine[0][rel, :, norm_tile : norm_tile + LANES] = tile.astype(jnp.bfloat16)

    for rel in ring.order():
        fill(rel)
        ring.ready(0, rel)
    ring.step(0, ring.far)
    for D in range(ring.far - 1, 0, -1):
        ring.step(1, D)
        ring.step(0, D)
        if D == ring.far - 1:
            for copy in loads:
                copy.wait()
            grad_tokens[...] = grad_residual[...] + contract(grads[...], joint[...], 1, 1)
    ring.step(1, 0)
    ring.step(0, 0)
    ring.deliver(1)
    ring.deliver(0)
    ring.finish(1)
    ring.finish(0)
    for copy in pair:
        copy.wait_send()
    for block in range(rows // LANES):
        hand_over(block).wait_send()


def settle(count, back, experts, gates, grad_logit, tokens, joint, grad_residual, grad_norms, part_output):
    rows, width = tokens.shape
    shard_rows = width // count
    f32, bf = jnp.float32, jnp.bfloat16
    V = pltpu.VMEM
    return pl.pallas_call(
        functools.partial(settle_kernel, count),
        out_shape=[jax.ShapeDtypeStruct((rows, width), f32), jax.ShapeDtypeStruct((shard_rows, JOINT), f32),
                   jax.ShapeDtypeStruct((part_output.shape[1], width), f32)],
        in_specs=[VMEM] * 5 + [ANY, ANY, VMEM, ANY],
        out_specs=[VMEM, VMEM, ANY],
        scratch_shapes=[V((rows, JOINT), bf), V((rows, JOINT // 2), bf), V((rows, width), bf), V((width, 2 * rows), bf), V((8, width), f32), V((width, LANES), f32),
                        V((width, JOINT), bf), V((rows, width), f32)]
        + Scatter.scratch(count, (SPLITS["joint"], SPLITS["output"]), [shard_rows, part_output.shape[1]])
        + [DMA((2 + rows // LANES,)), DMA((2 + rows // LANES,)), DMA((2,))],
        compiler_params=pltpu.CompilerParams(collective_id=5, has_side_effects=True, vmem_limit_bytes=60 << 20),
    )(back, experts, gates, grad_logit, tokens, joint, grad_residual, grad_norms, part_output)


def publish_kernel(joint_w, output_w, inner_w, outer_w, layer, tokens_in,
                   query, key, value, value_router, output_router, norms, output_out, inner_out, outer_out, layer_out, tokens_out,
                   *refs):
    held, turned, tail, load, store = refs[:6], refs[6], refs[7], refs[8], refs[9]
    sources = (joint_w, tokens_in, inner_w, outer_w, layer, output_w)
    loads = [pltpu.make_async_copy(src, buf, load.at[i]) for i, (src, buf) in enumerate(zip(sources, held))]
    for copy in loads:
        copy.start()
    half, small = inner_w.shape[1] // 2, CHUNK // 2
    stores = []

    def put(src, dst):
        copy = pltpu.make_async_copy(src, dst, store.at[len(stores)])
        copy.start()
        stores.append(copy)

    loads[0].wait()
    turned[...] = held[0][...].T
    for first, target in ((0, query), (QCOLS, key), (2 * QCOLS, value), (ROUTERS, value_router)):
        put(turned.at[pl.ds(first, target.shape[0])], target)
    tail[...] = turned[ROUTERS + HEADS * EXP : NORM, :]
    put(tail, output_router)
    norms[...] = turned[NORM : NORM + 8, :]
    for i, target in enumerate((tokens_out, inner_out, outer_out, layer_out, output_out)):
        loads[1 + i].wait()
        if i != 1:
            put(held[1 + i], target)
            continue
        for core in range(2):
            for chunk in range(half // small):
                put(held[1 + i].at[:, pl.ds(core * half + chunk * small, small)], target.at[:, pl.ds(chunk * CHUNK + core * small, small)])
    for copy in stores:
        copy.wait()


def publish(joint_w, output_w, inner_w, outer_w, layer, tokens):
    rows = joint_w.shape[0]
    f32 = jnp.float32
    columns = [QCOLS, QCOLS, VCOLS, HEADS * EXP, HEADS * EXP]
    rest = (output_w, inner_w, outer_w, layer, tokens)
    return pl.pallas_call(
        publish_kernel,
        out_shape=[jax.ShapeDtypeStruct((c, rows), f32) for c in columns] + [jax.ShapeDtypeStruct((8, rows), f32)]
        + [jax.ShapeDtypeStruct(x.shape, x.dtype) for x in rest],
        in_specs=[ANY] * 6,
        out_specs=[ANY] * 5 + [VMEM] + [ANY] * 5,
        scratch_shapes=[pltpu.VMEM(x.shape, x.dtype) for x in (joint_w, tokens, inner_w, outer_w, layer, output_w)]
        + [pltpu.VMEM((JOINT, rows), f32), pltpu.VMEM((HEADS * EXP, rows), f32)]
        + [DMA((6,)), DMA((9 + inner_w.shape[1] // (CHUNK // 2),))],
        compiler_params=pltpu.CompilerParams(vmem_limit_bytes=63 << 20),
    )(joint_w, *rest)


def on_device(
    tokens, value_routes, output_routes, cont_gap, query_weight, key_weight, value_weight, value_router,
    output_router, output_weight, norm_gain, norm_bias, inner_weight, outer_weight, cotangent,
):
    count = lax.axis_size("fsdp")
    inputs = tokens[0]
    rows, width = inputs.shape
    norm = jnp.stack([norm_gain, norm_bias])
    routes = jnp.concatenate([value_routes[0].reshape(rows, -1), output_routes[0].reshape(rows, -1)], axis=1)
    joint, tables, turned, qkv, experts, gates, norms = project(
        count, query_weight.T, key_weight.T, value_weight.T, value_router.T, output_router.T, norm, inputs, routes, cont_gap)
    att, store, outputs, logs, inner_full, outer_full, output_full = attend(
        count, qkv, tables, (inner_weight, outer_weight, output_weight), (SPLITS["inner"], SPLITS["outer"], SPLITS["output"]))
    layer, grad_residual, grad_att, grad_logit, grad_norms, part_output, part_inner, outer_w = feed(
        count, att, gates, inputs, cotangent[0], norms, output_full.reshape(VCOLS, width), inner_full.reshape(width, -1),
        outer_full.reshape(-1, width))
    back, inner_w = retreat(
        count, grad_att, turned, store, outputs, logs, part_inner.reshape(count, -1, part_inner.shape[1]), INNER_PARTS)
    grad_input, joint_w, output_w = settle(
        count, back, experts, gates, grad_logit, inputs, joint, grad_residual, grad_norms,
        part_output.reshape(count, -1, part_output.shape[1]))
    query, key, value, value_r, output_r, norm_w, output_w, inner_w, outer_w, layer, grad_input = publish(
        joint_w, output_w, inner_w, outer_w, layer, grad_input)
    return (layer[None], grad_input[None], query.T, key.T, value.T, value_r.T, output_r.T, output_w, norm_w[0], norm_w[1], inner_w, outer_w)


def solution(mesh):
    wide = P("fsdp", None)
    part = P("fsdp", "seq", None)
    routes = P("fsdp", "seq", None, None)
    return jax.shard_map(
        on_device,
        mesh=mesh,
        in_specs=(part, routes, routes, P()) + (wide,) * 6 + (P("fsdp"), P("fsdp"), wide, wide, part),
        out_specs=(part, part) + (wide,) * 6 + (P("fsdp"), P("fsdp"), wide, wide),
        check_vma=False,
    )
```

```python
import functools
import jax
import jax.numpy as jnp
from jax import lax
from jax.experimental import pallas as pl
from jax.experimental.pallas import tpu as pltpu
from jax.sharding import PartitionSpec as P

HEADS = 4
DH = 112
EXP = 5
CONT = 1024
GSLOTS = 4
PSLOTS = 2
BLOCK = 512
LANES = 128
EPSILON = 1e-05
NEGATIVE = -1e30
LOG2E = 1.4426950408889634
MESH = pl.DeviceIdType.MESH
ANY = pl.BlockSpec(memory_space=pl.ANY)
VMEM = pl.BlockSpec(memory_space=pltpu.VMEM)
SMEM = pl.BlockSpec(memory_space=pltpu.SMEM)
DMA = pltpu.SemaphoreType.DMA

QCOLS = HEADS * DH
VCOLS = HEADS * EXP * DH
ROUTERS = 2 * QCOLS + VCOLS
NORM = ROUTERS + 2 * HEADS * EXP
JOINT = 3328
SPLITS = {"joint": (640, 512), "output": (256, 128), "inner": (768, 640), "outer": (256, 128)}
INNER_PARTS = ((512, 768),)


def ring_place(index, count):
    return (index // 2) * (1 - index % 2) + (count - 1 - index // 2) * (index % 2)


def ring_index(place, count):
    upper = place // (count // 2)
    return 2 * place * (1 - upper) + (2 * (count - 1 - place) + 1) * upper


def enter(devices):
    barrier = pltpu.get_barrier_semaphore()
    for device in devices:
        pl.semaphore_signal(barrier, inc=1, device_id=device, device_id_type=MESH)
    pl.semaphore_wait(barrier, len(devices))


class Ring:
    def __init__(self, count, splits):
        self.count, self.splits = count, splits
        self.seq, self.fsdp = lax.axis_index("seq"), lax.axis_index("fsdp")
        self.plane, self.core = self.seq // 2, self.seq % 2
        self.place = ring_place(self.fsdp, count)
        self.right = (self.seq, ring_index((self.place + 1) % count, count))
        self.left = (self.seq, ring_index((self.place + count - 1) % count, count))
        self.core_mate = (self.seq + 1 - 2 * self.core, self.fsdp)
        self.plane_mate = ((self.seq + 2) % 4, self.fsdp)
        self.far = count // 2

    def neighbours(self):
        return [self.right, self.left, self.core_mate, self.plane_mate]

    def reach(self, kind, way):
        return self.far if kind == way else self.count - 1 - self.far

    def kinds(self, t):
        return [kind for kind in (1, 0) if self.splits[t][kind] > 0]

    def half(self, t):
        return self.splits[t][0] + 2 * self.splits[t][1]

    def cols(self, t, kind, plane, core):
        both, single = self.splits[t]
        if kind == 0:
            return pl.ds(pl.multiple_of(core * self.half(t), LANES), both)
        return pl.ds(pl.multiple_of(core * self.half(t) + both + plane * single, LANES), single)

    def behind(self, way, k):
        step = self.count - k if way == 0 else k
        return ring_index((self.place + step) % self.count, self.count)

    def next(self, way):
        return self.right if way == 0 else self.left

    def slot(self, kind, way, k):
        return k - 1 if way == 0 else self.reach(kind, 0) + k - 1


class Gather(Ring):
    def __init__(self, count, splits, shards, at, send, recv, local):
        super().__init__(count, splits)
        self.shards, self.at, self.send, self.recv, self.local = shards, at, send, recv, local

    @staticmethod
    def sems(count, tensors):
        return [DMA((6 * tensors * (count - 1),)), DMA((6 * tensors * (count - 1),)), DMA((tensors,))]

    def copy(self, src, dst, group, t, slot, device):
        i = (group * len(self.splits) + t) * (self.count - 1) + slot
        return pltpu.make_async_remote_copy(
            src, dst, self.send.at[i], self.recv.at[i], device_id=device, device_id_type=MESH
        )

    def same(self, group, t, kind, way, k, plane, core, device):
        ref = self.at(t, self.behind(way, k), self.cols(t, kind, plane, core))
        return self.copy(ref, ref, group, t, self.slot(kind, way, k), device)

    def hop(self, t, kind, way, k):
        if k > 1:
            ref = self.at(t, self.behind(way, k - 1), self.cols(t, kind, self.plane, self.core))
            return self.copy(ref, ref, kind, t, self.slot(kind, way, k), self.next(way))
        cols = self.cols(t, kind, self.plane, self.core)
        return self.copy(
            self.shards[t].at[:, cols], self.at(t, self.fsdp, cols), kind, t, self.slot(kind, way, 1), self.next(way)
        )

    def arrived(self, t, kind, way, k):
        return self.same(kind, t, kind, way, k, self.plane, self.core, self.next(way))

    def to_core(self, t, kind, way, k, core):
        return self.same(2 + kind, t, kind, way, k, self.plane, core, self.core_mate)

    def to_plane(self, t, way, k, plane):
        return self.same(4, t, 1, way, k, plane, self.core, self.plane_mate)

    def plane_to_core(self, t, way, k, core):
        return self.same(5, t, 1, way, k, 1 - self.plane, core, self.core_mate)

    def own(self, t):
        return pltpu.make_async_copy(self.shards[t], self.at(t, self.fsdp, slice(None)), self.local.at[t])

    def start(self, t):
        for kind in self.kinds(t):
            for way in (0, 1):
                if self.reach(kind, way):
                    self.hop(t, kind, way, 1).start()
        self.own(t).start()

    def arrive(self, t, k):
        for kind in self.kinds(t):
            for way in (0, 1):
                if k <= self.reach(kind, way):
                    self.arrived(t, kind, way, k).wait_recv()
                    if k < self.reach(kind, way):
                        self.hop(t, kind, way, k + 1).start()
                    if kind:
                        self.to_plane(t, way, k, self.plane).start()
                    self.to_core(t, kind, way, k, self.core).start()

    def plane_arrive(self, t, k):
        if 1 in self.kinds(t):
            for way in (0, 1):
                if k <= self.reach(1, way):
                    self.to_plane(t, way, k, 1 - self.plane).wait_recv()
                    self.plane_to_core(t, way, k, self.core).start()

    def finish(self, t):
        self.own(t).wait()
        for kind in self.kinds(t):
            for way in (0, 1):
                for k in range(1, self.reach(kind, way) + 1):
                    self.hop(t, kind, way, k).wait_send()
                    self.to_core(t, kind, way, k, self.core).wait_send()
                    self.to_core(t, kind, way, k, 1 - self.core).wait_recv()
                    if kind:
                        self.to_plane(t, way, k, self.plane).wait_send()
                        self.plane_to_core(t, way, k, self.core).wait_send()
                        self.plane_to_core(t, way, k, 1 - self.core).wait_recv()

    def events(self):
        tensors = range(len(self.splits))
        out = []
        for k in range(1, self.far + 1):
            for t in tensors:
                out.append(functools.partial(self.arrive, t, k))
                if k > 1:
                    out.append(functools.partial(self.plane_arrive, t, k - 1))
        for t in tensors:
            out.append(functools.partial(self.plane_arrive, t, self.far))
        for t in tensors:
            out.append(functools.partial(self.finish, t))
        return out


TABLE = 5632
TABLE_ZERO = 5120
TURNED_ZERO = 512


def route_lanes(routes, lane):
    hit = None
    for head in range(2 * HEADS):
        for choice in range(2):
            place = head * EXP + routes[:, 2 * head + choice : 2 * head + choice + 1]
            here = lane == place
            hit = here if hit is None else hit | here
    return hit.astype(jnp.float32)


def project_kernel(count, query, key, value, value_router, output_router, norm, tokens, routes, gaps,
                   joint_out, tables_out, turned_out, qkv, experts, gates, norms,
                   shard, shard_t, joint, tables, turned_tables, product, load, store, send, recv, local):
    rows = shard.shape[0]
    splits = (SPLITS["joint"],)
    at = lambda t, g, cols: joint.at[pl.ds(pl.multiple_of(g * rows, rows), rows), cols]
    ring = Gather(count, splits, [shard], at, send, recv, local)
    loads = []
    for i, (src, first) in enumerate(((query, 0), (key, QCOLS), (value, 2 * QCOLS))):
        loads.append(pltpu.make_async_copy(src, shard_t.at[pl.ds(first, src.shape[0])], load.at[i]))
        loads[-1].start()
    small = [ref[...].astype(jnp.float32) for ref in (value_router, output_router, norm)]
    small.append(jnp.zeros((JOINT - NORM - 2, rows), jnp.float32))
    shard_t[ROUTERS:, :] = jnp.concatenate(small, axis=0).astype(jnp.bfloat16)
    for copy in loads:
        copy.wait()
    shard[...] = shard_t[...].T
    enter(ring.neighbours())
    ring.start(0)
    slope = jnp.float32(0.0)
    for head in range(HEADS):
        slope = jnp.where(ring.seq // 1 == head, -0.5 * 0.5**head * LOG2E, slope)
    group = ring.fsdp // GSLOTS
    pair = jnp.maximum(ring.fsdp % GSLOTS - PSLOTS, 0) * 2
    gap_values = [jnp.int32(0), gaps[group, pair], gaps[group, pair + 1]]

    def table_column(step, carry):
        start = pl.multiple_of(step * 256, 256)
        lanes = lax.broadcasted_iota(jnp.int32, (8, 256 + LANES), 1) + (start - LANES)
        for which in range(3):
            for turned in range(2):
                if turned:
                    distance = lanes - TURNED_ZERO + gap_values[which]
                else:
                    distance = TABLE_ZERO - lanes + gap_values[which]
                bias = slope * jnp.log(1.0 + jnp.maximum(distance, 0).astype(jnp.float32))
                bias = jnp.where(distance >= 0, bias, NEGATIVE)
                wide = jnp.broadcast_to(bias[:1], (LANES, 256 + LANES))
                rolled = pltpu.roll(wide, 0, 1, stride=1, stride_axis=0)
                target = turned_tables if turned else tables
                target[which, :, pl.ds(start, 256)] = rolled[:, LANES:]
        return carry

    events = []
    for k in range(1, ring.far + 1):
        events.append(functools.partial(ring.arrive, 0, k))
        if k > 1:
            events.append(functools.partial(ring.plane_arrive, 0, k - 1))
    events += [functools.partial(ring.plane_arrive, 0, ring.far), functools.partial(ring.finish, 0)]
    cut = max(1, TABLE // 256 // (len(events) - 2))
    done = 0
    saves = [(tables, tables_out), (turned_tables, turned_out), (joint, joint_out)]
    saves = [pltpu.make_async_copy(src, dst, store.at[i]) for i, (src, dst) in enumerate(saves)]
    for i, event in enumerate(events):
        upto = min(TABLE // 256, (i + 1) * cut)
        if i == len(events) - 2:
            upto = TABLE // 256
        if upto > done:
            lax.fori_loop(done, upto, table_column, 0)
            done = upto
            if done == TABLE // 256:
                saves[0].start()
                saves[1].start()
        event()
    saves[2].start()

    def column(step, carry):
        cols = pl.ds(pl.multiple_of(step * 256, 256), 256)
        product[:, cols] = jnp.dot(tokens[...], joint[:, cols], preferred_element_type=jnp.float32)
        return carry

    lax.fori_loop(0, JOINT // 256, column, 0)
    norm_tile = NORM // LANES * LANES
    turned_norm = joint[:, norm_tile : norm_tile + LANES].astype(jnp.float32).T
    norms[...] = turned_norm[NORM - norm_tile : NORM - norm_tile + 8]
    logits = product[:, ROUTERS : ROUTERS + 2 * HEADS * EXP]
    local_rows = tokens.shape[0]
    wide = jnp.concatenate([logits, jnp.zeros((local_rows, LANES - 2 * HEADS * EXP), jnp.float32)], axis=1)
    lane = lax.broadcasted_iota(jnp.int32, (local_rows, LANES), 1)
    mask = route_lanes(routes[...], lane)
    gate = 1.0 / (1.0 + jnp.exp(-wide))
    gates[0] = gate * mask
    gates[1] = gate * mask * (1.0 - gate)
    pad = jnp.zeros((local_rows, LANES - DH), jnp.float32)
    ones = jnp.ones((local_rows, LANES - DH), jnp.float32)
    for head in range(HEADS):
        first = head * DH
        qkv[head, 0] = jnp.concatenate([product[:, first : first + DH], pad], axis=1).astype(jnp.bfloat16)
        first = QCOLS + head * DH
        qkv[head, 1] = jnp.concatenate([product[:, first : first + DH], pad], axis=1).astype(jnp.bfloat16)
        total = None
        for expert in range(EXP):
            which = head * EXP + expert
            first = 2 * QCOLS + which * DH
            piece = product[:, first : first + DH]
            experts[which] = jnp.concatenate([piece, pad], axis=1).astype(jnp.bfloat16)
            term = piece * gates[0, :, which : which + 1]
            total = term if total is None else total + term
        qkv[head, 2] = jnp.concatenate([total, ones], axis=1).astype(jnp.bfloat16)
    for copy in saves:
        copy.wait()


def project(count, query, key, value, value_router, output_router, norm, tokens, routes, gaps):
    rows, shard_rows = tokens.shape[0], query.shape[1]
    f32, bf = jnp.float32, jnp.bfloat16
    V = pltpu.VMEM
    return pl.pallas_call(
        functools.partial(project_kernel, count),
        out_shape=[
            jax.ShapeDtypeStruct((shard_rows * count, JOINT), bf),
            jax.ShapeDtypeStruct((3, LANES, TABLE), f32),
            jax.ShapeDtypeStruct((3, LANES, TABLE), f32),
            jax.ShapeDtypeStruct((HEADS, 3, rows, LANES), bf),
            jax.ShapeDtypeStruct((HEADS * EXP, rows, LANES), bf),
            jax.ShapeDtypeStruct((2, rows, LANES), f32),
            jax.ShapeDtypeStruct((8, shard_rows * count), f32),
        ],
        in_specs=[ANY] * 3 + [VMEM] * 5 + [SMEM],
        out_specs=[ANY] * 3 + [VMEM] * 4,
        scratch_shapes=[
            V((shard_rows, JOINT), bf), V((JOINT, shard_rows), bf), V((shard_rows * count, JOINT), bf),
            V((3, LANES, TABLE), f32), V((3, LANES, TABLE), f32), V((rows, JOINT), f32), DMA((3,)), DMA((3,)),
        ]
        + Gather.sems(count, 1),
        compiler_params=pltpu.CompilerParams(collective_id=1, has_side_effects=True, vmem_limit_bytes=62 << 20),
    )(query, key, value, value_router, output_router, norm, tokens, routes, gaps)


def seq_mates(ring):
    return [ring.core_mate, ring.plane_mate, (3 - ring.seq, ring.fsdp)]


def slot_mates(ring):
    f = ring.fsdp
    return [(ring.seq, f + 1 - 2 * (f % 2)), (ring.seq, f + 2 - 4 * ((f // 2) % 2))]


def tile_place(slot, seq, phase, key_block, query_block):
    cont = slot // PSLOTS
    own = 1 - jnp.minimum(phase, 1)
    piece = jnp.where(slot == 3, 2 - phase, phase - 1)
    source = jnp.where(phase == 0, 0, 1 + piece)
    first = cont * 2 * (query_block // 2)
    active = jnp.where(
        phase == 0,
        (key_block <= query_block) & (key_block >= first),
        jnp.where(phase == 1, slot >= 1, slot >= 2),
    )
    far_column = jnp.where(
        cont == 1,
        2048 * piece + BLOCK * key_block - BLOCK * (query_block % 2) - 4096,
        BLOCK * key_block - 2048 - BLOCK * query_block,
    )
    column = jnp.where(phase == 0, BLOCK * (key_block - query_block), far_column)
    table = jnp.where((phase > 0) & (cont == 1), 1 + query_block // 2, 0)
    return source, active, table, column


STRIP = 512


def near_first(ring, j):
    odd, high = j % 2, j // 2
    core = ring.core + odd - 2 * ring.core * odd
    plane = ring.plane + high - 2 * ring.plane * high
    return 2 * plane + core


def block_rows(block):
    return pl.ds(pl.multiple_of(block * BLOCK, BLOCK), BLOCK)


def attend_kernel(count, splits, steps, qkv, tables_in, *refs):
    T = len(splits)
    shards, refs = refs[:T], refs[T:]
    att, store, outputs, logs = refs[:4]
    fulls, refs = refs[4 : 4 + T], refs[4 + T :]
    acc, top, att_low, tables, kv_send, kv_recv, q_send, q_recv, sh_send, sh_recv, out_send, out_recv, here = refs[:13]
    at = lambda t, g, cols: fulls[t].at[g, :, cols]
    ring = Gather(count, splits, shards, at, *refs[13:])
    table_load = pltpu.make_async_copy(tables_in, tables, here.at[2])
    table_load.start()
    seq, slot = ring.seq, ring.fsdp % GSLOTS
    mates, (x_mate, z_mate) = seq_mates(ring), slot_mates(ring)
    enter(ring.neighbours() + mates[2:] + [x_mate, z_mate])

    def remote(src, dst, send, recv, device):
        return pltpu.make_async_remote_copy(src, dst, send, recv, device_id=device, device_id_type=MESH)

    mine = block_rows(seq)

    def kv_copy(mate):
        return remote(qkv.at[mate[0], pl.ds(1, 2)], store.at[pl.ds(1, 2), mine], kv_send.at[mate[0]], kv_recv.at[seq], mate)

    def q_copy(mate):
        return remote(qkv.at[mate[0], 0], store.at[0, mine], q_send.at[mate[0]], q_recv.at[seq], mate)

    for mate in mates[1:] + mates[:1]:
        kv_copy(mate).start()
    own_copy = pltpu.make_async_copy(qkv.at[seq], store.at[pl.ds(0, 3), mine], here.at[0])
    own_copy.start()
    for mate in mates[1:] + mates[:1]:
        q_copy(mate).start()
    acc[...] = jnp.zeros_like(acc)
    top[...] = jnp.full_like(top, NEGATIVE)

    def far_rows(piece, chunk):
        return store.at[pl.ds(3 + 2 * piece, 2), block_rows(near_first(ring, chunk))]

    def first_hop(chunk, way):
        src = store.at[pl.ds(1, 2), block_rows(near_first(ring, chunk))]
        piece = slot % 2
        return remote(src, far_rows(piece, chunk), sh_send.at[4 * way + chunk], sh_recv.at[4 * piece + chunk],
                      x_mate if way == 0 else z_mate)

    def second_hop(chunk):
        piece = slot % 2
        return remote(far_rows(piece, chunk), far_rows(piece, chunk), sh_send.at[8 + chunk], sh_recv.at[4 * piece + chunk], x_mate)

    def share(chunk):
        @pl.when(slot < 2)
        def _():
            first_hop(chunk, 1).start()

        @pl.when(slot == 0)
        def _():
            first_hop(chunk, 0).start()

    def pass_on(chunk):
        @pl.when(slot >= 1)
        def _():
            piece = jnp.where(slot == 3, 1, 0)
            remote(far_rows(piece, chunk), far_rows(piece, chunk), sh_send.at[chunk], sh_recv.at[4 * piece + chunk], x_mate).wait_recv()

        @pl.when(slot >= 2)
        def _():
            second_hop(chunk).start()

    def last_piece(chunk):
        @pl.when(slot >= 2)
        def _():
            piece = 3 - slot
            remote(far_rows(piece, chunk), far_rows(piece, chunk), sh_send.at[chunk], sh_recv.at[4 * piece + chunk], x_mate).wait_recv()

    own_copy.wait()
    share(0)
    for chunk, mate in enumerate(mates):
        other = mate[0]
        src = store.at[pl.ds(1, 2), block_rows(other)]
        remote(src, src, kv_send.at[other], kv_recv.at[other], mate).wait_recv()
        share(1 + chunk)
    for mate in mates:
        src = store.at[0, block_rows(mate[0])]
        remote(src, src, q_send.at[mate[0]], q_recv.at[mate[0]], mate).wait_recv()

    def tile(source, table, column, key_block, first, rows):
        keys = store[1 + 2 * source, block_rows(key_block), :]
        values = store[2 + 2 * source, block_rows(key_block), :]
        for strip in range(rows // STRIP):
            part = pl.ds(pl.multiple_of(first + strip * STRIP, STRIP), STRIP)
            scores = lax.dot_general(store[0, part, :], keys, (((1,), (1,)), ((), ())), preferred_element_type=jnp.float32)
            start = column + TABLE_ZERO - strip * STRIP
            bias = [tables[table, :, pl.ds(pl.multiple_of(start - LANES * i, LANES), BLOCK)] for i in range(STRIP // LANES)]
            scores = scores * (DH**-0.5 * LOG2E) + jnp.concatenate(bias, axis=0)
            before = top[part, :]
            after = jnp.maximum(before, jnp.max(scores, axis=1, keepdims=True))
            terms = jnp.exp2(scores - after[:, :1])
            acc[part, :] = acc[part, :] * jnp.exp2(before - after) + jnp.dot(
                terms.astype(jnp.bfloat16), values, preferred_element_type=jnp.float32)
            top[part, :] = after

    def near_tile(step):
        key_block, query_block = near_first(ring, step // 4), step % 4
        source, active, table, column = tile_place(slot, seq, 0, key_block, query_block)

        @pl.when(active)
        def _():
            tile(source, table, column, key_block, query_block * BLOCK, BLOCK)

    def far_tile(step):
        phase, key_block, query_block = step // 8, near_first(ring, (step // 2) % 4), 2 * (step % 2)
        source, active, table, column = tile_place(slot, seq, phase, key_block, query_block)

        @pl.when(active)
        def _():
            tile(source, table, column, key_block, query_block * BLOCK, 2 * BLOCK)

    table_load.wait()
    events = {}
    for chunk in range(4):
        events.setdefault(4 * chunk + 3, []).append(functools.partial(pass_on, chunk))
        events.setdefault(24 + 2 * chunk, []).append(functools.partial(last_piece, chunk))
    begin, first, gap = steps
    for t in range(T):
        if begin + t < 0:
            ring.start(t)
        else:
            events.setdefault(begin + t, []).append(functools.partial(ring.start, t))
    rest = []
    for i, event in enumerate(ring.events()):
        step = int(first + gap * i)
        if step < 32:
            events.setdefault(step, []).append(event)
        else:
            rest.append(event)

    def step_body(step, carry):
        for when, actions in sorted(events.items()):
            @pl.when(step == when)
            def _():
                for action in actions:
                    action()
        pl.when(step < 16)(lambda: near_tile(step))
        pl.when(step >= 16)(lambda: far_tile(step - 8))
        return carry

    lax.fori_loop(0, 32, step_body, 0)
    total = acc[:, DH : DH + 1]
    result = acc[...] / total
    outputs[...] = result
    log_total = top[...] + jnp.log2(total)
    for block in range(4):
        logs[:, block * BLOCK : (block + 1) * BLOCK] = log_total[block * BLOCK : (block + 1) * BLOCK].T[:8]
    att_low[...] = result.astype(jnp.bfloat16)

    def out_copy(mate):
        return remote(att_low.at[block_rows(mate[0])], att.at[seq], out_send.at[mate[0]], out_recv.at[seq], mate)

    for mate in mates[1:] + mates[:1]:
        out_copy(mate).start()
    own_out = pltpu.make_async_copy(att_low.at[mine], att.at[seq], here.at[1])
    own_out.start()
    for event in rest:
        event()
    own_out.wait()
    for mate in mates:
        kv_copy(mate).wait_send()
        q_copy(mate).wait_send()
        out_copy(mate).wait_send()
        ref = att.at[mate[0]]
        remote(ref, ref, out_send.at[mate[0]], out_recv.at[mate[0]], mate).wait_recv()
    for chunk in range(4):
        @pl.when(slot < 2)
        def _():
            first_hop(chunk, 1).wait_send()

        @pl.when(slot == 0)
        def _():
            first_hop(chunk, 0).wait_send()

        @pl.when(slot >= 2)
        def _():
            second_hop(chunk).wait_send()


def attend(count, qkv, tables, shards, splits, steps=(0, 18, 2)):
    rows = qkv.shape[2]
    own = 4 * rows
    T = len(shards)
    return pl.pallas_call(
        functools.partial(attend_kernel, count, splits, steps),
        out_shape=[
            jax.ShapeDtypeStruct((HEADS, rows, LANES), jnp.bfloat16),
            jax.ShapeDtypeStruct((7, own, LANES), jnp.bfloat16),
            jax.ShapeDtypeStruct((own, LANES), jnp.float32),
            jax.ShapeDtypeStruct((8, own), jnp.float32),
        ]
        + [jax.ShapeDtypeStruct((count,) + w.shape, w.dtype) for w in shards],
        in_specs=[VMEM, ANY] + [VMEM] * T,
        out_specs=[VMEM] * 4 + [ANY] * T,
        scratch_shapes=[
            pltpu.VMEM((own, LANES), jnp.float32),
            pltpu.VMEM((own, LANES), jnp.float32),
            pltpu.VMEM((own, LANES), jnp.bfloat16),
            pltpu.VMEM((3, LANES, TABLE), jnp.float32),
            DMA((4,)), DMA((4,)), DMA((4,)), DMA((4,)), DMA((12,)), DMA((8,)), DMA((4,)), DMA((4,)), DMA((3,)),
        ]
        + Gather.sems(count, T),
        compiler_params=pltpu.CompilerParams(collective_id=2, has_side_effects=True, vmem_limit_bytes=56 << 20),
    )(qkv, tables, *shards)


class Scatter(Ring):
    def __init__(self, count, splits, parts, outs, bufs, sems):
        super().__init__(count, splits)
        self.parts, self.outs = parts, outs
        T = len(splits)
        self.mine, self.plane_in = bufs[:T], bufs[T : 2 * T]
        self.ring0, self.ring1 = bufs[2 * T : 3 * T], bufs[3 * T : 4 * T]
        self.low, self.low_in, self.done = bufs[4 * T : 5 * T], bufs[5 * T : 6 * T], bufs[6 * T : 7 * T]
        (self.load, self.plane_s, self.plane_r, self.ring_s, self.ring_r, self.end_s, self.end_r, self.put) = sems

    @staticmethod
    def scratch(count, splits, rows):
        half = [a + 2 * b for a, b in splits]
        bf = jnp.bfloat16
        out = [pltpu.VMEM((count, r, h), bf) for r, h in zip(rows, half)]
        out += [pltpu.VMEM((count, r, b), bf) for r, (a, b) in zip(rows, splits)]
        out += [pltpu.VMEM((count - 1 if a else 1, r, max(a, LANES)), bf) for r, (a, b) in zip(rows, splits)]
        out += [pltpu.VMEM((count - 1, r, b), bf) for r, (a, b) in zip(rows, splits)]
        out += [pltpu.VMEM((r, a + b), bf) for r, (a, b) in zip(rows, splits)]
        out += [pltpu.VMEM((r, a + b), bf) for r, (a, b) in zip(rows, splits)]
        out += [pltpu.VMEM((r, h), jnp.float32) for r, h in zip(rows, half)]
        T = len(splits)
        return out + [DMA((T * count,))] * 3 + [DMA((2 * T * (count - 1),))] * 2 + [DMA((2 * T,))] * 2 + [DMA((T,))]

    def dest(self, rel):
        return ring_index((self.place + rel) % self.count, self.count)

    def load_copy(self, t, rel):
        part, first = self.parts[t]
        src = part.at[self.dest(rel), :, pl.ds(first, self.half(t))]
        return pltpu.make_async_copy(src, self.mine[t].at[rel], self.load.at[t * self.count + rel])

    def remote(self, src, dst, s, r, i, device):
        return pltpu.make_async_remote_copy(src, dst, s.at[i], r.at[i], device_id=device, device_id_type=MESH)

    def single(self, t, plane):
        both, single = self.splits[t]
        return pl.ds(pl.multiple_of(both + plane * single, LANES), single)

    def plane_copy(self, t, rel):
        src = self.mine[t].at[rel, :, self.single(t, 1 - self.plane)]
        return self.remote(src, self.plane_in[t].at[rel], self.plane_s, self.plane_r, t * self.count + rel, self.plane_mate)

    def rels(self, D):
        return sorted({D % self.count, (-D) % self.count})

    def order(self):
        out = []
        for D in range(self.far, -1, -1):
            out += self.rels(D)
        return out

    def start(self, t):
        for rel in self.order():
            self.load_copy(t, rel).start()

    def ready(self, t, rel):
        if self.parts[t]:
            self.load_copy(t, rel).wait()
        self.plane_copy(t, rel).start()

    def all_ready(self, t):
        for rel in self.order():
            self.ready(t, rel)

    def step(self, t, D):
        self.combine(t, D)
        if D:
            self.chain(t, D)
        else:
            self.close(t)

    def buffer(self, t, kind, slot):
        if kind:
            return self.ring1[t].at[slot]
        return self.ring0[t].at[slot]

    def own_ref(self, t, kind, rel):
        if kind:
            return self.mine[t].at[rel, :, self.single(t, self.plane)]
        return self.mine[t].at[rel, :, pl.ds(0, self.splits[t][0])]

    def ring_copy(self, t, kind, way, D):
        slot = self.slot(kind, way, D)
        if D == self.reach(kind, way):
            src = self.own_ref(t, kind, D % self.count if way == 0 else (-D) % self.count)
        else:
            src = self.buffer(t, kind, self.slot(kind, way, D + 1))
        i = (2 * t + kind) * (self.count - 1) + slot
        return self.remote(src, self.buffer(t, kind, slot), self.ring_s, self.ring_r, i, self.next(way))

    def ring_wait(self, t, kind, way, D):
        slot = self.slot(kind, way, D)
        ref = self.buffer(t, kind, slot)
        i = (2 * t + kind) * (self.count - 1) + slot
        self.remote(ref, ref, self.ring_s, self.ring_r, i, self.next(way)).wait_recv()

    def combine(self, t, D):
        for rel in self.rels(D):
            self.plane_copy(t, rel).wait_send()
            ref = self.plane_in[t].at[rel]
            self.remote(ref, ref, self.plane_s, self.plane_r, t * self.count + rel, self.plane_mate).wait_recv()
            own = self.own_ref(t, 1, rel)
            own[...] = (own[...].astype(jnp.float32) + self.plane_in[t][rel].astype(jnp.float32)).astype(jnp.bfloat16)

    def chain(self, t, D):
        for kind in self.kinds(t):
            for way in (0, 1):
                if D > self.reach(kind, way):
                    continue
                if D < self.reach(kind, way):
                    self.ring_wait(t, kind, way, D + 1)
                    rel = D % self.count if way == 0 else (-D) % self.count
                    ref = self.buffer(t, kind, self.slot(kind, way, D + 1))
                    ref[...] = (ref[...].astype(jnp.float32) + self.own_ref(t, kind, rel)[...].astype(jnp.float32)).astype(jnp.bfloat16)
                self.ring_copy(t, kind, way, D).start()

    def end_copy(self, t):
        return self.remote(self.low[t], self.low_in[t], self.end_s, self.end_r, 2 * t, self.plane_mate)

    def close(self, t):
        both, single = self.splits[t]
        for kind in self.kinds(t):
            total = self.own_ref(t, kind, 0)[...].astype(jnp.float32)
            for way in (0, 1):
                if self.reach(kind, way):
                    self.ring_wait(t, kind, way, 1)
                    total = total + self.buffer(t, kind, self.slot(kind, way, 1))[...].astype(jnp.float32)
            if kind:
                self.low[t][:, both:] = total.astype(jnp.bfloat16)
            else:
                self.low[t][:, :both] = total.astype(jnp.bfloat16)
        self.end_copy(t).start()

    def out_ref(self, t, core):
        out, whole, first = self.outs[t]
        return out.at[:, pl.ds(pl.multiple_of(core * whole + first, LANES), self.half(t))]

    def out_copy(self, t):
        return self.remote(self.done[t], self.out_ref(t, self.core), self.end_s, self.end_r, 2 * t + 1, self.core_mate)

    def put_copy(self, t):
        return pltpu.make_async_copy(self.done[t], self.out_ref(t, self.core), self.put.at[t])

    def deliver(self, t):
        both, single = self.splits[t]
        self.end_copy(t).wait_send()
        ref = self.low_in[t]
        self.remote(ref, ref, self.end_s, self.end_r, 2 * t, self.plane_mate).wait_recv()
        if both:
            self.done[t][:, :both] = self.low[t][:, :both].astype(jnp.float32) + self.low_in[t][:, :both].astype(jnp.float32)
        if single:
            self.done[t][:, self.single(t, self.plane)] = self.low[t][:, both:].astype(jnp.float32)
            self.done[t][:, self.single(t, 1 - self.plane)] = self.low_in[t][:, both:].astype(jnp.float32)
        self.out_copy(t).start()
        self.put_copy(t).start()

    def finish(self, t):
        for kind in self.kinds(t):
            for way in (0, 1):
                for D in range(1, self.reach(kind, way) + 1):
                    self.ring_copy(t, kind, way, D).wait_send()
        self.out_copy(t).wait_send()
        self.put_copy(t).wait()
        ref = self.out_ref(t, 1 - self.core)
        self.remote(ref, ref, self.end_s, self.end_r, 2 * t + 1, self.core_mate).wait_recv()


def retreat_kernel(count, splits, steps, grad_att, turned_in, store_in, outputs, logs, part, back, out, *refs):
    T = len(splits)
    (grads, delta, grad_q, grad_kv, send_kv, kv_in0, kv_in1, low, in_send, in_recv, up_send, up_recv,
     turned, store, out_send, out_recv, here) = refs[:17]
    refs = refs[17:]
    loads = [pltpu.make_async_copy(turned_in, turned, here.at[2]), pltpu.make_async_copy(store_in, store, here.at[3])]
    for copy in loads:
        copy.start()
    halves = [a + 2 * b for a, b in splits]
    firsts = [sum(halves[:t]) for t in range(T)]
    ring = Scatter(
        count, splits, [(part, first) for first in firsts], [(out, sum(halves), first) for first in firsts],
        refs[: 7 * T], refs[7 * T :])
    seq, slot = ring.seq, ring.fsdp % GSLOTS
    mates, (x_mate, z_mate) = seq_mates(ring), slot_mates(ring)
    enter(ring.neighbours() + mates[2:] + [x_mate, z_mate])

    def remote(src, dst, send, recv, device):
        return pltpu.make_async_remote_copy(src, dst, send, recv, device_id=device, device_id_type=MESH)

    mine = block_rows(seq)

    def in_copy(mate):
        return remote(grad_att.at[mate[0]], grads.at[mine], in_send.at[mate[0]], in_recv.at[seq], mate)

    for mate in mates[1:] + mates[:1]:
        in_copy(mate).start()
    own_copy = pltpu.make_async_copy(grad_att.at[seq], grads.at[mine], here.at[0])
    own_copy.start()
    grad_q[...] = jnp.zeros_like(grad_q)
    grad_kv[...] = jnp.zeros_like(grad_kv)
    own_copy.wait()
    for mate in mates:
        ref = grads.at[block_rows(mate[0])]
        remote(ref, ref, in_send.at[mate[0]], in_recv.at[mate[0]], mate).wait_recv()
    for block in range(4):
        rows = pl.ds(block * BLOCK, BLOCK)
        sums = jnp.sum(grads[rows, :].astype(jnp.float32) * outputs[rows, :], axis=1, keepdims=True)
        delta[:, rows] = jnp.broadcast_to(sums, (BLOCK, LANES)).T[:8]

    for copy in loads:
        copy.wait()

    def tile(forward_phase, key_block, query_block, blocks):
        source, active, table, column = tile_place(slot, seq, forward_phase, key_block, query_block)

        @pl.when(active)
        def _():
            size = blocks * BLOCK
            key_rows, rows = block_rows(key_block), pl.ds(pl.multiple_of(query_block * BLOCK, BLOCK), size)
            keys, values = store[1 + 2 * source, key_rows, :], store[2 + 2 * source, key_rows, :]
            queries, tops = store[0, rows, :], grads[rows, :]
            scores = lax.dot_general(keys, queries, (((1,), (1,)), ((), ())), preferred_element_type=jnp.float32)
            bias = jnp.concatenate(
                [turned[table, :, pl.ds(pl.multiple_of(TURNED_ZERO - column - LANES * part, LANES), size)] for part in range(BLOCK // LANES)],
                axis=0,
            )
            weights = jnp.exp2(scores * (DH**-0.5 * LOG2E) + (bias - logs[:1, rows]))
            grad_weights = lax.dot_general(values, tops, (((1,), (1,)), ((), ())), preferred_element_type=jnp.float32)
            grad_scores = (weights * (grad_weights - delta[:1, rows])).astype(jnp.bfloat16)
            grad_kv[source, 1, key_rows, :] += jnp.dot(weights.astype(jnp.bfloat16), tops, preferred_element_type=jnp.float32)
            grad_kv[source, 0, key_rows, :] += jnp.dot(grad_scores, queries, preferred_element_type=jnp.float32)
            grad_q[rows, :] += lax.dot_general(grad_scores, keys, (((0,), (0,)), ((), ())), preferred_element_type=jnp.float32)

    def far_tile(step):
        phase = step // 8
        piece = jnp.where(slot == 2, 1 - phase, phase)
        tile(jnp.where(slot == 3, 2 - piece, 1 + piece), (step // 2) % 4, 2 * (step % 2), 2)

    def near_tile(step):
        tile(0, step // 4, step % 4, 1)

    scale = DH**-0.5

    def rounded(source, chunk, extra):
        rows = block_rows(chunk)
        keys = grad_kv[source, 0, rows, :] * scale
        values = grad_kv[source, 1, rows, :]
        for more in extra:
            keys = keys + more[0].astype(jnp.float32)
            values = values + more[1].astype(jnp.float32)
        return keys.astype(jnp.bfloat16), values.astype(jnp.bfloat16)

    def x_send(chunk):
        src = send_kv.at[0, :, block_rows(chunk)]
        return remote(src, kv_in0.at[:, block_rows(chunk)], up_send.at[chunk], up_recv.at[chunk], x_mate)

    def z_send(chunk):
        src = send_kv.at[1, :, block_rows(chunk)]
        return remote(src, kv_in1.at[:, block_rows(chunk)], up_send.at[4 + chunk], up_recv.at[4 + chunk], z_mate)

    def x_wait(chunk):
        ref = kv_in0.at[:, block_rows(chunk)]
        remote(ref, ref, up_send.at[chunk], up_recv.at[chunk], x_mate).wait_recv()

    def z_wait(chunk):
        ref = kv_in1.at[:, block_rows(chunk)]
        remote(ref, ref, up_send.at[4 + chunk], up_recv.at[4 + chunk], z_mate).wait_recv()

    def first_done(chunk):
        @pl.when(slot >= 1)
        def _():
            source = jnp.where(slot == 2, 2, 1)
            keys, values = rounded(source, chunk, [])
            send_kv[0, 0, block_rows(chunk), :] = keys
            send_kv[0, 1, block_rows(chunk), :] = values
            x_send(chunk).start()

    def second_done(chunk):
        @pl.when(slot >= 2)
        def _():
            x_wait(chunk)
            source = slot - 1
            keys, values = rounded(source, chunk, [kv_in0[:, block_rows(chunk), :]])
            send_kv[1, 0, block_rows(chunk), :] = keys
            send_kv[1, 1, block_rows(chunk), :] = values
            z_send(chunk).start()

    def out_copy(mate):
        src = low.at[:, block_rows(mate[0])]
        return remote(src, back.at[seq], out_send.at[mate[0]], out_recv.at[seq], mate)

    def own_done(chunk):
        rows = block_rows(chunk)
        low[0, rows, :] = (grad_q[rows, :] * scale).astype(jnp.bfloat16)

        @pl.when(slot == 0)
        def _():
            x_wait(chunk)
            z_wait(chunk)
            low[1, rows, :], low[2, rows, :] = rounded(0, chunk, [kv_in0[:, rows, :], kv_in1[:, rows, :]])

        @pl.when(slot == 1)
        def _():
            z_wait(chunk)
            low[1, rows, :], low[2, rows, :] = rounded(0, chunk, [kv_in1[:, rows, :]])

        @pl.when(slot >= 2)
        def _():
            low[1, rows, :], low[2, rows, :] = rounded(0, chunk, [])

    events = {}
    for chunk in range(4):
        events.setdefault(2 * chunk + 2, []).append(functools.partial(first_done, chunk))
        events.setdefault(10 + 2 * chunk, []).append(functools.partial(second_done, chunk))
    begin, ready, first, hop, lag = steps
    rest = []
    for t in range(T):
        plan = [(begin, functools.partial(ring.start, t)), (ready, functools.partial(ring.all_ready, t))]
        when = first + lag * t
        for D in range(ring.far, -1, -1):
            plan.append((when, functools.partial(ring.step, t, D)))
            when += hop
        plan.append((when, functools.partial(ring.deliver, t)))
        plan.append((when + hop, functools.partial(ring.finish, t)))
        for when, event in plan:
            if when < 32:
                events.setdefault(int(when), []).append(event)
            else:
                rest.append((when, event))
    rest = [event for when, event in sorted(rest, key=lambda pair: pair[0])]

    def step_body(step, carry):
        for when, actions in sorted(events.items()):
            @pl.when(step == when)
            def _():
                for action in actions:
                    action()
        pl.when(step < 16)(lambda: far_tile(step))
        pl.when(step >= 16)(lambda: near_tile(step - 16))
        return carry

    lax.fori_loop(0, 32, step_body, 0)
    for chunk in range(4):
        own_done(chunk)
    for mate in mates[1:] + mates[:1]:
        out_copy(mate).start()
    own_out = pltpu.make_async_copy(low.at[:, mine], back.at[seq], here.at[1])
    own_out.start()
    for event in rest:
        event()
    own_out.wait()
    for mate in mates:
        in_copy(mate).wait_send()
        out_copy(mate).wait_send()
        ref = back.at[mate[0]]
        remote(ref, ref, out_send.at[mate[0]], out_recv.at[mate[0]], mate).wait_recv()
    for chunk in range(4):
        @pl.when(slot >= 1)
        def _():
            x_send(chunk).wait_send()

        @pl.when(slot >= 2)
        def _():
            z_send(chunk).wait_send()


def retreat(count, grad_att, turned, store, outputs, logs, part, splits, steps=(0, 1, 2, 3, 1)):
    rows = grad_att.shape[1]
    own = 4 * rows
    _, shard_rows, half = part.shape
    return pl.pallas_call(
        functools.partial(retreat_kernel, count, splits, steps),
        out_shape=[jax.ShapeDtypeStruct((HEADS, 3, rows, LANES), jnp.bfloat16), jax.ShapeDtypeStruct((shard_rows, 2 * half), jnp.float32)],
        in_specs=[VMEM, ANY, ANY, VMEM, VMEM, ANY],
        out_specs=[VMEM, ANY],
        scratch_shapes=[
            pltpu.VMEM((own, LANES), jnp.bfloat16),
            pltpu.VMEM((8, own), jnp.float32),
            pltpu.VMEM((own, LANES), jnp.float32),
            pltpu.VMEM((3, 2, own, LANES), jnp.float32),
            pltpu.VMEM((2, 2, own, LANES), jnp.bfloat16),
            pltpu.VMEM((2, own, LANES), jnp.bfloat16),
            pltpu.VMEM((2, own, LANES), jnp.bfloat16),
            pltpu.VMEM((3, own, LANES), jnp.bfloat16),
            DMA((4,)), DMA((4,)), DMA((8,)), DMA((8,)),
            pltpu.VMEM((3, LANES, TABLE), jnp.float32), pltpu.VMEM((7, own, LANES), jnp.bfloat16),
            DMA((4,)), DMA((4,)), DMA((4,)),
        ]
        + Scatter.scratch(count, splits, [shard_rows] * len(splits)),
        compiler_params=pltpu.CompilerParams(collective_id=3, has_side_effects=True, vmem_limit_bytes=60 << 20),
    )(grad_att, turned, store, outputs, logs, part)


CHUNK = 512
SPOTS = (2, 4, 7, 12)


def gelu_pair(v):
    root = 0.7978845608028654
    square = v * v
    t = jnp.tanh(root * (v + 0.044715 * square * v))
    up = 0.5 * (1.0 + t)
    return v * up, up + 0.5 * v * (1.0 - t * t) * (root * (1.0 + 3.0 * 0.044715 * square))


def contract(left, right, left_axis, right_axis):
    return lax.dot_general(left, right, (((left_axis,), (right_axis,)), ((), ())), preferred_element_type=jnp.float32)


def feed_kernel(count, att, gates, tokens, cotangent, norms, output_w, inner_w, outer_w,
                layer_out, grad_residual, grad_att, grad_logit, grad_norms, part_output, part_inner, outer_out,
                w_out, w_in, w_up, acts, act_in, slopes, slope_in, scaled, scaled_in, scaled_t, cot_in, cot_t,
                acc, normed, grad_scaled, branch_low, branch_in, branch_t, att_in, gates_in,
                stage_inner, stage_output,
                load_out, load_in, load_up, pair_s, pair_r, act_s, act_r, slope_s, slope_r, put_inner, put_output, *refs):
    half = cotangent.shape[1] // 2
    ring = Scatter(count, (SPLITS["outer"],), [None], [(outer_out, half, 0)], refs[:7], refs[7:])
    core, mate = ring.core, ring.core_mate
    experts = HEADS * EXP
    chunks = inner_w.shape[1] // CHUNK
    small = CHUNK // 2
    shards = max(1, count // chunks)

    def out_load(e):
        return pltpu.make_async_copy(output_w.at[pl.ds(e * DH, DH)], w_out.at[e, pl.ds(0, DH)], load_out.at[e])

    def ffn_load(chunk, slot):
        cols = pl.ds(pl.multiple_of(chunk * CHUNK, CHUNK), CHUNK)
        return (pltpu.make_async_copy(inner_w.at[:, cols], w_in.at[slot], load_in.at[slot]),
                pltpu.make_async_copy(outer_w.at[cols], w_up.at[slot], load_up.at[slot]))

    def chunk_of(step):
        if count != chunks:
            return step
        D = ring.far - (step + 1) // 2
        odd = step % 2
        return ring.dest((odd * D + (1 - odd) * (count - D)) % count)

    for e in range(experts):
        out_load(e).start()
    for sub in range(2):
        for copy in ffn_load(chunk_of(sub), sub):
            copy.start()
    enter(ring.neighbours())

    def remote(src, dst, send, recv):
        return pltpu.make_async_remote_copy(src, dst, send, recv, device_id=mate, device_id_type=MESH)

    mine = pl.ds(pl.multiple_of(core * half, LANES), half)
    yours = pl.ds(pl.multiple_of((1 - core) * half, LANES), half)
    pair = [
        remote(att, att_in, pair_s.at[0], pair_r.at[0]),
        remote(gates.at[0], gates_in, pair_s.at[1], pair_r.at[1]),
        remote(cotangent.at[:, yours], cot_in, pair_s.at[2], pair_r.at[2]),
        remote(scaled, scaled_in, pair_s.at[3], pair_r.at[3]),
        remote(branch_low.at[:, yours], branch_in, pair_s.at[4], pair_r.at[4]),
    ]
    for copy in pair[:3]:
        copy.start()

    def mixed_pair(att_ref, gate, two):
        tiles = []
        for which in (2 * two, 2 * two + 1):
            column = gate[:, experts + which : experts + which + 1]
            tiles.append((att_ref[which // EXP].astype(jnp.float32) * column).astype(jnp.bfloat16))
        return jnp.concatenate(tiles, axis=1)

    w_out[:, DH:, :] = jnp.zeros((experts, LANES - DH, w_out.shape[2]), jnp.bfloat16)
    acc[...] = tokens[...].astype(jnp.float32)
    for two in range(experts // 2):
        out_load(2 * two).wait()
        out_load(2 * two + 1).wait()
        weights = w_out[2 * two : 2 * two + 2].reshape(2 * LANES, w_out.shape[2])
        acc[...] += jnp.dot(mixed_pair(att, gates.at[0], two), weights, preferred_element_type=jnp.float32)
    residual = acc[...]
    centred = residual - jnp.mean(residual, axis=1, keepdims=True)
    inverse = lax.rsqrt(jnp.mean(centred * centred, axis=1, keepdims=True) + EPSILON)
    normed[...] = centred * inverse
    scaled[...] = (normed[...] * norms[:1] + norms[1:2]).astype(jnp.bfloat16)
    pair[3].start()
    rows = tokens.shape[0]
    scaled_t[:, :rows] = scaled[...].T
    cot_t[:, :rows] = cotangent[:, mine].T
    grad_scaled[...] = jnp.zeros_like(grad_scaled)
    pair[2].wait_recv()
    cot_t[:, rows:] = cot_in[...].T
    pair[3].wait_recv()
    scaled_t[:, rows:] = scaled_in[...].T

    small_mine = pl.ds(pl.multiple_of(core * small, LANES), small)
    small_yours = pl.ds(pl.multiple_of((1 - core) * small, LANES), small)

    def act_copy(step, sub):
        return remote(acts.at[sub], act_in.at[step], act_s.at[sub], act_r.at[step])

    def slope_copy(step):
        return remote(slopes.at[step, :, small_yours], slope_in.at[step], slope_s.at[step], slope_r.at[step])

    def put_inner_copy(step, sub):
        cols = pl.ds(pl.multiple_of(chunk_of(step) * small, small), small)
        return pltpu.make_async_copy(stage_inner.at[sub], part_inner.at[:, cols], put_inner.at[sub])

    def forward_backward(step, sub):
        for copy in ffn_load(chunk_of(step), sub):
            copy.wait()

        @pl.when(step > 1)
        def _():
            act_copy(step, sub).wait_send()

        act, slope = gelu_pair(jnp.dot(scaled[...], w_in[sub], preferred_element_type=jnp.float32))
        acts[sub] = act.astype(jnp.bfloat16)
        act_copy(step, sub).start()
        slopes[step] = (contract(cotangent[...], w_up[sub], 1, 1) * slope).astype(jnp.bfloat16)
        slope_copy(step).start()
        acc[...] += jnp.dot(acts[sub], w_up[sub], preferred_element_type=jnp.float32)

        following = (step + 2) % chunks
        ffn_load(chunk_of(following), sub)[0].start()

        @pl.when(step + 2 < chunks)
        def _():
            ffn_load(chunk_of(following), sub)[1].start()

    def weight_parts(step, sub):
        remote(act_in.at[step], act_in.at[step], act_s.at[sub], act_r.at[step]).wait_recv()
        total = jnp.dot(cot_t[:, :rows], acts[sub], preferred_element_type=jnp.float32)
        total = total + jnp.dot(cot_t[:, rows:], act_in[step], preferred_element_type=jnp.float32)
        turned = total.astype(jnp.bfloat16).T
        shard_rows = CHUNK // shards
        for q in range(shards):
            rel = (ring_place(chunk_of(step) * shards + q, count) - ring.place + count) % count
            ring.mine[0][rel] = turned[q * shard_rows : (q + 1) * shard_rows]

    def backward(step, sub):
        ffn_load(chunk_of(step), sub)[0].wait()
        slope_copy(step).wait()
        grad_scaled[...] += contract(slopes[step], w_in[sub], 1, 1)

        @pl.when(step + 2 < chunks)
        def _():
            ffn_load(chunk_of(step + 2), sub)[0].start()

        @pl.when(step > 1)
        def _():
            put_inner_copy(step, sub).wait()

        total = jnp.dot(scaled_t[:, :rows], slopes[step, :, small_mine], preferred_element_type=jnp.float32)
        total = total + jnp.dot(scaled_t[:, rows:], slope_in[step], preferred_element_type=jnp.float32)
        stage_inner[sub] = total.astype(jnp.bfloat16)
        put_inner_copy(step, sub).start()

    events = {}
    if count == chunks:
        for step, rel in enumerate(ring.order()):
            events.setdefault(step, []).append(functools.partial(ring.ready, 0, rel))
        for D in range(ring.far, 0, -1):
            events.setdefault(SPOTS[min(ring.far - D, 3)], []).append(functools.partial(ring.step, 0, D))

    def after(step):
        for when, actions in sorted(events.items()):
            @pl.when(step == when)
            def _():
                for action in actions:
                    action()

    def first_pass(i, carry):
        forward_backward(2 * i, 0)

        @pl.when(i > 0)
        def _():
            weight_parts(2 * i - 1, 1)
            after(2 * i - 1)

        forward_backward(2 * i + 1, 1)
        weight_parts(2 * i, 0)
        after(2 * i)
        return carry

    def second_pass(i, carry):
        for sub in range(2):
            backward(2 * i + sub, sub)
            after(chunks + 2 * i + sub)
        return carry

    lax.fori_loop(0, chunks // 2, first_pass, 0)
    weight_parts(chunks - 1, 1)
    if count == chunks:
        for action in events[chunks - 1]:
            action()
    else:
        ring.all_ready(0)
    lax.fori_loop(0, chunks // 2, second_pass, 0)
    if count != chunks:
        for D in range(ring.far, 0, -1):
            ring.step(0, D)
    layer_out[...] = acc[...].astype(jnp.bfloat16)
    slope = grad_scaled[...]
    grad_norms[...] = jnp.concatenate(
        [jnp.sum(slope * normed[...], axis=0, keepdims=True), jnp.sum(slope, axis=0, keepdims=True),
         jnp.zeros((6, slope.shape[1]), jnp.float32)], axis=0)
    slope = slope * norms[:1]
    total = cotangent[...].astype(jnp.float32) + inverse * (
        slope - jnp.mean(slope, axis=1, keepdims=True)
        - normed[...] * jnp.mean(slope * normed[...], axis=1, keepdims=True))
    grad_residual[...] = total
    branch_low[...] = total.astype(jnp.bfloat16)
    pair[4].start()
    branch_t[:, :rows] = branch_low[:, mine].T
    ring.step(0, 0)
    lane = lax.broadcasted_iota(jnp.int32, (rows, LANES), 1)
    logit = jnp.zeros((rows, LANES), jnp.float32)
    head_total = None
    for which in range(experts):
        if which % 2 == 0:
            weights = w_out[which : which + 2].reshape(2 * LANES, w_out.shape[2])
            both = contract(branch_low[...], weights, 1, 1)
        grad_mixed = both[:, which % 2 * LANES : (which % 2 + 1) * LANES]
        head, expert = which // EXP, which % EXP
        column = slice(experts + which, experts + which + 1)
        term = grad_mixed * gates[0, :, column]
        head_total = term if expert == 0 else head_total + term
        if expert == EXP - 1:
            grad_att[head] = head_total.astype(jnp.bfloat16)
        sums = jnp.sum(grad_mixed * att[head].astype(jnp.float32), axis=1, keepdims=True)
        logit = jnp.where(lane == experts + which, sums, logit)
    grad_logit[...] = logit * gates[1]
    ring.deliver(0)
    pair[0].wait_recv()
    pair[1].wait_recv()
    pair[4].wait_recv()
    branch_t[:, rows:] = branch_in[...].T

    def put_output_copy(which):
        return pltpu.make_async_copy(stage_output.at[which % 4, pl.ds(0, DH)], part_output.at[pl.ds(which * DH, DH)], put_output.at[which % 4])

    for two in range(experts // 2):
        total = jnp.dot(branch_t[:, :rows], mixed_pair(att, gates.at[0], two), preferred_element_type=jnp.float32)
        total = total + jnp.dot(branch_t[:, rows:], mixed_pair(att_in, gates_in, two), preferred_element_type=jnp.float32)
        turned = total.astype(jnp.bfloat16).T
        for side in range(2):
            which = 2 * two + side
            if which >= 4:
                put_output_copy(which - 4).wait()
            stage_output[which % 4] = turned[side * LANES : (side + 1) * LANES]
            put_output_copy(which).start()
    for which in range(experts - 4, experts):
        put_output_copy(which).wait()
    for sub in range(2):
        put_inner_copy(sub, sub).wait()
        act_copy(sub, sub).wait_send()
    ring.finish(0)
    for copy in pair:
        copy.wait_send()


def feed(count, att, gates, tokens, cotangent, norms, output_w, inner_w, outer_w):
    rows, width = tokens.shape
    wide = inner_w.shape[1]
    half = width // 2
    f32, bf = jnp.float32, jnp.bfloat16
    experts, chunks = HEADS * EXP, wide // CHUNK
    V = pltpu.VMEM
    return pl.pallas_call(
        functools.partial(feed_kernel, count),
        out_shape=[
            jax.ShapeDtypeStruct((rows, width), bf),
            jax.ShapeDtypeStruct((rows, width), f32),
            jax.ShapeDtypeStruct((HEADS, rows, LANES), bf),
            jax.ShapeDtypeStruct((rows, LANES), f32),
            jax.ShapeDtypeStruct((8, width), f32),
            jax.ShapeDtypeStruct((VCOLS, half), bf),
            jax.ShapeDtypeStruct((width, wide // 2), bf),
            jax.ShapeDtypeStruct((wide // count, width), f32),
        ],
        in_specs=[VMEM] * 5 + [ANY] * 3,
        out_specs=[VMEM] * 5 + [ANY] * 3,
        scratch_shapes=[
            V((experts, LANES, width), bf), V((2, width, CHUNK), bf), V((2, CHUNK, width), bf),
            V((2, rows, CHUNK), bf), V((chunks, rows, CHUNK), bf), V((chunks, rows, CHUNK), bf), V((chunks, rows, CHUNK // 2), bf),
            V((rows, width), bf), V((rows, width), bf), V((width, 2 * rows), bf), V((rows, half), bf), V((half, 2 * rows), bf),
            V((rows, width), f32), V((rows, width), f32), V((rows, width), f32),
            V((rows, width), bf), V((rows, half), bf), V((half, 2 * rows), bf), V((HEADS, rows, LANES), bf), V((rows, LANES), f32),
            V((2, width, CHUNK // 2), bf), V((4, LANES, half), bf),
            DMA((experts,)), DMA((2,)), DMA((2,)), DMA((5,)), DMA((5,)), DMA((2,)), DMA((chunks,)), DMA((chunks,)), DMA((chunks,)),
            DMA((2,)), DMA((4,)),
        ]
        + Scatter.scratch(count, (SPLITS["outer"],), [wide // count]),
        compiler_params=pltpu.CompilerParams(collective_id=4, has_side_effects=True, vmem_limit_bytes=63 << 20),
    )(att, gates, tokens, cotangent, norms, output_w, inner_w, outer_w)


def settle_kernel(count, back, experts, gates, grad_logit, tokens, joint_in, residual_in, grad_norms, part_output,
                  grad_tokens, joint_out, output_out, grads, grads_in, tokens_in, tokens_t, norms_in, norm_columns, joint, grad_residual, *refs):
    splits = (SPLITS["joint"], SPLITS["output"])
    pair_s, pair_r, load = refs[-3:]
    loads = [pltpu.make_async_copy(joint_in, joint, load.at[0]), pltpu.make_async_copy(residual_in, grad_residual, load.at[1])]
    for copy in loads:
        copy.start()
    half, output_half = JOINT // 2, part_output.shape[2]
    outs = [(joint_out, half, 0), (output_out, output_half, 0)]
    ring = Scatter(count, splits, [None, (part_output, 0)], outs, refs[:14], refs[14:-3])
    ring.start(1)
    enter(ring.neighbours())
    core = ring.core

    def remote(src, dst, i):
        return pltpu.make_async_remote_copy(src, dst, pair_s.at[i], pair_r.at[i], device_id=ring.core_mate, device_id_type=MESH)

    mine = pl.ds(pl.multiple_of(core * half, LANES), half)
    yours = pl.ds(pl.multiple_of((1 - core) * half, LANES), half)
    pair = [remote(tokens, tokens_in, 0), remote(grad_norms, norms_in, 1)]
    pair[0].start()
    pair[1].start()
    ring.all_ready(1)
    rows = tokens.shape[0]
    lane = lax.broadcasted_iota(jnp.int32, (LANES, LANES), 1)
    width = HEADS * EXP

    def hand_over(block):
        part = pl.ds(pl.multiple_of(block * LANES, LANES), LANES)
        return remote(grads.at[part, yours], grads_in.at[part], 2 + block)


    def assemble(block, carry):
        part = pl.ds(pl.multiple_of(block * LANES, LANES), LANES)
        pieces = [back[head, which, part, :][:, :DH].astype(jnp.float32) for which in range(2) for head in range(HEADS)]
        logit = grad_logit[part, :]
        for head in range(HEADS):
            values = back[head, 2, part, :].astype(jnp.float32)
            for expert in range(EXP):
                which = head * EXP + expert
                pieces.append((values * gates[0, part, which : which + 1])[:, :DH])
                sums = jnp.sum(values * experts[which, part, :].astype(jnp.float32), axis=1, keepdims=True)
                logit = jnp.where(lane == which, sums * gates[1, part, which : which + 1], logit)
        pieces.append(jnp.where(lane < 2 * width, logit, 0.0))
        pieces.append(jnp.zeros((LANES, JOINT - ROUTERS - LANES), jnp.float32))
        grads[part, :] = jnp.concatenate(pieces, axis=1).astype(jnp.bfloat16)
        hand_over(block).start()
        return carry

    lax.fori_loop(0, rows // LANES, assemble, 0)
    ring.step(1, ring.far)
    tokens_t[:, :rows] = tokens[...].T
    for copy in pair:
        copy.wait_recv()
    tokens_t[:, rows:] = tokens_in[...].T
    norm_tile = NORM // LANES * LANES - half
    first = NORM - half - norm_tile
    both = grad_norms[...] + norms_in[...]
    for block in range(both.shape[1] // LANES):
        columns = jnp.concatenate([both[:, block * LANES : (block + 1) * LANES], jnp.zeros((LANES - 8, LANES), jnp.float32)], axis=0)
        norm_columns[block * LANES : (block + 1) * LANES, :] = columns.T
    for block in range(rows // LANES):
        hand_over(block).wait_recv()
    shard_rows = tokens_t.shape[0] // count
    tile_lane = lax.broadcasted_iota(jnp.int32, (shard_rows, LANES), 1)

    def fill(rel):
        part = pl.ds(pl.multiple_of(ring.dest(rel) * shard_rows, shard_rows), shard_rows)
        total = jnp.dot(tokens_t[part, :rows], grads[:, mine], preferred_element_type=jnp.float32)
        total = total + jnp.dot(tokens_t[part, rows:], grads_in[...], preferred_element_type=jnp.float32)
        ring.mine[0][rel] = total.astype(jnp.bfloat16)
        extra = jnp.where(tile_lane == first, norm_columns[part, 0:1], 0.0) + jnp.where(tile_lane == first + 1, norm_columns[part, 1:2], 0.0)
        tile = total[:, norm_tile : norm_tile + LANES] + extra * core.astype(jnp.float32)
        ring.mine[0][rel, :, norm_tile : norm_tile + LANES] = tile.astype(jnp.bfloat16)

    for rel in ring.order():
        fill(rel)
        ring.ready(0, rel)
    ring.step(0, ring.far)
    for D in range(ring.far - 1, 0, -1):
        ring.step(1, D)
        ring.step(0, D)
        if D == ring.far - 1:
            for copy in loads:
                copy.wait()
            grad_tokens[...] = grad_residual[...] + contract(grads[...], joint[...], 1, 1)
    ring.step(1, 0)
    ring.step(0, 0)
    ring.deliver(1)
    ring.deliver(0)
    ring.finish(1)
    ring.finish(0)
    for copy in pair:
        copy.wait_send()
    for block in range(rows // LANES):
        hand_over(block).wait_send()


def settle(count, back, experts, gates, grad_logit, tokens, joint, grad_residual, grad_norms, part_output):
    rows, width = tokens.shape
    shard_rows = width // count
    f32, bf = jnp.float32, jnp.bfloat16
    V = pltpu.VMEM
    return pl.pallas_call(
        functools.partial(settle_kernel, count),
        out_shape=[jax.ShapeDtypeStruct((rows, width), f32), jax.ShapeDtypeStruct((shard_rows, JOINT), f32),
                   jax.ShapeDtypeStruct((part_output.shape[1], width), f32)],
        in_specs=[VMEM] * 5 + [ANY, ANY, VMEM, ANY],
        out_specs=[VMEM, VMEM, ANY],
        scratch_shapes=[V((rows, JOINT), bf), V((rows, JOINT // 2), bf), V((rows, width), bf), V((width, 2 * rows), bf), V((8, width), f32), V((width, LANES), f32),
                        V((width, JOINT), bf), V((rows, width), f32)]
        + Scatter.scratch(count, (SPLITS["joint"], SPLITS["output"]), [shard_rows, part_output.shape[1]])
        + [DMA((2 + rows // LANES,)), DMA((2 + rows // LANES,)), DMA((2,))],
        compiler_params=pltpu.CompilerParams(collective_id=5, has_side_effects=True, vmem_limit_bytes=60 << 20),
    )(back, experts, gates, grad_logit, tokens, joint, grad_residual, grad_norms, part_output)


def publish_kernel(joint_w, output_w, inner_w, outer_w, layer, tokens_in,
                   query, key, value, value_router, output_router, norms, output_out, inner_out, outer_out, layer_out, tokens_out,
                   *refs):
    held, turned, tail, load, store = refs[:6], refs[6], refs[7], refs[8], refs[9]
    sources = (joint_w, tokens_in, inner_w, outer_w, layer, output_w)
    loads = [pltpu.make_async_copy(src, buf, load.at[i]) for i, (src, buf) in enumerate(zip(sources, held))]
    for copy in loads:
        copy.start()
    half, small = inner_w.shape[1] // 2, CHUNK // 2
    stores = []

    def put(src, dst):
        copy = pltpu.make_async_copy(src, dst, store.at[len(stores)])
        copy.start()
        stores.append(copy)

    loads[0].wait()
    turned[...] = held[0][...].T
    for first, target in ((0, query), (QCOLS, key), (2 * QCOLS, value), (ROUTERS, value_router)):
        put(turned.at[pl.ds(first, target.shape[0])], target)
    tail[...] = turned[ROUTERS + HEADS * EXP : NORM, :]
    put(tail, output_router)
    norms[...] = turned[NORM : NORM + 8, :]
    for i, target in enumerate((tokens_out, inner_out, outer_out, layer_out, output_out)):
        loads[1 + i].wait()
        if i != 1:
            put(held[1 + i], target)
            continue
        for core in range(2):
            for chunk in range(half // small):
                put(held[1 + i].at[:, pl.ds(core * half + chunk * small, small)], target.at[:, pl.ds(chunk * CHUNK + core * small, small)])
    for copy in stores:
        copy.wait()


def publish(joint_w, output_w, inner_w, outer_w, layer, tokens):
    rows = joint_w.shape[0]
    f32 = jnp.float32
    columns = [QCOLS, QCOLS, VCOLS, HEADS * EXP, HEADS * EXP]
    rest = (output_w, inner_w, outer_w, layer, tokens)
    return pl.pallas_call(
        publish_kernel,
        out_shape=[jax.ShapeDtypeStruct((c, rows), f32) for c in columns] + [jax.ShapeDtypeStruct((8, rows), f32)]
        + [jax.ShapeDtypeStruct(x.shape, x.dtype) for x in rest],
        in_specs=[ANY] * 6,
        out_specs=[ANY] * 5 + [VMEM] + [ANY] * 5,
        scratch_shapes=[pltpu.VMEM(x.shape, x.dtype) for x in (joint_w, tokens, inner_w, outer_w, layer, output_w)]
        + [pltpu.VMEM((JOINT, rows), f32), pltpu.VMEM((HEADS * EXP, rows), f32)]
        + [DMA((6,)), DMA((9 + inner_w.shape[1] // (CHUNK // 2),))],
        compiler_params=pltpu.CompilerParams(vmem_limit_bytes=63 << 20),
    )(joint_w, *rest)


def on_device(
    tokens, value_routes, output_routes, cont_gap, query_weight, key_weight, value_weight, value_router,
    output_router, output_weight, norm_gain, norm_bias, inner_weight, outer_weight, cotangent,
):
    count = lax.axis_size("fsdp")
    inputs = tokens[0]
    rows, width = inputs.shape
    norm = jnp.stack([norm_gain, norm_bias])
    routes = jnp.concatenate([value_routes[0].reshape(rows, -1), output_routes[0].reshape(rows, -1)], axis=1)
    joint, tables, turned, qkv, experts, gates, norms = project(
        count, query_weight.T, key_weight.T, value_weight.T, value_router.T, output_router.T, norm, inputs, routes, cont_gap)
    att, store, outputs, logs, inner_full, outer_full, output_full = attend(
        count, qkv, tables, (inner_weight, outer_weight, output_weight), (SPLITS["inner"], SPLITS["outer"], SPLITS["output"]))
    layer, grad_residual, grad_att, grad_logit, grad_norms, part_output, part_inner, outer_w = feed(
        count, att, gates, inputs, cotangent[0], norms, output_full.reshape(VCOLS, width), inner_full.reshape(width, -1),
        outer_full.reshape(-1, width))
    back, inner_w = retreat(
        count, grad_att, turned, store, outputs, logs, part_inner.reshape(count, -1, part_inner.shape[1]), INNER_PARTS)
    grad_input, joint_w, output_w = settle(
        count, back, experts, gates, grad_logit, inputs, joint, grad_residual, grad_norms,
        part_output.reshape(count, -1, part_output.shape[1]))
    query, key, value, value_r, output_r, norm_w, output_w, inner_w, outer_w, layer, grad_input = publish(
        joint_w, output_w, inner_w, outer_w, layer, grad_input)
    return (layer[None], grad_input[None], query.T, key.T, value.T, value_r.T, output_r.T, output_w, norm_w[0], norm_w[1], inner_w, outer_w)


def solution(mesh):
    wide = P("fsdp", None)
    part = P("fsdp", "seq", None)
    routes = P("fsdp", "seq", None, None)
    return jax.shard_map(
        on_device,
        mesh=mesh,
        in_specs=(part, routes, routes, P()) + (wide,) * 6 + (P("fsdp"), P("fsdp"), wide, wide, part),
        out_specs=(part, part) + (wide,) * 6 + (P("fsdp"), P("fsdp"), wide, wide),
        check_vma=False,
    )
```

```python
import functools
import jax
import jax.numpy as jnp
from jax import lax
from jax.experimental import pallas as pl
from jax.experimental.pallas import tpu as pltpu
from jax.sharding import PartitionSpec as P

HEADS = 4
DH = 112
EXP = 5
CONT = 1024
GSLOTS = 4
PSLOTS = 2
BLOCK = 512
LANES = 128
EPSILON = 1e-05
NEGATIVE = -1e30
LOG2E = 1.4426950408889634
MESH = pl.DeviceIdType.MESH
ANY = pl.BlockSpec(memory_space=pl.ANY)
VMEM = pl.BlockSpec(memory_space=pltpu.VMEM)
SMEM = pl.BlockSpec(memory_space=pltpu.SMEM)
DMA = pltpu.SemaphoreType.DMA

QCOLS = HEADS * DH
VCOLS = HEADS * EXP * DH
ROUTERS = 2 * QCOLS + VCOLS
NORM = ROUTERS + 2 * HEADS * EXP
JOINT = 3328
SPLITS = {"joint": (640, 512), "output": (256, 128), "inner": (768, 640), "outer": (256, 128)}
INNER_PARTS = ((512, 768),)


def ring_place(index, count):
    return (index // 2) * (1 - index % 2) + (count - 1 - index // 2) * (index % 2)


def ring_index(place, count):
    upper = place // (count // 2)
    return 2 * place * (1 - upper) + (2 * (count - 1 - place) + 1) * upper


def enter(devices):
    barrier = pltpu.get_barrier_semaphore()
    for device in devices:
        pl.semaphore_signal(barrier, inc=1, device_id=device, device_id_type=MESH)
    pl.semaphore_wait(barrier, len(devices))


class Ring:
    def __init__(self, count, splits):
        self.count, self.splits = count, splits
        self.seq, self.fsdp = lax.axis_index("seq"), lax.axis_index("fsdp")
        self.plane, self.core = self.seq // 2, self.seq % 2
        self.place = ring_place(self.fsdp, count)
        self.right = (self.seq, ring_index((self.place + 1) % count, count))
        self.left = (self.seq, ring_index((self.place + count - 1) % count, count))
        self.core_mate = (self.seq + 1 - 2 * self.core, self.fsdp)
        self.plane_mate = ((self.seq + 2) % 4, self.fsdp)
        self.far = count // 2

    def neighbours(self):
        return [self.right, self.left, self.core_mate, self.plane_mate]

    def reach(self, kind, way):
        return self.far if kind == way else self.count - 1 - self.far

    def kinds(self, t):
        return [kind for kind in (1, 0) if self.splits[t][kind] > 0]

    def half(self, t):
        return self.splits[t][0] + 2 * self.splits[t][1]

    def cols(self, t, kind, plane, core):
        both, single = self.splits[t]
        if kind == 0:
            return pl.ds(pl.multiple_of(core * self.half(t), LANES), both)
        return pl.ds(pl.multiple_of(core * self.half(t) + both + plane * single, LANES), single)

    def behind(self, way, k):
        step = self.count - k if way == 0 else k
        return ring_index((self.place + step) % self.count, self.count)

    def next(self, way):
        return self.right if way == 0 else self.left

    def slot(self, kind, way, k):
        return k - 1 if way == 0 else self.reach(kind, 0) + k - 1


class Gather(Ring):
    def __init__(self, count, splits, shards, at, send, recv, local):
        super().__init__(count, splits)
        self.shards, self.at, self.send, self.recv, self.local = shards, at, send, recv, local

    @staticmethod
    def sems(count, tensors):
        return [DMA((6 * tensors * (count - 1),)), DMA((6 * tensors * (count - 1),)), DMA((tensors,))]

    def copy(self, src, dst, group, t, slot, device):
        i = (group * len(self.splits) + t) * (self.count - 1) + slot
        return pltpu.make_async_remote_copy(
            src, dst, self.send.at[i], self.recv.at[i], device_id=device, device_id_type=MESH
        )

    def same(self, group, t, kind, way, k, plane, core, device):
        ref = self.at(t, self.behind(way, k), self.cols(t, kind, plane, core))
        return self.copy(ref, ref, group, t, self.slot(kind, way, k), device)

    def hop(self, t, kind, way, k):
        if k > 1:
            ref = self.at(t, self.behind(way, k - 1), self.cols(t, kind, self.plane, self.core))
            return self.copy(ref, ref, kind, t, self.slot(kind, way, k), self.next(way))
        cols = self.cols(t, kind, self.plane, self.core)
        return self.copy(
            self.shards[t].at[:, cols], self.at(t, self.fsdp, cols), kind, t, self.slot(kind, way, 1), self.next(way)
        )

    def arrived(self, t, kind, way, k):
        return self.same(kind, t, kind, way, k, self.plane, self.core, self.next(way))

    def to_core(self, t, kind, way, k, core):
        return self.same(2 + kind, t, kind, way, k, self.plane, core, self.core_mate)

    def to_plane(self, t, way, k, plane):
        return self.same(4, t, 1, way, k, plane, self.core, self.plane_mate)

    def plane_to_core(self, t, way, k, core):
        return self.same(5, t, 1, way, k, 1 - self.plane, core, self.core_mate)

    def own(self, t):
        return pltpu.make_async_copy(self.shards[t], self.at(t, self.fsdp, slice(None)), self.local.at[t])

    def start(self, t):
        for kind in self.kinds(t):
            for way in (0, 1):
                if self.reach(kind, way):
                    self.hop(t, kind, way, 1).start()
        self.own(t).start()

    def arrive(self, t, k):
        for kind in self.kinds(t):
            for way in (0, 1):
                if k <= self.reach(kind, way):
                    self.arrived(t, kind, way, k).wait_recv()
                    if k < self.reach(kind, way):
                        self.hop(t, kind, way, k + 1).start()
                    if kind:
                        self.to_plane(t, way, k, self.plane).start()
                    self.to_core(t, kind, way, k, self.core).start()

    def plane_arrive(self, t, k):
        if 1 in self.kinds(t):
            for way in (0, 1):
                if k <= self.reach(1, way):
                    self.to_plane(t, way, k, 1 - self.plane).wait_recv()
                    self.plane_to_core(t, way, k, self.core).start()

    def finish(self, t):
        self.own(t).wait()
        for kind in self.kinds(t):
            for way in (0, 1):
                for k in range(1, self.reach(kind, way) + 1):
                    self.hop(t, kind, way, k).wait_send()
                    self.to_core(t, kind, way, k, self.core).wait_send()
                    self.to_core(t, kind, way, k, 1 - self.core).wait_recv()
                    if kind:
                        self.to_plane(t, way, k, self.plane).wait_send()
                        self.plane_to_core(t, way, k, self.core).wait_send()
                        self.plane_to_core(t, way, k, 1 - self.core).wait_recv()

    def events(self):
        tensors = range(len(self.splits))
        out = []
        for k in range(1, self.far + 1):
            for t in tensors:
                out.append(functools.partial(self.arrive, t, k))
                if k > 1:
                    out.append(functools.partial(self.plane_arrive, t, k - 1))
        for t in tensors:
            out.append(functools.partial(self.plane_arrive, t, self.far))
        for t in tensors:
            out.append(functools.partial(self.finish, t))
        return out


TABLE = 5632
TABLE_ZERO = 5120
TURNED_ZERO = 512


def route_lanes(routes, lane):
    hit = None
    for head in range(2 * HEADS):
        for choice in range(2):
            place = head * EXP + routes[:, 2 * head + choice : 2 * head + choice + 1]
            here = lane == place
            hit = here if hit is None else hit | here
    return hit.astype(jnp.float32)


def project_kernel(count, query, key, value, value_router, output_router, norm, tokens, routes, gaps,
                   joint_out, tables_out, turned_out, qkv, experts, gates, norms,
                   shard, shard_t, joint, tables, turned_tables, product, load, store, send, recv, local):
    rows = shard.shape[0]
    splits = (SPLITS["joint"],)
    at = lambda t, g, cols: joint.at[pl.ds(pl.multiple_of(g * rows, rows), rows), cols]
    ring = Gather(count, splits, [shard], at, send, recv, local)
    loads = []
    for i, (src, first) in enumerate(((query, 0), (key, QCOLS), (value, 2 * QCOLS))):
        loads.append(pltpu.make_async_copy(src, shard_t.at[pl.ds(first, src.shape[0])], load.at[i]))
        loads[-1].start()
    small = [ref[...].astype(jnp.float32) for ref in (value_router, output_router, norm)]
    small.append(jnp.zeros((JOINT - NORM - 2, rows), jnp.float32))
    shard_t[ROUTERS:, :] = jnp.concatenate(small, axis=0).astype(jnp.bfloat16)
    for copy in loads:
        copy.wait()
    shard[...] = shard_t[...].T
    enter(ring.neighbours())
    ring.start(0)
    slope = jnp.float32(0.0)
    for head in range(HEADS):
        slope = jnp.where(ring.seq // 1 == head, -0.5 * 0.5**head * LOG2E, slope)
    group = ring.fsdp // GSLOTS
    pair = jnp.maximum(ring.fsdp % GSLOTS - PSLOTS, 0) * 2
    gap_values = [jnp.int32(0), gaps[group, pair], gaps[group, pair + 1]]

    def table_column(step, carry):
        start = pl.multiple_of(step * 256, 256)
        lanes = lax.broadcasted_iota(jnp.int32, (8, 256 + LANES), 1) + (start - LANES)
        for which in range(3):
            for turned in range(2):
                if turned:
                    distance = lanes - TURNED_ZERO + gap_values[which]
                else:
                    distance = TABLE_ZERO - lanes + gap_values[which]
                bias = slope * jnp.log(1.0 + jnp.maximum(distance, 0).astype(jnp.float32))
                bias = jnp.where(distance >= 0, bias, NEGATIVE)
                wide = jnp.broadcast_to(bias[:1], (LANES, 256 + LANES))
                rolled = pltpu.roll(wide, 0, 1, stride=1, stride_axis=0)
                target = turned_tables if turned else tables
                target[which, :, pl.ds(start, 256)] = rolled[:, LANES:]
        return carry

    events = []
    for k in range(1, ring.far + 1):
        events.append(functools.partial(ring.arrive, 0, k))
        if k > 1:
            events.append(functools.partial(ring.plane_arrive, 0, k - 1))
    events += [functools.partial(ring.plane_arrive, 0, ring.far), functools.partial(ring.finish, 0)]
    cut = max(1, TABLE // 256 // (len(events) - 2))
    done = 0
    saves = [(tables, tables_out), (turned_tables, turned_out), (joint, joint_out)]
    saves = [pltpu.make_async_copy(src, dst, store.at[i]) for i, (src, dst) in enumerate(saves)]
    for i, event in enumerate(events):
        upto = min(TABLE // 256, (i + 1) * cut)
        if i == len(events) - 2:
            upto = TABLE // 256
        if upto > done:
            lax.fori_loop(done, upto, table_column, 0)
            done = upto
            if done == TABLE // 256:
                saves[0].start()
                saves[1].start()
        event()
    saves[2].start()

    def column(step, carry):
        cols = pl.ds(pl.multiple_of(step * 256, 256), 256)
        product[:, cols] = jnp.dot(tokens[...], joint[:, cols], preferred_element_type=jnp.float32)
        return carry

    lax.fori_loop(0, JOINT // 256, column, 0)
    norm_tile = NORM // LANES * LANES
    turned_norm = joint[:, norm_tile : norm_tile + LANES].astype(jnp.float32).T
    norms[...] = turned_norm[NORM - norm_tile : NORM - norm_tile + 8]
    logits = product[:, ROUTERS : ROUTERS + 2 * HEADS * EXP]
    local_rows = tokens.shape[0]
    wide = jnp.concatenate([logits, jnp.zeros((local_rows, LANES - 2 * HEADS * EXP), jnp.float32)], axis=1)
    lane = lax.broadcasted_iota(jnp.int32, (local_rows, LANES), 1)
    mask = route_lanes(routes[...], lane)
    gate = 1.0 / (1.0 + jnp.exp(-wide))
    gates[0] = gate * mask
    gates[1] = gate * mask * (1.0 - gate)
    pad = jnp.zeros((local_rows, LANES - DH), jnp.float32)
    ones = jnp.ones((local_rows, LANES - DH), jnp.float32)
    for head in range(HEADS):
        first = head * DH
        qkv[head, 0] = jnp.concatenate([product[:, first : first + DH], pad], axis=1).astype(jnp.bfloat16)
        first = QCOLS + head * DH
        qkv[head, 1] = jnp.concatenate([product[:, first : first + DH], pad], axis=1).astype(jnp.bfloat16)
        total = None
        for expert in range(EXP):
            which = head * EXP + expert
            first = 2 * QCOLS + which * DH
            piece = product[:, first : first + DH]
            experts[which] = jnp.concatenate([piece, pad], axis=1).astype(jnp.bfloat16)
            term = piece * gates[0, :, which : which + 1]
            total = term if total is None else total + term
        qkv[head, 2] = jnp.concatenate([total, ones], axis=1).astype(jnp.bfloat16)
    for copy in saves:
        copy.wait()


def project(count, query, key, value, value_router, output_router, norm, tokens, routes, gaps):
    rows, shard_rows = tokens.shape[0], query.shape[1]
    f32, bf = jnp.float32, jnp.bfloat16
    V = pltpu.VMEM
    return pl.pallas_call(
        functools.partial(project_kernel, count),
        out_shape=[
            jax.ShapeDtypeStruct((shard_rows * count, JOINT), bf),
            jax.ShapeDtypeStruct((3, LANES, TABLE), f32),
            jax.ShapeDtypeStruct((3, LANES, TABLE), f32),
            jax.ShapeDtypeStruct((HEADS, 3, rows, LANES), bf),
            jax.ShapeDtypeStruct((HEADS * EXP, rows, LANES), bf),
            jax.ShapeDtypeStruct((2, rows, LANES), f32),
            jax.ShapeDtypeStruct((8, shard_rows * count), f32),
        ],
        in_specs=[ANY] * 3 + [VMEM] * 5 + [SMEM],
        out_specs=[ANY] * 3 + [VMEM] * 4,
        scratch_shapes=[
            V((shard_rows, JOINT), bf), V((JOINT, shard_rows), bf), V((shard_rows * count, JOINT), bf),
            V((3, LANES, TABLE), f32), V((3, LANES, TABLE), f32), V((rows, JOINT), f32), DMA((3,)), DMA((3,)),
        ]
        + Gather.sems(count, 1),
        compiler_params=pltpu.CompilerParams(collective_id=1, has_side_effects=True, vmem_limit_bytes=62 << 20),
    )(query, key, value, value_router, output_router, norm, tokens, routes, gaps)


def seq_mates(ring):
    return [ring.core_mate, ring.plane_mate, (3 - ring.seq, ring.fsdp)]


def slot_mates(ring):
    f = ring.fsdp
    return [(ring.seq, f + 1 - 2 * (f % 2)), (ring.seq, f + 2 - 4 * ((f // 2) % 2))]


def tile_place(slot, seq, phase, key_block, query_block):
    cont = slot // PSLOTS
    own = 1 - jnp.minimum(phase, 1)
    piece = jnp.where(slot == 3, 2 - phase, phase - 1)
    source = jnp.where(phase == 0, 0, 1 + piece)
    first = cont * 2 * (query_block // 2)
    active = jnp.where(
        phase == 0,
        (key_block <= query_block) & (key_block >= first),
        jnp.where(phase == 1, slot >= 1, slot >= 2),
    )
    far_column = jnp.where(
        cont == 1,
        2048 * piece + BLOCK * key_block - BLOCK * (query_block % 2) - 4096,
        BLOCK * key_block - 2048 - BLOCK * query_block,
    )
    column = jnp.where(phase == 0, BLOCK * (key_block - query_block), far_column)
    table = jnp.where((phase > 0) & (cont == 1), 1 + query_block // 2, 0)
    return source, active, table, column


STRIP = 512


def near_first(ring, j):
    odd, high = j % 2, j // 2
    core = ring.core + odd - 2 * ring.core * odd
    plane = ring.plane + high - 2 * ring.plane * high
    return 2 * plane + core


def block_rows(block):
    return pl.ds(pl.multiple_of(block * BLOCK, BLOCK), BLOCK)


def attend_kernel(count, splits, steps, qkv, tables_in, *refs):
    T = len(splits)
    shards, refs = refs[:T], refs[T:]
    att, store, outputs, logs = refs[:4]
    fulls, refs = refs[4 : 4 + T], refs[4 + T :]
    acc, top, att_low, tables, kv_send, kv_recv, q_send, q_recv, sh_send, sh_recv, out_send, out_recv, here = refs[:13]
    at = lambda t, g, cols: fulls[t].at[g, :, cols]
    ring = Gather(count, splits, shards, at, *refs[13:])
    table_load = pltpu.make_async_copy(tables_in, tables, here.at[2])
    table_load.start()
    seq, slot = ring.seq, ring.fsdp % GSLOTS
    mates, (x_mate, z_mate) = seq_mates(ring), slot_mates(ring)
    enter(ring.neighbours() + mates[2:] + [x_mate, z_mate])

    def remote(src, dst, send, recv, device):
        return pltpu.make_async_remote_copy(src, dst, send, recv, device_id=device, device_id_type=MESH)

    mine = block_rows(seq)

    def kv_copy(mate):
        return remote(qkv.at[mate[0], pl.ds(1, 2)], store.at[pl.ds(1, 2), mine], kv_send.at[mate[0]], kv_recv.at[seq], mate)

    def q_copy(mate):
        return remote(qkv.at[mate[0], 0], store.at[0, mine], q_send.at[mate[0]], q_recv.at[seq], mate)

    for mate in mates[1:] + mates[:1]:
        kv_copy(mate).start()
    own_copy = pltpu.make_async_copy(qkv.at[seq], store.at[pl.ds(0, 3), mine], here.at[0])
    own_copy.start()
    for mate in mates[1:] + mates[:1]:
        q_copy(mate).start()
    acc[...] = jnp.zeros_like(acc)
    top[...] = jnp.full_like(top, NEGATIVE)

    def far_rows(piece, chunk):
        return store.at[pl.ds(3 + 2 * piece, 2), block_rows(near_first(ring, chunk))]

    def first_hop(chunk, way):
        src = store.at[pl.ds(1, 2), block_rows(near_first(ring, chunk))]
        piece = slot % 2
        return remote(src, far_rows(piece, chunk), sh_send.at[4 * way + chunk], sh_recv.at[4 * piece + chunk],
                      x_mate if way == 0 else z_mate)

    def second_hop(chunk):
        piece = slot % 2
        return remote(far_rows(piece, chunk), far_rows(piece, chunk), sh_send.at[8 + chunk], sh_recv.at[4 * piece + chunk], x_mate)

    def share(chunk):
        @pl.when(slot < 2)
        def _():
            first_hop(chunk, 1).start()

        @pl.when(slot == 0)
        def _():
            first_hop(chunk, 0).start()

    def pass_on(chunk):
        @pl.when(slot >= 1)
        def _():
            piece = jnp.where(slot == 3, 1, 0)
            remote(far_rows(piece, chunk), far_rows(piece, chunk), sh_send.at[chunk], sh_recv.at[4 * piece + chunk], x_mate).wait_recv()

        @pl.when(slot >= 2)
        def _():
            second_hop(chunk).start()

    def last_piece(chunk):
        @pl.when(slot >= 2)
        def _():
            piece = 3 - slot
            remote(far_rows(piece, chunk), far_rows(piece, chunk), sh_send.at[chunk], sh_recv.at[4 * piece + chunk], x_mate).wait_recv()

    own_copy.wait()
    share(0)
    for chunk, mate in enumerate(mates):
        other = mate[0]
        src = store.at[pl.ds(1, 2), block_rows(other)]
        remote(src, src, kv_send.at[other], kv_recv.at[other], mate).wait_recv()
        share(1 + chunk)
    for mate in mates:
        src = store.at[0, block_rows(mate[0])]
        remote(src, src, q_send.at[mate[0]], q_recv.at[mate[0]], mate).wait_recv()

    def tile(source, table, column, key_block, first, rows):
        keys = store[1 + 2 * source, block_rows(key_block), :]
        values = store[2 + 2 * source, block_rows(key_block), :]
        for strip in range(rows // STRIP):
            part = pl.ds(pl.multiple_of(first + strip * STRIP, STRIP), STRIP)
            scores = lax.dot_general(store[0, part, :], keys, (((1,), (1,)), ((), ())), preferred_element_type=jnp.float32)
            start = column + TABLE_ZERO - strip * STRIP
            bias = [tables[table, :, pl.ds(pl.multiple_of(start - LANES * i, LANES), BLOCK)] for i in range(STRIP // LANES)]
            scores = scores * (DH**-0.5 * LOG2E) + jnp.concatenate(bias, axis=0)
            before = top[part, :]
            after = jnp.maximum(before, jnp.max(scores, axis=1, keepdims=True))
            terms = jnp.exp2(scores - after[:, :1])
            acc[part, :] = acc[part, :] * jnp.exp2(before - after) + jnp.dot(
                terms.astype(jnp.bfloat16), values, preferred_element_type=jnp.float32)
            top[part, :] = after

    def near_tile(step):
        key_block, query_block = near_first(ring, step // 4), step % 4
        source, active, table, column = tile_place(slot, seq, 0, key_block, query_block)

        @pl.when(active)
        def _():
            tile(source, table, column, key_block, query_block * BLOCK, BLOCK)

    def far_tile(step):
        phase, key_block, query_block = step // 8, near_first(ring, (step // 2) % 4), 2 * (step % 2)
        source, active, table, column = tile_place(slot, seq, phase, key_block, query_block)

        @pl.when(active)
        def _():
            tile(source, table, column, key_block, query_block * BLOCK, 2 * BLOCK)

    table_load.wait()
    events = {}
    for chunk in range(4):
        events.setdefault(4 * chunk + 3, []).append(functools.partial(pass_on, chunk))
        events.setdefault(24 + 2 * chunk, []).append(functools.partial(last_piece, chunk))
    begin, first, gap = steps
    for t in range(T):
        if begin + t < 0:
            ring.start(t)
        else:
            events.setdefault(begin + t, []).append(functools.partial(ring.start, t))
    rest = []
    for i, event in enumerate(ring.events()):
        step = int(first + gap * i)
        if step < 32:
            events.setdefault(step, []).append(event)
        else:
            rest.append(event)

    def step_body(step, carry):
        for when, actions in sorted(events.items()):
            @pl.when(step == when)
            def _():
                for action in actions:
                    action()
        pl.when(step < 16)(lambda: near_tile(step))
        pl.when(step >= 16)(lambda: far_tile(step - 8))
        return carry

    lax.fori_loop(0, 32, step_body, 0)
    total = acc[:, DH : DH + 1]
    result = acc[...] / total
    outputs[...] = result
    log_total = top[...] + jnp.log2(total)
    for block in range(4):
        logs[:, block * BLOCK : (block + 1) * BLOCK] = log_total[block * BLOCK : (block + 1) * BLOCK].T[:8]
    att_low[...] = result.astype(jnp.bfloat16)

    def out_copy(mate):
        return remote(att_low.at[block_rows(mate[0])], att.at[seq], out_send.at[mate[0]], out_recv.at[seq], mate)

    for mate in mates[1:] + mates[:1]:
        out_copy(mate).start()
    own_out = pltpu.make_async_copy(att_low.at[mine], att.at[seq], here.at[1])
    own_out.start()
    for event in rest:
        event()
    own_out.wait()
    for mate in mates:
        kv_copy(mate).wait_send()
        q_copy(mate).wait_send()
        out_copy(mate).wait_send()
        ref = att.at[mate[0]]
        remote(ref, ref, out_send.at[mate[0]], out_recv.at[mate[0]], mate).wait_recv()
    for chunk in range(4):
        @pl.when(slot < 2)
        def _():
            first_hop(chunk, 1).wait_send()

        @pl.when(slot == 0)
        def _():
            first_hop(chunk, 0).wait_send()

        @pl.when(slot >= 2)
        def _():
            second_hop(chunk).wait_send()


def attend(count, qkv, tables, shards, splits, steps=(0, 18, 2)):
    rows = qkv.shape[2]
    own = 4 * rows
    T = len(shards)
    return pl.pallas_call(
        functools.partial(attend_kernel, count, splits, steps),
        out_shape=[
            jax.ShapeDtypeStruct((HEADS, rows, LANES), jnp.bfloat16),
            jax.ShapeDtypeStruct((7, own, LANES), jnp.bfloat16),
            jax.ShapeDtypeStruct((own, LANES), jnp.float32),
            jax.ShapeDtypeStruct((8, own), jnp.float32),
        ]
        + [jax.ShapeDtypeStruct((count,) + w.shape, w.dtype) for w in shards],
        in_specs=[VMEM, ANY] + [VMEM] * T,
        out_specs=[VMEM] * 4 + [ANY] * T,
        scratch_shapes=[
            pltpu.VMEM((own, LANES), jnp.float32),
            pltpu.VMEM((own, LANES), jnp.float32),
            pltpu.VMEM((own, LANES), jnp.bfloat16),
            pltpu.VMEM((3, LANES, TABLE), jnp.float32),
            DMA((4,)), DMA((4,)), DMA((4,)), DMA((4,)), DMA((12,)), DMA((8,)), DMA((4,)), DMA((4,)), DMA((3,)),
        ]
        + Gather.sems(count, T),
        compiler_params=pltpu.CompilerParams(collective_id=2, has_side_effects=True, vmem_limit_bytes=56 << 20),
    )(qkv, tables, *shards)


class Scatter(Ring):
    def __init__(self, count, splits, parts, outs, bufs, sems):
        super().__init__(count, splits)
        self.parts, self.outs = parts, outs
        T = len(splits)
        self.mine, self.plane_in = bufs[:T], bufs[T : 2 * T]
        self.ring0, self.ring1 = bufs[2 * T : 3 * T], bufs[3 * T : 4 * T]
        self.low, self.low_in, self.done = bufs[4 * T : 5 * T], bufs[5 * T : 6 * T], bufs[6 * T : 7 * T]
        (self.load, self.plane_s, self.plane_r, self.ring_s, self.ring_r, self.end_s, self.end_r, self.put) = sems

    @staticmethod
    def scratch(count, splits, rows):
        half = [a + 2 * b for a, b in splits]
        bf = jnp.bfloat16
        out = [pltpu.VMEM((count, r, h), bf) for r, h in zip(rows, half)]
        out += [pltpu.VMEM((count, r, b), bf) for r, (a, b) in zip(rows, splits)]
        out += [pltpu.VMEM((count - 1 if a else 1, r, max(a, LANES)), bf) for r, (a, b) in zip(rows, splits)]
        out += [pltpu.VMEM((count - 1, r, b), bf) for r, (a, b) in zip(rows, splits)]
        out += [pltpu.VMEM((r, a + b), bf) for r, (a, b) in zip(rows, splits)]
        out += [pltpu.VMEM((r, a + b), bf) for r, (a, b) in zip(rows, splits)]
        out += [pltpu.VMEM((r, h), jnp.float32) for r, h in zip(rows, half)]
        T = len(splits)
        return out + [DMA((T * count,))] * 3 + [DMA((2 * T * (count - 1),))] * 2 + [DMA((2 * T,))] * 2 + [DMA((T,))]

    def dest(self, rel):
        return ring_index((self.place + rel) % self.count, self.count)

    def load_copy(self, t, rel):
        part, first = self.parts[t]
        src = part.at[self.dest(rel), :, pl.ds(first, self.half(t))]
        return pltpu.make_async_copy(src, self.mine[t].at[rel], self.load.at[t * self.count + rel])

    def remote(self, src, dst, s, r, i, device):
        return pltpu.make_async_remote_copy(src, dst, s.at[i], r.at[i], device_id=device, device_id_type=MESH)

    def single(self, t, plane):
        both, single = self.splits[t]
        return pl.ds(pl.multiple_of(both + plane * single, LANES), single)

    def plane_copy(self, t, rel):
        src = self.mine[t].at[rel, :, self.single(t, 1 - self.plane)]
        return self.remote(src, self.plane_in[t].at[rel], self.plane_s, self.plane_r, t * self.count + rel, self.plane_mate)

    def rels(self, D):
        return sorted({D % self.count, (-D) % self.count})

    def order(self):
        out = []
        for D in range(self.far, -1, -1):
            out += self.rels(D)
        return out

    def start(self, t):
        for rel in self.order():
            self.load_copy(t, rel).start()

    def ready(self, t, rel):
        if self.parts[t]:
            self.load_copy(t, rel).wait()
        self.plane_copy(t, rel).start()

    def open(self, t):
        for rel in self.rels(self.far):
            self.ready(t, rel)

    def step(self, t, D, ahead=True):
        if ahead and D:
            for rel in self.rels(D - 1):
                self.ready(t, rel)
        self.combine(t, D)
        if D:
            self.chain(t, D)
        else:
            self.close(t)

    def buffer(self, t, kind, slot):
        if kind:
            return self.ring1[t].at[slot]
        return self.ring0[t].at[slot]

    def own_ref(self, t, kind, rel):
        if kind:
            return self.mine[t].at[rel, :, self.single(t, self.plane)]
        return self.mine[t].at[rel, :, pl.ds(0, self.splits[t][0])]

    def ring_copy(self, t, kind, way, D):
        slot = self.slot(kind, way, D)
        if D == self.reach(kind, way):
            src = self.own_ref(t, kind, D % self.count if way == 0 else (-D) % self.count)
        else:
            src = self.buffer(t, kind, self.slot(kind, way, D + 1))
        i = (2 * t + kind) * (self.count - 1) + slot
        return self.remote(src, self.buffer(t, kind, slot), self.ring_s, self.ring_r, i, self.next(way))

    def ring_wait(self, t, kind, way, D):
        slot = self.slot(kind, way, D)
        ref = self.buffer(t, kind, slot)
        i = (2 * t + kind) * (self.count - 1) + slot
        self.remote(ref, ref, self.ring_s, self.ring_r, i, self.next(way)).wait_recv()

    def combine(self, t, D):
        for rel in self.rels(D):
            self.plane_copy(t, rel).wait_send()
            ref = self.plane_in[t].at[rel]
            self.remote(ref, ref, self.plane_s, self.plane_r, t * self.count + rel, self.plane_mate).wait_recv()
            own = self.own_ref(t, 1, rel)
            own[...] = own[...] + self.plane_in[t][rel]

    def chain(self, t, D):
        for kind in self.kinds(t):
            for way in (0, 1):
                if D > self.reach(kind, way):
                    continue
                if D < self.reach(kind, way):
                    self.ring_wait(t, kind, way, D + 1)
                    rel = D % self.count if way == 0 else (-D) % self.count
                    ref = self.buffer(t, kind, self.slot(kind, way, D + 1))
                    ref[...] = ref[...] + self.own_ref(t, kind, rel)[...]
                self.ring_copy(t, kind, way, D).start()

    def end_copy(self, t):
        return self.remote(self.low[t], self.low_in[t], self.end_s, self.end_r, 2 * t, self.plane_mate)

    def close(self, t):
        both, single = self.splits[t]
        for kind in self.kinds(t):
            total = self.own_ref(t, kind, 0)[...].astype(jnp.float32)
            for way in (0, 1):
                if self.reach(kind, way):
                    self.ring_wait(t, kind, way, 1)
                    total = total + self.buffer(t, kind, self.slot(kind, way, 1))[...].astype(jnp.float32)
            if kind:
                self.low[t][:, both:] = total.astype(jnp.bfloat16)
            else:
                self.low[t][:, :both] = total.astype(jnp.bfloat16)
        self.end_copy(t).start()

    def out_ref(self, t, core):
        out, whole, first = self.outs[t]
        return out.at[:, pl.ds(pl.multiple_of(core * whole + first, LANES), self.half(t))]

    def out_copy(self, t):
        return self.remote(self.done[t], self.out_ref(t, self.core), self.end_s, self.end_r, 2 * t + 1, self.core_mate)

    def put_copy(self, t):
        return pltpu.make_async_copy(self.done[t], self.out_ref(t, self.core), self.put.at[t])

    def deliver(self, t):
        both, single = self.splits[t]
        self.end_copy(t).wait_send()
        ref = self.low_in[t]
        self.remote(ref, ref, self.end_s, self.end_r, 2 * t, self.plane_mate).wait_recv()
        if both:
            self.done[t][:, :both] = self.low[t][:, :both].astype(jnp.float32) + self.low_in[t][:, :both].astype(jnp.float32)
        if single:
            self.done[t][:, self.single(t, self.plane)] = self.low[t][:, both:].astype(jnp.float32)
            self.done[t][:, self.single(t, 1 - self.plane)] = self.low_in[t][:, both:].astype(jnp.float32)
        self.out_copy(t).start()
        self.put_copy(t).start()

    def finish(self, t):
        for kind in self.kinds(t):
            for way in (0, 1):
                for D in range(1, self.reach(kind, way) + 1):
                    self.ring_copy(t, kind, way, D).wait_send()
        self.out_copy(t).wait_send()
        self.put_copy(t).wait()
        ref = self.out_ref(t, 1 - self.core)
        self.remote(ref, ref, self.end_s, self.end_r, 2 * t + 1, self.core_mate).wait_recv()


def retreat_kernel(count, splits, steps, grad_att, turned_in, store_in, outputs, logs, part, back, out, *refs):
    T = len(splits)
    (grads, delta, grad_q, grad_kv, send_kv, kv_in0, kv_in1, low, in_send, in_recv, up_send, up_recv,
     turned, store, out_send, out_recv, here) = refs[:17]
    refs = refs[17:]
    loads = [pltpu.make_async_copy(turned_in, turned, here.at[2]), pltpu.make_async_copy(store_in, store, here.at[3])]
    for copy in loads:
        copy.start()
    halves = [a + 2 * b for a, b in splits]
    firsts = [sum(halves[:t]) for t in range(T)]
    ring = Scatter(
        count, splits, [(part, first) for first in firsts], [(out, sum(halves), first) for first in firsts],
        refs[: 7 * T], refs[7 * T :])
    seq, slot = ring.seq, ring.fsdp % GSLOTS
    mates, (x_mate, z_mate) = seq_mates(ring), slot_mates(ring)
    enter(ring.neighbours() + mates[2:] + [x_mate, z_mate])

    def remote(src, dst, send, recv, device):
        return pltpu.make_async_remote_copy(src, dst, send, recv, device_id=device, device_id_type=MESH)

    mine = block_rows(seq)

    def in_copy(mate):
        return remote(grad_att.at[mate[0]], grads.at[mine], in_send.at[mate[0]], in_recv.at[seq], mate)

    for mate in mates[1:] + mates[:1]:
        in_copy(mate).start()
    own_copy = pltpu.make_async_copy(grad_att.at[seq], grads.at[mine], here.at[0])
    own_copy.start()
    grad_q[...] = jnp.zeros_like(grad_q)
    grad_kv[...] = jnp.zeros_like(grad_kv)
    own_copy.wait()
    for mate in mates:
        ref = grads.at[block_rows(mate[0])]
        remote(ref, ref, in_send.at[mate[0]], in_recv.at[mate[0]], mate).wait_recv()
    for block in range(4):
        rows = pl.ds(block * BLOCK, BLOCK)
        sums = jnp.sum(grads[rows, :].astype(jnp.float32) * outputs[rows, :], axis=1, keepdims=True)
        delta[:, rows] = jnp.broadcast_to(sums, (BLOCK, LANES)).T[:8]

    for copy in loads:
        copy.wait()

    def tile(forward_phase, key_block, query_block, blocks):
        source, active, table, column = tile_place(slot, seq, forward_phase, key_block, query_block)

        @pl.when(active)
        def _():
            size = blocks * BLOCK
            key_rows, rows = block_rows(key_block), pl.ds(pl.multiple_of(query_block * BLOCK, BLOCK), size)
            keys, values = store[1 + 2 * source, key_rows, :], store[2 + 2 * source, key_rows, :]
            queries, tops = store[0, rows, :], grads[rows, :]
            scores = lax.dot_general(keys, queries, (((1,), (1,)), ((), ())), preferred_element_type=jnp.float32)
            bias = jnp.concatenate(
                [turned[table, :, pl.ds(pl.multiple_of(TURNED_ZERO - column - LANES * part, LANES), size)] for part in range(BLOCK // LANES)],
                axis=0,
            )
            weights = jnp.exp2(scores * (DH**-0.5 * LOG2E) + (bias - logs[:1, rows]))
            grad_weights = lax.dot_general(values, tops, (((1,), (1,)), ((), ())), preferred_element_type=jnp.float32)
            grad_scores = (weights * (grad_weights - delta[:1, rows])).astype(jnp.bfloat16)
            grad_kv[source, 1, key_rows, :] += jnp.dot(weights.astype(jnp.bfloat16), tops, preferred_element_type=jnp.float32)
            grad_kv[source, 0, key_rows, :] += jnp.dot(grad_scores, queries, preferred_element_type=jnp.float32)
            grad_q[rows, :] += lax.dot_general(grad_scores, keys, (((0,), (0,)), ((), ())), preferred_element_type=jnp.float32)

    def far_tile(step):
        phase = step // 8
        piece = jnp.where(slot == 2, 1 - phase, phase)
        tile(jnp.where(slot == 3, 2 - piece, 1 + piece), (step // 2) % 4, 2 * (step % 2), 2)

    def near_tile(step):
        tile(0, step // 4, step % 4, 1)

    scale = DH**-0.5

    def rounded(source, chunk, extra):
        rows = block_rows(chunk)
        keys = grad_kv[source, 0, rows, :] * scale
        values = grad_kv[source, 1, rows, :]
        for more in extra:
            keys = keys + more[0].astype(jnp.float32)
            values = values + more[1].astype(jnp.float32)
        return keys.astype(jnp.bfloat16), values.astype(jnp.bfloat16)

    def x_send(chunk):
        src = send_kv.at[0, :, block_rows(chunk)]
        return remote(src, kv_in0.at[:, block_rows(chunk)], up_send.at[chunk], up_recv.at[chunk], x_mate)

    def z_send(chunk):
        src = send_kv.at[1, :, block_rows(chunk)]
        return remote(src, kv_in1.at[:, block_rows(chunk)], up_send.at[4 + chunk], up_recv.at[4 + chunk], z_mate)

    def x_wait(chunk):
        ref = kv_in0.at[:, block_rows(chunk)]
        remote(ref, ref, up_send.at[chunk], up_recv.at[chunk], x_mate).wait_recv()

    def z_wait(chunk):
        ref = kv_in1.at[:, block_rows(chunk)]
        remote(ref, ref, up_send.at[4 + chunk], up_recv.at[4 + chunk], z_mate).wait_recv()

    def first_done(chunk):
        @pl.when(slot >= 1)
        def _():
            source = jnp.where(slot == 2, 2, 1)
            keys, values = rounded(source, chunk, [])
            send_kv[0, 0, block_rows(chunk), :] = keys
            send_kv[0, 1, block_rows(chunk), :] = values
            x_send(chunk).start()

    def second_done(chunk):
        @pl.when(slot >= 2)
        def _():
            x_wait(chunk)
            source = slot - 1
            keys, values = rounded(source, chunk, [kv_in0[:, block_rows(chunk), :]])
            send_kv[1, 0, block_rows(chunk), :] = keys
            send_kv[1, 1, block_rows(chunk), :] = values
            z_send(chunk).start()

    def out_copy(mate):
        src = low.at[:, block_rows(mate[0])]
        return remote(src, back.at[seq], out_send.at[mate[0]], out_recv.at[seq], mate)

    def own_done(chunk):
        rows = block_rows(chunk)
        low[0, rows, :] = (grad_q[rows, :] * scale).astype(jnp.bfloat16)

        @pl.when(slot == 0)
        def _():
            x_wait(chunk)
            z_wait(chunk)
            low[1, rows, :], low[2, rows, :] = rounded(0, chunk, [kv_in0[:, rows, :], kv_in1[:, rows, :]])

        @pl.when(slot == 1)
        def _():
            z_wait(chunk)
            low[1, rows, :], low[2, rows, :] = rounded(0, chunk, [kv_in1[:, rows, :]])

        @pl.when(slot >= 2)
        def _():
            low[1, rows, :], low[2, rows, :] = rounded(0, chunk, [])

    events = {}
    for chunk in range(4):
        events.setdefault(2 * chunk + 2, []).append(functools.partial(first_done, chunk))
        events.setdefault(10 + 2 * chunk, []).append(functools.partial(second_done, chunk))
    begin, ready, first, hop, lag = steps
    rest = []
    for t in range(T):
        plan = [(begin, functools.partial(ring.start, t)), (ready, functools.partial(ring.open, t))]
        when = first + lag * t
        for D in range(ring.far, -1, -1):
            plan.append((when, functools.partial(ring.step, t, D)))
            when += hop
        plan.append((when, functools.partial(ring.deliver, t)))
        plan.append((when + hop, functools.partial(ring.finish, t)))
        for when, event in plan:
            if when < 32:
                events.setdefault(int(when), []).append(event)
            else:
                rest.append((when, event))
    rest = [event for when, event in sorted(rest, key=lambda pair: pair[0])]

    def step_body(step, carry):
        for when, actions in sorted(events.items()):
            @pl.when(step == when)
            def _():
                for action in actions:
                    action()
        pl.when(step < 16)(lambda: far_tile(step))
        pl.when(step >= 16)(lambda: near_tile(step - 16))
        return carry

    lax.fori_loop(0, 32, step_body, 0)
    for chunk in range(4):
        own_done(chunk)
    for mate in mates[1:] + mates[:1]:
        out_copy(mate).start()
    own_out = pltpu.make_async_copy(low.at[:, mine], back.at[seq], here.at[1])
    own_out.start()
    for event in rest:
        event()
    own_out.wait()
    for mate in mates:
        in_copy(mate).wait_send()
        out_copy(mate).wait_send()
        ref = back.at[mate[0]]
        remote(ref, ref, out_send.at[mate[0]], out_recv.at[mate[0]], mate).wait_recv()
    for chunk in range(4):
        @pl.when(slot >= 1)
        def _():
            x_send(chunk).wait_send()

        @pl.when(slot >= 2)
        def _():
            z_send(chunk).wait_send()


def retreat(count, grad_att, turned, store, outputs, logs, part, splits, steps=(0, 1, 2, 3, 1)):
    rows = grad_att.shape[1]
    own = 4 * rows
    _, shard_rows, half = part.shape
    return pl.pallas_call(
        functools.partial(retreat_kernel, count, splits, steps),
        out_shape=[jax.ShapeDtypeStruct((HEADS, 3, rows, LANES), jnp.bfloat16), jax.ShapeDtypeStruct((shard_rows, 2 * half), jnp.float32)],
        in_specs=[VMEM, ANY, ANY, VMEM, VMEM, ANY],
        out_specs=[VMEM, ANY],
        scratch_shapes=[
            pltpu.VMEM((own, LANES), jnp.bfloat16),
            pltpu.VMEM((8, own), jnp.float32),
            pltpu.VMEM((own, LANES), jnp.float32),
            pltpu.VMEM((3, 2, own, LANES), jnp.float32),
            pltpu.VMEM((2, 2, own, LANES), jnp.bfloat16),
            pltpu.VMEM((2, own, LANES), jnp.bfloat16),
            pltpu.VMEM((2, own, LANES), jnp.bfloat16),
            pltpu.VMEM((3, own, LANES), jnp.bfloat16),
            DMA((4,)), DMA((4,)), DMA((8,)), DMA((8,)),
            pltpu.VMEM((3, LANES, TABLE), jnp.float32), pltpu.VMEM((7, own, LANES), jnp.bfloat16),
            DMA((4,)), DMA((4,)), DMA((4,)),
        ]
        + Scatter.scratch(count, splits, [shard_rows] * len(splits)),
        compiler_params=pltpu.CompilerParams(collective_id=3, has_side_effects=True, vmem_limit_bytes=60 << 20),
    )(grad_att, turned, store, outputs, logs, part)


CHUNK = 512


def gelu_pair(v):
    root = 0.7978845608028654
    square = v * v
    t = jnp.tanh(root * (v + 0.044715 * square * v))
    up = 0.5 * (1.0 + t)
    return v * up, up + 0.5 * v * (1.0 - t * t) * (root * (1.0 + 3.0 * 0.044715 * square))


def contract(left, right, left_axis, right_axis):
    return lax.dot_general(left, right, (((left_axis,), (right_axis,)), ((), ())), preferred_element_type=jnp.float32)


def feed_kernel(count, att, gates, tokens, cotangent, norms, output_w, inner_w, outer_w,
                layer_out, grad_residual, grad_att, grad_logit, grad_norms, part_output, part_inner, outer_out,
                w_out, w_in, w_up, acts, act_in, slopes, slope_in, scaled, scaled_in, scaled_t, cot_in, cot_t,
                acc, normed, grad_scaled, branch_low, branch_in, branch_t, att_in, gates_in,
                stage_inner, stage_output,
                load_out, load_in, load_up, pair_s, pair_r, act_s, act_r, slope_s, slope_r, put_inner, put_output, *refs):
    half = cotangent.shape[1] // 2
    ring = Scatter(count, (SPLITS["outer"],), [None], [(outer_out, half, 0)], refs[:7], refs[7:])
    core, mate = ring.core, ring.core_mate
    experts = HEADS * EXP
    chunks = inner_w.shape[1] // CHUNK
    small = CHUNK // 2
    shards = max(1, count // chunks)

    def out_load(e):
        return pltpu.make_async_copy(output_w.at[pl.ds(e * DH, DH)], w_out.at[e, pl.ds(0, DH)], load_out.at[e])

    def ffn_load(chunk, slot):
        cols = pl.ds(pl.multiple_of(chunk * CHUNK, CHUNK), CHUNK)
        return (pltpu.make_async_copy(inner_w.at[:, cols], w_in.at[slot], load_in.at[slot]),
                pltpu.make_async_copy(outer_w.at[cols], w_up.at[slot], load_up.at[slot]))

    def chunk_of(step):
        if count != chunks:
            return step
        D = ring.far - (step + 1) // 2
        odd = step % 2
        return ring.dest((odd * D + (1 - odd) * (count - D)) % count)

    for e in range(experts):
        out_load(e).start()
    for sub in range(2):
        for copy in ffn_load(chunk_of(sub), sub):
            copy.start()
    enter(ring.neighbours())

    def remote(src, dst, send, recv):
        return pltpu.make_async_remote_copy(src, dst, send, recv, device_id=mate, device_id_type=MESH)

    mine = pl.ds(pl.multiple_of(core * half, LANES), half)
    yours = pl.ds(pl.multiple_of((1 - core) * half, LANES), half)
    pair = [
        remote(att, att_in, pair_s.at[0], pair_r.at[0]),
        remote(gates.at[0], gates_in, pair_s.at[1], pair_r.at[1]),
        remote(cotangent.at[:, yours], cot_in, pair_s.at[2], pair_r.at[2]),
        remote(scaled, scaled_in, pair_s.at[3], pair_r.at[3]),
        remote(branch_low.at[:, yours], branch_in, pair_s.at[4], pair_r.at[4]),
    ]
    for copy in pair[:3]:
        copy.start()

    def mixed_pair(att_ref, gate, two):
        tiles = []
        for which in (2 * two, 2 * two + 1):
            column = gate[:, experts + which : experts + which + 1]
            tiles.append((att_ref[which // EXP].astype(jnp.float32) * column).astype(jnp.bfloat16))
        return jnp.concatenate(tiles, axis=1)

    w_out[:, DH:, :] = jnp.zeros((experts, LANES - DH, w_out.shape[2]), jnp.bfloat16)
    acc[...] = tokens[...].astype(jnp.float32)
    for two in range(experts // 2):
        out_load(2 * two).wait()
        out_load(2 * two + 1).wait()
        weights = w_out[2 * two : 2 * two + 2].reshape(2 * LANES, w_out.shape[2])
        acc[...] += jnp.dot(mixed_pair(att, gates.at[0], two), weights, preferred_element_type=jnp.float32)
    residual = acc[...]
    centred = residual - jnp.mean(residual, axis=1, keepdims=True)
    inverse = lax.rsqrt(jnp.mean(centred * centred, axis=1, keepdims=True) + EPSILON)
    normed[...] = centred * inverse
    scaled[...] = (normed[...] * norms[:1] + norms[1:2]).astype(jnp.bfloat16)
    pair[3].start()
    rows = tokens.shape[0]
    scaled_t[:, :rows] = scaled[...].T
    cot_t[:, :rows] = cotangent[:, mine].T
    grad_scaled[...] = jnp.zeros_like(grad_scaled)
    pair[2].wait_recv()
    cot_t[:, rows:] = cot_in[...].T
    pair[3].wait_recv()
    scaled_t[:, rows:] = scaled_in[...].T

    small_mine = pl.ds(pl.multiple_of(core * small, LANES), small)
    small_yours = pl.ds(pl.multiple_of((1 - core) * small, LANES), small)

    def act_copy(step, sub):
        return remote(acts.at[sub], act_in.at[step], act_s.at[sub], act_r.at[step])

    def slope_copy(step, sub):
        return remote(slopes.at[sub, :, small_yours], slope_in.at[step], slope_s.at[sub], slope_r.at[step])

    def put_inner_copy(step, sub):
        cols = pl.ds(pl.multiple_of(chunk_of(step) * small, small), small)
        return pltpu.make_async_copy(stage_inner.at[sub], part_inner.at[:, cols], put_inner.at[sub])

    def forward_backward(step, sub):
        for copy in ffn_load(chunk_of(step), sub):
            copy.wait()

        @pl.when(step > 1)
        def _():
            act_copy(step, sub).wait_send()
            slope_copy(step, sub).wait_send()

        act, slope = gelu_pair(jnp.dot(scaled[...], w_in[sub], preferred_element_type=jnp.float32))
        acts[sub] = act.astype(jnp.bfloat16)
        act_copy(step, sub).start()
        slopes[sub] = (contract(cotangent[...], w_up[sub], 1, 1) * slope).astype(jnp.bfloat16)
        slope_copy(step, sub).start()
        acc[...] += jnp.dot(acts[sub], w_up[sub], preferred_element_type=jnp.float32)
        grad_scaled[...] += contract(slopes[sub], w_in[sub], 1, 1)

        @pl.when(step + 2 < chunks)
        def _():
            for copy in ffn_load(chunk_of(step + 2), sub):
                copy.start()

    def weight_parts(step, sub):
        remote(act_in.at[step], act_in.at[step], act_s.at[sub], act_r.at[step]).wait_recv()
        total = jnp.dot(cot_t[:, :rows], acts[sub], preferred_element_type=jnp.float32)
        total = total + jnp.dot(cot_t[:, rows:], act_in[step], preferred_element_type=jnp.float32)
        turned = total.astype(jnp.bfloat16).T
        shard_rows = CHUNK // shards
        for q in range(shards):
            rel = (ring_place(chunk_of(step) * shards + q, count) - ring.place + count) % count
            ring.mine[0][rel] = turned[q * shard_rows : (q + 1) * shard_rows]
        remote(slope_in.at[step], slope_in.at[step], slope_s.at[sub], slope_r.at[step]).wait_recv()

        @pl.when(step > 1)
        def _():
            put_inner_copy(step, sub).wait()

        total = jnp.dot(scaled_t[:, :rows], slopes[sub, :, small_mine], preferred_element_type=jnp.float32)
        total = total + jnp.dot(scaled_t[:, rows:], slope_in[step], preferred_element_type=jnp.float32)
        stage_inner[sub] = total.astype(jnp.bfloat16)
        put_inner_copy(step, sub).start()

    events = {}
    if count == chunks:
        for step, rel in enumerate(ring.order()):
            events.setdefault(step, []).append(functools.partial(ring.ready, 0, rel))
        for D in range(ring.far, 0, -1):
            events.setdefault(2 * (ring.far - D) + 1, []).append(functools.partial(ring.step, 0, D, False))

    def after_parts(step):
        for when, actions in sorted(events.items()):
            @pl.when(step == when)
            def _():
                for action in actions:
                    action()

    def iteration(i, carry):
        forward_backward(2 * i, 0)

        @pl.when(i > 0)
        def _():
            weight_parts(2 * i - 1, 1)
            after_parts(2 * i - 1)

        forward_backward(2 * i + 1, 1)
        weight_parts(2 * i, 0)
        after_parts(2 * i)
        return carry

    lax.fori_loop(0, chunks // 2, iteration, 0)
    weight_parts(chunks - 1, 1)
    if count == chunks:
        for action in events[chunks - 1]:
            action()
    else:
        ring.open(0)
        for D in range(ring.far, 0, -1):
            ring.step(0, D)
    layer_out[...] = acc[...].astype(jnp.bfloat16)
    slope = grad_scaled[...]
    grad_norms[...] = jnp.concatenate(
        [jnp.sum(slope * normed[...], axis=0, keepdims=True), jnp.sum(slope, axis=0, keepdims=True),
         jnp.zeros((6, slope.shape[1]), jnp.float32)], axis=0)
    slope = slope * norms[:1]
    total = cotangent[...].astype(jnp.float32) + inverse * (
        slope - jnp.mean(slope, axis=1, keepdims=True)
        - normed[...] * jnp.mean(slope * normed[...], axis=1, keepdims=True))
    grad_residual[...] = total
    branch_low[...] = total.astype(jnp.bfloat16)
    pair[4].start()
    branch_t[:, :rows] = branch_low[:, mine].T
    ring.step(0, 0)
    lane = lax.broadcasted_iota(jnp.int32, (rows, LANES), 1)
    logit = jnp.zeros((rows, LANES), jnp.float32)
    head_total = None
    for which in range(experts):
        if which % 2 == 0:
            weights = w_out[which : which + 2].reshape(2 * LANES, w_out.shape[2])
            both = contract(branch_low[...], weights, 1, 1)
        grad_mixed = both[:, which % 2 * LANES : (which % 2 + 1) * LANES]
        head, expert = which // EXP, which % EXP
        column = slice(experts + which, experts + which + 1)
        term = grad_mixed * gates[0, :, column]
        head_total = term if expert == 0 else head_total + term
        if expert == EXP - 1:
            grad_att[head] = head_total.astype(jnp.bfloat16)
        sums = jnp.sum(grad_mixed * att[head].astype(jnp.float32), axis=1, keepdims=True)
        logit = jnp.where(lane == experts + which, sums, logit)
    grad_logit[...] = logit * gates[1]
    ring.deliver(0)
    pair[0].wait_recv()
    pair[1].wait_recv()
    pair[4].wait_recv()
    branch_t[:, rows:] = branch_in[...].T

    def put_output_copy(which):
        return pltpu.make_async_copy(stage_output.at[which % 4, pl.ds(0, DH)], part_output.at[pl.ds(which * DH, DH)], put_output.at[which % 4])

    for two in range(experts // 2):
        total = jnp.dot(branch_t[:, :rows], mixed_pair(att, gates.at[0], two), preferred_element_type=jnp.float32)
        total = total + jnp.dot(branch_t[:, rows:], mixed_pair(att_in, gates_in, two), preferred_element_type=jnp.float32)
        turned = total.astype(jnp.bfloat16).T
        for side in range(2):
            which = 2 * two + side
            if which >= 4:
                put_output_copy(which - 4).wait()
            stage_output[which % 4] = turned[side * LANES : (side + 1) * LANES]
            put_output_copy(which).start()
    for which in range(experts - 4, experts):
        put_output_copy(which).wait()
    for sub in range(2):
        put_inner_copy(sub, sub).wait()
        act_copy(sub, sub).wait_send()
        slope_copy(sub, sub).wait_send()
    ring.finish(0)
    for copy in pair:
        copy.wait_send()


def feed(count, att, gates, tokens, cotangent, norms, output_w, inner_w, outer_w):
    rows, width = tokens.shape
    wide = inner_w.shape[1]
    half = width // 2
    f32, bf = jnp.float32, jnp.bfloat16
    experts, chunks = HEADS * EXP, wide // CHUNK
    V = pltpu.VMEM
    return pl.pallas_call(
        functools.partial(feed_kernel, count),
        out_shape=[
            jax.ShapeDtypeStruct((rows, width), bf),
            jax.ShapeDtypeStruct((rows, width), f32),
            jax.ShapeDtypeStruct((HEADS, rows, LANES), bf),
            jax.ShapeDtypeStruct((rows, LANES), f32),
            jax.ShapeDtypeStruct((8, width), f32),
            jax.ShapeDtypeStruct((VCOLS, half), bf),
            jax.ShapeDtypeStruct((width, wide // 2), bf),
            jax.ShapeDtypeStruct((wide // count, width), f32),
        ],
        in_specs=[VMEM] * 5 + [ANY] * 3,
        out_specs=[VMEM] * 5 + [ANY] * 3,
        scratch_shapes=[
            V((experts, LANES, width), bf), V((2, width, CHUNK), bf), V((2, CHUNK, width), bf),
            V((2, rows, CHUNK), bf), V((chunks, rows, CHUNK), bf), V((2, rows, CHUNK), bf), V((chunks, rows, CHUNK // 2), bf),
            V((rows, width), bf), V((rows, width), bf), V((width, 2 * rows), bf), V((rows, half), bf), V((half, 2 * rows), bf),
            V((rows, width), f32), V((rows, width), f32), V((rows, width), f32),
            V((rows, width), bf), V((rows, half), bf), V((half, 2 * rows), bf), V((HEADS, rows, LANES), bf), V((rows, LANES), f32),
            V((2, width, CHUNK // 2), bf), V((4, LANES, half), bf),
            DMA((experts,)), DMA((2,)), DMA((2,)), DMA((5,)), DMA((5,)), DMA((2,)), DMA((chunks,)), DMA((2,)), DMA((chunks,)),
            DMA((2,)), DMA((4,)),
        ]
        + Scatter.scratch(count, (SPLITS["outer"],), [wide // count]),
        compiler_params=pltpu.CompilerParams(collective_id=4, has_side_effects=True, vmem_limit_bytes=63 << 20),
    )(att, gates, tokens, cotangent, norms, output_w, inner_w, outer_w)


def settle_kernel(count, back, experts, gates, grad_logit, tokens, joint_in, residual_in, grad_norms, part_output,
                  grad_tokens, joint_out, output_out, grads, grads_in, tokens_in, tokens_t, norms_in, norm_columns, joint, grad_residual, *refs):
    splits = (SPLITS["joint"], SPLITS["output"])
    pair_s, pair_r, load = refs[-3:]
    loads = [pltpu.make_async_copy(joint_in, joint, load.at[0]), pltpu.make_async_copy(residual_in, grad_residual, load.at[1])]
    for copy in loads:
        copy.start()
    half, output_half = JOINT // 2, part_output.shape[2]
    outs = [(joint_out, half, 0), (output_out, output_half, 0)]
    ring = Scatter(count, splits, [None, (part_output, 0)], outs, refs[:14], refs[14:-3])
    ring.start(1)
    enter(ring.neighbours())
    core = ring.core

    def remote(src, dst, i):
        return pltpu.make_async_remote_copy(src, dst, pair_s.at[i], pair_r.at[i], device_id=ring.core_mate, device_id_type=MESH)

    mine = pl.ds(pl.multiple_of(core * half, LANES), half)
    yours = pl.ds(pl.multiple_of((1 - core) * half, LANES), half)
    pair = [remote(tokens, tokens_in, 0), remote(grad_norms, norms_in, 1)]
    pair[0].start()
    pair[1].start()
    ring.open(1)
    rows = tokens.shape[0]
    lane = lax.broadcasted_iota(jnp.int32, (LANES, LANES), 1)
    width = HEADS * EXP

    def hand_over(block):
        part = pl.ds(pl.multiple_of(block * LANES, LANES), LANES)
        return remote(grads.at[part, yours], grads_in.at[part], 2 + block)


    def assemble(block, carry):
        part = pl.ds(pl.multiple_of(block * LANES, LANES), LANES)
        pieces = [back[head, which, part, :][:, :DH].astype(jnp.float32) for which in range(2) for head in range(HEADS)]
        logit = grad_logit[part, :]
        for head in range(HEADS):
            values = back[head, 2, part, :].astype(jnp.float32)
            for expert in range(EXP):
                which = head * EXP + expert
                pieces.append((values * gates[0, part, which : which + 1])[:, :DH])
                sums = jnp.sum(values * experts[which, part, :].astype(jnp.float32), axis=1, keepdims=True)
                logit = jnp.where(lane == which, sums * gates[1, part, which : which + 1], logit)
        pieces.append(jnp.where(lane < 2 * width, logit, 0.0))
        pieces.append(jnp.zeros((LANES, JOINT - ROUTERS - LANES), jnp.float32))
        grads[part, :] = jnp.concatenate(pieces, axis=1).astype(jnp.bfloat16)
        hand_over(block).start()
        return carry

    lax.fori_loop(0, rows // LANES, assemble, 0)
    ring.step(1, ring.far)
    tokens_t[:, :rows] = tokens[...].T
    for copy in pair:
        copy.wait_recv()
    tokens_t[:, rows:] = tokens_in[...].T
    norm_tile = NORM // LANES * LANES - half
    first = NORM - half - norm_tile
    both = grad_norms[...] + norms_in[...]
    for block in range(both.shape[1] // LANES):
        columns = jnp.concatenate([both[:, block * LANES : (block + 1) * LANES], jnp.zeros((LANES - 8, LANES), jnp.float32)], axis=0)
        norm_columns[block * LANES : (block + 1) * LANES, :] = columns.T
    for block in range(rows // LANES):
        hand_over(block).wait_recv()
    shard_rows = tokens_t.shape[0] // count
    tile_lane = lax.broadcasted_iota(jnp.int32, (shard_rows, LANES), 1)

    def fill(rel):
        part = pl.ds(pl.multiple_of(ring.dest(rel) * shard_rows, shard_rows), shard_rows)
        total = jnp.dot(tokens_t[part, :rows], grads[:, mine], preferred_element_type=jnp.float32)
        total = total + jnp.dot(tokens_t[part, rows:], grads_in[...], preferred_element_type=jnp.float32)
        ring.mine[0][rel] = total.astype(jnp.bfloat16)
        extra = jnp.where(tile_lane == first, norm_columns[part, 0:1], 0.0) + jnp.where(tile_lane == first + 1, norm_columns[part, 1:2], 0.0)
        tile = total[:, norm_tile : norm_tile + LANES] + extra * core.astype(jnp.float32)
        ring.mine[0][rel, :, norm_tile : norm_tile + LANES] = tile.astype(jnp.bfloat16)

    for i, rel in enumerate(ring.order()):
        fill(rel)
        if i == 0:
            ring.open(0)
    ring.step(0, ring.far)
    for D in range(ring.far - 1, 0, -1):
        ring.step(1, D)
        ring.step(0, D)
        if D == ring.far - 1:
            for copy in loads:
                copy.wait()
            grad_tokens[...] = grad_residual[...] + contract(grads[...], joint[...], 1, 1)
    ring.step(1, 0)
    ring.step(0, 0)
    ring.deliver(1)
    ring.deliver(0)
    ring.finish(1)
    ring.finish(0)
    for copy in pair:
        copy.wait_send()
    for block in range(rows // LANES):
        hand_over(block).wait_send()


def settle(count, back, experts, gates, grad_logit, tokens, joint, grad_residual, grad_norms, part_output):
    rows, width = tokens.shape
    shard_rows = width // count
    f32, bf = jnp.float32, jnp.bfloat16
    V = pltpu.VMEM
    return pl.pallas_call(
        functools.partial(settle_kernel, count),
        out_shape=[jax.ShapeDtypeStruct((rows, width), f32), jax.ShapeDtypeStruct((shard_rows, JOINT), f32),
                   jax.ShapeDtypeStruct((part_output.shape[1], width), f32)],
        in_specs=[VMEM] * 5 + [ANY, ANY, VMEM, ANY],
        out_specs=[VMEM, VMEM, ANY],
        scratch_shapes=[V((rows, JOINT), bf), V((rows, JOINT // 2), bf), V((rows, width), bf), V((width, 2 * rows), bf), V((8, width), f32), V((width, LANES), f32),
                        V((width, JOINT), bf), V((rows, width), f32)]
        + Scatter.scratch(count, (SPLITS["joint"], SPLITS["output"]), [shard_rows, part_output.shape[1]])
        + [DMA((2 + rows // LANES,)), DMA((2 + rows // LANES,)), DMA((2,))],
        compiler_params=pltpu.CompilerParams(collective_id=5, has_side_effects=True, vmem_limit_bytes=60 << 20),
    )(back, experts, gates, grad_logit, tokens, joint, grad_residual, grad_norms, part_output)


def publish_kernel(joint_w, output_w, inner_w, outer_w, layer, tokens_in,
                   query, key, value, value_router, output_router, norms, output_out, inner_out, outer_out, layer_out, tokens_out,
                   *refs):
    held, turned, tail, load, store = refs[:6], refs[6], refs[7], refs[8], refs[9]
    sources = (joint_w, tokens_in, inner_w, outer_w, layer, output_w)
    loads = [pltpu.make_async_copy(src, buf, load.at[i]) for i, (src, buf) in enumerate(zip(sources, held))]
    for copy in loads:
        copy.start()
    half, small = inner_w.shape[1] // 2, CHUNK // 2
    stores = []

    def put(src, dst):
        copy = pltpu.make_async_copy(src, dst, store.at[len(stores)])
        copy.start()
        stores.append(copy)

    loads[0].wait()
    turned[...] = held[0][...].T
    for first, target in ((0, query), (QCOLS, key), (2 * QCOLS, value), (ROUTERS, value_router)):
        put(turned.at[pl.ds(first, target.shape[0])], target)
    tail[...] = turned[ROUTERS + HEADS * EXP : NORM, :]
    put(tail, output_router)
    norms[...] = turned[NORM : NORM + 8, :]
    for i, target in enumerate((tokens_out, inner_out, outer_out, layer_out, output_out)):
        loads[1 + i].wait()
        if i != 1:
            put(held[1 + i], target)
            continue
        for core in range(2):
            for chunk in range(half // small):
                put(held[1 + i].at[:, pl.ds(core * half + chunk * small, small)], target.at[:, pl.ds(chunk * CHUNK + core * small, small)])
    for copy in stores:
        copy.wait()


def publish(joint_w, output_w, inner_w, outer_w, layer, tokens):
    rows = joint_w.shape[0]
    f32 = jnp.float32
    columns = [QCOLS, QCOLS, VCOLS, HEADS * EXP, HEADS * EXP]
    rest = (output_w, inner_w, outer_w, layer, tokens)
    return pl.pallas_call(
        publish_kernel,
        out_shape=[jax.ShapeDtypeStruct((c, rows), f32) for c in columns] + [jax.ShapeDtypeStruct((8, rows), f32)]
        + [jax.ShapeDtypeStruct(x.shape, x.dtype) for x in rest],
        in_specs=[ANY] * 6,
        out_specs=[ANY] * 5 + [VMEM] + [ANY] * 5,
        scratch_shapes=[pltpu.VMEM(x.shape, x.dtype) for x in (joint_w, tokens, inner_w, outer_w, layer, output_w)]
        + [pltpu.VMEM((JOINT, rows), f32), pltpu.VMEM((HEADS * EXP, rows), f32)]
        + [DMA((6,)), DMA((9 + inner_w.shape[1] // (CHUNK // 2),))],
        compiler_params=pltpu.CompilerParams(vmem_limit_bytes=63 << 20),
    )(joint_w, *rest)


def on_device(
    tokens, value_routes, output_routes, cont_gap, query_weight, key_weight, value_weight, value_router,
    output_router, output_weight, norm_gain, norm_bias, inner_weight, outer_weight, cotangent,
):
    count = lax.axis_size("fsdp")
    inputs = tokens[0]
    rows, width = inputs.shape
    norm = jnp.stack([norm_gain, norm_bias])
    routes = jnp.concatenate([value_routes[0].reshape(rows, -1), output_routes[0].reshape(rows, -1)], axis=1)
    joint, tables, turned, qkv, experts, gates, norms = project(
        count, query_weight.T, key_weight.T, value_weight.T, value_router.T, output_router.T, norm, inputs, routes, cont_gap)
    att, store, outputs, logs, inner_full, outer_full, output_full = attend(
        count, qkv, tables, (inner_weight, outer_weight, output_weight), (SPLITS["inner"], SPLITS["outer"], SPLITS["output"]))
    layer, grad_residual, grad_att, grad_logit, grad_norms, part_output, part_inner, outer_w = feed(
        count, att, gates, inputs, cotangent[0], norms, output_full.reshape(VCOLS, width), inner_full.reshape(width, -1),
        outer_full.reshape(-1, width))
    back, inner_w = retreat(
        count, grad_att, turned, store, outputs, logs, part_inner.reshape(count, -1, part_inner.shape[1]), INNER_PARTS)
    grad_input, joint_w, output_w = settle(
        count, back, experts, gates, grad_logit, inputs, joint, grad_residual, grad_norms,
        part_output.reshape(count, -1, part_output.shape[1]))
    query, key, value, value_r, output_r, norm_w, output_w, inner_w, outer_w, layer, grad_input = publish(
        joint_w, output_w, inner_w, outer_w, layer, grad_input)
    return (layer[None], grad_input[None], query.T, key.T, value.T, value_r.T, output_r.T, output_w, norm_w[0], norm_w[1], inner_w, outer_w)


def solution(mesh):
    wide = P("fsdp", None)
    part = P("fsdp", "seq", None)
    routes = P("fsdp", "seq", None, None)
    return jax.shard_map(
        on_device,
        mesh=mesh,
        in_specs=(part, routes, routes, P()) + (wide,) * 6 + (P("fsdp"), P("fsdp"), wide, wide, part),
        out_specs=(part, part) + (wide,) * 6 + (P("fsdp"), P("fsdp"), wide, wide),
        check_vma=False,
    )
```

```python
import functools
import jax
import jax.numpy as jnp
from jax import lax
from jax.experimental import pallas as pl
from jax.experimental.pallas import tpu as pltpu
from jax.sharding import PartitionSpec as P

HEADS = 4
DH = 112
EXP = 5
CONT = 1024
GSLOTS = 4
PSLOTS = 2
BLOCK = 512
LANES = 128
EPSILON = 1e-05
NEGATIVE = -1e30
LOG2E = 1.4426950408889634
MESH = pl.DeviceIdType.MESH
ANY = pl.BlockSpec(memory_space=pl.ANY)
VMEM = pl.BlockSpec(memory_space=pltpu.VMEM)
SMEM = pl.BlockSpec(memory_space=pltpu.SMEM)
DMA = pltpu.SemaphoreType.DMA

QCOLS = HEADS * DH
VCOLS = HEADS * EXP * DH
ROUTERS = 2 * QCOLS + VCOLS
NORM = ROUTERS + 2 * HEADS * EXP
JOINT = 3328
SPLITS = {"joint": (640, 512), "output": (256, 128), "inner": (768, 640), "outer": (256, 128)}
INNER_PARTS = ((512, 768),)


def ring_place(index, count):
    return (index // 2) * (1 - index % 2) + (count - 1 - index // 2) * (index % 2)


def ring_index(place, count):
    upper = place // (count // 2)
    return 2 * place * (1 - upper) + (2 * (count - 1 - place) + 1) * upper


def enter(devices):
    barrier = pltpu.get_barrier_semaphore()
    for device in devices:
        pl.semaphore_signal(barrier, inc=1, device_id=device, device_id_type=MESH)
    pl.semaphore_wait(barrier, len(devices))


class Ring:
    def __init__(self, count, splits):
        self.count, self.splits = count, splits
        self.seq, self.fsdp = lax.axis_index("seq"), lax.axis_index("fsdp")
        self.plane, self.core = self.seq // 2, self.seq % 2
        self.place = ring_place(self.fsdp, count)
        self.right = (self.seq, ring_index((self.place + 1) % count, count))
        self.left = (self.seq, ring_index((self.place + count - 1) % count, count))
        self.core_mate = (self.seq + 1 - 2 * self.core, self.fsdp)
        self.plane_mate = ((self.seq + 2) % 4, self.fsdp)
        self.far = count // 2

    def neighbours(self):
        return [self.right, self.left, self.core_mate, self.plane_mate]

    def reach(self, kind, way):
        return self.far if kind == way else self.count - 1 - self.far

    def kinds(self, t):
        return [kind for kind in (1, 0) if self.splits[t][kind] > 0]

    def half(self, t):
        return self.splits[t][0] + 2 * self.splits[t][1]

    def cols(self, t, kind, plane, core):
        both, single = self.splits[t]
        if kind == 0:
            return pl.ds(pl.multiple_of(core * self.half(t), LANES), both)
        return pl.ds(pl.multiple_of(core * self.half(t) + both + plane * single, LANES), single)

    def behind(self, way, k):
        step = self.count - k if way == 0 else k
        return ring_index((self.place + step) % self.count, self.count)

    def next(self, way):
        return self.right if way == 0 else self.left

    def slot(self, kind, way, k):
        return k - 1 if way == 0 else self.reach(kind, 0) + k - 1


class Gather(Ring):
    def __init__(self, count, splits, shards, at, send, recv, local):
        super().__init__(count, splits)
        self.shards, self.at, self.send, self.recv, self.local = shards, at, send, recv, local

    @staticmethod
    def sems(count, tensors):
        return [DMA((6 * tensors * (count - 1),)), DMA((6 * tensors * (count - 1),)), DMA((tensors,))]

    def copy(self, src, dst, group, t, slot, device):
        i = (group * len(self.splits) + t) * (self.count - 1) + slot
        return pltpu.make_async_remote_copy(
            src, dst, self.send.at[i], self.recv.at[i], device_id=device, device_id_type=MESH
        )

    def same(self, group, t, kind, way, k, plane, core, device):
        ref = self.at(t, self.behind(way, k), self.cols(t, kind, plane, core))
        return self.copy(ref, ref, group, t, self.slot(kind, way, k), device)

    def hop(self, t, kind, way, k):
        if k > 1:
            ref = self.at(t, self.behind(way, k - 1), self.cols(t, kind, self.plane, self.core))
            return self.copy(ref, ref, kind, t, self.slot(kind, way, k), self.next(way))
        cols = self.cols(t, kind, self.plane, self.core)
        return self.copy(
            self.shards[t].at[:, cols], self.at(t, self.fsdp, cols), kind, t, self.slot(kind, way, 1), self.next(way)
        )

    def arrived(self, t, kind, way, k):
        return self.same(kind, t, kind, way, k, self.plane, self.core, self.next(way))

    def to_core(self, t, kind, way, k, core):
        return self.same(2 + kind, t, kind, way, k, self.plane, core, self.core_mate)

    def to_plane(self, t, way, k, plane):
        return self.same(4, t, 1, way, k, plane, self.core, self.plane_mate)

    def plane_to_core(self, t, way, k, core):
        return self.same(5, t, 1, way, k, 1 - self.plane, core, self.core_mate)

    def own(self, t):
        return pltpu.make_async_copy(self.shards[t], self.at(t, self.fsdp, slice(None)), self.local.at[t])

    def start(self, t):
        for kind in self.kinds(t):
            for way in (0, 1):
                if self.reach(kind, way):
                    self.hop(t, kind, way, 1).start()
        self.own(t).start()

    def arrive(self, t, k):
        for kind in self.kinds(t):
            for way in (0, 1):
                if k <= self.reach(kind, way):
                    self.arrived(t, kind, way, k).wait_recv()
                    if k < self.reach(kind, way):
                        self.hop(t, kind, way, k + 1).start()
                    if kind:
                        self.to_plane(t, way, k, self.plane).start()
                    self.to_core(t, kind, way, k, self.core).start()

    def plane_arrive(self, t, k):
        if 1 in self.kinds(t):
            for way in (0, 1):
                if k <= self.reach(1, way):
                    self.to_plane(t, way, k, 1 - self.plane).wait_recv()
                    self.plane_to_core(t, way, k, self.core).start()

    def finish(self, t):
        self.own(t).wait()
        for kind in self.kinds(t):
            for way in (0, 1):
                for k in range(1, self.reach(kind, way) + 1):
                    self.hop(t, kind, way, k).wait_send()
                    self.to_core(t, kind, way, k, self.core).wait_send()
                    self.to_core(t, kind, way, k, 1 - self.core).wait_recv()
                    if kind:
                        self.to_plane(t, way, k, self.plane).wait_send()
                        self.plane_to_core(t, way, k, self.core).wait_send()
                        self.plane_to_core(t, way, k, 1 - self.core).wait_recv()

    def events(self):
        tensors = range(len(self.splits))
        out = []
        for k in range(1, self.far + 1):
            for t in tensors:
                out.append(functools.partial(self.arrive, t, k))
                if k > 1:
                    out.append(functools.partial(self.plane_arrive, t, k - 1))
        for t in tensors:
            out.append(functools.partial(self.plane_arrive, t, self.far))
        for t in tensors:
            out.append(functools.partial(self.finish, t))
        return out


TABLE = 5632
TABLE_ZERO = 5120
TURNED_ZERO = 512


def route_lanes(routes, lane):
    hit = None
    for head in range(2 * HEADS):
        for choice in range(2):
            place = head * EXP + routes[:, 2 * head + choice : 2 * head + choice + 1]
            here = lane == place
            hit = here if hit is None else hit | here
    return hit.astype(jnp.float32)


def project_kernel(count, query, key, value, value_router, output_router, norm, tokens, routes, gaps,
                   joint_out, tables_out, turned_out, qkv, experts, gates, norms,
                   shard, shard_t, joint, tables, turned_tables, product, load, store, send, recv, local):
    rows = shard.shape[0]
    splits = (SPLITS["joint"],)
    at = lambda t, g, cols: joint.at[pl.ds(pl.multiple_of(g * rows, rows), rows), cols]
    ring = Gather(count, splits, [shard], at, send, recv, local)
    loads = []
    for i, (src, first) in enumerate(((query, 0), (key, QCOLS), (value, 2 * QCOLS))):
        loads.append(pltpu.make_async_copy(src, shard_t.at[pl.ds(first, src.shape[0])], load.at[i]))
        loads[-1].start()
    small = [ref[...].astype(jnp.float32) for ref in (value_router, output_router, norm)]
    small.append(jnp.zeros((JOINT - NORM - 2, rows), jnp.float32))
    shard_t[ROUTERS:, :] = jnp.concatenate(small, axis=0).astype(jnp.bfloat16)
    for copy in loads:
        copy.wait()
    shard[...] = shard_t[...].T
    enter(ring.neighbours())
    ring.start(0)
    slope = jnp.float32(0.0)
    for head in range(HEADS):
        slope = jnp.where(ring.seq // 1 == head, -0.5 * 0.5**head * LOG2E, slope)
    group = ring.fsdp // GSLOTS
    pair = jnp.maximum(ring.fsdp % GSLOTS - PSLOTS, 0) * 2
    gap_values = [jnp.int32(0), gaps[group, pair], gaps[group, pair + 1]]

    def table_column(step, carry):
        start = pl.multiple_of(step * 256, 256)
        lanes = lax.broadcasted_iota(jnp.int32, (8, 256 + LANES), 1) + (start - LANES)
        for which in range(3):
            for turned in range(2):
                if turned:
                    distance = lanes - TURNED_ZERO + gap_values[which]
                else:
                    distance = TABLE_ZERO - lanes + gap_values[which]
                bias = slope * jnp.log(1.0 + jnp.maximum(distance, 0).astype(jnp.float32))
                bias = jnp.where(distance >= 0, bias, NEGATIVE)
                wide = jnp.broadcast_to(bias[:1], (LANES, 256 + LANES))
                rolled = pltpu.roll(wide, 0, 1, stride=1, stride_axis=0)
                target = turned_tables if turned else tables
                target[which, :, pl.ds(start, 256)] = rolled[:, LANES:]
        return carry

    events = []
    for k in range(1, ring.far + 1):
        events.append(functools.partial(ring.arrive, 0, k))
        if k > 1:
            events.append(functools.partial(ring.plane_arrive, 0, k - 1))
    events += [functools.partial(ring.plane_arrive, 0, ring.far), functools.partial(ring.finish, 0)]
    cut = max(1, TABLE // 256 // (len(events) - 2))
    done = 0
    saves = [(tables, tables_out), (turned_tables, turned_out), (joint, joint_out)]
    saves = [pltpu.make_async_copy(src, dst, store.at[i]) for i, (src, dst) in enumerate(saves)]
    for i, event in enumerate(events):
        upto = min(TABLE // 256, (i + 1) * cut)
        if i == len(events) - 2:
            upto = TABLE // 256
        if upto > done:
            lax.fori_loop(done, upto, table_column, 0)
            done = upto
            if done == TABLE // 256:
                saves[0].start()
                saves[1].start()
        event()
    saves[2].start()

    def column(step, carry):
        cols = pl.ds(pl.multiple_of(step * 256, 256), 256)
        product[:, cols] = jnp.dot(tokens[...], joint[:, cols], preferred_element_type=jnp.float32)
        return carry

    lax.fori_loop(0, JOINT // 256, column, 0)
    norm_tile = NORM // LANES * LANES
    turned_norm = joint[:, norm_tile : norm_tile + LANES].astype(jnp.float32).T
    norms[...] = turned_norm[NORM - norm_tile : NORM - norm_tile + 8]
    logits = product[:, ROUTERS : ROUTERS + 2 * HEADS * EXP]
    local_rows = tokens.shape[0]
    wide = jnp.concatenate([logits, jnp.zeros((local_rows, LANES - 2 * HEADS * EXP), jnp.float32)], axis=1)
    lane = lax.broadcasted_iota(jnp.int32, (local_rows, LANES), 1)
    mask = route_lanes(routes[...], lane)
    gate = 1.0 / (1.0 + jnp.exp(-wide))
    gates[0] = gate * mask
    gates[1] = gate * mask * (1.0 - gate)
    pad = jnp.zeros((local_rows, LANES - DH), jnp.float32)
    ones = jnp.ones((local_rows, LANES - DH), jnp.float32)
    for head in range(HEADS):
        first = head * DH
        qkv[head, 0] = jnp.concatenate([product[:, first : first + DH], pad], axis=1).astype(jnp.bfloat16)
        first = QCOLS + head * DH
        qkv[head, 1] = jnp.concatenate([product[:, first : first + DH], pad], axis=1).astype(jnp.bfloat16)
        total = None
        for expert in range(EXP):
            which = head * EXP + expert
            first = 2 * QCOLS + which * DH
            piece = product[:, first : first + DH]
            experts[which] = jnp.concatenate([piece, pad], axis=1).astype(jnp.bfloat16)
            term = piece * gates[0, :, which : which + 1]
            total = term if total is None else total + term
        qkv[head, 2] = jnp.concatenate([total, ones], axis=1).astype(jnp.bfloat16)
    for copy in saves:
        copy.wait()


def project(count, query, key, value, value_router, output_router, norm, tokens, routes, gaps):
    rows, shard_rows = tokens.shape[0], query.shape[1]
    f32, bf = jnp.float32, jnp.bfloat16
    V = pltpu.VMEM
    return pl.pallas_call(
        functools.partial(project_kernel, count),
        out_shape=[
            jax.ShapeDtypeStruct((shard_rows * count, JOINT), bf),
            jax.ShapeDtypeStruct((3, LANES, TABLE), f32),
            jax.ShapeDtypeStruct((3, LANES, TABLE), f32),
            jax.ShapeDtypeStruct((HEADS, 3, rows, LANES), bf),
            jax.ShapeDtypeStruct((HEADS * EXP, rows, LANES), bf),
            jax.ShapeDtypeStruct((2, rows, LANES), f32),
            jax.ShapeDtypeStruct((8, shard_rows * count), f32),
        ],
        in_specs=[ANY] * 3 + [VMEM] * 5 + [SMEM],
        out_specs=[ANY] * 3 + [VMEM] * 4,
        scratch_shapes=[
            V((shard_rows, JOINT), bf), V((JOINT, shard_rows), bf), V((shard_rows * count, JOINT), bf),
            V((3, LANES, TABLE), f32), V((3, LANES, TABLE), f32), V((rows, JOINT), f32), DMA((3,)), DMA((3,)),
        ]
        + Gather.sems(count, 1),
        compiler_params=pltpu.CompilerParams(collective_id=1, has_side_effects=True, vmem_limit_bytes=62 << 20),
    )(query, key, value, value_router, output_router, norm, tokens, routes, gaps)


def seq_mates(ring):
    return [ring.core_mate, ring.plane_mate, (3 - ring.seq, ring.fsdp)]


def slot_mates(ring):
    f = ring.fsdp
    return [(ring.seq, f + 1 - 2 * (f % 2)), (ring.seq, f + 2 - 4 * ((f // 2) % 2))]


def tile_place(slot, seq, phase, key_block, query_block):
    cont = slot // PSLOTS
    own = 1 - jnp.minimum(phase, 1)
    piece = jnp.where(slot == 3, 2 - phase, phase - 1)
    source = jnp.where(phase == 0, 0, 1 + piece)
    first = cont * 2 * (query_block // 2)
    active = jnp.where(
        phase == 0,
        (key_block <= query_block) & (key_block >= first),
        jnp.where(phase == 1, slot >= 1, slot >= 2),
    )
    far_column = jnp.where(
        cont == 1,
        2048 * piece + BLOCK * key_block - BLOCK * (query_block % 2) - 4096,
        BLOCK * key_block - 2048 - BLOCK * query_block,
    )
    column = jnp.where(phase == 0, BLOCK * (key_block - query_block), far_column)
    table = jnp.where((phase > 0) & (cont == 1), 1 + query_block // 2, 0)
    return source, active, table, column


STRIP = 512


def near_first(ring, j):
    odd, high = j % 2, j // 2
    core = ring.core + odd - 2 * ring.core * odd
    plane = ring.plane + high - 2 * ring.plane * high
    return 2 * plane + core


def block_rows(block):
    return pl.ds(pl.multiple_of(block * BLOCK, BLOCK), BLOCK)


def attend_kernel(count, splits, steps, qkv, tables_in, *refs):
    T = len(splits)
    shards, refs = refs[:T], refs[T:]
    att, store, outputs, logs = refs[:4]
    fulls, refs = refs[4 : 4 + T], refs[4 + T :]
    acc, top, att_low, tables, kv_send, kv_recv, q_send, q_recv, sh_send, sh_recv, out_send, out_recv, here = refs[:13]
    at = lambda t, g, cols: fulls[t].at[g, :, cols]
    ring = Gather(count, splits, shards, at, *refs[13:])
    table_load = pltpu.make_async_copy(tables_in, tables, here.at[2])
    table_load.start()
    seq, slot = ring.seq, ring.fsdp % GSLOTS
    mates, (x_mate, z_mate) = seq_mates(ring), slot_mates(ring)
    enter(ring.neighbours() + mates[2:] + [x_mate, z_mate])

    def remote(src, dst, send, recv, device):
        return pltpu.make_async_remote_copy(src, dst, send, recv, device_id=device, device_id_type=MESH)

    mine = block_rows(seq)

    def kv_copy(mate):
        return remote(qkv.at[mate[0], pl.ds(1, 2)], store.at[pl.ds(1, 2), mine], kv_send.at[mate[0]], kv_recv.at[seq], mate)

    def q_copy(mate):
        return remote(qkv.at[mate[0], 0], store.at[0, mine], q_send.at[mate[0]], q_recv.at[seq], mate)

    for mate in mates[1:] + mates[:1]:
        kv_copy(mate).start()
    own_copy = pltpu.make_async_copy(qkv.at[seq], store.at[pl.ds(0, 3), mine], here.at[0])
    own_copy.start()
    for mate in mates[1:] + mates[:1]:
        q_copy(mate).start()
    acc[...] = jnp.zeros_like(acc)
    top[...] = jnp.full_like(top, NEGATIVE)

    def far_rows(piece, chunk):
        return store.at[pl.ds(3 + 2 * piece, 2), block_rows(near_first(ring, chunk))]

    def first_hop(chunk, way):
        src = store.at[pl.ds(1, 2), block_rows(near_first(ring, chunk))]
        piece = slot % 2
        return remote(src, far_rows(piece, chunk), sh_send.at[4 * way + chunk], sh_recv.at[4 * piece + chunk],
                      x_mate if way == 0 else z_mate)

    def second_hop(chunk):
        piece = slot % 2
        return remote(far_rows(piece, chunk), far_rows(piece, chunk), sh_send.at[8 + chunk], sh_recv.at[4 * piece + chunk], x_mate)

    def share(chunk):
        @pl.when(slot < 2)
        def _():
            first_hop(chunk, 1).start()

        @pl.when(slot == 0)
        def _():
            first_hop(chunk, 0).start()

    def pass_on(chunk):
        @pl.when(slot >= 1)
        def _():
            piece = jnp.where(slot == 3, 1, 0)
            remote(far_rows(piece, chunk), far_rows(piece, chunk), sh_send.at[chunk], sh_recv.at[4 * piece + chunk], x_mate).wait_recv()

        @pl.when(slot >= 2)
        def _():
            second_hop(chunk).start()

    def last_piece(chunk):
        @pl.when(slot >= 2)
        def _():
            piece = 3 - slot
            remote(far_rows(piece, chunk), far_rows(piece, chunk), sh_send.at[chunk], sh_recv.at[4 * piece + chunk], x_mate).wait_recv()

    own_copy.wait()
    share(0)
    for chunk, mate in enumerate(mates):
        other = mate[0]
        src = store.at[pl.ds(1, 2), block_rows(other)]
        remote(src, src, kv_send.at[other], kv_recv.at[other], mate).wait_recv()
        share(1 + chunk)
    for mate in mates:
        src = store.at[0, block_rows(mate[0])]
        remote(src, src, q_send.at[mate[0]], q_recv.at[mate[0]], mate).wait_recv()

    def tile(source, table, column, key_block, first, rows):
        keys = store[1 + 2 * source, block_rows(key_block), :]
        values = store[2 + 2 * source, block_rows(key_block), :]
        for strip in range(rows // STRIP):
            part = pl.ds(pl.multiple_of(first + strip * STRIP, STRIP), STRIP)
            scores = lax.dot_general(store[0, part, :], keys, (((1,), (1,)), ((), ())), preferred_element_type=jnp.float32)
            start = column + TABLE_ZERO - strip * STRIP
            bias = [tables[table, :, pl.ds(pl.multiple_of(start - LANES * i, LANES), BLOCK)] for i in range(STRIP // LANES)]
            scores = scores * (DH**-0.5 * LOG2E) + jnp.concatenate(bias, axis=0)
            before = top[part, :]
            after = jnp.maximum(before, jnp.max(scores, axis=1, keepdims=True))
            terms = jnp.exp2(scores - after[:, :1])
            acc[part, :] = acc[part, :] * jnp.exp2(before - after) + jnp.dot(
                terms.astype(jnp.bfloat16), values, preferred_element_type=jnp.float32)
            top[part, :] = after

    def near_tile(step):
        key_block, query_block = near_first(ring, step // 4), step % 4
        source, active, table, column = tile_place(slot, seq, 0, key_block, query_block)

        @pl.when(active)
        def _():
            tile(source, table, column, key_block, query_block * BLOCK, BLOCK)

    def far_tile(step):
        phase, key_block, query_block = step // 8, near_first(ring, (step // 2) % 4), 2 * (step % 2)
        source, active, table, column = tile_place(slot, seq, phase, key_block, query_block)

        @pl.when(active)
        def _():
            tile(source, table, column, key_block, query_block * BLOCK, 2 * BLOCK)

    table_load.wait()
    events = {}
    for chunk in range(4):
        events.setdefault(4 * chunk + 3, []).append(functools.partial(pass_on, chunk))
        events.setdefault(24 + 2 * chunk, []).append(functools.partial(last_piece, chunk))
    begin, first, gap = steps
    for t in range(T):
        if begin + t < 0:
            ring.start(t)
        else:
            events.setdefault(begin + t, []).append(functools.partial(ring.start, t))
    rest = []
    for i, event in enumerate(ring.events()):
        step = int(first + gap * i)
        if step < 32:
            events.setdefault(step, []).append(event)
        else:
            rest.append(event)

    def step_body(step, carry):
        for when, actions in sorted(events.items()):
            @pl.when(step == when)
            def _():
                for action in actions:
                    action()
        pl.when(step < 16)(lambda: near_tile(step))
        pl.when(step >= 16)(lambda: far_tile(step - 8))
        return carry

    lax.fori_loop(0, 32, step_body, 0)
    total = acc[:, DH : DH + 1]
    result = acc[...] / total
    outputs[...] = result
    log_total = top[...] + jnp.log2(total)
    for block in range(4):
        logs[:, block * BLOCK : (block + 1) * BLOCK] = log_total[block * BLOCK : (block + 1) * BLOCK].T[:8]
    att_low[...] = result.astype(jnp.bfloat16)

    def out_copy(mate):
        return remote(att_low.at[block_rows(mate[0])], att.at[seq], out_send.at[mate[0]], out_recv.at[seq], mate)

    for mate in mates[1:] + mates[:1]:
        out_copy(mate).start()
    own_out = pltpu.make_async_copy(att_low.at[mine], att.at[seq], here.at[1])
    own_out.start()
    for event in rest:
        event()
    own_out.wait()
    for mate in mates:
        kv_copy(mate).wait_send()
        q_copy(mate).wait_send()
        out_copy(mate).wait_send()
        ref = att.at[mate[0]]
        remote(ref, ref, out_send.at[mate[0]], out_recv.at[mate[0]], mate).wait_recv()
    for chunk in range(4):
        @pl.when(slot < 2)
        def _():
            first_hop(chunk, 1).wait_send()

        @pl.when(slot == 0)
        def _():
            first_hop(chunk, 0).wait_send()

        @pl.when(slot >= 2)
        def _():
            second_hop(chunk).wait_send()


def attend(count, qkv, tables, shards, splits, steps=(0, 18, 2)):
    rows = qkv.shape[2]
    own = 4 * rows
    T = len(shards)
    return pl.pallas_call(
        functools.partial(attend_kernel, count, splits, steps),
        out_shape=[
            jax.ShapeDtypeStruct((HEADS, rows, LANES), jnp.bfloat16),
            jax.ShapeDtypeStruct((7, own, LANES), jnp.bfloat16),
            jax.ShapeDtypeStruct((own, LANES), jnp.float32),
            jax.ShapeDtypeStruct((8, own), jnp.float32),
        ]
        + [jax.ShapeDtypeStruct((count,) + w.shape, w.dtype) for w in shards],
        in_specs=[VMEM, ANY] + [VMEM] * T,
        out_specs=[VMEM] * 4 + [ANY] * T,
        scratch_shapes=[
            pltpu.VMEM((own, LANES), jnp.float32),
            pltpu.VMEM((own, LANES), jnp.float32),
            pltpu.VMEM((own, LANES), jnp.bfloat16),
            pltpu.VMEM((3, LANES, TABLE), jnp.float32),
            DMA((4,)), DMA((4,)), DMA((4,)), DMA((4,)), DMA((12,)), DMA((8,)), DMA((4,)), DMA((4,)), DMA((3,)),
        ]
        + Gather.sems(count, T),
        compiler_params=pltpu.CompilerParams(collective_id=2, has_side_effects=True, vmem_limit_bytes=56 << 20),
    )(qkv, tables, *shards)


class Scatter(Ring):
    def __init__(self, count, splits, parts, outs, bufs, sems):
        super().__init__(count, splits)
        self.parts, self.outs = parts, outs
        T = len(splits)
        self.mine, self.plane_in = bufs[:T], bufs[T : 2 * T]
        self.ring0, self.ring1 = bufs[2 * T : 3 * T], bufs[3 * T : 4 * T]
        self.low, self.low_in, self.done = bufs[4 * T : 5 * T], bufs[5 * T : 6 * T], bufs[6 * T : 7 * T]
        (self.load, self.plane_s, self.plane_r, self.ring_s, self.ring_r, self.end_s, self.end_r, self.put) = sems

    @staticmethod
    def scratch(count, splits, rows):
        half = [a + 2 * b for a, b in splits]
        bf = jnp.bfloat16
        out = [pltpu.VMEM((count, r, h), bf) for r, h in zip(rows, half)]
        out += [pltpu.VMEM((count, r, b), bf) for r, (a, b) in zip(rows, splits)]
        out += [pltpu.VMEM((count - 1 if a else 1, r, max(a, LANES)), bf) for r, (a, b) in zip(rows, splits)]
        out += [pltpu.VMEM((count - 1, r, b), bf) for r, (a, b) in zip(rows, splits)]
        out += [pltpu.VMEM((r, a + b), bf) for r, (a, b) in zip(rows, splits)]
        out += [pltpu.VMEM((r, a + b), bf) for r, (a, b) in zip(rows, splits)]
        out += [pltpu.VMEM((r, h), jnp.float32) for r, h in zip(rows, half)]
        T = len(splits)
        return out + [DMA((T * count,))] * 3 + [DMA((2 * T * (count - 1),))] * 2 + [DMA((2 * T,))] * 2 + [DMA((T,))]

    def dest(self, rel):
        return ring_index((self.place + rel) % self.count, self.count)

    def load_copy(self, t, rel):
        part, first = self.parts[t]
        src = part.at[self.dest(rel), :, pl.ds(first, self.half(t))]
        return pltpu.make_async_copy(src, self.mine[t].at[rel], self.load.at[t * self.count + rel])

    def remote(self, src, dst, s, r, i, device):
        return pltpu.make_async_remote_copy(src, dst, s.at[i], r.at[i], device_id=device, device_id_type=MESH)

    def single(self, t, plane):
        both, single = self.splits[t]
        return pl.ds(pl.multiple_of(both + plane * single, LANES), single)

    def plane_copy(self, t, rel):
        src = self.mine[t].at[rel, :, self.single(t, 1 - self.plane)]
        return self.remote(src, self.plane_in[t].at[rel], self.plane_s, self.plane_r, t * self.count + rel, self.plane_mate)

    def rels(self, D):
        return sorted({D % self.count, (-D) % self.count})

    def order(self):
        out = []
        for D in range(self.far, -1, -1):
            out += self.rels(D)
        return out

    def start(self, t):
        for rel in self.order():
            self.load_copy(t, rel).start()

    def ready(self, t, rel):
        if self.parts[t]:
            self.load_copy(t, rel).wait()
        self.plane_copy(t, rel).start()

    def open(self, t):
        for rel in self.rels(self.far):
            self.ready(t, rel)

    def step(self, t, D, ahead=True):
        if ahead and D:
            for rel in self.rels(D - 1):
                self.ready(t, rel)
        self.combine(t, D)
        if D:
            self.chain(t, D)
        else:
            self.close(t)

    def buffer(self, t, kind, slot):
        if kind:
            return self.ring1[t].at[slot]
        return self.ring0[t].at[slot]

    def own_ref(self, t, kind, rel):
        if kind:
            return self.mine[t].at[rel, :, self.single(t, self.plane)]
        return self.mine[t].at[rel, :, pl.ds(0, self.splits[t][0])]

    def ring_copy(self, t, kind, way, D):
        slot = self.slot(kind, way, D)
        if D == self.reach(kind, way):
            src = self.own_ref(t, kind, D % self.count if way == 0 else (-D) % self.count)
        else:
            src = self.buffer(t, kind, self.slot(kind, way, D + 1))
        i = (2 * t + kind) * (self.count - 1) + slot
        return self.remote(src, self.buffer(t, kind, slot), self.ring_s, self.ring_r, i, self.next(way))

    def ring_wait(self, t, kind, way, D):
        slot = self.slot(kind, way, D)
        ref = self.buffer(t, kind, slot)
        i = (2 * t + kind) * (self.count - 1) + slot
        self.remote(ref, ref, self.ring_s, self.ring_r, i, self.next(way)).wait_recv()

    def combine(self, t, D):
        for rel in self.rels(D):
            self.plane_copy(t, rel).wait_send()
            ref = self.plane_in[t].at[rel]
            self.remote(ref, ref, self.plane_s, self.plane_r, t * self.count + rel, self.plane_mate).wait_recv()
            own = self.own_ref(t, 1, rel)
            own[...] = own[...] + self.plane_in[t][rel]

    def chain(self, t, D):
        for kind in self.kinds(t):
            for way in (0, 1):
                if D > self.reach(kind, way):
                    continue
                if D < self.reach(kind, way):
                    self.ring_wait(t, kind, way, D + 1)
                    rel = D % self.count if way == 0 else (-D) % self.count
                    ref = self.buffer(t, kind, self.slot(kind, way, D + 1))
                    ref[...] = ref[...] + self.own_ref(t, kind, rel)[...]
                self.ring_copy(t, kind, way, D).start()

    def end_copy(self, t):
        return self.remote(self.low[t], self.low_in[t], self.end_s, self.end_r, 2 * t, self.plane_mate)

    def close(self, t):
        both, single = self.splits[t]
        for kind in self.kinds(t):
            total = self.own_ref(t, kind, 0)[...].astype(jnp.float32)
            for way in (0, 1):
                if self.reach(kind, way):
                    self.ring_wait(t, kind, way, 1)
                    total = total + self.buffer(t, kind, self.slot(kind, way, 1))[...].astype(jnp.float32)
            if kind:
                self.low[t][:, both:] = total.astype(jnp.bfloat16)
            else:
                self.low[t][:, :both] = total.astype(jnp.bfloat16)
        self.end_copy(t).start()

    def out_ref(self, t, core):
        out, whole, first = self.outs[t]
        return out.at[:, pl.ds(pl.multiple_of(core * whole + first, LANES), self.half(t))]

    def out_copy(self, t):
        return self.remote(self.done[t], self.out_ref(t, self.core), self.end_s, self.end_r, 2 * t + 1, self.core_mate)

    def put_copy(self, t):
        return pltpu.make_async_copy(self.done[t], self.out_ref(t, self.core), self.put.at[t])

    def deliver(self, t):
        both, single = self.splits[t]
        self.end_copy(t).wait_send()
        ref = self.low_in[t]
        self.remote(ref, ref, self.end_s, self.end_r, 2 * t, self.plane_mate).wait_recv()
        if both:
            self.done[t][:, :both] = self.low[t][:, :both].astype(jnp.float32) + self.low_in[t][:, :both].astype(jnp.float32)
        if single:
            self.done[t][:, self.single(t, self.plane)] = self.low[t][:, both:].astype(jnp.float32)
            self.done[t][:, self.single(t, 1 - self.plane)] = self.low_in[t][:, both:].astype(jnp.float32)
        self.out_copy(t).start()
        self.put_copy(t).start()

    def finish(self, t):
        for kind in self.kinds(t):
            for way in (0, 1):
                for D in range(1, self.reach(kind, way) + 1):
                    self.ring_copy(t, kind, way, D).wait_send()
        self.out_copy(t).wait_send()
        self.put_copy(t).wait()
        ref = self.out_ref(t, 1 - self.core)
        self.remote(ref, ref, self.end_s, self.end_r, 2 * t + 1, self.core_mate).wait_recv()


def retreat_kernel(count, splits, steps, grad_att, turned_in, store_in, outputs, logs, part, back, out, *refs):
    T = len(splits)
    (grads, delta, grad_q, grad_kv, send_kv, kv_in0, kv_in1, low, in_send, in_recv, up_send, up_recv,
     turned, store, out_send, out_recv, here) = refs[:17]
    refs = refs[17:]
    loads = [pltpu.make_async_copy(turned_in, turned, here.at[2]), pltpu.make_async_copy(store_in, store, here.at[3])]
    for copy in loads:
        copy.start()
    halves = [a + 2 * b for a, b in splits]
    firsts = [sum(halves[:t]) for t in range(T)]
    ring = Scatter(
        count, splits, [(part, first) for first in firsts], [(out, sum(halves), first) for first in firsts],
        refs[: 7 * T], refs[7 * T :])
    seq, slot = ring.seq, ring.fsdp % GSLOTS
    mates, (x_mate, z_mate) = seq_mates(ring), slot_mates(ring)
    enter(ring.neighbours() + mates[2:] + [x_mate, z_mate])

    def remote(src, dst, send, recv, device):
        return pltpu.make_async_remote_copy(src, dst, send, recv, device_id=device, device_id_type=MESH)

    mine = block_rows(seq)

    def in_copy(mate):
        return remote(grad_att.at[mate[0]], grads.at[mine], in_send.at[mate[0]], in_recv.at[seq], mate)

    for mate in mates[1:] + mates[:1]:
        in_copy(mate).start()
    own_copy = pltpu.make_async_copy(grad_att.at[seq], grads.at[mine], here.at[0])
    own_copy.start()
    grad_q[...] = jnp.zeros_like(grad_q)
    grad_kv[...] = jnp.zeros_like(grad_kv)
    own_copy.wait()
    for mate in mates:
        ref = grads.at[block_rows(mate[0])]
        remote(ref, ref, in_send.at[mate[0]], in_recv.at[mate[0]], mate).wait_recv()
    for block in range(4):
        rows = pl.ds(block * BLOCK, BLOCK)
        sums = jnp.sum(grads[rows, :].astype(jnp.float32) * outputs[rows, :], axis=1, keepdims=True)
        delta[:, rows] = jnp.broadcast_to(sums, (BLOCK, LANES)).T[:8]

    for copy in loads:
        copy.wait()

    def tile(forward_phase, key_block, query_block, blocks):
        source, active, table, column = tile_place(slot, seq, forward_phase, key_block, query_block)

        @pl.when(active)
        def _():
            size = blocks * BLOCK
            key_rows, rows = block_rows(key_block), pl.ds(pl.multiple_of(query_block * BLOCK, BLOCK), size)
            keys, values = store[1 + 2 * source, key_rows, :], store[2 + 2 * source, key_rows, :]
            queries, tops = store[0, rows, :], grads[rows, :]
            scores = lax.dot_general(keys, queries, (((1,), (1,)), ((), ())), preferred_element_type=jnp.float32)
            bias = jnp.concatenate(
                [turned[table, :, pl.ds(pl.multiple_of(TURNED_ZERO - column - LANES * part, LANES), size)] for part in range(BLOCK // LANES)],
                axis=0,
            )
            weights = jnp.exp2(scores * (DH**-0.5 * LOG2E) + (bias - logs[:1, rows]))
            grad_weights = lax.dot_general(values, tops, (((1,), (1,)), ((), ())), preferred_element_type=jnp.float32)
            grad_scores = (weights * (grad_weights - delta[:1, rows])).astype(jnp.bfloat16)
            grad_kv[source, 1, key_rows, :] += jnp.dot(weights.astype(jnp.bfloat16), tops, preferred_element_type=jnp.float32)
            grad_kv[source, 0, key_rows, :] += jnp.dot(grad_scores, queries, preferred_element_type=jnp.float32)
            grad_q[rows, :] += lax.dot_general(grad_scores, keys, (((0,), (0,)), ((), ())), preferred_element_type=jnp.float32)

    def far_tile(step):
        phase = step // 8
        piece = jnp.where(slot == 2, 1 - phase, phase)
        tile(jnp.where(slot == 3, 2 - piece, 1 + piece), (step // 2) % 4, 2 * (step % 2), 2)

    def near_tile(step):
        tile(0, step // 4, step % 4, 1)

    scale = DH**-0.5

    def rounded(source, chunk, extra):
        rows = block_rows(chunk)
        keys = grad_kv[source, 0, rows, :] * scale
        values = grad_kv[source, 1, rows, :]
        for more in extra:
            keys = keys + more[0].astype(jnp.float32)
            values = values + more[1].astype(jnp.float32)
        return keys.astype(jnp.bfloat16), values.astype(jnp.bfloat16)

    def x_send(chunk):
        src = send_kv.at[0, :, block_rows(chunk)]
        return remote(src, kv_in0.at[:, block_rows(chunk)], up_send.at[chunk], up_recv.at[chunk], x_mate)

    def z_send(chunk):
        src = send_kv.at[1, :, block_rows(chunk)]
        return remote(src, kv_in1.at[:, block_rows(chunk)], up_send.at[4 + chunk], up_recv.at[4 + chunk], z_mate)

    def x_wait(chunk):
        ref = kv_in0.at[:, block_rows(chunk)]
        remote(ref, ref, up_send.at[chunk], up_recv.at[chunk], x_mate).wait_recv()

    def z_wait(chunk):
        ref = kv_in1.at[:, block_rows(chunk)]
        remote(ref, ref, up_send.at[4 + chunk], up_recv.at[4 + chunk], z_mate).wait_recv()

    def first_done(chunk):
        @pl.when(slot >= 1)
        def _():
            source = jnp.where(slot == 2, 2, 1)
            keys, values = rounded(source, chunk, [])
            send_kv[0, 0, block_rows(chunk), :] = keys
            send_kv[0, 1, block_rows(chunk), :] = values
            x_send(chunk).start()

    def second_done(chunk):
        @pl.when(slot >= 2)
        def _():
            x_wait(chunk)
            source = slot - 1
            keys, values = rounded(source, chunk, [kv_in0[:, block_rows(chunk), :]])
            send_kv[1, 0, block_rows(chunk), :] = keys
            send_kv[1, 1, block_rows(chunk), :] = values
            z_send(chunk).start()

    def out_copy(mate):
        src = low.at[:, block_rows(mate[0])]
        return remote(src, back.at[seq], out_send.at[mate[0]], out_recv.at[seq], mate)

    def own_done(chunk):
        rows = block_rows(chunk)
        low[0, rows, :] = (grad_q[rows, :] * scale).astype(jnp.bfloat16)

        @pl.when(slot == 0)
        def _():
            x_wait(chunk)
            z_wait(chunk)
            low[1, rows, :], low[2, rows, :] = rounded(0, chunk, [kv_in0[:, rows, :], kv_in1[:, rows, :]])

        @pl.when(slot == 1)
        def _():
            z_wait(chunk)
            low[1, rows, :], low[2, rows, :] = rounded(0, chunk, [kv_in1[:, rows, :]])

        @pl.when(slot >= 2)
        def _():
            low[1, rows, :], low[2, rows, :] = rounded(0, chunk, [])

    events = {}
    for chunk in range(4):
        events.setdefault(2 * chunk + 2, []).append(functools.partial(first_done, chunk))
        events.setdefault(10 + 2 * chunk, []).append(functools.partial(second_done, chunk))
    begin, ready, first, hop, lag = steps
    rest = []
    for t in range(T):
        plan = [(begin, functools.partial(ring.start, t)), (ready, functools.partial(ring.open, t))]
        when = first + lag * t
        for D in range(ring.far, -1, -1):
            plan.append((when, functools.partial(ring.step, t, D)))
            when += hop
        plan.append((when, functools.partial(ring.deliver, t)))
        plan.append((when + hop, functools.partial(ring.finish, t)))
        for when, event in plan:
            if when < 32:
                events.setdefault(int(when), []).append(event)
            else:
                rest.append((when, event))
    rest = [event for when, event in sorted(rest, key=lambda pair: pair[0])]

    def step_body(step, carry):
        for when, actions in sorted(events.items()):
            @pl.when(step == when)
            def _():
                for action in actions:
                    action()
        pl.when(step < 16)(lambda: far_tile(step))
        pl.when(step >= 16)(lambda: near_tile(step - 16))
        return carry

    lax.fori_loop(0, 32, step_body, 0)
    for chunk in range(4):
        own_done(chunk)
    for mate in mates[1:] + mates[:1]:
        out_copy(mate).start()
    own_out = pltpu.make_async_copy(low.at[:, mine], back.at[seq], here.at[1])
    own_out.start()
    for event in rest:
        event()
    own_out.wait()
    for mate in mates:
        in_copy(mate).wait_send()
        out_copy(mate).wait_send()
        ref = back.at[mate[0]]
        remote(ref, ref, out_send.at[mate[0]], out_recv.at[mate[0]], mate).wait_recv()
    for chunk in range(4):
        @pl.when(slot >= 1)
        def _():
            x_send(chunk).wait_send()

        @pl.when(slot >= 2)
        def _():
            z_send(chunk).wait_send()


def retreat(count, grad_att, turned, store, outputs, logs, part, splits, steps=(0, 1, 2, 3, 1)):
    rows = grad_att.shape[1]
    own = 4 * rows
    _, shard_rows, half = part.shape
    return pl.pallas_call(
        functools.partial(retreat_kernel, count, splits, steps),
        out_shape=[jax.ShapeDtypeStruct((HEADS, 3, rows, LANES), jnp.bfloat16), jax.ShapeDtypeStruct((shard_rows, 2 * half), jnp.float32)],
        in_specs=[VMEM, ANY, ANY, VMEM, VMEM, ANY],
        out_specs=[VMEM, ANY],
        scratch_shapes=[
            pltpu.VMEM((own, LANES), jnp.bfloat16),
            pltpu.VMEM((8, own), jnp.float32),
            pltpu.VMEM((own, LANES), jnp.float32),
            pltpu.VMEM((3, 2, own, LANES), jnp.float32),
            pltpu.VMEM((2, 2, own, LANES), jnp.bfloat16),
            pltpu.VMEM((2, own, LANES), jnp.bfloat16),
            pltpu.VMEM((2, own, LANES), jnp.bfloat16),
            pltpu.VMEM((3, own, LANES), jnp.bfloat16),
            DMA((4,)), DMA((4,)), DMA((8,)), DMA((8,)),
            pltpu.VMEM((3, LANES, TABLE), jnp.float32), pltpu.VMEM((7, own, LANES), jnp.bfloat16),
            DMA((4,)), DMA((4,)), DMA((4,)),
        ]
        + Scatter.scratch(count, splits, [shard_rows] * len(splits)),
        compiler_params=pltpu.CompilerParams(collective_id=3, has_side_effects=True, vmem_limit_bytes=60 << 20),
    )(grad_att, turned, store, outputs, logs, part)


CHUNK = 512


def gelu_pair(v):
    root = 0.7978845608028654
    square = v * v
    t = jnp.tanh(root * (v + 0.044715 * square * v))
    up = 0.5 * (1.0 + t)
    return v * up, up + 0.5 * v * (1.0 - t * t) * (root * (1.0 + 3.0 * 0.044715 * square))


def contract(left, right, left_axis, right_axis):
    return lax.dot_general(left, right, (((left_axis,), (right_axis,)), ((), ())), preferred_element_type=jnp.float32)


def feed_kernel(count, att, gates, tokens, cotangent, norms, output_w, inner_w, outer_w,
                layer_out, grad_residual, grad_att, grad_logit, grad_norms, part_output, part_inner, outer_out,
                w_out, w_in, w_up, acts, act_in, slopes, slope_in, scaled, scaled_in, scaled_t, cot_in, cot_t,
                acc, normed, grad_scaled, branch_low, branch_in, branch_t, att_in, gates_in,
                stage_inner, stage_output,
                load_out, load_in, load_up, pair_s, pair_r, act_s, act_r, slope_s, slope_r, put_inner, put_output, *refs):
    half = cotangent.shape[1] // 2
    ring = Scatter(count, (SPLITS["outer"],), [None], [(outer_out, half, 0)], refs[:7], refs[7:])
    core, mate = ring.core, ring.core_mate
    experts = HEADS * EXP
    chunks = inner_w.shape[1] // CHUNK
    small = CHUNK // 2
    shards = max(1, count // chunks)

    def out_load(e):
        return pltpu.make_async_copy(output_w.at[pl.ds(e * DH, DH)], w_out.at[e, pl.ds(0, DH)], load_out.at[e])

    def ffn_load(chunk, slot):
        cols = pl.ds(pl.multiple_of(chunk * CHUNK, CHUNK), CHUNK)
        return (pltpu.make_async_copy(inner_w.at[:, cols], w_in.at[slot], load_in.at[slot]),
                pltpu.make_async_copy(outer_w.at[cols], w_up.at[slot], load_up.at[slot]))

    def chunk_of(step):
        if count != chunks:
            return step
        D = ring.far - (step + 1) // 2
        odd = step % 2
        return ring.dest((odd * D + (1 - odd) * (count - D)) % count)

    for e in range(experts):
        out_load(e).start()
    for sub in range(2):
        for copy in ffn_load(chunk_of(sub), sub):
            copy.start()
    enter(ring.neighbours())

    def remote(src, dst, send, recv):
        return pltpu.make_async_remote_copy(src, dst, send, recv, device_id=mate, device_id_type=MESH)

    mine = pl.ds(pl.multiple_of(core * half, LANES), half)
    yours = pl.ds(pl.multiple_of((1 - core) * half, LANES), half)
    pair = [
        remote(att, att_in, pair_s.at[0], pair_r.at[0]),
        remote(gates.at[0], gates_in, pair_s.at[1], pair_r.at[1]),
        remote(cotangent.at[:, yours], cot_in, pair_s.at[2], pair_r.at[2]),
        remote(scaled, scaled_in, pair_s.at[3], pair_r.at[3]),
        remote(branch_low.at[:, yours], branch_in, pair_s.at[4], pair_r.at[4]),
    ]
    for copy in pair[:3]:
        copy.start()

    def mixed_pair(att_ref, gate, two):
        tiles = []
        for which in (2 * two, 2 * two + 1):
            column = gate[:, experts + which : experts + which + 1]
            tiles.append((att_ref[which // EXP].astype(jnp.float32) * column).astype(jnp.bfloat16))
        return jnp.concatenate(tiles, axis=1)

    w_out[:, DH:, :] = jnp.zeros((experts, LANES - DH, w_out.shape[2]), jnp.bfloat16)
    acc[...] = tokens[...].astype(jnp.float32)
    for two in range(experts // 2):
        out_load(2 * two).wait()
        out_load(2 * two + 1).wait()
        weights = w_out[2 * two : 2 * two + 2].reshape(2 * LANES, w_out.shape[2])
        acc[...] += jnp.dot(mixed_pair(att, gates.at[0], two), weights, preferred_element_type=jnp.float32)
    residual = acc[...]
    centred = residual - jnp.mean(residual, axis=1, keepdims=True)
    inverse = lax.rsqrt(jnp.mean(centred * centred, axis=1, keepdims=True) + EPSILON)
    normed[...] = centred * inverse
    scaled[...] = (normed[...] * norms[:1] + norms[1:2]).astype(jnp.bfloat16)
    pair[3].start()
    rows = tokens.shape[0]
    scaled_t[:, :rows] = scaled[...].T
    cot_t[:, :rows] = cotangent[:, mine].T
    grad_scaled[...] = jnp.zeros_like(grad_scaled)
    pair[2].wait_recv()
    cot_t[:, rows:] = cot_in[...].T
    pair[3].wait_recv()
    scaled_t[:, rows:] = scaled_in[...].T

    small_mine = pl.ds(pl.multiple_of(core * small, LANES), small)
    small_yours = pl.ds(pl.multiple_of((1 - core) * small, LANES), small)

    def act_copy(step, sub):
        return remote(acts.at[sub], act_in.at[step], act_s.at[sub], act_r.at[step])

    def slope_copy(step, sub):
        return remote(slopes.at[sub, :, small_yours], slope_in.at[step], slope_s.at[sub], slope_r.at[step])

    def put_inner_copy(step, sub):
        cols = pl.ds(pl.multiple_of(chunk_of(step) * small, small), small)
        return pltpu.make_async_copy(stage_inner.at[sub], part_inner.at[:, cols], put_inner.at[sub])

    def forward_backward(step, sub):
        for copy in ffn_load(chunk_of(step), sub):
            copy.wait()

        @pl.when(step > 1)
        def _():
            act_copy(step, sub).wait_send()
            slope_copy(step, sub).wait_send()

        act, slope = gelu_pair(jnp.dot(scaled[...], w_in[sub], preferred_element_type=jnp.float32))
        acts[sub] = act.astype(jnp.bfloat16)
        act_copy(step, sub).start()
        slopes[sub] = (contract(cotangent[...], w_up[sub], 1, 1) * slope).astype(jnp.bfloat16)
        slope_copy(step, sub).start()
        acc[...] += jnp.dot(acts[sub], w_up[sub], preferred_element_type=jnp.float32)
        grad_scaled[...] += contract(slopes[sub], w_in[sub], 1, 1)

        @pl.when(step + 2 < chunks)
        def _():
            for copy in ffn_load(chunk_of(step + 2), sub):
                copy.start()

    def weight_parts(step, sub):
        remote(act_in.at[step], act_in.at[step], act_s.at[sub], act_r.at[step]).wait_recv()
        total = jnp.dot(cot_t[:, :rows], acts[sub], preferred_element_type=jnp.float32)
        total = total + jnp.dot(cot_t[:, rows:], act_in[step], preferred_element_type=jnp.float32)
        turned = total.astype(jnp.bfloat16).T
        shard_rows = CHUNK // shards
        for q in range(shards):
            rel = (ring_place(chunk_of(step) * shards + q, count) - ring.place + count) % count
            ring.mine[0][rel] = turned[q * shard_rows : (q + 1) * shard_rows]
        remote(slope_in.at[step], slope_in.at[step], slope_s.at[sub], slope_r.at[step]).wait_recv()

        @pl.when(step > 1)
        def _():
            put_inner_copy(step, sub).wait()

        total = jnp.dot(scaled_t[:, :rows], slopes[sub, :, small_mine], preferred_element_type=jnp.float32)
        total = total + jnp.dot(scaled_t[:, rows:], slope_in[step], preferred_element_type=jnp.float32)
        stage_inner[sub] = total.astype(jnp.bfloat16)
        put_inner_copy(step, sub).start()

    events = {}
    if count == chunks:
        for step, rel in enumerate(ring.order()):
            events.setdefault(step, []).append(functools.partial(ring.ready, 0, rel))
        for D in range(ring.far, 0, -1):
            events.setdefault(2 * (ring.far - D) + 1, []).append(functools.partial(ring.step, 0, D, False))

    def after_parts(step):
        for when, actions in sorted(events.items()):
            @pl.when(step == when)
            def _():
                for action in actions:
                    action()

    def iteration(i, carry):
        forward_backward(2 * i, 0)

        @pl.when(i > 0)
        def _():
            weight_parts(2 * i - 1, 1)
            after_parts(2 * i - 1)

        forward_backward(2 * i + 1, 1)
        weight_parts(2 * i, 0)
        after_parts(2 * i)
        return carry

    lax.fori_loop(0, chunks // 2, iteration, 0)
    weight_parts(chunks - 1, 1)
    if count == chunks:
        for action in events[chunks - 1]:
            action()
    else:
        ring.open(0)
        for D in range(ring.far, 0, -1):
            ring.step(0, D)
    layer_out[...] = acc[...].astype(jnp.bfloat16)
    slope = grad_scaled[...]
    grad_norms[...] = jnp.concatenate(
        [jnp.sum(slope * normed[...], axis=0, keepdims=True), jnp.sum(slope, axis=0, keepdims=True),
         jnp.zeros((6, slope.shape[1]), jnp.float32)], axis=0)
    slope = slope * norms[:1]
    total = cotangent[...].astype(jnp.float32) + inverse * (
        slope - jnp.mean(slope, axis=1, keepdims=True)
        - normed[...] * jnp.mean(slope * normed[...], axis=1, keepdims=True))
    grad_residual[...] = total
    branch_low[...] = total.astype(jnp.bfloat16)
    pair[4].start()
    branch_t[:, :rows] = branch_low[:, mine].T
    lane = lax.broadcasted_iota(jnp.int32, (rows, LANES), 1)
    logit = jnp.zeros((rows, LANES), jnp.float32)
    head_total = None
    for which in range(experts):
        if which % 2 == 0:
            weights = w_out[which : which + 2].reshape(2 * LANES, w_out.shape[2])
            both = contract(branch_low[...], weights, 1, 1)
        grad_mixed = both[:, which % 2 * LANES : (which % 2 + 1) * LANES]
        head, expert = which // EXP, which % EXP
        column = slice(experts + which, experts + which + 1)
        term = grad_mixed * gates[0, :, column]
        head_total = term if expert == 0 else head_total + term
        if expert == EXP - 1:
            grad_att[head] = head_total.astype(jnp.bfloat16)
        sums = jnp.sum(grad_mixed * att[head].astype(jnp.float32), axis=1, keepdims=True)
        logit = jnp.where(lane == experts + which, sums, logit)
    grad_logit[...] = logit * gates[1]
    ring.step(0, 0)
    pair[0].wait_recv()
    pair[1].wait_recv()
    pair[4].wait_recv()
    branch_t[:, rows:] = branch_in[...].T

    def put_output_copy(which):
        return pltpu.make_async_copy(stage_output.at[which % 4, pl.ds(0, DH)], part_output.at[pl.ds(which * DH, DH)], put_output.at[which % 4])

    for two in range(experts // 2):
        total = jnp.dot(branch_t[:, :rows], mixed_pair(att, gates.at[0], two), preferred_element_type=jnp.float32)
        total = total + jnp.dot(branch_t[:, rows:], mixed_pair(att_in, gates_in, two), preferred_element_type=jnp.float32)
        turned = total.astype(jnp.bfloat16).T
        for side in range(2):
            which = 2 * two + side
            if which >= 4:
                put_output_copy(which - 4).wait()
            stage_output[which % 4] = turned[side * LANES : (side + 1) * LANES]
            put_output_copy(which).start()
    ring.deliver(0)
    for which in range(experts - 4, experts):
        put_output_copy(which).wait()
    for sub in range(2):
        put_inner_copy(sub, sub).wait()
        act_copy(sub, sub).wait_send()
        slope_copy(sub, sub).wait_send()
    ring.finish(0)
    for copy in pair:
        copy.wait_send()


def feed(count, att, gates, tokens, cotangent, norms, output_w, inner_w, outer_w):
    rows, width = tokens.shape
    wide = inner_w.shape[1]
    half = width // 2
    f32, bf = jnp.float32, jnp.bfloat16
    experts, chunks = HEADS * EXP, wide // CHUNK
    V = pltpu.VMEM
    return pl.pallas_call(
        functools.partial(feed_kernel, count),
        out_shape=[
            jax.ShapeDtypeStruct((rows, width), bf),
            jax.ShapeDtypeStruct((rows, width), f32),
            jax.ShapeDtypeStruct((HEADS, rows, LANES), bf),
            jax.ShapeDtypeStruct((rows, LANES), f32),
            jax.ShapeDtypeStruct((8, width), f32),
            jax.ShapeDtypeStruct((VCOLS, half), bf),
            jax.ShapeDtypeStruct((width, wide // 2), bf),
            jax.ShapeDtypeStruct((wide // count, width), f32),
        ],
        in_specs=[VMEM] * 5 + [ANY] * 3,
        out_specs=[VMEM] * 5 + [ANY] * 3,
        scratch_shapes=[
            V((experts, LANES, width), bf), V((2, width, CHUNK), bf), V((2, CHUNK, width), bf),
            V((2, rows, CHUNK), bf), V((chunks, rows, CHUNK), bf), V((2, rows, CHUNK), bf), V((chunks, rows, CHUNK // 2), bf),
            V((rows, width), bf), V((rows, width), bf), V((width, 2 * rows), bf), V((rows, half), bf), V((half, 2 * rows), bf),
            V((rows, width), f32), V((rows, width), f32), V((rows, width), f32),
            V((rows, width), bf), V((rows, half), bf), V((half, 2 * rows), bf), V((HEADS, rows, LANES), bf), V((rows, LANES), f32),
            V((2, width, CHUNK // 2), bf), V((4, LANES, half), bf),
            DMA((experts,)), DMA((2,)), DMA((2,)), DMA((5,)), DMA((5,)), DMA((2,)), DMA((chunks,)), DMA((2,)), DMA((chunks,)),
            DMA((2,)), DMA((4,)),
        ]
        + Scatter.scratch(count, (SPLITS["outer"],), [wide // count]),
        compiler_params=pltpu.CompilerParams(collective_id=4, has_side_effects=True, vmem_limit_bytes=63 << 20),
    )(att, gates, tokens, cotangent, norms, output_w, inner_w, outer_w)


def settle_kernel(count, back, experts, gates, grad_logit, tokens, joint_in, residual_in, grad_norms, part_output,
                  grad_tokens, joint_out, output_out, grads, grads_in, tokens_in, tokens_t, norms_in, norm_columns, joint, grad_residual, *refs):
    splits = (SPLITS["joint"], SPLITS["output"])
    pair_s, pair_r, load = refs[-3:]
    loads = [pltpu.make_async_copy(joint_in, joint, load.at[0]), pltpu.make_async_copy(residual_in, grad_residual, load.at[1])]
    for copy in loads:
        copy.start()
    half, output_half = JOINT // 2, part_output.shape[2]
    outs = [(joint_out, half, 0), (output_out, output_half, 0)]
    ring = Scatter(count, splits, [None, (part_output, 0)], outs, refs[:14], refs[14:-3])
    ring.start(1)
    enter(ring.neighbours())
    core = ring.core

    def remote(src, dst, i):
        return pltpu.make_async_remote_copy(src, dst, pair_s.at[i], pair_r.at[i], device_id=ring.core_mate, device_id_type=MESH)

    mine = pl.ds(pl.multiple_of(core * half, LANES), half)
    yours = pl.ds(pl.multiple_of((1 - core) * half, LANES), half)
    pair = [remote(tokens, tokens_in, 0), remote(grad_norms, norms_in, 1)]
    pair[0].start()
    pair[1].start()
    ring.open(1)
    rows = tokens.shape[0]
    lane = lax.broadcasted_iota(jnp.int32, (LANES, LANES), 1)
    width = HEADS * EXP

    def hand_over(block):
        part = pl.ds(pl.multiple_of(block * LANES, LANES), LANES)
        return remote(grads.at[part, yours], grads_in.at[part], 2 + block)


    def assemble(block, carry):
        part = pl.ds(pl.multiple_of(block * LANES, LANES), LANES)
        pieces = [back[head, which, part, :][:, :DH].astype(jnp.float32) for which in range(2) for head in range(HEADS)]
        logit = grad_logit[part, :]
        for head in range(HEADS):
            values = back[head, 2, part, :].astype(jnp.float32)
            for expert in range(EXP):
                which = head * EXP + expert
                pieces.append((values * gates[0, part, which : which + 1])[:, :DH])
                sums = jnp.sum(values * experts[which, part, :].astype(jnp.float32), axis=1, keepdims=True)
                logit = jnp.where(lane == which, sums * gates[1, part, which : which + 1], logit)
        pieces.append(jnp.where(lane < 2 * width, logit, 0.0))
        pieces.append(jnp.zeros((LANES, JOINT - ROUTERS - LANES), jnp.float32))
        grads[part, :] = jnp.concatenate(pieces, axis=1).astype(jnp.bfloat16)
        hand_over(block).start()
        return carry

    lax.fori_loop(0, rows // LANES, assemble, 0)
    ring.step(1, ring.far)
    tokens_t[:, :rows] = tokens[...].T
    for copy in pair:
        copy.wait_recv()
    tokens_t[:, rows:] = tokens_in[...].T
    norm_tile = NORM // LANES * LANES - half
    first = NORM - half - norm_tile
    both = grad_norms[...] + norms_in[...]
    for block in range(both.shape[1] // LANES):
        columns = jnp.concatenate([both[:, block * LANES : (block + 1) * LANES], jnp.zeros((LANES - 8, LANES), jnp.float32)], axis=0)
        norm_columns[block * LANES : (block + 1) * LANES, :] = columns.T
    for block in range(rows // LANES):
        hand_over(block).wait_recv()
    shard_rows = tokens_t.shape[0] // count
    tile_lane = lax.broadcasted_iota(jnp.int32, (shard_rows, LANES), 1)

    def fill(rel):
        part = pl.ds(pl.multiple_of(ring.dest(rel) * shard_rows, shard_rows), shard_rows)
        total = jnp.dot(tokens_t[part, :rows], grads[:, mine], preferred_element_type=jnp.float32)
        total = total + jnp.dot(tokens_t[part, rows:], grads_in[...], preferred_element_type=jnp.float32)
        ring.mine[0][rel] = total.astype(jnp.bfloat16)
        extra = jnp.where(tile_lane == first, norm_columns[part, 0:1], 0.0) + jnp.where(tile_lane == first + 1, norm_columns[part, 1:2], 0.0)
        tile = total[:, norm_tile : norm_tile + LANES] + extra * core.astype(jnp.float32)
        ring.mine[0][rel, :, norm_tile : norm_tile + LANES] = tile.astype(jnp.bfloat16)

    for i, rel in enumerate(ring.order()):
        fill(rel)
        if i == 0:
            ring.open(0)
    ring.step(0, ring.far)
    for D in range(ring.far - 1, 0, -1):
        ring.step(1, D)
        ring.step(0, D)
        if D == ring.far - 1:
            for copy in loads:
                copy.wait()
            grad_tokens[...] = grad_residual[...] + contract(grads[...], joint[...], 1, 1)
    ring.step(1, 0)
    ring.step(0, 0)
    ring.deliver(1)
    ring.deliver(0)
    ring.finish(1)
    ring.finish(0)
    for copy in pair:
        copy.wait_send()
    for block in range(rows // LANES):
        hand_over(block).wait_send()


def settle(count, back, experts, gates, grad_logit, tokens, joint, grad_residual, grad_norms, part_output):
    rows, width = tokens.shape
    shard_rows = width // count
    f32, bf = jnp.float32, jnp.bfloat16
    V = pltpu.VMEM
    return pl.pallas_call(
        functools.partial(settle_kernel, count),
        out_shape=[jax.ShapeDtypeStruct((rows, width), f32), jax.ShapeDtypeStruct((shard_rows, JOINT), f32),
                   jax.ShapeDtypeStruct((part_output.shape[1], width), f32)],
        in_specs=[VMEM] * 5 + [ANY, ANY, VMEM, ANY],
        out_specs=[VMEM, VMEM, ANY],
        scratch_shapes=[V((rows, JOINT), bf), V((rows, JOINT // 2), bf), V((rows, width), bf), V((width, 2 * rows), bf), V((8, width), f32), V((width, LANES), f32),
                        V((width, JOINT), bf), V((rows, width), f32)]
        + Scatter.scratch(count, (SPLITS["joint"], SPLITS["output"]), [shard_rows, part_output.shape[1]])
        + [DMA((2 + rows // LANES,)), DMA((2 + rows // LANES,)), DMA((2,))],
        compiler_params=pltpu.CompilerParams(collective_id=5, has_side_effects=True, vmem_limit_bytes=60 << 20),
    )(back, experts, gates, grad_logit, tokens, joint, grad_residual, grad_norms, part_output)


def publish_kernel(joint_w, output_w, inner_w, outer_w, layer, tokens_in,
                   query, key, value, value_router, output_router, norms, output_out, inner_out, outer_out, layer_out, tokens_out,
                   *refs):
    held, turned, tail, load, store = refs[:6], refs[6], refs[7], refs[8], refs[9]
    sources = (joint_w, tokens_in, inner_w, outer_w, layer, output_w)
    loads = [pltpu.make_async_copy(src, buf, load.at[i]) for i, (src, buf) in enumerate(zip(sources, held))]
    for copy in loads:
        copy.start()
    half, small = inner_w.shape[1] // 2, CHUNK // 2
    stores = []

    def put(src, dst):
        copy = pltpu.make_async_copy(src, dst, store.at[len(stores)])
        copy.start()
        stores.append(copy)

    for i, target in enumerate((tokens_out, inner_out, outer_out, layer_out, output_out)):
        loads[1 + i].wait()
        if i != 1:
            put(held[1 + i], target)
            continue
        for core in range(2):
            for chunk in range(half // small):
                put(held[1 + i].at[:, pl.ds(core * half + chunk * small, small)], target.at[:, pl.ds(chunk * CHUNK + core * small, small)])
    loads[0].wait()
    turned[...] = held[0][...].T
    for first, target in ((0, query), (QCOLS, key), (2 * QCOLS, value), (ROUTERS, value_router)):
        put(turned.at[pl.ds(first, target.shape[0])], target)
    tail[...] = turned[ROUTERS + HEADS * EXP : NORM, :]
    put(tail, output_router)
    norms[...] = turned[NORM : NORM + 8, :]
    for copy in stores:
        copy.wait()


def publish(joint_w, output_w, inner_w, outer_w, layer, tokens):
    rows = joint_w.shape[0]
    f32 = jnp.float32
    columns = [QCOLS, QCOLS, VCOLS, HEADS * EXP, HEADS * EXP]
    rest = (output_w, inner_w, outer_w, layer, tokens)
    return pl.pallas_call(
        publish_kernel,
        out_shape=[jax.ShapeDtypeStruct((c, rows), f32) for c in columns] + [jax.ShapeDtypeStruct((8, rows), f32)]
        + [jax.ShapeDtypeStruct(x.shape, x.dtype) for x in rest],
        in_specs=[ANY] * 6,
        out_specs=[ANY] * 5 + [VMEM] + [ANY] * 5,
        scratch_shapes=[pltpu.VMEM(x.shape, x.dtype) for x in (joint_w, tokens, inner_w, outer_w, layer, output_w)]
        + [pltpu.VMEM((JOINT, rows), f32), pltpu.VMEM((HEADS * EXP, rows), f32)]
        + [DMA((6,)), DMA((9 + inner_w.shape[1] // (CHUNK // 2),))],
        compiler_params=pltpu.CompilerParams(vmem_limit_bytes=63 << 20),
    )(joint_w, *rest)


def on_device(
    tokens, value_routes, output_routes, cont_gap, query_weight, key_weight, value_weight, value_router,
    output_router, output_weight, norm_gain, norm_bias, inner_weight, outer_weight, cotangent,
):
    count = lax.axis_size("fsdp")
    inputs = tokens[0]
    rows, width = inputs.shape
    norm = jnp.stack([norm_gain, norm_bias])
    routes = jnp.concatenate([value_routes[0].reshape(rows, -1), output_routes[0].reshape(rows, -1)], axis=1)
    joint, tables, turned, qkv, experts, gates, norms = project(
        count, query_weight.T, key_weight.T, value_weight.T, value_router.T, output_router.T, norm, inputs, routes, cont_gap)
    att, store, outputs, logs, inner_full, outer_full, output_full = attend(
        count, qkv, tables, (inner_weight, outer_weight, output_weight), (SPLITS["inner"], SPLITS["outer"], SPLITS["output"]))
    layer, grad_residual, grad_att, grad_logit, grad_norms, part_output, part_inner, outer_w = feed(
        count, att, gates, inputs, cotangent[0], norms, output_full.reshape(VCOLS, width), inner_full.reshape(width, -1),
        outer_full.reshape(-1, width))
    back, inner_w = retreat(
        count, grad_att, turned, store, outputs, logs, part_inner.reshape(count, -1, part_inner.shape[1]), INNER_PARTS)
    grad_input, joint_w, output_w = settle(
        count, back, experts, gates, grad_logit, inputs, joint, grad_residual, grad_norms,
        part_output.reshape(count, -1, part_output.shape[1]))
    query, key, value, value_r, output_r, norm_w, output_w, inner_w, outer_w, layer, grad_input = publish(
        joint_w, output_w, inner_w, outer_w, layer, grad_input)
    return (layer[None], grad_input[None], query.T, key.T, value.T, value_r.T, output_r.T, output_w, norm_w[0], norm_w[1], inner_w, outer_w)


def solution(mesh):
    wide = P("fsdp", None)
    part = P("fsdp", "seq", None)
    routes = P("fsdp", "seq", None, None)
    return jax.shard_map(
        on_device,
        mesh=mesh,
        in_specs=(part, routes, routes, P()) + (wide,) * 6 + (P("fsdp"), P("fsdp"), wide, wide, part),
        out_specs=(part, part) + (wide,) * 6 + (P("fsdp"), P("fsdp"), wide, wide),
        check_vma=False,
    )
```

```python
import functools
import jax
import jax.numpy as jnp
from jax import lax
from jax.experimental import pallas as pl
from jax.experimental.pallas import tpu as pltpu
from jax.sharding import PartitionSpec as P

HEADS = 4
DH = 112
EXP = 5
CONT = 1024
GSLOTS = 4
PSLOTS = 2
BLOCK = 512
LANES = 128
EPSILON = 1e-05
NEGATIVE = -1e30
LOG2E = 1.4426950408889634
MESH = pl.DeviceIdType.MESH
ANY = pl.BlockSpec(memory_space=pl.ANY)
VMEM = pl.BlockSpec(memory_space=pltpu.VMEM)
SMEM = pl.BlockSpec(memory_space=pltpu.SMEM)
DMA = pltpu.SemaphoreType.DMA

QCOLS = HEADS * DH
VCOLS = HEADS * EXP * DH
ROUTERS = 2 * QCOLS + VCOLS
NORM = ROUTERS + 2 * HEADS * EXP
JOINT = 3328
SPLITS = {"joint": (640, 512), "output": (256, 128), "inner": (768, 640), "outer": (256, 128)}
INNER_PARTS = ((512, 768),)


def ring_place(index, count):
    return (index // 2) * (1 - index % 2) + (count - 1 - index // 2) * (index % 2)


def ring_index(place, count):
    upper = place // (count // 2)
    return 2 * place * (1 - upper) + (2 * (count - 1 - place) + 1) * upper


def enter(devices):
    barrier = pltpu.get_barrier_semaphore()
    for device in devices:
        pl.semaphore_signal(barrier, inc=1, device_id=device, device_id_type=MESH)
    pl.semaphore_wait(barrier, len(devices))


class Ring:
    def __init__(self, count, splits):
        self.count, self.splits = count, splits
        self.seq, self.fsdp = lax.axis_index("seq"), lax.axis_index("fsdp")
        self.plane, self.core = self.seq // 2, self.seq % 2
        self.place = ring_place(self.fsdp, count)
        self.right = (self.seq, ring_index((self.place + 1) % count, count))
        self.left = (self.seq, ring_index((self.place + count - 1) % count, count))
        self.core_mate = (self.seq + 1 - 2 * self.core, self.fsdp)
        self.plane_mate = ((self.seq + 2) % 4, self.fsdp)
        self.far = count // 2

    def neighbours(self):
        return [self.right, self.left, self.core_mate, self.plane_mate]

    def reach(self, kind, way):
        return self.far if kind == way else self.count - 1 - self.far

    def kinds(self, t):
        return [kind for kind in (1, 0) if self.splits[t][kind] > 0]

    def half(self, t):
        return self.splits[t][0] + 2 * self.splits[t][1]

    def cols(self, t, kind, plane, core):
        both, single = self.splits[t]
        if kind == 0:
            return pl.ds(pl.multiple_of(core * self.half(t), LANES), both)
        return pl.ds(pl.multiple_of(core * self.half(t) + both + plane * single, LANES), single)

    def behind(self, way, k):
        step = self.count - k if way == 0 else k
        return ring_index((self.place + step) % self.count, self.count)

    def next(self, way):
        return self.right if way == 0 else self.left

    def slot(self, kind, way, k):
        return k - 1 if way == 0 else self.reach(kind, 0) + k - 1


class Gather(Ring):
    def __init__(self, count, splits, shards, at, send, recv, local):
        super().__init__(count, splits)
        self.shards, self.at, self.send, self.recv, self.local = shards, at, send, recv, local

    @staticmethod
    def sems(count, tensors):
        return [DMA((6 * tensors * (count - 1),)), DMA((6 * tensors * (count - 1),)), DMA((tensors,))]

    def copy(self, src, dst, group, t, slot, device):
        i = (group * len(self.splits) + t) * (self.count - 1) + slot
        return pltpu.make_async_remote_copy(
            src, dst, self.send.at[i], self.recv.at[i], device_id=device, device_id_type=MESH
        )

    def same(self, group, t, kind, way, k, plane, core, device):
        ref = self.at(t, self.behind(way, k), self.cols(t, kind, plane, core))
        return self.copy(ref, ref, group, t, self.slot(kind, way, k), device)

    def hop(self, t, kind, way, k):
        if k > 1:
            ref = self.at(t, self.behind(way, k - 1), self.cols(t, kind, self.plane, self.core))
            return self.copy(ref, ref, kind, t, self.slot(kind, way, k), self.next(way))
        cols = self.cols(t, kind, self.plane, self.core)
        return self.copy(
            self.shards[t].at[:, cols], self.at(t, self.fsdp, cols), kind, t, self.slot(kind, way, 1), self.next(way)
        )

    def arrived(self, t, kind, way, k):
        return self.same(kind, t, kind, way, k, self.plane, self.core, self.next(way))

    def to_core(self, t, kind, way, k, core):
        return self.same(2 + kind, t, kind, way, k, self.plane, core, self.core_mate)

    def to_plane(self, t, way, k, plane):
        return self.same(4, t, 1, way, k, plane, self.core, self.plane_mate)

    def plane_to_core(self, t, way, k, core):
        return self.same(5, t, 1, way, k, 1 - self.plane, core, self.core_mate)

    def own(self, t):
        return pltpu.make_async_copy(self.shards[t], self.at(t, self.fsdp, slice(None)), self.local.at[t])

    def start(self, t):
        for kind in self.kinds(t):
            for way in (0, 1):
                if self.reach(kind, way):
                    self.hop(t, kind, way, 1).start()
        self.own(t).start()

    def arrive(self, t, k):
        for kind in self.kinds(t):
            for way in (0, 1):
                if k <= self.reach(kind, way):
                    self.arrived(t, kind, way, k).wait_recv()
                    if k < self.reach(kind, way):
                        self.hop(t, kind, way, k + 1).start()
                    if kind:
                        self.to_plane(t, way, k, self.plane).start()
                    self.to_core(t, kind, way, k, self.core).start()

    def plane_arrive(self, t, k):
        if 1 in self.kinds(t):
            for way in (0, 1):
                if k <= self.reach(1, way):
                    self.to_plane(t, way, k, 1 - self.plane).wait_recv()
                    self.plane_to_core(t, way, k, self.core).start()

    def finish(self, t):
        self.own(t).wait()
        for kind in self.kinds(t):
            for way in (0, 1):
                for k in range(1, self.reach(kind, way) + 1):
                    self.hop(t, kind, way, k).wait_send()
                    self.to_core(t, kind, way, k, self.core).wait_send()
                    self.to_core(t, kind, way, k, 1 - self.core).wait_recv()
                    if kind:
                        self.to_plane(t, way, k, self.plane).wait_send()
                        self.plane_to_core(t, way, k, self.core).wait_send()
                        self.plane_to_core(t, way, k, 1 - self.core).wait_recv()

    def events(self):
        tensors = range(len(self.splits))
        out = []
        for k in range(1, self.far + 1):
            for t in tensors:
                out.append(functools.partial(self.arrive, t, k))
                if k > 1:
                    out.append(functools.partial(self.plane_arrive, t, k - 1))
        for t in tensors:
            out.append(functools.partial(self.plane_arrive, t, self.far))
        for t in tensors:
            out.append(functools.partial(self.finish, t))
        return out


TABLE = 5632
TABLE_ZERO = 5120
TURNED_ZERO = 512


def route_lanes(routes, lane):
    hit = None
    for head in range(2 * HEADS):
        for choice in range(2):
            place = head * EXP + routes[:, 2 * head + choice : 2 * head + choice + 1]
            here = lane == place
            hit = here if hit is None else hit | here
    return hit.astype(jnp.float32)


def project_kernel(count, query, key, value, value_router, output_router, norm, tokens, routes, gaps,
                   joint_out, tables_out, turned_out, qkv, experts, gates, norms,
                   shard, shard_t, joint, tables, turned_tables, product, load, store, send, recv, local):
    rows = shard.shape[0]
    splits = (SPLITS["joint"],)
    at = lambda t, g, cols: joint.at[pl.ds(pl.multiple_of(g * rows, rows), rows), cols]
    ring = Gather(count, splits, [shard], at, send, recv, local)
    loads = []
    for i, (src, first) in enumerate(((query, 0), (key, QCOLS), (value, 2 * QCOLS))):
        loads.append(pltpu.make_async_copy(src, shard_t.at[pl.ds(first, src.shape[0])], load.at[i]))
        loads[-1].start()
    small = [ref[...].astype(jnp.float32) for ref in (value_router, output_router, norm)]
    small.append(jnp.zeros((JOINT - NORM - 2, rows), jnp.float32))
    shard_t[ROUTERS:, :] = jnp.concatenate(small, axis=0).astype(jnp.bfloat16)
    for copy in loads:
        copy.wait()
    shard[...] = shard_t[...].T
    enter(ring.neighbours())
    ring.start(0)
    slope = jnp.float32(0.0)
    for head in range(HEADS):
        slope = jnp.where(ring.seq // 1 == head, -0.5 * 0.5**head * LOG2E, slope)
    group = ring.fsdp // GSLOTS
    pair = jnp.maximum(ring.fsdp % GSLOTS - PSLOTS, 0) * 2
    gap_values = [jnp.int32(0), gaps[group, pair], gaps[group, pair + 1]]

    def table_column(step, carry):
        start = pl.multiple_of(step * 256, 256)
        lanes = lax.broadcasted_iota(jnp.int32, (8, 256 + LANES), 1) + (start - LANES)
        for which in range(3):
            for turned in range(2):
                if turned:
                    distance = lanes - TURNED_ZERO + gap_values[which]
                else:
                    distance = TABLE_ZERO - lanes + gap_values[which]
                bias = slope * jnp.log(1.0 + jnp.maximum(distance, 0).astype(jnp.float32))
                bias = jnp.where(distance >= 0, bias, NEGATIVE)
                wide = jnp.broadcast_to(bias[:1], (LANES, 256 + LANES))
                rolled = pltpu.roll(wide, 0, 1, stride=1, stride_axis=0)
                target = turned_tables if turned else tables
                target[which, :, pl.ds(start, 256)] = rolled[:, LANES:]
        return carry

    events = []
    for k in range(1, ring.far + 1):
        events.append(functools.partial(ring.arrive, 0, k))
        if k > 1:
            events.append(functools.partial(ring.plane_arrive, 0, k - 1))
    events += [functools.partial(ring.plane_arrive, 0, ring.far), functools.partial(ring.finish, 0)]
    cut = max(1, TABLE // 256 // (len(events) - 2))
    done = 0
    saves = [(tables, tables_out), (turned_tables, turned_out), (joint, joint_out)]
    saves = [pltpu.make_async_copy(src, dst, store.at[i]) for i, (src, dst) in enumerate(saves)]
    for i, event in enumerate(events):
        upto = min(TABLE // 256, (i + 1) * cut)
        if i == len(events) - 2:
            upto = TABLE // 256
        if upto > done:
            lax.fori_loop(done, upto, table_column, 0)
            done = upto
            if done == TABLE // 256:
                saves[0].start()
                saves[1].start()
        event()
    saves[2].start()

    def column(step, carry):
        cols = pl.ds(pl.multiple_of(step * 256, 256), 256)
        product[:, cols] = jnp.dot(tokens[...], joint[:, cols], preferred_element_type=jnp.float32)
        return carry

    lax.fori_loop(0, JOINT // 256, column, 0)
    norm_tile = NORM // LANES * LANES
    turned_norm = joint[:, norm_tile : norm_tile + LANES].astype(jnp.float32).T
    norms[...] = turned_norm[NORM - norm_tile : NORM - norm_tile + 8]
    logits = product[:, ROUTERS : ROUTERS + 2 * HEADS * EXP]
    local_rows = tokens.shape[0]
    wide = jnp.concatenate([logits, jnp.zeros((local_rows, LANES - 2 * HEADS * EXP), jnp.float32)], axis=1)
    lane = lax.broadcasted_iota(jnp.int32, (local_rows, LANES), 1)
    chosen = jnp.concatenate([routes[...].astype(jnp.float32), jnp.zeros((LANES - routes.shape[0], local_rows), jnp.float32)], axis=0)
    mask = route_lanes(chosen.T.astype(jnp.int32), lane)
    gate = 1.0 / (1.0 + jnp.exp(-wide))
    gates[0] = gate * mask
    gates[1] = gate * mask * (1.0 - gate)
    pad = jnp.zeros((local_rows, LANES - DH), jnp.float32)
    ones = jnp.ones((local_rows, LANES - DH), jnp.float32)
    for head in range(HEADS):
        first = head * DH
        qkv[head, 0] = jnp.concatenate([product[:, first : first + DH], pad], axis=1).astype(jnp.bfloat16)
        first = QCOLS + head * DH
        qkv[head, 1] = jnp.concatenate([product[:, first : first + DH], pad], axis=1).astype(jnp.bfloat16)
        total = None
        for expert in range(EXP):
            which = head * EXP + expert
            first = 2 * QCOLS + which * DH
            piece = product[:, first : first + DH]
            experts[which] = jnp.concatenate([piece, pad], axis=1).astype(jnp.bfloat16)
            term = piece * gates[0, :, which : which + 1]
            total = term if total is None else total + term
        qkv[head, 2] = jnp.concatenate([total, ones], axis=1).astype(jnp.bfloat16)
    for copy in saves:
        copy.wait()


def project(count, query, key, value, value_router, output_router, norm, tokens, routes, gaps):
    rows, shard_rows = tokens.shape[0], query.shape[1]
    f32, bf = jnp.float32, jnp.bfloat16
    V = pltpu.VMEM
    return pl.pallas_call(
        functools.partial(project_kernel, count),
        out_shape=[
            jax.ShapeDtypeStruct((shard_rows * count, JOINT), bf),
            jax.ShapeDtypeStruct((3, LANES, TABLE), f32),
            jax.ShapeDtypeStruct((3, LANES, TABLE), f32),
            jax.ShapeDtypeStruct((HEADS, 3, rows, LANES), bf),
            jax.ShapeDtypeStruct((HEADS * EXP, rows, LANES), bf),
            jax.ShapeDtypeStruct((2, rows, LANES), f32),
            jax.ShapeDtypeStruct((8, shard_rows * count), f32),
        ],
        in_specs=[ANY] * 3 + [VMEM] * 5 + [SMEM],
        out_specs=[ANY] * 3 + [VMEM] * 4,
        scratch_shapes=[
            V((shard_rows, JOINT), bf), V((JOINT, shard_rows), bf), V((shard_rows * count, JOINT), bf),
            V((3, LANES, TABLE), f32), V((3, LANES, TABLE), f32), V((rows, JOINT), f32), DMA((3,)), DMA((3,)),
        ]
        + Gather.sems(count, 1),
        compiler_params=pltpu.CompilerParams(collective_id=1, has_side_effects=True, vmem_limit_bytes=62 << 20),
    )(query, key, value, value_router, output_router, norm, tokens, routes, gaps)


def seq_mates(ring):
    return [ring.core_mate, ring.plane_mate, (3 - ring.seq, ring.fsdp)]


def slot_mates(ring):
    f = ring.fsdp
    return [(ring.seq, f + 1 - 2 * (f % 2)), (ring.seq, f + 2 - 4 * ((f // 2) % 2))]


def tile_place(slot, seq, phase, key_block, query_block):
    cont = slot // PSLOTS
    own = 1 - jnp.minimum(phase, 1)
    piece = jnp.where(slot == 3, 2 - phase, phase - 1)
    source = jnp.where(phase == 0, 0, 1 + piece)
    first = cont * 2 * (query_block // 2)
    active = jnp.where(
        phase == 0,
        (key_block <= query_block) & (key_block >= first),
        jnp.where(phase == 1, slot >= 1, slot >= 2),
    )
    far_column = jnp.where(
        cont == 1,
        2048 * piece + BLOCK * key_block - BLOCK * (query_block % 2) - 4096,
        BLOCK * key_block - 2048 - BLOCK * query_block,
    )
    column = jnp.where(phase == 0, BLOCK * (key_block - query_block), far_column)
    table = jnp.where((phase > 0) & (cont == 1), 1 + query_block // 2, 0)
    return source, active, table, column


STRIP = 512


def near_first(ring, j):
    odd, high = j % 2, j // 2
    core = ring.core + odd - 2 * ring.core * odd
    plane = ring.plane + high - 2 * ring.plane * high
    return 2 * plane + core


def block_rows(block):
    return pl.ds(pl.multiple_of(block * BLOCK, BLOCK), BLOCK)


def attend_kernel(count, splits, steps, qkv, tables_in, *refs):
    T = len(splits)
    shards, refs = refs[:T], refs[T:]
    att, store, outputs, logs = refs[:4]
    fulls, refs = refs[4 : 4 + T], refs[4 + T :]
    acc, top, att_low, tables, kv_send, kv_recv, q_send, q_recv, sh_send, sh_recv, out_send, out_recv, here = refs[:13]
    at = lambda t, g, cols: fulls[t].at[g, :, cols]
    ring = Gather(count, splits, shards, at, *refs[13:])
    table_load = pltpu.make_async_copy(tables_in, tables, here.at[2])
    table_load.start()
    seq, slot = ring.seq, ring.fsdp % GSLOTS
    mates, (x_mate, z_mate) = seq_mates(ring), slot_mates(ring)
    enter(ring.neighbours() + mates[2:] + [x_mate, z_mate])

    def remote(src, dst, send, recv, device):
        return pltpu.make_async_remote_copy(src, dst, send, recv, device_id=device, device_id_type=MESH)

    mine = block_rows(seq)

    def kv_copy(mate):
        return remote(qkv.at[mate[0], pl.ds(1, 2)], store.at[pl.ds(1, 2), mine], kv_send.at[mate[0]], kv_recv.at[seq], mate)

    def q_copy(mate):
        return remote(qkv.at[mate[0], 0], store.at[0, mine], q_send.at[mate[0]], q_recv.at[seq], mate)

    for mate in mates[1:] + mates[:1]:
        kv_copy(mate).start()
    own_copy = pltpu.make_async_copy(qkv.at[seq], store.at[pl.ds(0, 3), mine], here.at[0])
    own_copy.start()
    for mate in mates[1:] + mates[:1]:
        q_copy(mate).start()
    acc[...] = jnp.zeros_like(acc)
    top[...] = jnp.full_like(top, NEGATIVE)

    def far_rows(piece, chunk):
        return store.at[pl.ds(3 + 2 * piece, 2), block_rows(near_first(ring, chunk))]

    def first_hop(chunk, way):
        src = store.at[pl.ds(1, 2), block_rows(near_first(ring, chunk))]
        piece = slot % 2
        return remote(src, far_rows(piece, chunk), sh_send.at[4 * way + chunk], sh_recv.at[4 * piece + chunk],
                      x_mate if way == 0 else z_mate)

    def second_hop(chunk):
        piece = slot % 2
        return remote(far_rows(piece, chunk), far_rows(piece, chunk), sh_send.at[8 + chunk], sh_recv.at[4 * piece + chunk], x_mate)

    def share(chunk):
        @pl.when(slot < 2)
        def _():
            first_hop(chunk, 1).start()

        @pl.when(slot == 0)
        def _():
            first_hop(chunk, 0).start()

    def pass_on(chunk):
        @pl.when(slot >= 1)
        def _():
            piece = jnp.where(slot == 3, 1, 0)
            remote(far_rows(piece, chunk), far_rows(piece, chunk), sh_send.at[chunk], sh_recv.at[4 * piece + chunk], x_mate).wait_recv()

        @pl.when(slot >= 2)
        def _():
            second_hop(chunk).start()

    def last_piece(chunk):
        @pl.when(slot >= 2)
        def _():
            piece = 3 - slot
            remote(far_rows(piece, chunk), far_rows(piece, chunk), sh_send.at[chunk], sh_recv.at[4 * piece + chunk], x_mate).wait_recv()

    own_copy.wait()
    share(0)
    for chunk, mate in enumerate(mates):
        other = mate[0]
        src = store.at[pl.ds(1, 2), block_rows(other)]
        remote(src, src, kv_send.at[other], kv_recv.at[other], mate).wait_recv()
        share(1 + chunk)
    for mate in mates:
        src = store.at[0, block_rows(mate[0])]
        remote(src, src, q_send.at[mate[0]], q_recv.at[mate[0]], mate).wait_recv()

    def tile(source, table, column, key_block, first, rows):
        keys = store[1 + 2 * source, block_rows(key_block), :]
        values = store[2 + 2 * source, block_rows(key_block), :]
        for strip in range(rows // STRIP):
            part = pl.ds(pl.multiple_of(first + strip * STRIP, STRIP), STRIP)
            scores = lax.dot_general(store[0, part, :], keys, (((1,), (1,)), ((), ())), preferred_element_type=jnp.float32)
            start = column + TABLE_ZERO - strip * STRIP
            bias = [tables[table, :, pl.ds(pl.multiple_of(start - LANES * i, LANES), BLOCK)] for i in range(STRIP // LANES)]
            scores = scores * (DH**-0.5 * LOG2E) + jnp.concatenate(bias, axis=0)
            before = top[part, :]
            after = jnp.maximum(before, jnp.max(scores, axis=1, keepdims=True))
            terms = jnp.exp2(scores - after[:, :1])
            acc[part, :] = acc[part, :] * jnp.exp2(before - after) + jnp.dot(
                terms.astype(jnp.bfloat16), values, preferred_element_type=jnp.float32)
            top[part, :] = after

    def near_tile(step):
        key_block, query_block = near_first(ring, step // 4), step % 4
        source, active, table, column = tile_place(slot, seq, 0, key_block, query_block)

        @pl.when(active)
        def _():
            tile(source, table, column, key_block, query_block * BLOCK, BLOCK)

    def far_tile(step):
        phase, key_block, query_block = step // 8, near_first(ring, (step // 2) % 4), 2 * (step % 2)
        source, active, table, column = tile_place(slot, seq, phase, key_block, query_block)

        @pl.when(active)
        def _():
            tile(source, table, column, key_block, query_block * BLOCK, 2 * BLOCK)

    table_load.wait()
    events = {}
    for chunk in range(4):
        events.setdefault(4 * chunk + 3, []).append(functools.partial(pass_on, chunk))
        events.setdefault(24 + 2 * chunk, []).append(functools.partial(last_piece, chunk))
    begin, first, gap = steps
    for t in range(T):
        if begin + t < 0:
            ring.start(t)
        else:
            events.setdefault(begin + t, []).append(functools.partial(ring.start, t))
    rest = []
    for i, event in enumerate(ring.events()):
        step = int(first + gap * i)
        if step < 32:
            events.setdefault(step, []).append(event)
        else:
            rest.append(event)

    def step_body(step, carry):
        for when, actions in sorted(events.items()):
            @pl.when(step == when)
            def _():
                for action in actions:
                    action()
        pl.when(step < 16)(lambda: near_tile(step))
        pl.when(step >= 16)(lambda: far_tile(step - 8))
        return carry

    lax.fori_loop(0, 32, step_body, 0)
    total = acc[:, DH : DH + 1]
    result = acc[...] / total
    outputs[...] = result
    log_total = top[...] + jnp.log2(total)
    for block in range(4):
        logs[:, block * BLOCK : (block + 1) * BLOCK] = log_total[block * BLOCK : (block + 1) * BLOCK].T[:8]
    att_low[...] = result.astype(jnp.bfloat16)

    def out_copy(mate):
        return remote(att_low.at[block_rows(mate[0])], att.at[seq], out_send.at[mate[0]], out_recv.at[seq], mate)

    for mate in mates[1:] + mates[:1]:
        out_copy(mate).start()
    own_out = pltpu.make_async_copy(att_low.at[mine], att.at[seq], here.at[1])
    own_out.start()
    for event in rest:
        event()
    own_out.wait()
    for mate in mates:
        kv_copy(mate).wait_send()
        q_copy(mate).wait_send()
        out_copy(mate).wait_send()
        ref = att.at[mate[0]]
        remote(ref, ref, out_send.at[mate[0]], out_recv.at[mate[0]], mate).wait_recv()
    for chunk in range(4):
        @pl.when(slot < 2)
        def _():
            first_hop(chunk, 1).wait_send()

        @pl.when(slot == 0)
        def _():
            first_hop(chunk, 0).wait_send()

        @pl.when(slot >= 2)
        def _():
            second_hop(chunk).wait_send()


def attend(count, qkv, tables, shards, splits, steps=(0, 18, 2)):
    rows = qkv.shape[2]
    own = 4 * rows
    T = len(shards)
    return pl.pallas_call(
        functools.partial(attend_kernel, count, splits, steps),
        out_shape=[
            jax.ShapeDtypeStruct((HEADS, rows, LANES), jnp.bfloat16),
            jax.ShapeDtypeStruct((7, own, LANES), jnp.bfloat16),
            jax.ShapeDtypeStruct((own, LANES), jnp.float32),
            jax.ShapeDtypeStruct((8, own), jnp.float32),
        ]
        + [jax.ShapeDtypeStruct((count,) + w.shape, w.dtype) for w in shards],
        in_specs=[VMEM, ANY] + [VMEM] * T,
        out_specs=[VMEM] * 4 + [ANY] * T,
        scratch_shapes=[
            pltpu.VMEM((own, LANES), jnp.float32),
            pltpu.VMEM((own, LANES), jnp.float32),
            pltpu.VMEM((own, LANES), jnp.bfloat16),
            pltpu.VMEM((3, LANES, TABLE), jnp.float32),
            DMA((4,)), DMA((4,)), DMA((4,)), DMA((4,)), DMA((12,)), DMA((8,)), DMA((4,)), DMA((4,)), DMA((3,)),
        ]
        + Gather.sems(count, T),
        compiler_params=pltpu.CompilerParams(collective_id=2, has_side_effects=True, vmem_limit_bytes=56 << 20),
    )(qkv, tables, *shards)


class Scatter(Ring):
    def __init__(self, count, splits, parts, outs, bufs, sems):
        super().__init__(count, splits)
        self.parts, self.outs = parts, outs
        T = len(splits)
        self.mine, self.plane_in = bufs[:T], bufs[T : 2 * T]
        self.ring0, self.ring1 = bufs[2 * T : 3 * T], bufs[3 * T : 4 * T]
        self.low, self.low_in, self.done = bufs[4 * T : 5 * T], bufs[5 * T : 6 * T], bufs[6 * T : 7 * T]
        (self.load, self.plane_s, self.plane_r, self.ring_s, self.ring_r, self.end_s, self.end_r, self.put) = sems

    @staticmethod
    def scratch(count, splits, rows):
        half = [a + 2 * b for a, b in splits]
        bf = jnp.bfloat16
        out = [pltpu.VMEM((count, r, h), bf) for r, h in zip(rows, half)]
        out += [pltpu.VMEM((count, r, b), bf) for r, (a, b) in zip(rows, splits)]
        out += [pltpu.VMEM((count - 1 if a else 1, r, max(a, LANES)), bf) for r, (a, b) in zip(rows, splits)]
        out += [pltpu.VMEM((count - 1, r, b), bf) for r, (a, b) in zip(rows, splits)]
        out += [pltpu.VMEM((r, a + b), bf) for r, (a, b) in zip(rows, splits)]
        out += [pltpu.VMEM((r, a + b), bf) for r, (a, b) in zip(rows, splits)]
        out += [pltpu.VMEM((r, h), jnp.float32) for r, h in zip(rows, half)]
        T = len(splits)
        return out + [DMA((T * count,))] * 3 + [DMA((2 * T * (count - 1),))] * 2 + [DMA((2 * T,))] * 2 + [DMA((T,))]

    def dest(self, rel):
        return ring_index((self.place + rel) % self.count, self.count)

    def load_copy(self, t, rel):
        part, first = self.parts[t]
        src = part.at[self.dest(rel), :, pl.ds(first, self.half(t))]
        return pltpu.make_async_copy(src, self.mine[t].at[rel], self.load.at[t * self.count + rel])

    def remote(self, src, dst, s, r, i, device):
        return pltpu.make_async_remote_copy(src, dst, s.at[i], r.at[i], device_id=device, device_id_type=MESH)

    def single(self, t, plane):
        both, single = self.splits[t]
        return pl.ds(pl.multiple_of(both + plane * single, LANES), single)

    def plane_copy(self, t, rel):
        src = self.mine[t].at[rel, :, self.single(t, 1 - self.plane)]
        return self.remote(src, self.plane_in[t].at[rel], self.plane_s, self.plane_r, t * self.count + rel, self.plane_mate)

    def rels(self, D):
        return sorted({D % self.count, (-D) % self.count})

    def order(self):
        out = []
        for D in range(self.far, -1, -1):
            out += self.rels(D)
        return out

    def start(self, t):
        for rel in self.order():
            self.load_copy(t, rel).start()

    def ready(self, t, rel):
        if self.parts[t]:
            self.load_copy(t, rel).wait()
        self.plane_copy(t, rel).start()

    def open(self, t):
        for rel in self.rels(self.far):
            self.ready(t, rel)

    def step(self, t, D, ahead=True):
        if ahead and D:
            for rel in self.rels(D - 1):
                self.ready(t, rel)
        self.combine(t, D)
        if D:
            self.chain(t, D)
        else:
            self.close(t)

    def buffer(self, t, kind, slot):
        if kind:
            return self.ring1[t].at[slot]
        return self.ring0[t].at[slot]

    def own_ref(self, t, kind, rel):
        if kind:
            return self.mine[t].at[rel, :, self.single(t, self.plane)]
        return self.mine[t].at[rel, :, pl.ds(0, self.splits[t][0])]

    def ring_copy(self, t, kind, way, D):
        slot = self.slot(kind, way, D)
        if D == self.reach(kind, way):
            src = self.own_ref(t, kind, D % self.count if way == 0 else (-D) % self.count)
        else:
            src = self.buffer(t, kind, self.slot(kind, way, D + 1))
        i = (2 * t + kind) * (self.count - 1) + slot
        return self.remote(src, self.buffer(t, kind, slot), self.ring_s, self.ring_r, i, self.next(way))

    def ring_wait(self, t, kind, way, D):
        slot = self.slot(kind, way, D)
        ref = self.buffer(t, kind, slot)
        i = (2 * t + kind) * (self.count - 1) + slot
        self.remote(ref, ref, self.ring_s, self.ring_r, i, self.next(way)).wait_recv()

    def combine(self, t, D):
        for rel in self.rels(D):
            self.plane_copy(t, rel).wait_send()
            ref = self.plane_in[t].at[rel]
            self.remote(ref, ref, self.plane_s, self.plane_r, t * self.count + rel, self.plane_mate).wait_recv()
            own = self.own_ref(t, 1, rel)
            own[...] = own[...] + self.plane_in[t][rel]

    def chain(self, t, D):
        for kind in self.kinds(t):
            for way in (0, 1):
                if D > self.reach(kind, way):
                    continue
                if D < self.reach(kind, way):
                    self.ring_wait(t, kind, way, D + 1)
                    rel = D % self.count if way == 0 else (-D) % self.count
                    ref = self.buffer(t, kind, self.slot(kind, way, D + 1))
                    ref[...] = ref[...] + self.own_ref(t, kind, rel)[...]
                self.ring_copy(t, kind, way, D).start()

    def end_copy(self, t):
        return self.remote(self.low[t], self.low_in[t], self.end_s, self.end_r, 2 * t, self.plane_mate)

    def close(self, t):
        both, single = self.splits[t]
        for kind in self.kinds(t):
            total = self.own_ref(t, kind, 0)[...].astype(jnp.float32)
            for way in (0, 1):
                if self.reach(kind, way):
                    self.ring_wait(t, kind, way, 1)
                    total = total + self.buffer(t, kind, self.slot(kind, way, 1))[...].astype(jnp.float32)
            if kind:
                self.low[t][:, both:] = total.astype(jnp.bfloat16)
            else:
                self.low[t][:, :both] = total.astype(jnp.bfloat16)
        self.end_copy(t).start()

    def out_ref(self, t, core):
        out, whole, first = self.outs[t]
        return out.at[:, pl.ds(pl.multiple_of(core * whole + first, LANES), self.half(t))]

    def out_copy(self, t):
        return self.remote(self.done[t], self.out_ref(t, self.core), self.end_s, self.end_r, 2 * t + 1, self.core_mate)

    def put_copy(self, t):
        return pltpu.make_async_copy(self.done[t], self.out_ref(t, self.core), self.put.at[t])

    def deliver(self, t):
        both, single = self.splits[t]
        self.end_copy(t).wait_send()
        ref = self.low_in[t]
        self.remote(ref, ref, self.end_s, self.end_r, 2 * t, self.plane_mate).wait_recv()
        if both:
            self.done[t][:, :both] = self.low[t][:, :both].astype(jnp.float32) + self.low_in[t][:, :both].astype(jnp.float32)
        if single:
            self.done[t][:, self.single(t, self.plane)] = self.low[t][:, both:].astype(jnp.float32)
            self.done[t][:, self.single(t, 1 - self.plane)] = self.low_in[t][:, both:].astype(jnp.float32)
        self.out_copy(t).start()
        self.put_copy(t).start()

    def finish(self, t):
        for kind in self.kinds(t):
            for way in (0, 1):
                for D in range(1, self.reach(kind, way) + 1):
                    self.ring_copy(t, kind, way, D).wait_send()
        self.out_copy(t).wait_send()
        self.put_copy(t).wait()
        ref = self.out_ref(t, 1 - self.core)
        self.remote(ref, ref, self.end_s, self.end_r, 2 * t + 1, self.core_mate).wait_recv()


def retreat_kernel(count, splits, steps, grad_att, turned_in, store_in, outputs, logs, part, back, out, *refs):
    T = len(splits)
    (grads, delta, grad_q, grad_kv, send_kv, kv_in0, kv_in1, low, in_send, in_recv, up_send, up_recv,
     turned, store, out_send, out_recv, here) = refs[:17]
    refs = refs[17:]
    loads = [pltpu.make_async_copy(turned_in, turned, here.at[2]), pltpu.make_async_copy(store_in, store, here.at[3])]
    for copy in loads:
        copy.start()
    halves = [a + 2 * b for a, b in splits]
    firsts = [sum(halves[:t]) for t in range(T)]
    ring = Scatter(
        count, splits, [(part, first) for first in firsts], [(out, sum(halves), first) for first in firsts],
        refs[: 7 * T], refs[7 * T :])
    seq, slot = ring.seq, ring.fsdp % GSLOTS
    mates, (x_mate, z_mate) = seq_mates(ring), slot_mates(ring)
    enter(ring.neighbours() + mates[2:] + [x_mate, z_mate])

    def remote(src, dst, send, recv, device):
        return pltpu.make_async_remote_copy(src, dst, send, recv, device_id=device, device_id_type=MESH)

    mine = block_rows(seq)

    def in_copy(mate):
        return remote(grad_att.at[mate[0]], grads.at[mine], in_send.at[mate[0]], in_recv.at[seq], mate)

    for mate in mates[1:] + mates[:1]:
        in_copy(mate).start()
    own_copy = pltpu.make_async_copy(grad_att.at[seq], grads.at[mine], here.at[0])
    own_copy.start()
    grad_q[...] = jnp.zeros_like(grad_q)
    grad_kv[...] = jnp.zeros_like(grad_kv)
    own_copy.wait()
    for mate in mates:
        ref = grads.at[block_rows(mate[0])]
        remote(ref, ref, in_send.at[mate[0]], in_recv.at[mate[0]], mate).wait_recv()
    for block in range(4):
        rows = pl.ds(block * BLOCK, BLOCK)
        sums = jnp.sum(grads[rows, :].astype(jnp.float32) * outputs[rows, :], axis=1, keepdims=True)
        delta[:, rows] = jnp.broadcast_to(sums, (BLOCK, LANES)).T[:8]

    for copy in loads:
        copy.wait()

    def tile(forward_phase, key_block, query_block, blocks):
        source, active, table, column = tile_place(slot, seq, forward_phase, key_block, query_block)

        @pl.when(active)
        def _():
            size = blocks * BLOCK
            key_rows, rows = block_rows(key_block), pl.ds(pl.multiple_of(query_block * BLOCK, BLOCK), size)
            keys, values = store[1 + 2 * source, key_rows, :], store[2 + 2 * source, key_rows, :]
            queries, tops = store[0, rows, :], grads[rows, :]
            scores = lax.dot_general(keys, queries, (((1,), (1,)), ((), ())), preferred_element_type=jnp.float32)
            bias = jnp.concatenate(
                [turned[table, :, pl.ds(pl.multiple_of(TURNED_ZERO - column - LANES * part, LANES), size)] for part in range(BLOCK // LANES)],
                axis=0,
            )
            weights = jnp.exp2(scores * (DH**-0.5 * LOG2E) + (bias - logs[:1, rows]))
            grad_weights = lax.dot_general(values, tops, (((1,), (1,)), ((), ())), preferred_element_type=jnp.float32)
            grad_scores = (weights * (grad_weights - delta[:1, rows])).astype(jnp.bfloat16)
            grad_kv[source, 1, key_rows, :] += jnp.dot(weights.astype(jnp.bfloat16), tops, preferred_element_type=jnp.float32)
            grad_kv[source, 0, key_rows, :] += jnp.dot(grad_scores, queries, preferred_element_type=jnp.float32)
            grad_q[rows, :] += lax.dot_general(grad_scores, keys, (((0,), (0,)), ((), ())), preferred_element_type=jnp.float32)

    def far_tile(step):
        phase = step // 8
        piece = jnp.where(slot == 2, 1 - phase, phase)
        tile(jnp.where(slot == 3, 2 - piece, 1 + piece), (step // 2) % 4, 2 * (step % 2), 2)

    def near_tile(step):
        tile(0, step // 4, step % 4, 1)

    scale = DH**-0.5

    def rounded(source, chunk, extra):
        rows = block_rows(chunk)
        keys = grad_kv[source, 0, rows, :] * scale
        values = grad_kv[source, 1, rows, :]
        for more in extra:
            keys = keys + more[0].astype(jnp.float32)
            values = values + more[1].astype(jnp.float32)
        return keys.astype(jnp.bfloat16), values.astype(jnp.bfloat16)

    def x_send(chunk):
        src = send_kv.at[0, :, block_rows(chunk)]
        return remote(src, kv_in0.at[:, block_rows(chunk)], up_send.at[chunk], up_recv.at[chunk], x_mate)

    def z_send(chunk):
        src = send_kv.at[1, :, block_rows(chunk)]
        return remote(src, kv_in1.at[:, block_rows(chunk)], up_send.at[4 + chunk], up_recv.at[4 + chunk], z_mate)

    def x_wait(chunk):
        ref = kv_in0.at[:, block_rows(chunk)]
        remote(ref, ref, up_send.at[chunk], up_recv.at[chunk], x_mate).wait_recv()

    def z_wait(chunk):
        ref = kv_in1.at[:, block_rows(chunk)]
        remote(ref, ref, up_send.at[4 + chunk], up_recv.at[4 + chunk], z_mate).wait_recv()

    def first_done(chunk):
        @pl.when(slot >= 1)
        def _():
            source = jnp.where(slot == 2, 2, 1)
            keys, values = rounded(source, chunk, [])
            send_kv[0, 0, block_rows(chunk), :] = keys
            send_kv[0, 1, block_rows(chunk), :] = values
            x_send(chunk).start()

    def second_done(chunk):
        @pl.when(slot >= 2)
        def _():
            x_wait(chunk)
            source = slot - 1
            keys, values = rounded(source, chunk, [kv_in0[:, block_rows(chunk), :]])
            send_kv[1, 0, block_rows(chunk), :] = keys
            send_kv[1, 1, block_rows(chunk), :] = values
            z_send(chunk).start()

    def out_copy(mate):
        src = low.at[:, block_rows(mate[0])]
        return remote(src, back.at[seq], out_send.at[mate[0]], out_recv.at[seq], mate)

    def own_done(chunk):
        rows = block_rows(chunk)
        low[0, rows, :] = (grad_q[rows, :] * scale).astype(jnp.bfloat16)

        @pl.when(slot == 0)
        def _():
            x_wait(chunk)
            z_wait(chunk)
            low[1, rows, :], low[2, rows, :] = rounded(0, chunk, [kv_in0[:, rows, :], kv_in1[:, rows, :]])

        @pl.when(slot == 1)
        def _():
            z_wait(chunk)
            low[1, rows, :], low[2, rows, :] = rounded(0, chunk, [kv_in1[:, rows, :]])

        @pl.when(slot >= 2)
        def _():
            low[1, rows, :], low[2, rows, :] = rounded(0, chunk, [])

    events = {}
    for chunk in range(4):
        events.setdefault(2 * chunk + 2, []).append(functools.partial(first_done, chunk))
        events.setdefault(10 + 2 * chunk, []).append(functools.partial(second_done, chunk))
    begin, ready, first, hop, lag = steps
    rest = []
    for t in range(T):
        plan = [(begin, functools.partial(ring.start, t)), (ready, functools.partial(ring.open, t))]
        when = first + lag * t
        for D in range(ring.far, -1, -1):
            plan.append((when, functools.partial(ring.step, t, D)))
            when += hop
        plan.append((when, functools.partial(ring.deliver, t)))
        plan.append((when + hop, functools.partial(ring.finish, t)))
        for when, event in plan:
            if when < 32:
                events.setdefault(int(when), []).append(event)
            else:
                rest.append((when, event))
    rest = [event for when, event in sorted(rest, key=lambda pair: pair[0])]

    def step_body(step, carry):
        for when, actions in sorted(events.items()):
            @pl.when(step == when)
            def _():
                for action in actions:
                    action()
        pl.when(step < 16)(lambda: far_tile(step))
        pl.when(step >= 16)(lambda: near_tile(step - 16))
        return carry

    lax.fori_loop(0, 32, step_body, 0)
    for chunk in range(4):
        own_done(chunk)
    for mate in mates[1:] + mates[:1]:
        out_copy(mate).start()
    own_out = pltpu.make_async_copy(low.at[:, mine], back.at[seq], here.at[1])
    own_out.start()
    for event in rest:
        event()
    own_out.wait()
    for mate in mates:
        in_copy(mate).wait_send()
        out_copy(mate).wait_send()
        ref = back.at[mate[0]]
        remote(ref, ref, out_send.at[mate[0]], out_recv.at[mate[0]], mate).wait_recv()
    for chunk in range(4):
        @pl.when(slot >= 1)
        def _():
            x_send(chunk).wait_send()

        @pl.when(slot >= 2)
        def _():
            z_send(chunk).wait_send()


def retreat(count, grad_att, turned, store, outputs, logs, part, splits, steps=(0, 1, 2, 3, 1)):
    rows = grad_att.shape[1]
    own = 4 * rows
    _, shard_rows, half = part.shape
    return pl.pallas_call(
        functools.partial(retreat_kernel, count, splits, steps),
        out_shape=[jax.ShapeDtypeStruct((HEADS, 3, rows, LANES), jnp.bfloat16), jax.ShapeDtypeStruct((shard_rows, 2 * half), jnp.float32)],
        in_specs=[VMEM, ANY, ANY, VMEM, VMEM, ANY],
        out_specs=[VMEM, ANY],
        scratch_shapes=[
            pltpu.VMEM((own, LANES), jnp.bfloat16),
            pltpu.VMEM((8, own), jnp.float32),
            pltpu.VMEM((own, LANES), jnp.float32),
            pltpu.VMEM((3, 2, own, LANES), jnp.float32),
            pltpu.VMEM((2, 2, own, LANES), jnp.bfloat16),
            pltpu.VMEM((2, own, LANES), jnp.bfloat16),
            pltpu.VMEM((2, own, LANES), jnp.bfloat16),
            pltpu.VMEM((3, own, LANES), jnp.bfloat16),
            DMA((4,)), DMA((4,)), DMA((8,)), DMA((8,)),
            pltpu.VMEM((3, LANES, TABLE), jnp.float32), pltpu.VMEM((7, own, LANES), jnp.bfloat16),
            DMA((4,)), DMA((4,)), DMA((4,)),
        ]
        + Scatter.scratch(count, splits, [shard_rows] * len(splits)),
        compiler_params=pltpu.CompilerParams(collective_id=3, has_side_effects=True, vmem_limit_bytes=60 << 20),
    )(grad_att, turned, store, outputs, logs, part)


CHUNK = 512


def gelu_pair(v):
    root = 0.7978845608028654
    square = v * v
    t = jnp.tanh(root * (v + 0.044715 * square * v))
    up = 0.5 * (1.0 + t)
    return v * up, up + 0.5 * v * (1.0 - t * t) * (root * (1.0 + 3.0 * 0.044715 * square))


def contract(left, right, left_axis, right_axis):
    return lax.dot_general(left, right, (((left_axis,), (right_axis,)), ((), ())), preferred_element_type=jnp.float32)


def feed_kernel(count, att, gates, tokens, cotangent, norms, output_w, inner_w, outer_w,
                layer_out, grad_residual, grad_att, grad_logit, grad_norms, part_output, part_inner, outer_out,
                w_out, w_in, w_up, acts, act_in, slopes, slope_in, scaled, scaled_in, scaled_t, cot_in, cot_t,
                acc, normed, grad_scaled, branch_low, branch_in, branch_t, att_in, gates_in,
                stage_inner, stage_output,
                load_out, load_in, load_up, pair_s, pair_r, act_s, act_r, slope_s, slope_r, put_inner, put_output, *refs):
    half = cotangent.shape[1] // 2
    ring = Scatter(count, (SPLITS["outer"],), [None], [(outer_out, half, 0)], refs[:7], refs[7:])
    core, mate = ring.core, ring.core_mate
    experts = HEADS * EXP
    chunks = inner_w.shape[1] // CHUNK
    small = CHUNK // 2
    shards = max(1, count // chunks)

    def out_load(e):
        return pltpu.make_async_copy(output_w.at[pl.ds(e * DH, DH)], w_out.at[e, pl.ds(0, DH)], load_out.at[e])

    def ffn_load(chunk, slot):
        cols = pl.ds(pl.multiple_of(chunk * CHUNK, CHUNK), CHUNK)
        return (pltpu.make_async_copy(inner_w.at[:, cols], w_in.at[slot], load_in.at[slot]),
                pltpu.make_async_copy(outer_w.at[cols], w_up.at[slot], load_up.at[slot]))

    def chunk_of(step):
        if count != chunks:
            return step
        D = ring.far - (step + 1) // 2
        odd = step % 2
        return ring.dest((odd * D + (1 - odd) * (count - D)) % count)

    for e in range(experts):
        out_load(e).start()
    for sub in range(2):
        for copy in ffn_load(chunk_of(sub), sub):
            copy.start()
    enter(ring.neighbours())

    def remote(src, dst, send, recv):
        return pltpu.make_async_remote_copy(src, dst, send, recv, device_id=mate, device_id_type=MESH)

    mine = pl.ds(pl.multiple_of(core * half, LANES), half)
    yours = pl.ds(pl.multiple_of((1 - core) * half, LANES), half)
    pair = [
        remote(att, att_in, pair_s.at[0], pair_r.at[0]),
        remote(gates.at[0], gates_in, pair_s.at[1], pair_r.at[1]),
        remote(cotangent.at[:, yours], cot_in, pair_s.at[2], pair_r.at[2]),
        remote(scaled, scaled_in, pair_s.at[3], pair_r.at[3]),
        remote(branch_low.at[:, yours], branch_in, pair_s.at[4], pair_r.at[4]),
    ]
    for copy in pair[:3]:
        copy.start()

    def mixed_pair(att_ref, gate, two):
        tiles = []
        for which in (2 * two, 2 * two + 1):
            column = gate[:, experts + which : experts + which + 1]
            tiles.append((att_ref[which // EXP].astype(jnp.float32) * column).astype(jnp.bfloat16))
        return jnp.concatenate(tiles, axis=1)

    w_out[:, DH:, :] = jnp.zeros((experts, LANES - DH, w_out.shape[2]), jnp.bfloat16)
    acc[...] = tokens[...].astype(jnp.float32)
    for two in range(experts // 2):
        out_load(2 * two).wait()
        out_load(2 * two + 1).wait()
        weights = w_out[2 * two : 2 * two + 2].reshape(2 * LANES, w_out.shape[2])
        acc[...] += jnp.dot(mixed_pair(att, gates.at[0], two), weights, preferred_element_type=jnp.float32)
    residual = acc[...]
    centred = residual - jnp.mean(residual, axis=1, keepdims=True)
    inverse = lax.rsqrt(jnp.mean(centred * centred, axis=1, keepdims=True) + EPSILON)
    normed[...] = centred * inverse
    scaled[...] = (normed[...] * norms[:1] + norms[1:2]).astype(jnp.bfloat16)
    pair[3].start()
    rows = tokens.shape[0]
    scaled_t[:, :rows] = scaled[...].T
    cot_t[:, :rows] = cotangent[:, mine].T
    grad_scaled[...] = jnp.zeros_like(grad_scaled)
    pair[2].wait_recv()
    cot_t[:, rows:] = cot_in[...].T
    pair[3].wait_recv()
    scaled_t[:, rows:] = scaled_in[...].T

    small_mine = pl.ds(pl.multiple_of(core * small, LANES), small)
    small_yours = pl.ds(pl.multiple_of((1 - core) * small, LANES), small)

    def act_copy(step, sub):
        return remote(acts.at[sub], act_in.at[step], act_s.at[sub], act_r.at[step])

    def slope_copy(step, sub):
        return remote(slopes.at[sub, :, small_yours], slope_in.at[step], slope_s.at[sub], slope_r.at[step])

    def put_inner_copy(step, sub):
        cols = pl.ds(pl.multiple_of(chunk_of(step) * small, small), small)
        return pltpu.make_async_copy(stage_inner.at[sub], part_inner.at[:, cols], put_inner.at[sub])

    def forward_backward(step, sub):
        for copy in ffn_load(chunk_of(step), sub):
            copy.wait()

        @pl.when(step > 1)
        def _():
            act_copy(step, sub).wait_send()
            slope_copy(step, sub).wait_send()

        act, slope = gelu_pair(jnp.dot(scaled[...], w_in[sub], preferred_element_type=jnp.float32))
        acts[sub] = act.astype(jnp.bfloat16)
        act_copy(step, sub).start()
        slopes[sub] = (contract(cotangent[...], w_up[sub], 1, 1) * slope).astype(jnp.bfloat16)
        slope_copy(step, sub).start()
        acc[...] += jnp.dot(acts[sub], w_up[sub], preferred_element_type=jnp.float32)
        grad_scaled[...] += contract(slopes[sub], w_in[sub], 1, 1)

        @pl.when(step + 2 < chunks)
        def _():
            for copy in ffn_load(chunk_of(step + 2), sub):
                copy.start()

    def weight_parts(step, sub):
        remote(act_in.at[step], act_in.at[step], act_s.at[sub], act_r.at[step]).wait_recv()
        total = jnp.dot(cot_t[:, :rows], acts[sub], preferred_element_type=jnp.float32)
        total = total + jnp.dot(cot_t[:, rows:], act_in[step], preferred_element_type=jnp.float32)
        turned = total.astype(jnp.bfloat16).T
        shard_rows = CHUNK // shards
        for q in range(shards):
            rel = (ring_place(chunk_of(step) * shards + q, count) - ring.place + count) % count
            ring.mine[0][rel] = turned[q * shard_rows : (q + 1) * shard_rows]
        remote(slope_in.at[step], slope_in.at[step], slope_s.at[sub], slope_r.at[step]).wait_recv()

        @pl.when(step > 1)
        def _():
            put_inner_copy(step, sub).wait()

        total = jnp.dot(scaled_t[:, :rows], slopes[sub, :, small_mine], preferred_element_type=jnp.float32)
        total = total + jnp.dot(scaled_t[:, rows:], slope_in[step], preferred_element_type=jnp.float32)
        stage_inner[sub] = total.astype(jnp.bfloat16)
        put_inner_copy(step, sub).start()

    events = {}
    if count == chunks:
        for step, rel in enumerate(ring.order()):
            events.setdefault(step, []).append(functools.partial(ring.ready, 0, rel))
        for D in range(ring.far, 0, -1):
            events.setdefault(2 * (ring.far - D) + 1, []).append(functools.partial(ring.step, 0, D, False))

    def after_parts(step):
        for when, actions in sorted(events.items()):
            @pl.when(step == when)
            def _():
                for action in actions:
                    action()

    def iteration(i, carry):
        forward_backward(2 * i, 0)

        @pl.when(i > 0)
        def _():
            weight_parts(2 * i - 1, 1)
            after_parts(2 * i - 1)

        forward_backward(2 * i + 1, 1)
        weight_parts(2 * i, 0)
        after_parts(2 * i)
        return carry

    lax.fori_loop(0, chunks // 2, iteration, 0)
    weight_parts(chunks - 1, 1)
    if count == chunks:
        for action in events[chunks - 1]:
            action()
    else:
        ring.open(0)
        for D in range(ring.far, 0, -1):
            ring.step(0, D)
    layer_out[...] = acc[...].astype(jnp.bfloat16)
    slope = grad_scaled[...]
    grad_norms[...] = jnp.concatenate(
        [jnp.sum(slope * normed[...], axis=0, keepdims=True), jnp.sum(slope, axis=0, keepdims=True),
         jnp.zeros((6, slope.shape[1]), jnp.float32)], axis=0)
    slope = slope * norms[:1]
    total = cotangent[...].astype(jnp.float32) + inverse * (
        slope - jnp.mean(slope, axis=1, keepdims=True)
        - normed[...] * jnp.mean(slope * normed[...], axis=1, keepdims=True))
    grad_residual[...] = total
    branch_low[...] = total.astype(jnp.bfloat16)
    pair[4].start()
    branch_t[:, :rows] = branch_low[:, mine].T
    lane = lax.broadcasted_iota(jnp.int32, (rows, LANES), 1)
    logit = jnp.zeros((rows, LANES), jnp.float32)
    head_total = None
    for which in range(experts):
        if which % 2 == 0:
            weights = w_out[which : which + 2].reshape(2 * LANES, w_out.shape[2])
            both = contract(branch_low[...], weights, 1, 1)
        grad_mixed = both[:, which % 2 * LANES : (which % 2 + 1) * LANES]
        head, expert = which // EXP, which % EXP
        column = slice(experts + which, experts + which + 1)
        term = grad_mixed * gates[0, :, column]
        head_total = term if expert == 0 else head_total + term
        if expert == EXP - 1:
            grad_att[head] = head_total.astype(jnp.bfloat16)
        sums = jnp.sum(grad_mixed * att[head].astype(jnp.float32), axis=1, keepdims=True)
        logit = jnp.where(lane == experts + which, sums, logit)
    grad_logit[...] = logit * gates[1]
    ring.step(0, 0)
    pair[0].wait_recv()
    pair[1].wait_recv()
    pair[4].wait_recv()
    branch_t[:, rows:] = branch_in[...].T

    def put_output_copy(which):
        return pltpu.make_async_copy(stage_output.at[which % 4, pl.ds(0, DH)], part_output.at[pl.ds(which * DH, DH)], put_output.at[which % 4])

    for two in range(experts // 2):
        total = jnp.dot(branch_t[:, :rows], mixed_pair(att, gates.at[0], two), preferred_element_type=jnp.float32)
        total = total + jnp.dot(branch_t[:, rows:], mixed_pair(att_in, gates_in, two), preferred_element_type=jnp.float32)
        turned = total.astype(jnp.bfloat16).T
        for side in range(2):
            which = 2 * two + side
            if which >= 4:
                put_output_copy(which - 4).wait()
            stage_output[which % 4] = turned[side * LANES : (side + 1) * LANES]
            put_output_copy(which).start()
    ring.deliver(0)
    for which in range(experts - 4, experts):
        put_output_copy(which).wait()
    for sub in range(2):
        put_inner_copy(sub, sub).wait()
        act_copy(sub, sub).wait_send()
        slope_copy(sub, sub).wait_send()
    ring.finish(0)
    for copy in pair:
        copy.wait_send()


def feed(count, att, gates, tokens, cotangent, norms, output_w, inner_w, outer_w):
    rows, width = tokens.shape
    wide = inner_w.shape[1]
    half = width // 2
    f32, bf = jnp.float32, jnp.bfloat16
    experts, chunks = HEADS * EXP, wide // CHUNK
    V = pltpu.VMEM
    return pl.pallas_call(
        functools.partial(feed_kernel, count),
        out_shape=[
            jax.ShapeDtypeStruct((rows, width), bf),
            jax.ShapeDtypeStruct((rows, width), f32),
            jax.ShapeDtypeStruct((HEADS, rows, LANES), bf),
            jax.ShapeDtypeStruct((rows, LANES), f32),
            jax.ShapeDtypeStruct((8, width), f32),
            jax.ShapeDtypeStruct((VCOLS, half), bf),
            jax.ShapeDtypeStruct((width, wide // 2), bf),
            jax.ShapeDtypeStruct((wide // count, width), f32),
        ],
        in_specs=[VMEM] * 5 + [ANY] * 3,
        out_specs=[VMEM] * 5 + [ANY] * 3,
        scratch_shapes=[
            V((experts, LANES, width), bf), V((2, width, CHUNK), bf), V((2, CHUNK, width), bf),
            V((2, rows, CHUNK), bf), V((chunks, rows, CHUNK), bf), V((2, rows, CHUNK), bf), V((chunks, rows, CHUNK // 2), bf),
            V((rows, width), bf), V((rows, width), bf), V((width, 2 * rows), bf), V((rows, half), bf), V((half, 2 * rows), bf),
            V((rows, width), f32), V((rows, width), f32), V((rows, width), f32),
            V((rows, width), bf), V((rows, half), bf), V((half, 2 * rows), bf), V((HEADS, rows, LANES), bf), V((rows, LANES), f32),
            V((2, width, CHUNK // 2), bf), V((4, LANES, half), bf),
            DMA((experts,)), DMA((2,)), DMA((2,)), DMA((5,)), DMA((5,)), DMA((2,)), DMA((chunks,)), DMA((2,)), DMA((chunks,)),
            DMA((2,)), DMA((4,)),
        ]
        + Scatter.scratch(count, (SPLITS["outer"],), [wide // count]),
        compiler_params=pltpu.CompilerParams(collective_id=4, has_side_effects=True, vmem_limit_bytes=63 << 20),
    )(att, gates, tokens, cotangent, norms, output_w, inner_w, outer_w)


def settle_kernel(count, back, experts, gates, grad_logit, tokens, joint_in, residual_in, grad_norms, part_output,
                  grad_tokens, joint_out, output_out, grads, grads_in, tokens_in, tokens_t, norms_in, norm_columns, joint, grad_residual, *refs):
    splits = (SPLITS["joint"], SPLITS["output"])
    pair_s, pair_r, load = refs[-3:]
    loads = [pltpu.make_async_copy(joint_in, joint, load.at[0]), pltpu.make_async_copy(residual_in, grad_residual, load.at[1])]
    for copy in loads:
        copy.start()
    half, output_half = JOINT // 2, part_output.shape[2]
    outs = [(joint_out, half, 0), (output_out, output_half, 0)]
    ring = Scatter(count, splits, [None, (part_output, 0)], outs, refs[:14], refs[14:-3])
    ring.start(1)
    enter(ring.neighbours())
    core = ring.core

    def remote(src, dst, i):
        return pltpu.make_async_remote_copy(src, dst, pair_s.at[i], pair_r.at[i], device_id=ring.core_mate, device_id_type=MESH)

    mine = pl.ds(pl.multiple_of(core * half, LANES), half)
    yours = pl.ds(pl.multiple_of((1 - core) * half, LANES), half)
    pair = [remote(tokens, tokens_in, 0), remote(grad_norms, norms_in, 1)]
    pair[0].start()
    pair[1].start()
    ring.open(1)
    rows = tokens.shape[0]
    lane = lax.broadcasted_iota(jnp.int32, (LANES, LANES), 1)
    width = HEADS * EXP

    def hand_over(block):
        part = pl.ds(pl.multiple_of(block * LANES, LANES), LANES)
        return remote(grads.at[part, yours], grads_in.at[part], 2 + block)


    def assemble(block, carry):
        part = pl.ds(pl.multiple_of(block * LANES, LANES), LANES)
        pieces = [back[head, which, part, :][:, :DH].astype(jnp.float32) for which in range(2) for head in range(HEADS)]
        logit = grad_logit[part, :]
        for head in range(HEADS):
            values = back[head, 2, part, :].astype(jnp.float32)
            for expert in range(EXP):
                which = head * EXP + expert
                pieces.append((values * gates[0, part, which : which + 1])[:, :DH])
                sums = jnp.sum(values * experts[which, part, :].astype(jnp.float32), axis=1, keepdims=True)
                logit = jnp.where(lane == which, sums * gates[1, part, which : which + 1], logit)
        pieces.append(jnp.where(lane < 2 * width, logit, 0.0))
        pieces.append(jnp.zeros((LANES, JOINT - ROUTERS - LANES), jnp.float32))
        grads[part, :] = jnp.concatenate(pieces, axis=1).astype(jnp.bfloat16)
        hand_over(block).start()
        return carry

    split = rows // LANES // 2
    lax.fori_loop(0, split, assemble, 0)
    ring.step(1, ring.far)
    lax.fori_loop(split, rows // LANES, assemble, 0)
    tokens_t[:, :rows] = tokens[...].T
    for copy in pair:
        copy.wait_recv()
    tokens_t[:, rows:] = tokens_in[...].T
    norm_tile = NORM // LANES * LANES - half
    first = NORM - half - norm_tile
    both = grad_norms[...] + norms_in[...]
    for block in range(both.shape[1] // LANES):
        columns = jnp.concatenate([both[:, block * LANES : (block + 1) * LANES], jnp.zeros((LANES - 8, LANES), jnp.float32)], axis=0)
        norm_columns[block * LANES : (block + 1) * LANES, :] = columns.T
    for block in range(rows // LANES):
        hand_over(block).wait_recv()
    shard_rows = tokens_t.shape[0] // count
    tile_lane = lax.broadcasted_iota(jnp.int32, (shard_rows, LANES), 1)

    def fill(rel):
        part = pl.ds(pl.multiple_of(ring.dest(rel) * shard_rows, shard_rows), shard_rows)
        total = jnp.dot(tokens_t[part, :rows], grads[:, mine], preferred_element_type=jnp.float32)
        total = total + jnp.dot(tokens_t[part, rows:], grads_in[...], preferred_element_type=jnp.float32)
        ring.mine[0][rel] = total.astype(jnp.bfloat16)
        extra = jnp.where(tile_lane == first, norm_columns[part, 0:1], 0.0) + jnp.where(tile_lane == first + 1, norm_columns[part, 1:2], 0.0)
        tile = total[:, norm_tile : norm_tile + LANES] + extra * core.astype(jnp.float32)
        ring.mine[0][rel, :, norm_tile : norm_tile + LANES] = tile.astype(jnp.bfloat16)

    for i, rel in enumerate(ring.order()):
        fill(rel)
        if i == 0:
            ring.open(0)
    if ring.far > 1:
        ring.step(1, ring.far - 1)
    ring.step(0, ring.far)
    for copy in loads:
        copy.wait()
    for D in range(ring.far - 1, 0, -1):
        ring.step(1, D - 1)
        ring.step(0, D)
        if D == ring.far - 1:
            grad_tokens[...] = grad_residual[...] + contract(grads[...], joint[...], 1, 1)
    ring.deliver(1)
    ring.step(0, 0)
    ring.deliver(0)
    ring.finish(1)
    ring.finish(0)
    for copy in pair:
        copy.wait_send()
    for block in range(rows // LANES):
        hand_over(block).wait_send()


def settle(count, back, experts, gates, grad_logit, tokens, joint, grad_residual, grad_norms, part_output):
    rows, width = tokens.shape
    shard_rows = width // count
    f32, bf = jnp.float32, jnp.bfloat16
    V = pltpu.VMEM
    return pl.pallas_call(
        functools.partial(settle_kernel, count),
        out_shape=[jax.ShapeDtypeStruct((rows, width), f32), jax.ShapeDtypeStruct((shard_rows, JOINT), f32),
                   jax.ShapeDtypeStruct((part_output.shape[1], width), f32)],
        in_specs=[VMEM] * 5 + [ANY, ANY, VMEM, ANY],
        out_specs=[VMEM, VMEM, ANY],
        scratch_shapes=[V((rows, JOINT), bf), V((rows, JOINT // 2), bf), V((rows, width), bf), V((width, 2 * rows), bf), V((8, width), f32), V((width, LANES), f32),
                        V((width, JOINT), bf), V((rows, width), f32)]
        + Scatter.scratch(count, (SPLITS["joint"], SPLITS["output"]), [shard_rows, part_output.shape[1]])
        + [DMA((2 + rows // LANES,)), DMA((2 + rows // LANES,)), DMA((2,))],
        compiler_params=pltpu.CompilerParams(collective_id=5, has_side_effects=True, vmem_limit_bytes=60 << 20),
    )(back, experts, gates, grad_logit, tokens, joint, grad_residual, grad_norms, part_output)


def publish_kernel(joint_w, output_w, inner_w, outer_w, layer, tokens_in,
                   query, key, value, value_router, output_router, norms, output_out, inner_out, outer_out, layer_out, tokens_out,
                   *refs):
    held, turned, tail, load, store = refs[:6], refs[6], refs[7], refs[8], refs[9]
    sources = (joint_w, tokens_in, inner_w, outer_w, layer, output_w)
    loads = [pltpu.make_async_copy(src, buf, load.at[i]) for i, (src, buf) in enumerate(zip(sources, held))]
    for copy in loads:
        copy.start()
    half, small = inner_w.shape[1] // 2, CHUNK // 2
    stores = []

    def put(src, dst):
        copy = pltpu.make_async_copy(src, dst, store.at[len(stores)])
        copy.start()
        stores.append(copy)

    for i, target in enumerate((tokens_out, inner_out, outer_out, layer_out, output_out)):
        loads[1 + i].wait()
        if i != 1:
            put(held[1 + i], target)
            continue
        for core in range(2):
            for chunk in range(half // small):
                put(held[1 + i].at[:, pl.ds(core * half + chunk * small, small)], target.at[:, pl.ds(chunk * CHUNK + core * small, small)])
    loads[0].wait()
    turned[...] = held[0][...].T
    for first, target in ((0, query), (QCOLS, key), (2 * QCOLS, value), (ROUTERS, value_router)):
        put(turned.at[pl.ds(first, target.shape[0])], target)
    tail[...] = turned[ROUTERS + HEADS * EXP : NORM, :]
    put(tail, output_router)
    norms[...] = turned[NORM : NORM + 8, :]
    for copy in stores:
        copy.wait()


def publish(joint_w, output_w, inner_w, outer_w, layer, tokens):
    rows = joint_w.shape[0]
    f32 = jnp.float32
    columns = [QCOLS, QCOLS, VCOLS, HEADS * EXP, HEADS * EXP]
    rest = (output_w, inner_w, outer_w, layer, tokens)
    return pl.pallas_call(
        publish_kernel,
        out_shape=[jax.ShapeDtypeStruct((c, rows), f32) for c in columns] + [jax.ShapeDtypeStruct((8, rows), f32)]
        + [jax.ShapeDtypeStruct(x.shape, x.dtype) for x in rest],
        in_specs=[ANY] * 6,
        out_specs=[ANY] * 5 + [VMEM] + [ANY] * 5,
        scratch_shapes=[pltpu.VMEM(x.shape, x.dtype) for x in (joint_w, tokens, inner_w, outer_w, layer, output_w)]
        + [pltpu.VMEM((JOINT, rows), f32), pltpu.VMEM((HEADS * EXP, rows), f32)]
        + [DMA((6,)), DMA((9 + inner_w.shape[1] // (CHUNK // 2),))],
        compiler_params=pltpu.CompilerParams(vmem_limit_bytes=63 << 20),
    )(joint_w, *rest)


def on_device(
    tokens, value_routes, output_routes, cont_gap, query_weight, key_weight, value_weight, value_router,
    output_router, output_weight, norm_gain, norm_bias, inner_weight, outer_weight, cotangent,
):
    count = lax.axis_size("fsdp")
    inputs = tokens[0]
    rows, width = inputs.shape
    norm = jnp.stack([norm_gain, norm_bias])
    routes = jnp.concatenate([r[0].transpose(1, 2, 0).reshape(-1, rows) for r in (value_routes, output_routes)], axis=0)
    joint, tables, turned, qkv, experts, gates, norms = project(
        count, query_weight.T, key_weight.T, value_weight.T, value_router.T, output_router.T, norm, inputs, routes, cont_gap)
    att, store, outputs, logs, inner_full, outer_full, output_full = attend(
        count, qkv, tables, (inner_weight, outer_weight, output_weight), (SPLITS["inner"], SPLITS["outer"], SPLITS["output"]))
    layer, grad_residual, grad_att, grad_logit, grad_norms, part_output, part_inner, outer_w = feed(
        count, att, gates, inputs, cotangent[0], norms, output_full.reshape(VCOLS, width), inner_full.reshape(width, -1),
        outer_full.reshape(-1, width))
    back, inner_w = retreat(
        count, grad_att, turned, store, outputs, logs, part_inner.reshape(count, -1, part_inner.shape[1]), INNER_PARTS)
    grad_input, joint_w, output_w = settle(
        count, back, experts, gates, grad_logit, inputs, joint, grad_residual, grad_norms,
        part_output.reshape(count, -1, part_output.shape[1]))
    query, key, value, value_r, output_r, norm_w, output_w, inner_w, outer_w, layer, grad_input = publish(
        joint_w, output_w, inner_w, outer_w, layer, grad_input)
    return (layer[None], grad_input[None], query.T, key.T, value.T, value_r.T, output_r.T, output_w, norm_w[0], norm_w[1], inner_w, outer_w)


def solution(mesh):
    wide = P("fsdp", None)
    part = P("fsdp", "seq", None)
    routes = P("fsdp", "seq", None, None)
    return jax.shard_map(
        on_device,
        mesh=mesh,
        in_specs=(part, routes, routes, P()) + (wide,) * 6 + (P("fsdp"), P("fsdp"), wide, wide, part),
        out_specs=(part, part) + (wide,) * 6 + (P("fsdp"), P("fsdp"), wide, wide),
        check_vma=False,
    )
```
